32 devices in a mesh: fsdp: 4 (over z), rep: 8 (over y, x, core).
Axes of the slice: x: 2, y: 2, z: 4, core: 2. Of those that a mesh axis runs over, the one named last changes fastest.
Arguments:
- tokens: bfloat16 [8, 2048, 768], P('rep', 'fsdp'), may hold values from -6 to 6
- attention_gain: bfloat16 [768], P('fsdp'), may hold values from 0.25 to 1.75
- projection_in: bfloat16 [768, 2304], P('fsdp'), may hold values from -0.21875 to 0.21875
- attention_out: bfloat16 [768, 768], P('fsdp'), may hold values from -6 to 6
- feedforward_gain: bfloat16 [768], P('fsdp'), may hold values from 0.25 to 1.75
- expansion: bfloat16 [768, 2304], P('fsdp'), may hold values from -0.21875 to 0.21875
- contraction: bfloat16 [1152, 768], P('fsdp'), may hold values from -0.1875 to 0.1875
- cotangent: bfloat16 [8, 2048, 768], P('rep', 'fsdp'), may hold values from -6 to 6
Outputs:
- block_output: bfloat16 [8, 2048, 768], P('rep', 'fsdp')
- token_grad: float32 [8, 2048, 768], P('rep', 'fsdp')
- attention_gain_grad: float32 [768], P('fsdp')
- projection_in_grad: float32 [768, 2304], P('fsdp')
- attention_out_grad: float32 [768, 768], P('fsdp')
- feedforward_gain_grad: float32 [768], P('fsdp')
- expansion_grad: float32 [768, 2304], P('fsdp')
- contraction_grad: float32 [1152, 768], P('fsdp')
The draws below stay inside these ranges and needn't reach their ends.
All inputs are finite; a program needn't handle non-finite values.
Results may differ from the reference program's by a relative error of at most 0.018.
Values may be sent and summed in bfloat16 or wider, within the bound.
No kernel may reach another device: no remote copies, remote signals or barrier semaphores. Data moves between devices by JAX's collectives and lax.ppermute only.
A program may use at most 128 MiB of HBM per device.

```python
import math
import jax
import jax.numpy as jnp
from jax import lax

D = 768
HEADS = 12
HEAD_DIM = 64
FF = 1152
SEQ_LEN = 2048
SEQS = 8


def block_scale(own_key, dims, pieces, least, largest):
    def one(dim, blocks):
        steps = jax.random.uniform(jax.random.fold_in(jax.random.fold_in(own_key, 6), dim), (blocks,), jnp.float32, least / len(pieces), largest / len(pieces))
        return jnp.repeat(jnp.exp(steps), dims[dim] // blocks).reshape((-1,) + (1,) * (len(dims) - dim - 1))

    level = one(*pieces[0])
    for cut in pieces[1:]:
        level = level * one(*cut)
    return level


def noise(key, shape, scale, reach, pieces=(), kind=jnp.bfloat16):
    factor_of = block_scale(key, shape, pieces, -0.22, 0.18) if pieces else 1.0
    array = jax.random.normal(key, shape, jnp.float32) * scale * factor_of
    return jnp.minimum(jnp.maximum(array, -reach), reach).astype(kind)


def setup_inputs(seed: int = 0) -> dict:
    streams_of = jax.random.split(jax.random.key(seed), 9)
    return {
        "tokens": noise(streams_of[0], (SEQS, SEQ_LEN, D), 1.0, 6.0, ((0, 8), (1, 4))),
        "attention_gain": jnp.clip(1.0 + 0.15 * jax.random.normal(streams_of[1], (D,), jnp.float32), 0.25, 1.75).astype(jnp.bfloat16),
        "projection_in": noise(streams_of[2], (D, 3 * D), D ** -0.5, 0.21875, ((0, 4),)),
        "attention_out": noise(streams_of[3], (D, D), (3 * D / SEQ_LEN) ** -0.5, 6.0, ((0, 4),)),
        "feedforward_gain": jnp.clip(1.0 + 0.15 * jax.random.normal(streams_of[4], (D,), jnp.float32), 0.25, 1.75).astype(jnp.bfloat16),
        "expansion": noise(streams_of[5], (D, 2 * FF), D ** -0.5, 0.21875, ((0, 4),)),
        "contraction": noise(streams_of[6], (FF, D), FF ** -0.5, 0.1875, ((0, 4),)),
        "cotangent": noise(streams_of[7], (SEQS, SEQ_LEN, D), 1.0, 6.0, ((0, 8), (1, 4))),
    }


@jax.custom_vjp
def low(v):
    return lax.optimization_barrier(v.astype(jnp.bfloat16)).astype(jnp.float32)

@jax.custom_vjp
def low_back(v):
    return v

def low_keep(v):
    return (low(v), None)

def low_pass(kept, grad):
    return (grad,)

def back_keep(v):
    return (v, None)

def back_low(kept, grad):
    return (low(grad),)
low.defvjp(low_keep, low_pass)
low_back.defvjp(back_keep, back_low)
EPS = 1e-05
THETA = 160000.0
HIGH = lax.Precision.HIGHEST

def layer_norm(values, gain):
    centre = values - lax.optimization_barrier(jnp.mean(values, axis=-1, keepdims=True))
    spread = lax.optimization_barrier(jnp.mean(centre * centre, axis=-1, keepdims=True))
    return centre * lax.rsqrt(spread + EPS) * gain

def rotary_tables(count, offset):
    half = HEAD_DIM // 2
    freqs = THETA ** (-(jnp.arange(half, dtype=jnp.float32) * (2.0 / HEAD_DIM)))
    places = (offset + jnp.arange(count, dtype=jnp.int32)).astype(jnp.float32)
    angles = places[:, None] * freqs[None, :]
    return (jnp.cos(angles), jnp.sin(angles))

def rotate(values, cosine, sine):
    count = values.shape[0]
    half = HEAD_DIM // 2
    shaped = values.reshape(count, -1, HEAD_DIM)
    first = shaped[..., :half]
    second = shaped[..., half:]
    cos_three = cosine[:, None, :]
    sin_three = sine[:, None, :]
    turned = jnp.concatenate([first * cos_three - second * sin_three, second * cos_three + first * sin_three], axis=-1)
    return turned.reshape(count, -1)

def geglu(inner):
    width = inner.shape[-1] // 2
    return jax.nn.gelu(inner[:, :width], approximate=False) * inner[:, width:]

def heads_first(values):
    return values.reshape(values.shape[0], HEADS, HEAD_DIM).transpose(1, 0, 2)

def rows_first(values):
    return values.transpose(1, 0, 2).reshape(values.shape[1], -1)

def forward(tokens, attention_gain, projection_in, attention_out, feedforward_gain, expansion, contraction):
    cosine, sine = rotary_tables(SEQ_LEN, 0)
    scale = 1.0 / math.sqrt(HEAD_DIM)

    def one_head(parts):
        queries, keys, values = parts
        scores = low_back(jnp.dot(queries, keys.T, precision=HIGH) * scale)
        return jnp.dot(low(jax.nn.softmax(scores, axis=-1)), values, precision=HIGH)

    def sequence(carry, block):
        normed = low(layer_norm(block, attention_gain))
        projected = low_back(jnp.dot(normed, projection_in, precision=HIGH))
        turned = low(rotate(projected[:, :2 * D], cosine, sine))
        values = low(projected[:, 2 * D:])
        mixed = lax.map(jax.checkpoint(one_head), (heads_first(turned[:, :D]), heads_first(turned[:, D:]), heads_first(values)))
        merged = low_back(low(rows_first(mixed)))
        state = block + low_back(jnp.dot(merged, attention_out, precision=HIGH))
        normed_two = low(layer_norm(state, feedforward_gain))
        inner = low_back(jnp.dot(normed_two, expansion, precision=HIGH))
        active = low_back(low(geglu(inner)))
        return (carry, state + jnp.dot(active, contraction, precision=HIGH))
    _, result = lax.scan(jax.checkpoint(sequence), jnp.zeros((), jnp.float32), tokens)
    return result

def reference(tokens, attention_gain, projection_in, attention_out, feedforward_gain, expansion, contraction, cotangent):
    inputs = (tokens.astype(jnp.float32), attention_gain.astype(jnp.float32), projection_in.astype(jnp.float32), attention_out.astype(jnp.float32), feedforward_gain.astype(jnp.float32), expansion.astype(jnp.float32), contraction.astype(jnp.float32))
    result, pullback = jax.vjp(forward, *inputs)
    grads = pullback(cotangent.astype(jnp.float32))
    return (result.astype(jnp.bfloat16), grads[0], grads[1], grads[2], grads[3], grads[4], grads[5], grads[6])
```

```python
import functools
import math

import jax
import jax.numpy as jnp
from jax import lax
from jax.experimental import pallas as pl
from jax.experimental.pallas import tpu as pltpu
from jax.sharding import PartitionSpec as P

HEADS = 12
HEAD_DIM = 64
HALF = HEAD_DIM // 2
SCALE = 1.0 / math.sqrt(HEAD_DIM)
EPS = 1e-05
THETA = 160000.0
F32 = jnp.float32
BF16 = jnp.bfloat16
NN = (((1,), (0,)), ((), ()))
NT = (((1,), (1,)), ((), ()))
TN = (((0,), (0,)), ((), ()))
TT = (((0,), (1,)), ((), ()))


def mul(a, b, dims=NN):
    return lax.dot_general(a, b, dims, preferred_element_type=F32)


def layer_norm(values, gain):
    centre = values - jnp.mean(values, axis=-1, keepdims=True)
    spread = jnp.mean(centre * centre, axis=-1, keepdims=True)
    return centre * lax.rsqrt(spread + EPS) * gain


def layer_norm_back(values, gain, grad):
    centre = values - jnp.mean(values, axis=-1, keepdims=True)
    inverse = lax.rsqrt(jnp.mean(centre * centre, axis=-1, keepdims=True) + EPS)
    unit = centre * inverse
    scaled = grad * gain
    first = jnp.mean(scaled, axis=-1, keepdims=True)
    second = jnp.mean(scaled * unit, axis=-1, keepdims=True)
    return inverse * (scaled - first - unit * second)


def geglu(inner):
    width = inner.shape[-1] // 2
    return jax.nn.gelu(inner[:, :width], approximate=False) * inner[:, width:]


def rounded(values):
    return lax.optimization_barrier(values.astype(BF16)).astype(F32)


def attend_kernel(heads, q_ref, k_ref, v_ref, out_ref, log_ref):
    for head in range(heads):
        rows = pl.ds(head * HEAD_DIM, HEAD_DIM)
        scores = mul(k_ref[head], q_ref[rows, :])
        highest = jnp.max(scores, axis=0, keepdims=True)
        raised = jnp.exp(scores - highest)
        total = jnp.sum(raised, axis=0, keepdims=True)
        mixed = mul(v_ref[rows, :], raised.astype(BF16))
        out_ref[rows, :] = (mixed / total).astype(BF16)
        log_ref[pl.ds(head, 1), :] = highest + jnp.log(total)


def attend(queries, keys, values, step=256):
    width, count = queries.shape
    heads = keys.shape[0]
    return pl.pallas_call(
        functools.partial(attend_kernel, heads),
        grid=(count // step,),
        in_specs=[
            pl.BlockSpec((width, step), lambda i: (0, i)),
            pl.BlockSpec((heads, count, HEAD_DIM), lambda i: (0, 0, 0)),
            pl.BlockSpec((width, count), lambda i: (0, 0)),
        ],
        out_specs=[
            pl.BlockSpec((width, step), lambda i: (0, i)),
            pl.BlockSpec((heads, step), lambda i: (0, i)),
        ],
        out_shape=[
            jax.ShapeDtypeStruct((width, count), BF16),
            jax.ShapeDtypeStruct((heads, count), F32),
        ],
        compiler_params=pltpu.CompilerParams(vmem_limit_bytes=48 * 2**20),
        cost_estimate=pl.CostEstimate(
            flops=4 * heads * count * count * HEAD_DIM,
            bytes_accessed=8 * width * count,
            transcendentals=heads * count * count,
        ),
        name="attend",
    )(queries, keys, values)


def turn_back(values, cosine, sine):
    first, second = values[:HALF], values[HALF:]
    return jnp.concatenate([first * cosine + second * sine, second * cosine - first * sine], axis=0)


def attend_back_kernel(
    head, q_ref, kt_ref, k_ref, v_ref, up_ref, out_ref, log_ref, cos_ref, sin_ref, grad_ref, dk_ref, dv_ref
):
    index = pl.program_id(0)
    step = q_ref.shape[1]

    @pl.when(index == 0)
    def _():
        dk_ref[...] = jnp.zeros_like(dk_ref)
        dv_ref[...] = jnp.zeros_like(dv_ref)

    upstream = up_ref[...]
    inner_sum = jnp.sum(upstream.astype(F32) * out_ref[...].astype(F32), axis=0, keepdims=True)
    chances = jnp.exp(mul(k_ref[0], q_ref[...]) - log_ref[pl.ds(head, 1), :])
    prob_back = mul(v_ref[0], upstream)
    score_back = (chances * (prob_back - inner_sum)).astype(BF16)
    dv_ref[...] += mul(chances.astype(BF16), upstream, NT)
    dk_ref[...] += mul(score_back, q_ref[...], NT)
    columns = pl.ds(pl.multiple_of(index * step, step), step)
    query_back = mul(kt_ref[...], score_back) * SCALE
    grad_ref[pl.ds(0, HEAD_DIM), columns] = turn_back(
        query_back, cos_ref[:, columns], sin_ref[:, columns]
    ).astype(BF16)

    @pl.when(index == pl.num_programs(0) - 1)
    def _():
        key_back = turn_back(dk_ref[...].T, cos_ref[...], sin_ref[...])
        grad_ref[pl.ds(HEAD_DIM, HEAD_DIM), :] = key_back.astype(BF16)
        grad_ref[pl.ds(2 * HEAD_DIM, HEAD_DIM), :] = dv_ref[...].T.astype(BF16)


def attend_back(head, queries, keys_turned, keys, values, upstream, merged, logs, cosine, sine, step=256):
    count = queries.shape[1]
    heads = keys.shape[0]
    some = pl.BlockSpec((HEAD_DIM, step), lambda i: (head, i))
    rows = pl.BlockSpec((1, count, HEAD_DIM), lambda i: (head, 0, 0))
    whole = pl.BlockSpec((HALF, count), lambda i: (0, 0))
    return pl.pallas_call(
        functools.partial(attend_back_kernel, head),
        grid=(count // step,),
        in_specs=[
            some,
            pl.BlockSpec((HEAD_DIM, count), lambda i: (head, 0)),
            rows,
            rows,
            some,
            some,
            pl.BlockSpec((heads, step), lambda i: (0, i)),
            whole,
            whole,
        ],
        out_specs=pl.BlockSpec((3 * HEAD_DIM, count), lambda i: (0, 0)),
        out_shape=jax.ShapeDtypeStruct((3 * HEAD_DIM, count), BF16),
        scratch_shapes=[pltpu.VMEM((count, HEAD_DIM), F32), pltpu.VMEM((count, HEAD_DIM), F32)],
        compiler_params=pltpu.CompilerParams(vmem_limit_bytes=48 * 2**20),
        cost_estimate=pl.CostEstimate(
            flops=10 * count * count * HEAD_DIM,
            bytes_accessed=16 * HEAD_DIM * count,
            transcendentals=count * count,
        ),
        name="attend_back",
    )(queries, keys_turned, keys, values, upstream, merged, logs, cosine, sine)


def swap(values, axis, size, offset):
    return lax.ppermute(values, axis, [(i, i ^ offset) for i in range(size)])


def exchange(pieces, size):
    return [pieces[0]] + [swap(pieces[d], "fsdp", size, d) for d in range(1, size)]


def pick(blocks, index):
    return lax.dynamic_index_in_dim(blocks, index, 0, keepdims=False)


def reorder(blocks, z, size):
    return jnp.stack([pick(blocks, z ^ j) for j in range(size)])


def orders(ranks):
    far = []
    bit = 2
    while bit < ranks:
        far.append(bit)
        bit *= 2
    return far, far[::-1]


def place(r, bits):
    total = 0
    for k, bit in enumerate(bits):
        total = total + jnp.where(r & bit != 0, 1 << k, 0)
    return total


def grow(values, r, ranks, bits):
    for bit in bits:
        other = swap(values, "rep", ranks, bit)
        upper = r & bit != 0
        values = jnp.concatenate(
            [jnp.where(upper, other, values), jnp.where(upper, values, other)], axis=1
        )
    return values


def shrink(values, r, ranks, bits):
    for bit in bits:
        half = values.shape[1] // 2
        mine = jnp.where(r & bit != 0, half, 0)
        sent = lax.dynamic_slice_in_dim(values, half - mine, half, 1)
        kept = lax.dynamic_slice_in_dim(values, mine, half, 1)
        other = swap(sent, "rep", ranks, bit)
        values = (kept.astype(F32) + other.astype(F32)).astype(BF16)
    return values


def halves(values):
    middle = values.shape[-1] // 2
    return values[..., :middle], values[..., middle:]


def gather_rows(shard, z, r, size, ranks):
    rows = shard.shape[0] // ranks
    one, two = orders(ranks)
    left, right = halves(shard)
    piece = jnp.concatenate(
        [
            lax.dynamic_slice_in_dim(left, place(r, one + [1]) * rows, rows, 0),
            lax.dynamic_slice_in_dim(right, place(r, two + [1]) * rows, rows, 0),
        ],
        axis=1,
    )
    blocks = reorder(jnp.stack(exchange([piece] * size, size)), z, size)
    left, right = halves(blocks)
    both = jnp.concatenate([grow(left, r, ranks, one), grow(right, r, ranks, two)], axis=2)
    return grow(both, r, ranks, [1])


def reduce_rows(blocks, z, r, size, ranks):
    one, two = orders(ranks)
    left, right = halves(shrink(blocks, r, ranks, [1]))
    both = jnp.concatenate(
        [shrink(left, r, ranks, one[::-1]), shrink(right, r, ranks, two[::-1])], axis=2
    )
    arrived = exchange([pick(both, z ^ d) for d in range(size)], size)
    total = sum(part.astype(F32) for part in arrived).astype(BF16)[None]
    left, right = halves(total)
    both = jnp.concatenate([grow(left, r, ranks, one), grow(right, r, ranks, two)], axis=2)
    return grow(both, r, ranks, [1])[0]


def gather_rows_short(shard, z, r, size, ranks):
    rows = shard.shape[0] // ranks
    bits = orders(ranks)[0] + [1]
    piece = lax.dynamic_slice_in_dim(shard, place(r, bits) * rows, rows, 0)
    blocks = reorder(jnp.stack(exchange([piece] * size, size)), z, size)
    return grow(blocks, r, ranks, bits)


def reduce_rows_short(blocks, z, r, size, ranks):
    bits = orders(ranks)[0] + [1]
    mine = shrink(blocks, r, ranks, bits[::-1])
    arrived = exchange([pick(mine, z ^ d) for d in range(size)], size)
    return grow(reorder(jnp.stack(arrived), z, size), r, ranks, bits)


def local(size, ranks, tokens, gain_a, projection_in, attention_out, gain_b, expansion, contraction, cotangent):
    z = lax.axis_index("fsdp")
    r = lax.axis_index("rep")
    own = tokens[0]
    count, width = own.shape
    part = width // size
    hidden = contraction.shape[0]
    heads = HEADS // size

    gains = jnp.stack([gain_a, gain_b])
    gains = reorder(jnp.stack(exchange([gains] * size, size)), z, size)
    gain_one = gains[:, 0].reshape(width).astype(F32)
    gain_two = gains[:, 1].reshape(width).astype(F32)

    columns = [projection_in[:, t * width : (t + 1) * width] for t in range(3)]
    into = gather_rows_short(jnp.concatenate(columns, axis=0), z, r, size, ranks)
    into = into.reshape(size, 3, part, width).transpose(1, 3, 0, 2).reshape(3, width, width)
    blocks = exchange([own] * size, size)

    columns = [expansion[:, t * width : (t + 1) * width] for t in range(3)]
    stacked = jnp.concatenate([attention_out] + columns + [contraction], axis=0)
    pad = -stacked.shape[0] % (8 * ranks)
    stacked = jnp.concatenate([stacked, jnp.zeros((pad, width), BF16)], axis=0)
    rest = gather_rows(stacked, z, r, size, ranks)
    out_weight = reorder(rest[:, :part], z, size).reshape(width, width)
    expand = [rest[:, (1 + t) * part : (2 + t) * part].reshape(width, width) for t in range(3)]
    contract = rest[:, 4 * part : 4 * part + hidden].reshape(size * hidden, width)

    freqs = THETA ** (-(jnp.arange(HALF, dtype=F32) * (2.0 / HEAD_DIM)))
    places = jnp.concatenate([(z ^ d) * count + jnp.arange(count, dtype=jnp.int32) for d in range(size)])
    angles = freqs[:, None] * places.astype(F32)[None, :]
    cosine, sine = jnp.cos(angles), jnp.sin(angles)

    normed = jnp.concatenate([layer_norm(b.astype(F32), gain_one).astype(BF16) for b in blocks], axis=0)
    own_into = [lax.dynamic_slice_in_dim(into[t], z * part, part, 0) for t in range(3)]

    def rotate(values):
        shaped = values.reshape(heads, 2, HALF, size * count)
        first, second = shaped[:, 0], shaped[:, 1]
        turned = jnp.stack([first * cosine - second * sine, second * cosine + first * sine], axis=1)
        return turned.reshape(part, size * count)

    queries = (rotate(mul(own_into[0], normed, NT)).astype(BF16) * SCALE).astype(BF16)
    keys_turned = rotate(mul(own_into[1], normed, NT)).astype(BF16)
    keys = keys_turned.reshape(heads, HEAD_DIM, size * count).transpose(0, 2, 1)
    values_turned = mul(own_into[2], normed, NT).astype(BF16)
    values = values_turned.reshape(heads, HEAD_DIM, size * count).transpose(0, 2, 1)
    own_merged, logs = attend(queries, keys, values_turned)

    arrived = exchange([own_merged[:, d * count : (d + 1) * count] for d in range(size)], size)
    merged = jnp.concatenate(arrived, axis=0)
    inputs = own.astype(F32)
    state = inputs + mul(merged, out_weight, TN)
    normed_two = layer_norm(state, gain_two).astype(BF16)
    inner = jnp.concatenate([mul(normed_two, w) for w in expand], axis=1)
    active, glu_back = jax.vjp(geglu, inner)
    active = active.astype(BF16)
    block_output = (state + mul(active, contract)).astype(BF16)[None]

    upstream = cotangent[0]
    (inner_back,) = glu_back(rounded(mul(upstream, contract, NT)))
    inner_back = inner_back.astype(BF16)
    normed_two_back = sum(
        mul(inner_back[:, t * width : (t + 1) * width], expand[t], NT) for t in range(3)
    )
    state_back = upstream.astype(F32) + layer_norm_back(state, gain_two, normed_two_back)
    state_low = state_back.astype(BF16)
    merged_back = mul(out_weight, state_low, NT).astype(BF16)
    arrived = exchange([merged_back[d * part : (d + 1) * part] for d in range(size)], size)
    own_upstream = jnp.concatenate(arrived, axis=1)

    contraction_grad = mul(active, upstream, TN).astype(BF16).reshape(size, hidden, width)
    expansion_grad = [
        mul(normed_two, inner_back[:, t * width : (t + 1) * width], TN).astype(BF16).reshape(size, part, width)
        for t in range(3)
    ]
    out_grad = reorder(mul(merged, state_low).astype(BF16).reshape(size, part, width), z, size)
    grads = jnp.concatenate(
        [out_grad] + expansion_grad + [contraction_grad, jnp.zeros((size, pad, width), BF16)], axis=1
    )
    grads = reduce_rows(grads, z, r, size, ranks).astype(F32)
    attention_out_sum = grads[:part]
    expansion_sum = jnp.concatenate([grads[(1 + t) * part : (2 + t) * part] for t in range(3)], axis=1)
    contraction_sum = grads[4 * part : 4 * part + hidden]

    turned_backs = []
    received = []
    weights = []
    by_head = into.reshape(3, size, heads, HEAD_DIM, width)
    for head in range(heads):
        grad = attend_back(
            head, queries, keys_turned, keys, values, own_upstream, own_merged, logs, cosine, sine
        )
        turned_backs.append(grad)
        received += exchange([grad[:, d * count : (d + 1) * count] for d in range(size)], size)
        chosen = by_head[:, :, head].transpose(1, 0, 2, 3)
        weights.append(reorder(chosen, z, size).reshape(size * 3 * HEAD_DIM, width))
    projected_back = jnp.concatenate(received, axis=0)
    normed_back = mul(projected_back, jnp.concatenate(weights, axis=0), TN)
    token_grad = (state_back + layer_norm_back(inputs, gain_one, normed_back))[None]

    all_backs = jnp.stack(turned_backs).reshape(heads, 3, HEAD_DIM, size * count)
    all_backs = all_backs.transpose(1, 0, 2, 3).reshape(3 * part, size * count)
    into_grad = mul(normed, all_backs, TT).astype(BF16).reshape(size, part, 3 * part)
    into_sum = reduce_rows_short(into_grad, z, r, size, ranks)
    into_sum = into_sum.reshape(size, part, 3, part).transpose(1, 2, 0, 3).reshape(part, 3 * width).astype(F32)

    gain_one_sum = jnp.sum(into_sum * projection_in.astype(F32), axis=1) / gain_a.astype(F32)
    gain_two_sum = jnp.sum(expansion_sum * expansion.astype(F32), axis=1) / gain_b.astype(F32)
    return (
        block_output,
        token_grad,
        gain_one_sum,
        into_sum,
        attention_out_sum,
        gain_two_sum,
        expansion_sum,
        contraction_sum,
    )


def solution(mesh):
    tokens, rows, line = P("rep", "fsdp", None), P("fsdp", None), P("fsdp")
    in_specs = (tokens, line, rows, rows, line, rows, rows, tokens)
    out_specs = (tokens, tokens, line, rows, rows, line, rows, rows)
    body = functools.partial(local, mesh.shape["fsdp"], mesh.shape["rep"])
    return jax.shard_map(body, mesh=mesh, in_specs=in_specs, out_specs=out_specs, check_vma=False)
```

```python
import functools
import math

import jax
import jax.numpy as jnp
from jax import lax
from jax.experimental import pallas as pl
from jax.experimental.pallas import tpu as pltpu
from jax.sharding import PartitionSpec as P

HEADS = 12
HEAD_DIM = 64
HALF = HEAD_DIM // 2
SCALE = 1.0 / math.sqrt(HEAD_DIM)
EPS = 1e-05
THETA = 160000.0
F32 = jnp.float32
BF16 = jnp.bfloat16
NN = (((1,), (0,)), ((), ()))
NT = (((1,), (1,)), ((), ()))
TN = (((0,), (0,)), ((), ()))
TT = (((0,), (1,)), ((), ()))


def mul(a, b, dims=NN):
    return lax.dot_general(a, b, dims, preferred_element_type=F32)


def layer_norm(values, gain):
    centre = values - jnp.mean(values, axis=-1, keepdims=True)
    spread = jnp.mean(centre * centre, axis=-1, keepdims=True)
    return centre * lax.rsqrt(spread + EPS) * gain


def layer_norm_back(values, gain, grad):
    centre = values - jnp.mean(values, axis=-1, keepdims=True)
    inverse = lax.rsqrt(jnp.mean(centre * centre, axis=-1, keepdims=True) + EPS)
    unit = centre * inverse
    scaled = grad * gain
    first = jnp.mean(scaled, axis=-1, keepdims=True)
    second = jnp.mean(scaled * unit, axis=-1, keepdims=True)
    return inverse * (scaled - first - unit * second)


def geglu(inner):
    width = inner.shape[-1] // 2
    return jax.nn.gelu(inner[:, :width], approximate=False) * inner[:, width:]


def rounded(values):
    return lax.optimization_barrier(values.astype(BF16)).astype(F32)


def attend_kernel(q_ref, k_ref, v_ref, out_ref, log_ref):
    scores = mul(k_ref[0], q_ref[...])
    highest = jnp.max(scores, axis=0, keepdims=True)
    raised = jnp.exp(scores - highest)
    total = jnp.sum(raised, axis=0, keepdims=True)
    mixed = mul(v_ref[...], raised.astype(BF16))
    out_ref[...] = (mixed / total).astype(BF16)
    log_ref[...] = highest + jnp.log(total)


def attend(head, queries, keys, values, step=256):
    count = queries.shape[1]
    return pl.pallas_call(
        attend_kernel,
        grid=(count // step,),
        in_specs=[
            pl.BlockSpec((HEAD_DIM, step), lambda i: (head, i)),
            pl.BlockSpec((1, count, HEAD_DIM), lambda i: (head, 0, 0)),
            pl.BlockSpec((HEAD_DIM, count), lambda i: (head, 0)),
        ],
        out_specs=[
            pl.BlockSpec((HEAD_DIM, step), lambda i: (0, i)),
            pl.BlockSpec((1, step), lambda i: (0, i)),
        ],
        out_shape=[
            jax.ShapeDtypeStruct((HEAD_DIM, count), BF16),
            jax.ShapeDtypeStruct((1, count), F32),
        ],
        compiler_params=pltpu.CompilerParams(vmem_limit_bytes=48 * 2**20),
        cost_estimate=pl.CostEstimate(
            flops=40 * count * count * HEAD_DIM,
            bytes_accessed=8 * HEAD_DIM * count,
            transcendentals=count * count,
        ),
        name="attend",
    )(queries, keys, values)


def turn_back(values, cosine, sine):
    first, second = values[:HALF], values[HALF:]
    return jnp.concatenate([first * cosine + second * sine, second * cosine - first * sine], axis=0)


def attend_back_kernel(
    q_ref, kt_ref, k_ref, v_ref, up_ref, out_ref, log_ref, cos_ref, sin_ref, grad_ref, dk_ref, dv_ref
):
    index = pl.program_id(0)
    step = q_ref.shape[1]

    @pl.when(index == 0)
    def _():
        dk_ref[...] = jnp.zeros_like(dk_ref)
        dv_ref[...] = jnp.zeros_like(dv_ref)

    upstream = up_ref[...]
    inner_sum = jnp.sum(upstream.astype(F32) * out_ref[...].astype(F32), axis=0, keepdims=True)
    chances = jnp.exp(mul(k_ref[0], q_ref[...]) - log_ref[...])
    prob_back = mul(v_ref[0], upstream)
    score_back = (chances * (prob_back - inner_sum)).astype(BF16)
    dv_ref[...] += mul(chances.astype(BF16), upstream, NT)
    dk_ref[...] += mul(score_back, q_ref[...], NT)
    columns = pl.ds(pl.multiple_of(index * step, step), step)
    query_back = mul(kt_ref[...], score_back) * SCALE
    grad_ref[pl.ds(0, HEAD_DIM), columns] = turn_back(
        query_back, cos_ref[:, columns], sin_ref[:, columns]
    ).astype(BF16)

    @pl.when(index == pl.num_programs(0) - 1)
    def _():
        key_back = turn_back(dk_ref[...].T, cos_ref[...], sin_ref[...])
        grad_ref[pl.ds(HEAD_DIM, HEAD_DIM), :] = key_back.astype(BF16)
        grad_ref[pl.ds(2 * HEAD_DIM, HEAD_DIM), :] = dv_ref[...].T.astype(BF16)


def attend_back(head, queries, keys_turned, keys, values, upstream, merged, logs, cosine, sine, step=256):
    count = queries.shape[1]
    some = pl.BlockSpec((HEAD_DIM, step), lambda i: (head, i))
    rows = pl.BlockSpec((1, count, HEAD_DIM), lambda i: (head, 0, 0))
    whole = pl.BlockSpec((HALF, count), lambda i: (0, 0))
    return pl.pallas_call(
        attend_back_kernel,
        grid=(count // step,),
        in_specs=[
            some,
            pl.BlockSpec((HEAD_DIM, count), lambda i: (head, 0)),
            rows,
            rows,
            some,
            some,
            pl.BlockSpec((1, step), lambda i: (0, i)),
            whole,
            whole,
        ],
        out_specs=pl.BlockSpec((3 * HEAD_DIM, count), lambda i: (0, 0)),
        out_shape=jax.ShapeDtypeStruct((3 * HEAD_DIM, count), BF16),
        scratch_shapes=[pltpu.VMEM((count, HEAD_DIM), F32), pltpu.VMEM((count, HEAD_DIM), F32)],
        compiler_params=pltpu.CompilerParams(vmem_limit_bytes=48 * 2**20),
        cost_estimate=pl.CostEstimate(
            flops=56 * count * count * HEAD_DIM,
            bytes_accessed=16 * HEAD_DIM * count,
            transcendentals=count * count,
        ),
        name="attend_back",
    )(queries, keys_turned, keys, values, upstream, merged, logs, cosine, sine)


def after(values, *others):
    return lax.optimization_barrier((values, others))[0]


def swap(values, axis, size, offset):
    return lax.ppermute(values, axis, [(i, i ^ offset) for i in range(size)])


def exchange(pieces, size):
    return [pieces[0]] + [swap(pieces[d], "fsdp", size, d) for d in range(1, size)]


def column(values, size, ranks, pairs):
    full = [
        (z * ranks + r, to * ranks + (r & ~1) + core)
        for z in range(size)
        for r in range(ranks)
        for to, core in pairs(z, r & 1)
    ]
    return lax.ppermute(values, ("fsdp", "rep"), full)


def collect(own, home, size, ranks):
    first = column(
        own, size, ranks, lambda z, c: [(z ^ 1, c) if c == z >> 1 else (z ^ 2, 1 - c)]
    )
    second = column(first, size, ranks, lambda z, c: [] if c == z >> 1 else [(z ^ 1, c)])
    low = jnp.where(home, own, first)
    high = jnp.where(home, first, second)
    pair = jnp.concatenate([low, high], axis=0)
    other = swap(pair, "rep", ranks, 1)
    return pair, other, second


def trade_out(pieces, size, ranks):
    def round_of(k):
        return lambda z, c: [((2 * c + (z & 1)) ^ k, z >> 1)]

    return [column(pieces[k], size, ranks, round_of(k)) for k in range(size)]


def trade_back(pieces, size, ranks):
    def round_of(k):
        return lambda z, c: [(2 * c + ((z ^ k) & 1), (z ^ k) >> 1)]

    return [column(pieces[k], size, ranks, round_of(k)) for k in range(size)]


def pick(blocks, index):
    return lax.dynamic_index_in_dim(blocks, index, 0, keepdims=False)


def reorder(blocks, z, size):
    return jnp.stack([pick(blocks, z ^ j) for j in range(size)])


def orders(ranks):
    far = []
    bit = 2
    while bit < ranks:
        far.append(bit)
        bit *= 2
    return far, far[::-1]


def place(r, bits):
    total = 0
    for k, bit in enumerate(bits):
        total = total + jnp.where(r & bit != 0, 1 << k, 0)
    return total


def grow(values, r, ranks, bits):
    for bit in bits:
        other = swap(values, "rep", ranks, bit)
        upper = r & bit != 0
        values = jnp.concatenate(
            [jnp.where(upper, other, values), jnp.where(upper, values, other)], axis=1
        )
    return values


def shrink(values, r, ranks, bits):
    for bit in bits:
        half = values.shape[1] // 2
        mine = jnp.where(r & bit != 0, half, 0)
        sent = lax.dynamic_slice_in_dim(values, half - mine, half, 1)
        kept = lax.dynamic_slice_in_dim(values, mine, half, 1)
        other = swap(sent, "rep", ranks, bit)
        values = (kept.astype(F32) + other.astype(F32)).astype(BF16)
    return values


def halves(values):
    middle = values.shape[-1] // 2
    return values[..., :middle], values[..., middle:]


def split_rows(shard, r, ranks):
    rows = shard.shape[0] // ranks
    one, two = orders(ranks)
    left, right = halves(shard)
    return jnp.concatenate(
        [
            lax.dynamic_slice_in_dim(left, place(r, one + [1]) * rows, rows, 0),
            lax.dynamic_slice_in_dim(right, place(r, two + [1]) * rows, rows, 0),
        ],
        axis=1,
    )


def grow_both(values, r, ranks):
    one, two = orders(ranks)
    left, right = halves(values)
    return jnp.concatenate([grow(left, r, ranks, one), grow(right, r, ranks, two)], axis=2)


def shrink_both(values, r, ranks):
    one, two = orders(ranks)
    left, right = halves(values)
    return jnp.concatenate(
        [shrink(left, r, ranks, one[::-1]), shrink(right, r, ranks, two[::-1])], axis=2
    )


def local(size, ranks, tokens, gain_a, projection_in, attention_out, gain_b, expansion, contraction, cotangent):
    z = lax.axis_index("fsdp")
    r = lax.axis_index("rep")
    core = r & 1
    group = 2 * core + (z & 1)
    home = core == z >> 1
    own = tokens[0]
    count, width = own.shape
    part = width // size
    hidden = contraction.shape[0]
    heads = HEADS // size

    columns = [projection_in[:, t * width : (t + 1) * width] for t in range(3)]
    piece = split_rows(jnp.concatenate(columns, axis=0), r, ranks)
    pieces = exchange([piece] * size, size)
    gains = jnp.stack([gain_a, gain_b])
    gains = exchange([gains] * size, size)
    pair, other, second = collect(after(own, *pieces), home, size, ranks)
    into = grow(grow_both(reorder(jnp.stack(pieces), z, size), r, ranks), r, ranks, [1])
    into = into.reshape(size, 3, part, width)
    into = [into[:, t].reshape(width, width) for t in range(3)]
    gains = reorder(jnp.stack(gains), z, size)
    gain_one = gains[:, 0].reshape(width).astype(F32)
    gain_two = gains[:, 1].reshape(width).astype(F32)

    freqs = THETA ** (-(jnp.arange(HALF, dtype=F32) * (2.0 / HEAD_DIM)))
    places = jnp.concatenate([(group ^ d) * count + jnp.arange(count, dtype=jnp.int32) for d in range(size)])
    angles = freqs[:, None] * places.astype(F32)[None, :]
    cosine, sine = jnp.cos(angles), jnp.sin(angles)

    normed = jnp.concatenate(
        [layer_norm(b.astype(F32), gain_one).astype(BF16) for b in (pair, other)], axis=0
    )
    own_into = [lax.dynamic_slice_in_dim(into[t], group * part, part, 1) for t in range(3)]

    def rotate(values):
        shaped = values.reshape(heads, 2, HALF, size * count)
        first, second = shaped[:, 0], shaped[:, 1]
        turned = jnp.stack([first * cosine - second * sine, second * cosine + first * sine], axis=1)
        return turned.reshape(part, size * count)

    queries = (rotate(mul(own_into[0], normed, TT)).astype(BF16) * SCALE).astype(BF16)
    keys_turned = rotate(mul(own_into[1], normed, TT)).astype(BF16)
    keys = keys_turned.reshape(heads, HEAD_DIM, size * count).transpose(0, 2, 1)
    values_turned = mul(own_into[2], normed, TT).astype(BF16)
    values = values_turned.reshape(heads, HEAD_DIM, size * count).transpose(0, 2, 1)

    columns = [expansion[:, t * width : (t + 1) * width] for t in range(3)]
    stacked = jnp.concatenate([attention_out] + columns + [contraction], axis=0)
    pad = -stacked.shape[0] % (8 * ranks)
    stacked = jnp.concatenate([stacked, jnp.zeros((pad, width), BF16)], axis=0)
    piece = split_rows(after(stacked, second), r, ranks)
    pieces = exchange([piece] * size, size)
    merged = []
    logs = []
    rest = reorder(jnp.stack(pieces), z, size)
    for head in range(heads):
        tied = keys if head == 0 else after(keys, rest)
        if head == 1:
            rest = grow_both(rest, r, ranks)
        out, log = attend(head, queries, tied, values_turned)
        merged.append(out)
        logs.append(log)
    rest = grow(rest, r, ranks, [1])
    own_merged = jnp.concatenate(merged, axis=0)

    arrived = trade_out([own_merged[:, d * count : (d + 1) * count] for d in range(size)], size, ranks)
    merged = jnp.concatenate(arrived, axis=0)
    out_weight = reorder(rest[:, :part], z, size).reshape(width, width)
    expand = [rest[:, (1 + t) * part : (2 + t) * part].reshape(width, width) for t in range(3)]
    contract = rest[:, 4 * part : 4 * part + hidden].reshape(size * hidden, width)
    inputs = own.astype(F32)
    state = inputs + mul(merged, out_weight, TN)
    normed_two = layer_norm(state, gain_two).astype(BF16)
    inner = jnp.concatenate([mul(normed_two, w) for w in expand], axis=1)
    active, glu_back = jax.vjp(geglu, inner)
    active = active.astype(BF16)
    block_output = (state + mul(active, contract)).astype(BF16)[None]

    upstream = cotangent[0]
    (inner_back,) = glu_back(rounded(mul(upstream, contract, NT)))
    inner_back = inner_back.astype(BF16)
    normed_two_back = sum(
        mul(inner_back[:, t * width : (t + 1) * width], expand[t], NT) for t in range(3)
    )
    state_back = upstream.astype(F32) + layer_norm_back(state, gain_two, normed_two_back)
    state_low = state_back.astype(BF16)
    merged_back = mul(out_weight, state_low, NT).astype(BF16)
    arrived = trade_back([merged_back[d * part : (d + 1) * part] for d in range(size)], size, ranks)
    own_upstream = jnp.concatenate(arrived, axis=1)

    contraction_grad = mul(active, upstream, TN).astype(BF16).reshape(size, hidden, width)
    expansion_grad = [
        mul(normed_two, inner_back[:, t * width : (t + 1) * width], TN).astype(BF16).reshape(size, part, width)
        for t in range(3)
    ]
    out_grad = reorder(mul(merged, state_low).astype(BF16).reshape(size, part, width), z, size)
    grads = jnp.concatenate(
        [out_grad] + expansion_grad + [contraction_grad, jnp.zeros((size, pad, width), BF16)], axis=1
    )
    grads = shrink(grads, r, ranks, [1])

    turned_backs = []
    received = []
    tied = after(own_upstream, grads)
    for head in range(heads):
        if head == 2:
            grads = shrink_both(grads, r, ranks)
            tied = after(own_upstream, grads, *received[0])
        grad = attend_back(
            head, queries, keys_turned, keys, values, tied, own_merged, logs[head], cosine, sine
        )
        turned_backs.append(grad)
        received.append(trade_out([grad[:, d * count : (d + 1) * count] for d in range(size)], size, ranks))

    grads = exchange([pick(grads, z ^ d) for d in range(size)], size)
    grads = sum(part.astype(F32) for part in grads).astype(BF16)[None]
    grads = grow(grow_both(grads, r, ranks), r, ranks, [1])[0].astype(F32)
    attention_out_sum = grads[:part]
    expansion_sum = jnp.concatenate([grads[(1 + t) * part : (2 + t) * part] for t in range(3)], axis=1)
    contraction_sum = grads[4 * part : 4 * part + hidden]

    projected_back = jnp.stack([jnp.stack(pieces) for pieces in received], axis=1)
    projected_back = reorder(projected_back, z, size).reshape(size, heads, 3, HEAD_DIM, count)
    projected_back = projected_back.transpose(2, 0, 1, 3, 4).reshape(3, width, count)
    normed_back = sum(mul(projected_back[t], into[t], TT) for t in range(3))
    token_grad = (state_back + layer_norm_back(inputs, gain_one, normed_back))[None]

    all_backs = jnp.stack(turned_backs).reshape(heads, 3, HEAD_DIM, size * count)
    all_backs = all_backs.transpose(1, 0, 2, 3).reshape(3 * part, size * count)
    into_grad = mul(normed, all_backs, TT).astype(BF16).reshape(size, part, 3 * part)
    into_grad = shrink(into_grad, r, ranks, orders(ranks)[1])
    arrived = exchange([pick(into_grad, z ^ d) for d in range(size)], size)
    even = (arrived[0].astype(F32) + arrived[2].astype(F32)).astype(BF16)
    odd = (arrived[1].astype(F32) + arrived[3].astype(F32)).astype(BF16)
    low = z & 1 == 0
    into_sum = jnp.stack([jnp.where(low, even, odd), jnp.where(low, odd, even)])
    into_sum = grow(into_sum, r, ranks, orders(ranks)[0])
    partner = swap(into_sum, "rep", ranks, 1)
    low = core == 0
    into_sum = jnp.concatenate([jnp.where(low, into_sum, partner), jnp.where(low, partner, into_sum)], axis=0)
    into_sum = into_sum.reshape(size, part, 3, part).transpose(1, 2, 0, 3).reshape(part, 3 * width).astype(F32)

    gain_one_sum = jnp.sum(into_sum * projection_in.astype(F32), axis=1) / gain_a.astype(F32)
    gain_two_sum = jnp.sum(expansion_sum * expansion.astype(F32), axis=1) / gain_b.astype(F32)
    return (
        block_output,
        token_grad,
        gain_one_sum,
        into_sum,
        attention_out_sum,
        gain_two_sum,
        expansion_sum,
        contraction_sum,
    )


def solution(mesh):
    tokens, rows, line = P("rep", "fsdp", None), P("fsdp", None), P("fsdp")
    in_specs = (tokens, line, rows, rows, line, rows, rows, tokens)
    out_specs = (tokens, tokens, line, rows, rows, line, rows, rows)
    body = functools.partial(local, mesh.shape["fsdp"], mesh.shape["rep"])
    return jax.shard_map(body, mesh=mesh, in_specs=in_specs, out_specs=out_specs, check_vma=False)
```

```python
import functools
import math

import jax
import jax.numpy as jnp
from jax import lax
from jax.experimental import pallas as pl
from jax.experimental.pallas import tpu as pltpu
from jax.sharding import PartitionSpec as P

HEADS = 12
HEAD_DIM = 64
HALF = HEAD_DIM // 2
SCALE = 1.0 / math.sqrt(HEAD_DIM)
EPS = 1e-05
THETA = 160000.0
F32 = jnp.float32
BF16 = jnp.bfloat16
NN = (((1,), (0,)), ((), ()))
NT = (((1,), (1,)), ((), ()))
TN = (((0,), (0,)), ((), ()))
TT = (((0,), (1,)), ((), ()))


def mul(a, b, dims=NN):
    return lax.dot_general(a, b, dims, preferred_element_type=F32)


def layer_norm(values, gain):
    centre = values - jnp.mean(values, axis=-1, keepdims=True)
    spread = jnp.mean(centre * centre, axis=-1, keepdims=True)
    return centre * lax.rsqrt(spread + EPS) * gain


def layer_norm_back(values, gain, grad):
    centre = values - jnp.mean(values, axis=-1, keepdims=True)
    inverse = lax.rsqrt(jnp.mean(centre * centre, axis=-1, keepdims=True) + EPS)
    unit = centre * inverse
    scaled = grad * gain
    first = jnp.mean(scaled, axis=-1, keepdims=True)
    second = jnp.mean(scaled * unit, axis=-1, keepdims=True)
    return inverse * (scaled - first - unit * second)


def geglu(inner):
    width = inner.shape[-1] // 2
    return jax.nn.gelu(inner[:, :width], approximate=False) * inner[:, width:]


def rounded(values):
    return lax.optimization_barrier(values.astype(BF16)).astype(F32)


def attend_kernel(q_ref, k_ref, v_ref, out_ref, log_ref):
    scores = mul(k_ref[0], q_ref[...])
    highest = jnp.max(scores, axis=0, keepdims=True)
    raised = jnp.exp(scores - highest)
    total = jnp.sum(raised, axis=0, keepdims=True)
    mixed = mul(v_ref[...], raised.astype(BF16))
    out_ref[...] = (mixed / total).astype(BF16)
    log_ref[...] = highest + jnp.log(total)


def attend(head, queries, keys, values, step=256):
    count = queries.shape[1]
    return pl.pallas_call(
        attend_kernel,
        grid=(count // step,),
        in_specs=[
            pl.BlockSpec((HEAD_DIM, step), lambda i: (head, i)),
            pl.BlockSpec((1, count, HEAD_DIM), lambda i: (head, 0, 0)),
            pl.BlockSpec((HEAD_DIM, count), lambda i: (head, 0)),
        ],
        out_specs=[
            pl.BlockSpec((HEAD_DIM, step), lambda i: (0, i)),
            pl.BlockSpec((1, step), lambda i: (0, i)),
        ],
        out_shape=[
            jax.ShapeDtypeStruct((HEAD_DIM, count), BF16),
            jax.ShapeDtypeStruct((1, count), F32),
        ],
        compiler_params=pltpu.CompilerParams(vmem_limit_bytes=48 * 2**20),
        cost_estimate=pl.CostEstimate(
            flops=40 * count * count * HEAD_DIM,
            bytes_accessed=8 * HEAD_DIM * count,
            transcendentals=count * count,
        ),
        name="attend",
    )(queries, keys, values)


def turn_back(values, cosine, sine):
    first, second = values[:HALF], values[HALF:]
    return jnp.concatenate([first * cosine + second * sine, second * cosine - first * sine], axis=0)


def attend_back_kernel(
    q_ref, kt_ref, k_ref, v_ref, up_ref, out_ref, log_ref, cos_ref, sin_ref, grad_ref, dk_ref, dv_ref
):
    index = pl.program_id(0)
    step = q_ref.shape[1]

    @pl.when(index == 0)
    def _():
        dk_ref[...] = jnp.zeros_like(dk_ref)
        dv_ref[...] = jnp.zeros_like(dv_ref)

    upstream = up_ref[...]
    inner_sum = jnp.sum(upstream.astype(F32) * out_ref[...].astype(F32), axis=0, keepdims=True)
    chances = jnp.exp(mul(k_ref[0], q_ref[...]) - log_ref[...])
    prob_back = mul(v_ref[0], upstream)
    score_back = (chances * (prob_back - inner_sum)).astype(BF16)
    dv_ref[...] += mul(chances.astype(BF16), upstream, NT)
    dk_ref[...] += mul(score_back, q_ref[...], NT)
    columns = pl.ds(pl.multiple_of(index * step, step), step)
    query_back = mul(kt_ref[...], score_back) * SCALE
    grad_ref[pl.ds(0, HEAD_DIM), columns] = turn_back(
        query_back, cos_ref[:, columns], sin_ref[:, columns]
    ).astype(BF16)

    @pl.when(index == pl.num_programs(0) - 1)
    def _():
        key_back = turn_back(dk_ref[...].T, cos_ref[...], sin_ref[...])
        grad_ref[pl.ds(HEAD_DIM, HEAD_DIM), :] = key_back.astype(BF16)
        grad_ref[pl.ds(2 * HEAD_DIM, HEAD_DIM), :] = dv_ref[...].T.astype(BF16)


def attend_back(head, queries, keys_turned, keys, values, upstream, merged, logs, cosine, sine, step=256):
    count = queries.shape[1]
    some = pl.BlockSpec((HEAD_DIM, step), lambda i: (head, i))
    rows = pl.BlockSpec((1, count, HEAD_DIM), lambda i: (head, 0, 0))
    whole = pl.BlockSpec((HALF, count), lambda i: (0, 0))
    return pl.pallas_call(
        attend_back_kernel,
        grid=(count // step,),
        in_specs=[
            some,
            pl.BlockSpec((HEAD_DIM, count), lambda i: (head, 0)),
            rows,
            rows,
            some,
            some,
            pl.BlockSpec((1, step), lambda i: (0, i)),
            whole,
            whole,
        ],
        out_specs=pl.BlockSpec((3 * HEAD_DIM, count), lambda i: (0, 0)),
        out_shape=jax.ShapeDtypeStruct((3 * HEAD_DIM, count), BF16),
        scratch_shapes=[pltpu.VMEM((count, HEAD_DIM), F32), pltpu.VMEM((count, HEAD_DIM), F32)],
        compiler_params=pltpu.CompilerParams(vmem_limit_bytes=48 * 2**20),
        cost_estimate=pl.CostEstimate(
            flops=56 * count * count * HEAD_DIM,
            bytes_accessed=16 * HEAD_DIM * count,
            transcendentals=count * count,
        ),
        name="attend_back",
    )(queries, keys_turned, keys, values, upstream, merged, logs, cosine, sine)


def after(values, *others):
    return lax.optimization_barrier((values, others))[0]


def swap(values, axis, size, offset):
    return lax.ppermute(values, axis, [(i, i ^ offset) for i in range(size)])


def exchange(pieces, size):
    return [pieces[0]] + [swap(pieces[d], "fsdp", size, d) for d in range(1, size)]


def column(values, size, ranks, pairs):
    full = [
        (z * ranks + r, to * ranks + (r & ~1) + core)
        for z in range(size)
        for r in range(ranks)
        for to, core in pairs(z, r & 1)
    ]
    return lax.ppermute(values, ("fsdp", "rep"), full)


def collect(own, home, size, ranks):
    first = column(
        own, size, ranks, lambda z, c: [(z ^ 1, c) if c == z >> 1 else (z ^ 2, 1 - c)]
    )
    second = column(first, size, ranks, lambda z, c: [] if c == z >> 1 else [(z ^ 1, c)])
    low = jnp.where(home, own, first)
    high = jnp.where(home, first, second)
    pair = jnp.concatenate([low, high], axis=0)
    other = swap(pair, "rep", ranks, 1)
    return pair, other, second


def trade_out(pieces, size, ranks):
    def round_of(k):
        return lambda z, c: [((2 * c + (z & 1)) ^ k, z >> 1)]

    return [column(pieces[k], size, ranks, round_of(k)) for k in range(size)]


def trade_back(pieces, size, ranks):
    def round_of(k):
        return lambda z, c: [(2 * c + ((z ^ k) & 1), (z ^ k) >> 1)]

    return [column(pieces[k], size, ranks, round_of(k)) for k in range(size)]


def pick(blocks, index):
    return lax.dynamic_index_in_dim(blocks, index, 0, keepdims=False)


def reorder(blocks, z, size):
    return jnp.stack([pick(blocks, z ^ j) for j in range(size)])


def far(ranks):
    bits = []
    bit = 2
    while bit < ranks:
        bits.append(bit)
        bit *= 2
    return bits


def stage_bit(core, ranks, stage):
    bits = far(ranks)
    return bits[stage] if core == 0 else bits[len(bits) - 1 - stage]


def stage_swap(values, ranks, stage):
    return lax.ppermute(values, "rep", [(i, i ^ stage_bit(i & 1, ranks, stage)) for i in range(ranks)])


def stage_upper(r, ranks, stage):
    bit = jnp.where(r & 1 == 0, stage_bit(0, ranks, stage), stage_bit(1, ranks, stage))
    return r & bit != 0


def place(r, ranks):
    stages = len(far(ranks))
    total = jnp.where(r & 1 != 0, 1 << stages, 0)
    for stage in range(stages):
        total = total + jnp.where(stage_upper(r, ranks, stage), 1 << stage, 0)
    return total


def join(mine, other, upper):
    return jnp.concatenate([jnp.where(upper, other, mine), jnp.where(upper, mine, other)], axis=1)


def cut(values, upper):
    half = values.shape[1] // 2
    mine = jnp.where(upper, half, 0)
    sent = lax.dynamic_slice_in_dim(values, half - mine, half, 1)
    return sent, lax.dynamic_slice_in_dim(values, mine, half, 1)


def add(one, two):
    return (one.astype(F32) + two.astype(F32)).astype(BF16)


def grow(values, r, ranks, stages):
    for stage in stages:
        values = join(values, stage_swap(values, ranks, stage), stage_upper(r, ranks, stage))
    return values


def grow_core(values, r, ranks):
    return join(values, swap(values, "rep", ranks, 1), r & 1 != 0)


def shrink(values, r, ranks, stages):
    for stage in stages:
        sent, kept = cut(values, stage_upper(r, ranks, stage))
        values = add(kept, stage_swap(sent, ranks, stage))
    return values


def shrink_core(values, r, ranks):
    sent, kept = cut(values, r & 1 != 0)
    return add(kept, swap(sent, "rep", ranks, 1))


def split_rows(shard, r, ranks):
    rows = shard.shape[0] // ranks
    return lax.dynamic_slice_in_dim(shard, place(r, ranks) * rows, rows, 0)


def finish_into_kernel(low_ref, high_ref, weight_ref, gain_ref, sum_ref, gain_sum_ref):
    part = sum_ref.shape[0]
    total = jnp.zeros((part, 1), F32)
    for t in range(3):
        blocks = [ref[g, :, t * part : (t + 1) * part] for ref in (low_ref, high_ref) for g in range(2)]
        row = jnp.concatenate([block.astype(F32) for block in blocks], axis=1)
        width = row.shape[1]
        sum_ref[:, t * width : (t + 1) * width] = row
        weight = weight_ref[:, t * width : (t + 1) * width].astype(F32)
        total = total + jnp.sum(row * weight, axis=1, keepdims=True)
    gain_sum_ref[...] = total / gain_ref[...].astype(F32)


def finish_into(low, high, weight, gain):
    part = weight.shape[0]
    return pl.pallas_call(
        finish_into_kernel,
        out_shape=[
            jax.ShapeDtypeStruct(weight.shape, F32),
            jax.ShapeDtypeStruct((part, 1), F32),
        ],
        compiler_params=pltpu.CompilerParams(vmem_limit_bytes=32 * 2**20),
        name="finish_into",
    )(low, high, weight, gain[:, None])


def finish_rest_kernel(grads_ref, weight_ref, gain_ref, out_ref, expand_ref, contract_ref, gain_sum_ref):
    part, width = out_ref.shape
    hidden = contract_ref.shape[0]
    total = jnp.zeros((part, 1), F32)
    out_ref[...] = grads_ref[:part].astype(F32)
    for t in range(3):
        rows = grads_ref[(1 + t) * part : (2 + t) * part].astype(F32)
        expand_ref[:, t * width : (t + 1) * width] = rows
        weight = weight_ref[:, t * width : (t + 1) * width].astype(F32)
        total = total + jnp.sum(rows * weight, axis=1, keepdims=True)
    contract_ref[...] = grads_ref[4 * part : 4 * part + hidden].astype(F32)
    gain_sum_ref[...] = total / gain_ref[...].astype(F32)


def finish_rest(grads, weight, gain, hidden):
    part = weight.shape[0]
    width = grads.shape[1]
    return pl.pallas_call(
        finish_rest_kernel,
        out_shape=[
            jax.ShapeDtypeStruct((part, width), F32),
            jax.ShapeDtypeStruct(weight.shape, F32),
            jax.ShapeDtypeStruct((hidden, width), F32),
            jax.ShapeDtypeStruct((part, 1), F32),
        ],
        compiler_params=pltpu.CompilerParams(vmem_limit_bytes=32 * 2**20),
        name="finish_rest",
    )(grads, weight, gain[:, None])


def local(size, ranks, tokens, gain_a, projection_in, attention_out, gain_b, expansion, contraction, cotangent):
    z = lax.axis_index("fsdp")
    r = lax.axis_index("rep")
    core = r & 1
    group = 2 * core + (z & 1)
    home = core == z >> 1
    own = tokens[0]
    count, width = own.shape
    part = width // size
    hidden = contraction.shape[0]
    heads = HEADS // size

    stages = list(range(len(far(ranks))))
    columns = [projection_in[:, t * width : (t + 1) * width] for t in range(3)]
    piece = split_rows(jnp.concatenate(columns, axis=0), r, ranks)
    rows = piece.shape[0]
    gains = jnp.pad(jnp.concatenate([gain_a, gain_b])[None], ((0, 7), (0, width - 2 * part)))
    pieces = exchange([jnp.concatenate([piece, gains], axis=0)] * size, size)
    pair, other, second = collect(after(own, *pieces), home, size, ranks)
    pieces = reorder(jnp.stack(pieces), z, size)
    into = grow_core(grow(pieces[:, :rows], r, ranks, stages), r, ranks)
    into = into.reshape(size, 3, part, width)
    into = [into[:, t].reshape(width, width) for t in range(3)]
    gain_one = pieces[:, rows, :part].reshape(width).astype(F32)
    gain_two = pieces[:, rows, part : 2 * part].reshape(width).astype(F32)

    freqs = THETA ** (-(jnp.arange(HALF, dtype=F32) * (2.0 / HEAD_DIM)))
    places = jnp.concatenate([(group ^ d) * count + jnp.arange(count, dtype=jnp.int32) for d in range(size)])
    angles = freqs[:, None] * places.astype(F32)[None, :]
    cosine, sine = jnp.cos(angles), jnp.sin(angles)

    normed = jnp.concatenate(
        [layer_norm(b.astype(F32), gain_one).astype(BF16) for b in (pair, other)], axis=0
    )
    own_into = [lax.dynamic_slice_in_dim(into[t], group * part, part, 1) for t in range(3)]

    def rotate(values):
        shaped = values.reshape(heads, 2, HALF, size * count)
        first, second = shaped[:, 0], shaped[:, 1]
        turned = jnp.stack([first * cosine - second * sine, second * cosine + first * sine], axis=1)
        return turned.reshape(part, size * count)

    queries = (rotate(mul(own_into[0], normed, TT)).astype(BF16) * SCALE).astype(BF16)
    keys_turned = rotate(mul(own_into[1], normed, TT)).astype(BF16)
    keys = keys_turned.reshape(heads, HEAD_DIM, size * count).transpose(0, 2, 1)
    values_turned = mul(own_into[2], normed, TT).astype(BF16)
    values = values_turned.reshape(heads, HEAD_DIM, size * count).transpose(0, 2, 1)

    columns = [expansion[:, t * width : (t + 1) * width] for t in range(3)]
    stacked = jnp.concatenate([attention_out] + columns + [contraction], axis=0)
    pad = -stacked.shape[0] % (8 * ranks)
    stacked = jnp.concatenate([stacked, jnp.zeros((pad, width), BF16)], axis=0)
    piece = split_rows(after(stacked, queries), r, ranks)
    pieces = exchange([piece] * size, size)
    rest = reorder(jnp.stack(pieces), z, size)
    merged = []
    logs = []
    ahead = []
    for head in range(heads):
        out, log = attend(head, queries, after(keys, *ahead), values_turned)
        merged.append(out)
        logs.append(log)
        if head < 2:
            ahead = [rest]
            rest = grow(after(rest, out), r, ranks, stages[:1] if head == 0 else stages[1:])
    rest = grow_core(after(rest, merged[-1]), r, ranks)
    own_merged = jnp.concatenate(merged, axis=0)

    arrived = trade_out([own_merged[:, d * count : (d + 1) * count] for d in range(size)], size, ranks)
    merged = jnp.concatenate(arrived, axis=0)
    out_weight = reorder(rest[:, :part], z, size).reshape(width, width)
    expand = [rest[:, (1 + t) * part : (2 + t) * part].reshape(width, width) for t in range(3)]
    contract = rest[:, 4 * part : 4 * part + hidden].reshape(size * hidden, width)
    inputs = own.astype(F32)
    state = inputs + mul(merged, out_weight, TN)
    normed_two = layer_norm(state, gain_two).astype(BF16)
    inner = jnp.concatenate([mul(normed_two, w) for w in expand], axis=1)
    active, glu_back = jax.vjp(geglu, inner)
    active = active.astype(BF16)
    block_output = (state + mul(active, contract)).astype(BF16)[None]

    upstream = cotangent[0]
    (inner_back,) = glu_back(rounded(mul(upstream, contract, NT)))
    inner_back = inner_back.astype(BF16)
    normed_two_back = sum(
        mul(inner_back[:, t * width : (t + 1) * width], expand[t], NT) for t in range(3)
    )
    state_back = upstream.astype(F32) + layer_norm_back(state, gain_two, normed_two_back)
    state_low = state_back.astype(BF16)
    merged_back = mul(out_weight, state_low, NT).astype(BF16)
    upstream, active, inner_back, state_low = after((upstream, active, inner_back, state_low), merged_back)
    arrived = trade_back([merged_back[d * part : (d + 1) * part] for d in range(size)], size, ranks)
    own_upstream = jnp.concatenate(arrived, axis=1)

    contraction_grad = mul(active, upstream, TN).astype(BF16).reshape(size, hidden, width)
    expansion_grad = [
        mul(normed_two, inner_back[:, t * width : (t + 1) * width], TN).astype(BF16).reshape(size, part, width)
        for t in range(3)
    ]
    out_grad = reorder(mul(merged, state_low).astype(BF16).reshape(size, part, width), z, size)
    grads = jnp.concatenate(
        [out_grad] + expansion_grad + [contraction_grad, jnp.zeros((size, pad, width), BF16)], axis=1
    )
    grads = shrink_core(grads, r, ranks)

    turned_backs = []
    received = []
    ahead = [grads]
    for head in range(heads):
        grad = attend_back(
            head, queries, keys_turned, keys, values, after(own_upstream, *ahead), own_merged, logs[head], cosine, sine
        )
        turned_backs.append(grad)
        if head == 0:
            received = trade_out([grad[:, d * count : (d + 1) * count] for d in range(size)], size, ranks)
            grads = shrink(grads, r, ranks, stages[:0:-1])
            ahead = [grads]
        if head == 1:
            grads = shrink(grads, r, ranks, stages[:1])
            ahead = [grads] + received
    later = jnp.concatenate(turned_backs[1:], axis=0)
    later = trade_out([later[:, d * count : (d + 1) * count] for d in range(size)], size, ranks)
    received = [jnp.concatenate(both, axis=0) for both in zip(received, later)]

    grads = exchange([pick(grads, z ^ d) for d in range(size)], size)
    grads = sum(part.astype(F32) for part in grads).astype(BF16)[None]
    owned = grads
    grads = grow_core(grow(grads, r, ranks, stages), r, ranks)[0]
    attention_out_sum, expansion_sum, contraction_sum, gain_two_sum = finish_rest(
        grads, expansion, gain_b, hidden
    )

    projected_back = reorder(jnp.stack(received), z, size).reshape(size, heads, 3, HEAD_DIM, count)
    projected_back = projected_back.transpose(2, 0, 1, 3, 4).reshape(3, width, count)
    normed_back = sum(mul(projected_back[t], into[t], TT) for t in range(3))
    token_grad = (state_back + layer_norm_back(inputs, gain_one, normed_back))[None]

    all_backs = jnp.stack(turned_backs).reshape(heads, 3, HEAD_DIM, size * count)
    all_backs = all_backs.transpose(1, 0, 2, 3).reshape(3 * part, size * count)
    into_grad = mul(normed, all_backs, TT).astype(BF16).reshape(size, part, 3 * part)
    into_grad = after(shrink(into_grad, r, ranks, stages[::-1]), owned)
    arrived = exchange([pick(into_grad, z ^ d) for d in range(size)], size)
    even = (arrived[0].astype(F32) + arrived[2].astype(F32)).astype(BF16)
    odd = (arrived[1].astype(F32) + arrived[3].astype(F32)).astype(BF16)
    low = z & 1 == 0
    into_sum = jnp.stack([jnp.where(low, even, odd), jnp.where(low, odd, even)])
    into_sum = grow(into_sum, r, ranks, stages)
    partner = swap(into_sum, "rep", ranks, 1)
    low = core == 0
    into_sum, gain_one_sum = finish_into(
        jnp.where(low, into_sum, partner), jnp.where(low, partner, into_sum), projection_in, gain_a
    )
    return (
        block_output,
        token_grad,
        gain_one_sum[:, 0],
        into_sum,
        attention_out_sum,
        gain_two_sum[:, 0],
        expansion_sum,
        contraction_sum,
    )


def solution(mesh):
    tokens, rows, line = P("rep", "fsdp", None), P("fsdp", None), P("fsdp")
    in_specs = (tokens, line, rows, rows, line, rows, rows, tokens)
    out_specs = (tokens, tokens, line, rows, rows, line, rows, rows)
    body = functools.partial(local, mesh.shape["fsdp"], mesh.shape["rep"])
    return jax.shard_map(body, mesh=mesh, in_specs=in_specs, out_specs=out_specs, check_vma=False)
```

```python
import functools
import math

import jax
import jax.numpy as jnp
from jax import lax
from jax.experimental import pallas as pl
from jax.experimental.pallas import tpu as pltpu
from jax.sharding import PartitionSpec as P

HEADS = 12
HEAD_DIM = 64
HALF = HEAD_DIM // 2
SCALE = 1.0 / math.sqrt(HEAD_DIM)
EPS = 1e-05
THETA = 160000.0
F32 = jnp.float32
BF16 = jnp.bfloat16
NN = (((1,), (0,)), ((), ()))
NT = (((1,), (1,)), ((), ()))
TN = (((0,), (0,)), ((), ()))
TT = (((0,), (1,)), ((), ()))


def mul(a, b, dims=NN):
    return lax.dot_general(a, b, dims, preferred_element_type=F32)


def layer_norm_back(values, gain, grad):
    centre = values - jnp.mean(values, axis=-1, keepdims=True)
    inverse = lax.rsqrt(jnp.mean(centre * centre, axis=-1, keepdims=True) + EPS)
    unit = centre * inverse
    scaled = grad * gain
    first = jnp.mean(scaled, axis=-1, keepdims=True)
    second = jnp.mean(scaled * unit, axis=-1, keepdims=True)
    return inverse * (scaled - first - unit * second)


def attend_kernel(q_ref, k_ref, v_ref, out_ref, log_ref):
    scores = mul(k_ref[0], q_ref[...])
    highest = jnp.max(scores, axis=0, keepdims=True)
    raised = jnp.exp(scores - highest)
    total = jnp.sum(raised, axis=0, keepdims=True)
    mixed = mul(v_ref[...], raised.astype(BF16))
    out_ref[...] = (mixed / total).astype(BF16)
    log_ref[...] = highest + jnp.log(total)


def attend(head, queries, keys, values, step=256):
    count = queries.shape[1]
    return pl.pallas_call(
        attend_kernel,
        grid=(count // step,),
        in_specs=[
            pl.BlockSpec((HEAD_DIM, step), lambda i: (head, i)),
            pl.BlockSpec((1, count, HEAD_DIM), lambda i: (head, 0, 0)),
            pl.BlockSpec((HEAD_DIM, count), lambda i: (head, 0)),
        ],
        out_specs=[
            pl.BlockSpec((HEAD_DIM, step), lambda i: (0, i)),
            pl.BlockSpec((1, step), lambda i: (0, i)),
        ],
        out_shape=[
            jax.ShapeDtypeStruct((HEAD_DIM, count), BF16),
            jax.ShapeDtypeStruct((1, count), F32),
        ],
        compiler_params=pltpu.CompilerParams(vmem_limit_bytes=48 * 2**20),
        cost_estimate=pl.CostEstimate(
            flops=40 * count * count * HEAD_DIM,
            bytes_accessed=8 * HEAD_DIM * count,
            transcendentals=count * count,
        ),
        name="attend",
    )(queries, keys, values)


def turn_back(values, cosine, sine):
    first, second = values[:HALF], values[HALF:]
    return jnp.concatenate([first * cosine + second * sine, second * cosine - first * sine], axis=0)


def attend_back_kernel(
    q_ref, kt_ref, k_ref, v_ref, up_ref, out_ref, log_ref, cos_ref, sin_ref, grad_ref, dk_ref, dv_ref
):
    index = pl.program_id(0)
    step = q_ref.shape[1]

    @pl.when(index == 0)
    def _():
        dk_ref[...] = jnp.zeros_like(dk_ref)
        dv_ref[...] = jnp.zeros_like(dv_ref)

    upstream = up_ref[...]
    inner_sum = jnp.sum(upstream.astype(F32) * out_ref[...].astype(F32), axis=0, keepdims=True)
    chances = jnp.exp(mul(k_ref[0], q_ref[...]) - log_ref[...])
    prob_back = mul(v_ref[0], upstream)
    score_back = (chances * (prob_back - inner_sum)).astype(BF16)
    dv_ref[...] += mul(chances.astype(BF16), upstream, NT)
    dk_ref[...] += mul(score_back, q_ref[...], NT)
    columns = pl.ds(pl.multiple_of(index * step, step), step)
    query_back = mul(kt_ref[...], score_back) * SCALE
    grad_ref[pl.ds(0, HEAD_DIM), columns] = turn_back(
        query_back, cos_ref[:, columns], sin_ref[:, columns]
    ).astype(BF16)

    @pl.when(index == pl.num_programs(0) - 1)
    def _():
        key_back = turn_back(dk_ref[...].T, cos_ref[...], sin_ref[...])
        grad_ref[pl.ds(HEAD_DIM, HEAD_DIM), :] = key_back.astype(BF16)
        grad_ref[pl.ds(2 * HEAD_DIM, HEAD_DIM), :] = dv_ref[...].T.astype(BF16)


def attend_back(head, queries, keys_turned, keys, values, upstream, merged, logs, cosine, sine, step=256):
    count = queries.shape[1]
    some = pl.BlockSpec((HEAD_DIM, step), lambda i: (head, i))
    rows = pl.BlockSpec((1, count, HEAD_DIM), lambda i: (head, 0, 0))
    whole = pl.BlockSpec((HALF, count), lambda i: (0, 0))
    return pl.pallas_call(
        attend_back_kernel,
        grid=(count // step,),
        in_specs=[
            some,
            pl.BlockSpec((HEAD_DIM, count), lambda i: (head, 0)),
            rows,
            rows,
            some,
            some,
            pl.BlockSpec((1, step), lambda i: (0, i)),
            whole,
            whole,
        ],
        out_specs=pl.BlockSpec((3 * HEAD_DIM, count), lambda i: (0, 0)),
        out_shape=jax.ShapeDtypeStruct((3 * HEAD_DIM, count), BF16),
        scratch_shapes=[pltpu.VMEM((count, HEAD_DIM), F32), pltpu.VMEM((count, HEAD_DIM), F32)],
        compiler_params=pltpu.CompilerParams(vmem_limit_bytes=48 * 2**20),
        cost_estimate=pl.CostEstimate(
            flops=56 * count * count * HEAD_DIM,
            bytes_accessed=16 * HEAD_DIM * count,
            transcendentals=count * count,
        ),
        name="attend_back",
    )(queries, keys_turned, keys, values, upstream, merged, logs, cosine, sine)


def load_rows(place_ref, mine_ref, other_ref, buffer, sems):
    z, core = place_ref[0], place_ref[1]
    size, rows = mine_ref.shape[0], mine_ref.shape[1]
    copies = []
    for d in range(size):
        for k, (ref, side) in enumerate(((mine_ref, core), (other_ref, 1 - core))):
            start = pl.multiple_of(side * rows, 16)
            copies.append(
                pltpu.make_async_copy(ref.at[d], buffer.at[z ^ d, pl.ds(start, rows), :], sems.at[d, k])
            )
    for copy in copies:
        copy.start()
    for copy in copies:
        copy.wait()


def unit_of(values):
    centre = values - jnp.mean(values, axis=-1, keepdims=True)
    inverse = lax.rsqrt(jnp.mean(centre * centre, axis=-1, keepdims=True) + EPS)
    return centre * inverse, inverse


def turn(values, cosine, sine):
    first, second = values[:HALF], values[HALF:]
    return jnp.concatenate([first * cosine - second * sine, second * cosine + first * sine], axis=0)


def project_kernel(
    place_ref, pair_ref, other_ref, gain_ref, cos_ref, sin_ref, mine_ref, theirs_ref,
    normed_ref, q_ref, kt_ref, vt_ref, k_ref, v_ref, into_ref, buffer, weight, sems, out_sem,
):
    index = pl.program_id(0)
    part = q_ref.shape[0]
    size = buffer.shape[0]
    save = pltpu.make_async_copy(buffer, into_ref, out_sem)

    @pl.when(index == 0)
    def _():
        load_rows(place_ref, mine_ref, theirs_ref, buffer, sems)
        save.start()
        start = pl.multiple_of(place_ref[1] * 2 * part, 128)
        odd = place_ref[0] & 1 == 1
        for t in range(3):
            both = buffer[:, t * part : (t + 1) * part, pl.ds(start, 2 * part)].reshape(size * part, 2 * part)
            chosen = jnp.where(odd, both[:, part:].astype(F32), both[:, :part].astype(F32))
            weight[:, t * part : (t + 1) * part] = chosen.astype(BF16)

    block = jnp.where(index < 2, pair_ref[...].astype(F32), other_ref[...].astype(F32))
    normed = (unit_of(block)[0] * gain_ref[...]).astype(BF16)
    normed_ref[...] = normed
    projected = mul(normed, weight[...])
    turned = projected.T
    cosine, sine = cos_ref[...], sin_ref[...]
    for head in range(part // HEAD_DIM):
        rows = slice(head * HEAD_DIM, (head + 1) * HEAD_DIM)
        queries = turn(turned[rows], cosine, sine).astype(BF16)
        q_ref[rows, :] = (queries.astype(F32) * SCALE).astype(BF16)
        keys = turn(turned[part + head * HEAD_DIM : part + (head + 1) * HEAD_DIM], cosine, sine)
        kt_ref[rows, :] = keys.astype(BF16)
        k_ref[head] = keys.T.astype(BF16)
        start = 2 * part + head * HEAD_DIM
        v_ref[head] = projected[:, start : start + HEAD_DIM].astype(BF16)
    vt_ref[...] = turned[2 * part :].astype(BF16)

    @pl.when(index == pl.num_programs(0) - 1)
    def _():
        save.wait()


def project(where, pair, other, gain, cosine, sine, mine, theirs, count):
    width = pair.shape[1]
    size, rows = mine.shape[0], 2 * mine.shape[1]
    part = width // size
    heads = part // HEAD_DIM
    total = size * count
    anywhere = pl.BlockSpec(memory_space=pl.ANY)
    columns = pl.BlockSpec((part, count), lambda i: (0, i))
    return pl.pallas_call(
        project_kernel,
        grid=(size,),
        in_specs=[
            pl.BlockSpec(memory_space=pltpu.SMEM),
            pl.BlockSpec((count, width), lambda i: (jnp.minimum(i, 1), 0)),
            pl.BlockSpec((count, width), lambda i: (jnp.maximum(i - 2, 0), 0)),
            pl.BlockSpec((1, width), lambda i: (0, 0)),
            pl.BlockSpec((HALF, count), lambda i: (0, i)),
            pl.BlockSpec((HALF, count), lambda i: (0, i)),
            anywhere,
            anywhere,
        ],
        out_specs=[
            pl.BlockSpec((count, width), lambda i: (i, 0)),
            columns,
            columns,
            columns,
            pl.BlockSpec((heads, count, HEAD_DIM), lambda i: (0, i, 0)),
            pl.BlockSpec((heads, count, HEAD_DIM), lambda i: (0, i, 0)),
            anywhere,
        ],
        out_shape=[
            jax.ShapeDtypeStruct((total, width), BF16),
            jax.ShapeDtypeStruct((part, total), BF16),
            jax.ShapeDtypeStruct((part, total), BF16),
            jax.ShapeDtypeStruct((part, total), BF16),
            jax.ShapeDtypeStruct((heads, total, HEAD_DIM), BF16),
            jax.ShapeDtypeStruct((heads, total, HEAD_DIM), BF16),
            jax.ShapeDtypeStruct((size, rows, width), BF16),
        ],
        scratch_shapes=[
            pltpu.VMEM((size, rows, width), BF16),
            pltpu.VMEM((width, 3 * part), BF16),
            pltpu.SemaphoreType.DMA((size, 2)),
            pltpu.SemaphoreType.DMA,
        ],
        compiler_params=pltpu.CompilerParams(vmem_limit_bytes=48 * 2**20),
        cost_estimate=pl.CostEstimate(flops=8 * 10**9, bytes_accessed=20 * 10**6, transcendentals=0),
        name="project",
    )(where, pair, other, gain, cosine, sine, mine, theirs)


def forward_back_kernel(
    place_ref, m0_ref, m1_ref, m2_ref, m3_ref, tokens_ref, up_ref, gain_ref, mine_ref, theirs_ref,
    result_ref, state_back_ref, low_ref, normed_ref, active_ref, inner_back_ref, b0_ref, b1_ref, b2_ref, b3_ref,
    buffer, sems,
):
    part, width = m0_ref.shape[0], tokens_ref.shape[1]
    size = buffer.shape[0]
    hidden = active_ref.shape[1]
    z = place_ref[0]

    @pl.when(pl.program_id(0) == 0)
    def _():
        load_rows(place_ref, mine_ref, theirs_ref, buffer, sems)

    expand = [buffer[:, (1 + t) * part : (2 + t) * part, :].reshape(width, width) for t in range(3)]
    contract = buffer[:, 4 * part : 4 * part + hidden // size, :].reshape(hidden, width)
    gain = gain_ref[...]

    state = tokens_ref[...].astype(F32)
    for k, ref in enumerate((m0_ref, m1_ref, m2_ref, m3_ref)):
        state = state + mul(ref[...], buffer[z ^ k, :part, :], TN)
    unit, inverse = unit_of(state)
    normed = (unit * gain).astype(BF16)
    normed_ref[...] = normed
    inner = jnp.concatenate([mul(normed, weight) for weight in expand], axis=1)
    first, second = inner[:, :hidden], inner[:, hidden:]
    chance = 0.5 + 0.5 * lax.erf(first * math.sqrt(0.5))
    gated = first * chance
    slope = chance + first * (jnp.exp(-0.5 * first * first) * (1.0 / math.sqrt(2.0 * math.pi)))
    active = (gated * second).astype(BF16)
    active_ref[...] = active
    result_ref[...] = (state + mul(active, contract)).astype(BF16)

    upstream = up_ref[...]
    active_back = mul(upstream, contract, NT).astype(BF16).astype(F32)
    inner_back = jnp.concatenate(
        [(active_back * second * slope).astype(BF16), (active_back * gated).astype(BF16)], axis=1
    )
    inner_back_ref[...] = inner_back
    normed_back = mul(inner_back[:, :width], expand[0], NT)
    normed_back = normed_back + mul(inner_back[:, width : 2 * width], expand[1], NT)
    normed_back = normed_back + mul(inner_back[:, 2 * width :], expand[2], NT)
    scaled = normed_back * gain
    mean = jnp.mean(scaled, axis=-1, keepdims=True)
    lean = jnp.mean(scaled * unit, axis=-1, keepdims=True)
    state_back = upstream.astype(F32) + inverse * (scaled - mean - unit * lean)
    state_back_ref[...] = state_back
    low = state_back.astype(BF16)
    low_ref[...] = low
    for k, ref in enumerate((b0_ref, b1_ref, b2_ref, b3_ref)):
        ref[...] = mul(buffer[z ^ k, :part, :], low, NT).astype(BF16)


def forward_back(where, merged, tokens, upstream, gain, mine, theirs, hidden, step=256):
    count, width = tokens.shape
    size, rows = mine.shape[0], 2 * mine.shape[1]
    part = width // size
    anywhere = pl.BlockSpec(memory_space=pl.ANY)
    columns = pl.BlockSpec((part, step), lambda i: (0, i))

    def some(lanes):
        return pl.BlockSpec((step, lanes), lambda i: (i, 0))

    lanes = [width, width, width, width, hidden, 2 * hidden]
    kinds = [BF16, F32, BF16, BF16, BF16, BF16]
    return pl.pallas_call(
        forward_back_kernel,
        grid=(count // step,),
        in_specs=[pl.BlockSpec(memory_space=pltpu.SMEM)]
        + [columns] * size
        + [some(width), some(width), pl.BlockSpec((1, width), lambda i: (0, 0)), anywhere, anywhere],
        out_specs=[some(n) for n in lanes] + [columns] * size,
        out_shape=[jax.ShapeDtypeStruct((count, n), kind) for n, kind in zip(lanes, kinds)]
        + [jax.ShapeDtypeStruct((part, count), BF16)] * size,
        scratch_shapes=[pltpu.VMEM((size, rows, width), BF16), pltpu.SemaphoreType.DMA((size, 2))],
        compiler_params=pltpu.CompilerParams(vmem_limit_bytes=56 * 2**20),
        cost_estimate=pl.CostEstimate(flops=14 * 10**9, bytes_accessed=20 * 10**6, transcendentals=0),
        name="forward_back",
    )(where, *merged, tokens, upstream, gain, mine, theirs)


def gradients_kernel(
    place_ref, m0_ref, m1_ref, m2_ref, m3_ref, up_ref, low_ref, normed_ref, active_ref, inner_back_ref,
    sent_ref, kept_ref, buffer, sems,
):
    z, core = place_ref[0], place_ref[1]
    part, width = m0_ref.shape[0], up_ref.shape[1]
    size, rows = buffer.shape[0], sent_ref.shape[1]
    hidden = active_ref.shape[1]
    held = hidden // size
    low = low_ref[...]
    for k, ref in enumerate((m0_ref, m1_ref, m2_ref, m3_ref)):
        buffer[z ^ k, :part, :] = mul(ref[...], low).astype(BF16)
    normed = normed_ref[...]
    for t in range(3):
        grad = mul(normed, inner_back_ref[:, t * width : (t + 1) * width], TN)
        buffer[:, (1 + t) * part : (2 + t) * part, :] = grad.astype(BF16).reshape(size, part, width)
    grad = mul(active_ref[...], up_ref[...], TN)
    buffer[:, 4 * part : 4 * part + held, :] = grad.astype(BF16).reshape(size, held, width)
    if 2 * rows > 4 * part + held:
        buffer[:, 4 * part + held :, :] = jnp.zeros((size, 2 * rows - 4 * part - held, width), BF16)
    copies = []
    for k, (ref, side) in enumerate(((sent_ref, 1 - core), (kept_ref, core))):
        start = pl.multiple_of(side * rows, 16)
        copies.append(pltpu.make_async_copy(buffer.at[:, pl.ds(start, rows), :], ref, sems.at[k]))
    for copy in copies:
        copy.start()
    for copy in copies:
        copy.wait()


def gradients(where, merged, upstream, low, normed, active, inner_back, rows):
    size = len(merged)
    width = upstream.shape[1]
    inside = pl.BlockSpec(memory_space=pltpu.VMEM)
    half = jax.ShapeDtypeStruct((size, rows // 2, width), BF16)
    return pl.pallas_call(
        gradients_kernel,
        in_specs=[pl.BlockSpec(memory_space=pltpu.SMEM)] + [inside] * (size + 5),
        out_specs=[pl.BlockSpec(memory_space=pl.ANY)] * 2,
        out_shape=[half, half],
        scratch_shapes=[pltpu.VMEM((size, rows, width), BF16), pltpu.SemaphoreType.DMA((2,))],
        compiler_params=pltpu.CompilerParams(vmem_limit_bytes=56 * 2**20),
        cost_estimate=pl.CostEstimate(flops=12 * 10**9, bytes_accessed=20 * 10**6, transcendentals=0),
        name="gradients",
    )(where, *merged, upstream, low, normed, active, inner_back)


def after(values, *others):
    return lax.optimization_barrier((values, others))[0]


def swap(values, axis, size, offset):
    return lax.ppermute(values, axis, [(i, i ^ offset) for i in range(size)])


def exchange(pieces, size):
    return [pieces[0]] + [swap(pieces[d], "fsdp", size, d) for d in range(1, size)]


def column(values, size, ranks, pairs):
    full = [
        (z * ranks + r, to * ranks + (r & ~1) + core)
        for z in range(size)
        for r in range(ranks)
        for to, core in pairs(z, r & 1)
    ]
    return lax.ppermute(values, ("fsdp", "rep"), full)


def collect(own, home, size, ranks):
    first = column(
        own, size, ranks, lambda z, c: [(z ^ 1, c) if c == z >> 1 else (z ^ 2, 1 - c)]
    )
    second = column(first, size, ranks, lambda z, c: [] if c == z >> 1 else [(z ^ 1, c)])
    low = jnp.where(home, own, first)
    high = jnp.where(home, first, second)
    pair = jnp.concatenate([low, high], axis=0)
    other = swap(pair, "rep", ranks, 1)
    return pair, other, second


def trade_out(pieces, size, ranks):
    def round_of(k):
        return lambda z, c: [((2 * c + (z & 1)) ^ k, z >> 1)]

    return [column(pieces[k], size, ranks, round_of(k)) for k in range(size)]


def trade_back(pieces, size, ranks):
    def round_of(k):
        return lambda z, c: [(2 * c + ((z ^ k) & 1), (z ^ k) >> 1)]

    return [column(pieces[k], size, ranks, round_of(k)) for k in range(size)]


def pick(blocks, index):
    return lax.dynamic_index_in_dim(blocks, index, 0, keepdims=False)


def reorder(blocks, z, size):
    return jnp.stack([pick(blocks, z ^ j) for j in range(size)])


def far(ranks):
    bits = []
    bit = 2
    while bit < ranks:
        bits.append(bit)
        bit *= 2
    return bits


def stage_bit(core, ranks, stage):
    bits = far(ranks)
    return bits[stage] if core == 0 else bits[len(bits) - 1 - stage]


def stage_swap(values, ranks, stage):
    return lax.ppermute(values, "rep", [(i, i ^ stage_bit(i & 1, ranks, stage)) for i in range(ranks)])


def stage_upper(r, ranks, stage):
    bit = jnp.where(r & 1 == 0, stage_bit(0, ranks, stage), stage_bit(1, ranks, stage))
    return r & bit != 0


def place(r, ranks):
    stages = len(far(ranks))
    total = jnp.where(r & 1 != 0, 1 << stages, 0)
    for stage in range(stages):
        total = total + jnp.where(stage_upper(r, ranks, stage), 1 << stage, 0)
    return total


def join(mine, other, upper):
    return jnp.concatenate([jnp.where(upper, other, mine), jnp.where(upper, mine, other)], axis=1)


def cut(values, upper):
    half = values.shape[1] // 2
    mine = jnp.where(upper, half, 0)
    sent = lax.dynamic_slice_in_dim(values, half - mine, half, 1)
    return sent, lax.dynamic_slice_in_dim(values, mine, half, 1)


def add(one, two):
    return (one.astype(F32) + two.astype(F32)).astype(BF16)


def grow(values, r, ranks, stages):
    for stage in stages:
        values = join(values, stage_swap(values, ranks, stage), stage_upper(r, ranks, stage))
    return values


def grow_far_flat(values, r, ranks, stages):
    for stage in stages:
        other = stage_swap(values, ranks, stage)
        upper = stage_upper(r, ranks, stage)
        values = jnp.concatenate(
            [jnp.where(upper, other, values), jnp.where(upper, values, other)], axis=0
        )
    return values


def grow_core(values, r, ranks):
    return join(values, swap(values, "rep", ranks, 1), r & 1 != 0)


def shrink(values, r, ranks, stages):
    for stage in stages:
        sent, kept = cut(values, stage_upper(r, ranks, stage))
        values = add(kept, stage_swap(sent, ranks, stage))
    return values


def shrink_core(values, r, ranks):
    sent, kept = cut(values, r & 1 != 0)
    return add(kept, swap(sent, "rep", ranks, 1))


def halves(values):
    middle = values.shape[-1] // 2
    return [values[..., :middle], values[..., middle:]]


def split_rows(shard, r, ranks):
    rows = shard.shape[0] // ranks
    return lax.dynamic_slice_in_dim(shard, place(r, ranks) * rows, rows, 0)


def finish_into_kernel(low_ref, high_ref, weight_ref, gain_ref, sum_ref, gain_sum_ref):
    part = sum_ref.shape[0]
    total = jnp.zeros((part, 1), F32)
    for t in range(3):
        blocks = [ref[g, :, t * part : (t + 1) * part] for ref in (low_ref, high_ref) for g in range(2)]
        row = jnp.concatenate([block.astype(F32) for block in blocks], axis=1)
        width = row.shape[1]
        sum_ref[:, t * width : (t + 1) * width] = row
        weight = weight_ref[:, t * width : (t + 1) * width].astype(F32)
        total = total + jnp.sum(row * weight, axis=1, keepdims=True)
    gain_sum_ref[...] = total / gain_ref[...].astype(F32)


def finish_into(low, high, weight, gain):
    part = weight.shape[0]
    return pl.pallas_call(
        finish_into_kernel,
        out_shape=[
            jax.ShapeDtypeStruct(weight.shape, F32),
            jax.ShapeDtypeStruct((part, 1), F32),
        ],
        compiler_params=pltpu.CompilerParams(vmem_limit_bytes=32 * 2**20),
        name="finish_into",
    )(low, high, weight, gain[:, None])


def finish_rest_kernel(grads_ref, weight_ref, gain_ref, out_ref, expand_ref, contract_ref, gain_sum_ref):
    part, width = out_ref.shape
    hidden = contract_ref.shape[0]
    total = jnp.zeros((part, 1), F32)
    out_ref[...] = grads_ref[:part].astype(F32)
    for t in range(3):
        rows = grads_ref[(1 + t) * part : (2 + t) * part].astype(F32)
        expand_ref[:, t * width : (t + 1) * width] = rows
        weight = weight_ref[:, t * width : (t + 1) * width].astype(F32)
        total = total + jnp.sum(rows * weight, axis=1, keepdims=True)
    contract_ref[...] = grads_ref[4 * part : 4 * part + hidden].astype(F32)
    gain_sum_ref[...] = total / gain_ref[...].astype(F32)


def finish_rest(grads, weight, gain, hidden):
    part = weight.shape[0]
    width = grads.shape[1]
    return pl.pallas_call(
        finish_rest_kernel,
        out_shape=[
            jax.ShapeDtypeStruct((part, width), F32),
            jax.ShapeDtypeStruct(weight.shape, F32),
            jax.ShapeDtypeStruct((hidden, width), F32),
            jax.ShapeDtypeStruct((part, 1), F32),
        ],
        compiler_params=pltpu.CompilerParams(vmem_limit_bytes=32 * 2**20),
        name="finish_rest",
    )(grads, weight, gain[:, None])


def local(size, ranks, tokens, gain_a, projection_in, attention_out, gain_b, expansion, contraction, cotangent):
    z = lax.axis_index("fsdp")
    r = lax.axis_index("rep")
    core = r & 1
    group = 2 * core + (z & 1)
    home = core == z >> 1
    own = tokens[0]
    count, width = own.shape
    part = width // size
    hidden = contraction.shape[0]
    heads = HEADS // size

    stages = list(range(len(far(ranks))))
    where = jnp.stack([z, core]).astype(jnp.int32)
    columns = [projection_in[:, t * width : (t + 1) * width] for t in range(3)]
    piece = split_rows(jnp.concatenate(columns, axis=0), r, ranks)
    rows = piece.shape[0]
    gains = jnp.pad(jnp.concatenate([gain_a, gain_b])[None], ((0, 7), (0, width - 2 * part)))
    pieces = jnp.stack(exchange([jnp.concatenate([piece, gains], axis=0)] * size, size))
    pair, other, second = collect(own, home, size, ranks)
    gains = reorder(pieces[:, rows, : 2 * part], z, size).astype(F32)
    gain_one = gains[:, :part].reshape(1, width)
    gain_two = gains[:, part:].reshape(1, width)
    into = grow(pieces[:, :rows], r, ranks, stages)
    into_other = swap(into, "rep", ranks, 1)

    freqs = THETA ** (-(jnp.arange(HALF, dtype=F32) * (2.0 / HEAD_DIM)))
    places = jnp.concatenate([(group ^ d) * count + jnp.arange(count, dtype=jnp.int32) for d in range(size)])
    angles = freqs[:, None] * places.astype(F32)[None, :]
    cosine, sine = jnp.cos(angles), jnp.sin(angles)
    normed, queries, keys_turned, values_turned, keys, values, into = project(
        where, pair, other, gain_one, cosine, sine, into, into_other, count
    )

    columns = [expansion[:, t * width : (t + 1) * width] for t in range(3)]
    stacked = jnp.concatenate([attention_out] + columns + [contraction], axis=0)
    pad = -stacked.shape[0] % max(32, 8 * ranks)
    stacked = jnp.concatenate([stacked, jnp.zeros((pad, width), BF16)], axis=0)
    rest = exchange([split_rows(after(stacked, second), r, ranks)] * size, size)
    merged = []
    logs = []
    rest = grow(jnp.stack(after(rest, queries)), r, ranks, stages[:1])
    ahead = []
    for head in range(heads):
        out, log = attend(head, queries, after(keys, *ahead), values_turned)
        merged.append(out)
        logs.append(log)
        if head == 0:
            ahead = [rest]
            rest = grow(after(rest, out), r, ranks, stages[1:-1])
            sides = halves(rest)
        if head < 2:
            sides[head] = grow(after(sides[head], out), r, ranks, stages[-1:])
            ahead = ahead if head == 0 else [sides[0]]
    rest = after(jnp.concatenate(sides, axis=2), merged[-1])
    rest_other = swap(rest, "rep", ranks, 1)
    own_merged = jnp.concatenate(merged, axis=0)

    merged = trade_out([own_merged[:, d * count : (d + 1) * count] for d in range(size)], size, ranks)
    upstream = cotangent[0]
    block_output, state_back, state_low, normed_two, active, inner_back, *merged_back = forward_back(
        where, merged, own, upstream, gain_two, rest, rest_other, size * hidden
    )
    arrived = trade_back(merged_back, size, ranks)
    own_upstream = jnp.concatenate(arrived, axis=1)

    sent, kept = gradients(
        where, merged, upstream, state_low, normed_two, active, inner_back, stacked.shape[0]
    )
    grads = add(kept, swap(sent, "rep", ranks, 1))

    turned_backs = []
    received = []
    ahead = [grads]
    for head in range(heads):
        grad = attend_back(
            head, queries, keys_turned, keys, values, after(own_upstream, *ahead), own_merged, logs[head], cosine, sine
        )
        turned_backs.append(grad)
        if head == 0:
            received = trade_out([grad[:, d * count : (d + 1) * count] for d in range(size)], size, ranks)
            grads = shrink(grads, r, ranks, stages[:0:-1])
            ahead = [grads]
        if head == 1:
            grads = shrink(grads, r, ranks, stages[:1])
            ahead = [grads] + received
    grads = exchange([pick(grads, z ^ d) for d in range(size)], size)
    grads = sum(part.astype(F32) for part in grads).astype(BF16)
    later = jnp.concatenate(turned_backs[1:], axis=0)
    turned_backs[2], grads = after((turned_backs[2], grads), later)
    later = after(later, grads)
    later = trade_out([later[:, d * count : (d + 1) * count] for d in range(size)], size, ranks)
    received = [jnp.concatenate(both, axis=0) for both in zip(received, later)]

    into = [into[:, t * part : (t + 1) * part].reshape(width, width) for t in range(3)]
    projected_back = reorder(jnp.stack(received), z, size).reshape(size, heads, 3, HEAD_DIM, count)
    projected_back = projected_back.transpose(2, 0, 1, 3, 4).reshape(3, width, count)
    normed_back = sum(mul(projected_back[t], into[t], TT) for t in range(3))
    token_grad = (state_back + layer_norm_back(own.astype(F32), gain_one, normed_back))[None]

    all_backs = jnp.stack(turned_backs).reshape(heads, 3, HEAD_DIM, size * count)
    all_backs = all_backs.transpose(1, 0, 2, 3).reshape(3 * part, size * count)
    into_grad = mul(normed, all_backs, TT).astype(BF16).reshape(size, part, 3 * part)
    into_grad = shrink(into_grad, r, ranks, stages[::-1])
    arrived = exchange([pick(into_grad, z ^ d) for d in range(size)], size)
    even = (arrived[0].astype(F32) + arrived[2].astype(F32)).astype(BF16)
    odd = (arrived[1].astype(F32) + arrived[3].astype(F32)).astype(BF16)
    low = z & 1 == 0
    into_sum = jnp.stack([jnp.where(low, even, odd), jnp.where(low, odd, even)])
    flat = into_sum.reshape(-1, width)
    both = jnp.concatenate([flat, grads], axis=0)[None]
    both = grow_far_flat(both, r, ranks, stages)
    other = swap(both, "rep", ranks, 1)
    low = core == 0
    one, two = jnp.where(low, both, other), jnp.where(low, other, both)
    rows = flat.shape[0]
    shape = (-1, into_sum.shape[0]) + into_sum.shape[1:]
    low_into, high_into = [
        side[:, :rows].reshape(shape).transpose(1, 0, 2, 3).reshape(2, part, 3 * part) for side in (one, two)
    ]
    grads = jnp.concatenate([one[:, rows:].reshape(-1, width), two[:, rows:].reshape(-1, width)], axis=0)
    into_sum, gain_one_sum = finish_into(low_into, high_into, projection_in, gain_a)
    attention_out_sum, expansion_sum, contraction_sum, gain_two_sum = finish_rest(
        grads, expansion, gain_b, hidden
    )
    return (
        block_output[None],
        token_grad,
        gain_one_sum[:, 0],
        into_sum,
        attention_out_sum,
        gain_two_sum[:, 0],
        expansion_sum,
        contraction_sum,
    )


def solution(mesh):
    tokens, rows, line = P("rep", "fsdp", None), P("fsdp", None), P("fsdp")
    in_specs = (tokens, line, rows, rows, line, rows, rows, tokens)
    out_specs = (tokens, tokens, line, rows, rows, line, rows, rows)
    body = functools.partial(local, mesh.shape["fsdp"], mesh.shape["rep"])
    return jax.shard_map(body, mesh=mesh, in_specs=in_specs, out_specs=out_specs, check_vma=False)
```

```python
import functools
import math

import jax
import jax.numpy as jnp
from jax import lax
from jax.experimental import pallas as pl
from jax.experimental.pallas import tpu as pltpu
from jax.sharding import PartitionSpec as P

HEADS = 12
HEAD_DIM = 64
HALF = HEAD_DIM // 2
SCALE = 1.0 / math.sqrt(HEAD_DIM)
EPS = 1e-05
THETA = 160000.0
F32 = jnp.float32
BF16 = jnp.bfloat16
NN = (((1,), (0,)), ((), ()))
NT = (((1,), (1,)), ((), ()))
TN = (((0,), (0,)), ((), ()))
TT = (((0,), (1,)), ((), ()))


def mul(a, b, dims=NN):
    return lax.dot_general(a, b, dims, preferred_element_type=F32)


def layer_norm_back(values, gain, grad):
    centre = values - jnp.mean(values, axis=-1, keepdims=True)
    inverse = lax.rsqrt(jnp.mean(centre * centre, axis=-1, keepdims=True) + EPS)
    unit = centre * inverse
    scaled = grad * gain
    first = jnp.mean(scaled, axis=-1, keepdims=True)
    second = jnp.mean(scaled * unit, axis=-1, keepdims=True)
    return inverse * (scaled - first - unit * second)


def attend_kernel(q_ref, k_ref, v_ref, out_ref, log_ref):
    scores = mul(k_ref[0], q_ref[...])
    highest = jnp.max(scores, axis=0, keepdims=True)
    raised = jnp.exp(scores - highest)
    total = jnp.sum(raised, axis=0, keepdims=True)
    mixed = mul(v_ref[...], raised.astype(BF16))
    out_ref[...] = (mixed / total).astype(BF16)
    log_ref[...] = highest + jnp.log(total)


def attend(head, queries, keys, values, step=256):
    count = queries.shape[1]
    return pl.pallas_call(
        attend_kernel,
        grid=(count // step,),
        in_specs=[
            pl.BlockSpec((HEAD_DIM, step), lambda i: (head, i)),
            pl.BlockSpec((1, count, HEAD_DIM), lambda i: (head, 0, 0)),
            pl.BlockSpec((HEAD_DIM, count), lambda i: (head, 0)),
        ],
        out_specs=[
            pl.BlockSpec((HEAD_DIM, step), lambda i: (0, i)),
            pl.BlockSpec((1, step), lambda i: (0, i)),
        ],
        out_shape=[
            jax.ShapeDtypeStruct((HEAD_DIM, count), BF16),
            jax.ShapeDtypeStruct((1, count), F32),
        ],
        compiler_params=pltpu.CompilerParams(vmem_limit_bytes=48 * 2**20),
        cost_estimate=pl.CostEstimate(
            flops=40 * count * count * HEAD_DIM,
            bytes_accessed=8 * HEAD_DIM * count,
            transcendentals=count * count,
        ),
        name="attend",
    )(queries, keys, values)


def turn_back(values, cosine, sine):
    first, second = values[:HALF], values[HALF:]
    return jnp.concatenate([first * cosine + second * sine, second * cosine - first * sine], axis=0)


def attend_back_kernel(
    q_ref, kt_ref, k_ref, v_ref, up_ref, out_ref, log_ref, cos_ref, sin_ref, normed_ref, grad_ref, weight_ref, dk_ref, dv_ref
):
    index = pl.program_id(0)
    step = q_ref.shape[1]

    @pl.when(index == 0)
    def _():
        dk_ref[...] = jnp.zeros_like(dk_ref)
        dv_ref[...] = jnp.zeros_like(dv_ref)

    upstream = up_ref[...]
    inner_sum = jnp.sum(upstream.astype(F32) * out_ref[...].astype(F32), axis=0, keepdims=True)
    chances = jnp.exp(mul(k_ref[0], q_ref[...]) - log_ref[...])
    prob_back = mul(v_ref[0], upstream)
    score_back = (chances * (prob_back - inner_sum)).astype(BF16)
    dv_ref[...] += mul(chances.astype(BF16), upstream, NT)
    dk_ref[...] += mul(score_back, q_ref[...], NT)
    columns = pl.ds(pl.multiple_of(index * step, step), step)
    query_back = mul(kt_ref[...], score_back) * SCALE
    grad_ref[pl.ds(0, HEAD_DIM), columns] = turn_back(
        query_back, cos_ref[:, columns], sin_ref[:, columns]
    ).astype(BF16)

    @pl.when(index == pl.num_programs(0) - 1)
    def _():
        key_back = turn_back(dk_ref[...].T, cos_ref[...], sin_ref[...])
        grad_ref[pl.ds(HEAD_DIM, HEAD_DIM), :] = key_back.astype(BF16)
        grad_ref[pl.ds(2 * HEAD_DIM, HEAD_DIM), :] = dv_ref[...].T.astype(BF16)
        weight_ref[...] = mul(grad_ref[...], normed_ref[...]).astype(BF16)


def attend_back(head, queries, keys_turned, keys, values, upstream, merged, logs, cosine, sine, normed, step=256):
    count, width = normed.shape
    some = pl.BlockSpec((HEAD_DIM, step), lambda i: (head, i))
    rows = pl.BlockSpec((1, count, HEAD_DIM), lambda i: (head, 0, 0))
    whole = pl.BlockSpec((HALF, count), lambda i: (0, 0))
    return pl.pallas_call(
        attend_back_kernel,
        grid=(count // step,),
        in_specs=[
            some,
            pl.BlockSpec((HEAD_DIM, count), lambda i: (head, 0)),
            rows,
            rows,
            some,
            some,
            pl.BlockSpec((1, step), lambda i: (0, i)),
            whole,
            whole,
            pl.BlockSpec((count, width), lambda i: (0, 0)),
        ],
        out_specs=[
            pl.BlockSpec((3 * HEAD_DIM, count), lambda i: (0, 0)),
            pl.BlockSpec((3 * HEAD_DIM, width), lambda i: (0, 0)),
        ],
        out_shape=[
            jax.ShapeDtypeStruct((3 * HEAD_DIM, count), BF16),
            jax.ShapeDtypeStruct((3 * HEAD_DIM, width), BF16),
        ],
        scratch_shapes=[pltpu.VMEM((count, HEAD_DIM), F32), pltpu.VMEM((count, HEAD_DIM), F32)],
        compiler_params=pltpu.CompilerParams(vmem_limit_bytes=48 * 2**20),
        cost_estimate=pl.CostEstimate(
            flops=56 * count * count * HEAD_DIM,
            bytes_accessed=16 * HEAD_DIM * count,
            transcendentals=count * count,
        ),
        name="attend_back",
    )(queries, keys_turned, keys, values, upstream, merged, logs, cosine, sine, normed)


def load_rows(place_ref, mine_ref, other_ref, buffer, sems):
    z, core = place_ref[0], place_ref[1]
    size, rows = mine_ref.shape[0], mine_ref.shape[1]
    copies = []
    for d in range(size):
        for k, (ref, side) in enumerate(((mine_ref, core), (other_ref, 1 - core))):
            start = pl.multiple_of(side * rows, 16)
            copies.append(
                pltpu.make_async_copy(ref.at[d], buffer.at[z ^ d, pl.ds(start, rows), :], sems.at[d, k])
            )
    for copy in copies:
        copy.start()
    for copy in copies:
        copy.wait()


def unit_of(values):
    centre = values - jnp.mean(values, axis=-1, keepdims=True)
    inverse = lax.rsqrt(jnp.mean(centre * centre, axis=-1, keepdims=True) + EPS)
    return centre * inverse, inverse


def turn(values, cosine, sine):
    first, second = values[:HALF], values[HALF:]
    return jnp.concatenate([first * cosine - second * sine, second * cosine + first * sine], axis=0)


def project_kernel(
    place_ref, pair_ref, other_ref, gain_ref, cos_ref, sin_ref, mine_ref, theirs_ref,
    normed_ref, q_ref, kt_ref, vt_ref, k_ref, v_ref, into_ref, buffer, weight, sems, out_sem,
):
    index = pl.program_id(0)
    part = q_ref.shape[0]
    size = buffer.shape[0]
    save = pltpu.make_async_copy(buffer, into_ref, out_sem)

    @pl.when(index == 0)
    def _():
        load_rows(place_ref, mine_ref, theirs_ref, buffer, sems)
        save.start()
        start = pl.multiple_of(place_ref[1] * 2 * part, 128)
        odd = place_ref[0] & 1 == 1
        for t in range(3):
            both = buffer[:, t * part : (t + 1) * part, pl.ds(start, 2 * part)].reshape(size * part, 2 * part)
            chosen = jnp.where(odd, both[:, part:].astype(F32), both[:, :part].astype(F32))
            weight[:, t * part : (t + 1) * part] = chosen.astype(BF16)

    block = jnp.where(index < 2, pair_ref[...].astype(F32), other_ref[...].astype(F32))
    normed = (unit_of(block)[0] * gain_ref[...]).astype(BF16)
    normed_ref[...] = normed
    projected = mul(normed, weight[...])
    turned = projected.T
    cosine, sine = cos_ref[...], sin_ref[...]
    for head in range(part // HEAD_DIM):
        rows = slice(head * HEAD_DIM, (head + 1) * HEAD_DIM)
        queries = turn(turned[rows], cosine, sine).astype(BF16)
        q_ref[rows, :] = (queries.astype(F32) * SCALE).astype(BF16)
        keys = turn(turned[part + head * HEAD_DIM : part + (head + 1) * HEAD_DIM], cosine, sine)
        kt_ref[rows, :] = keys.astype(BF16)
        k_ref[head] = keys.T.astype(BF16)
        start = 2 * part + head * HEAD_DIM
        v_ref[head] = projected[:, start : start + HEAD_DIM].astype(BF16)
    vt_ref[...] = turned[2 * part :].astype(BF16)

    @pl.when(index == pl.num_programs(0) - 1)
    def _():
        save.wait()


def project(where, pair, other, gain, cosine, sine, mine, theirs, count):
    width = pair.shape[1]
    size, rows = mine.shape[0], 2 * mine.shape[1]
    part = width // size
    heads = part // HEAD_DIM
    total = size * count
    anywhere = pl.BlockSpec(memory_space=pl.ANY)
    columns = pl.BlockSpec((part, count), lambda i: (0, i))
    return pl.pallas_call(
        project_kernel,
        grid=(size,),
        in_specs=[
            pl.BlockSpec(memory_space=pltpu.SMEM),
            pl.BlockSpec((count, width), lambda i: (jnp.minimum(i, 1), 0)),
            pl.BlockSpec((count, width), lambda i: (jnp.maximum(i - 2, 0), 0)),
            pl.BlockSpec((1, width), lambda i: (0, 0)),
            pl.BlockSpec((HALF, count), lambda i: (0, i)),
            pl.BlockSpec((HALF, count), lambda i: (0, i)),
            anywhere,
            anywhere,
        ],
        out_specs=[
            pl.BlockSpec((count, width), lambda i: (i, 0)),
            columns,
            columns,
            columns,
            pl.BlockSpec((heads, count, HEAD_DIM), lambda i: (0, i, 0)),
            pl.BlockSpec((heads, count, HEAD_DIM), lambda i: (0, i, 0)),
            anywhere,
        ],
        out_shape=[
            jax.ShapeDtypeStruct((total, width), BF16),
            jax.ShapeDtypeStruct((part, total), BF16),
            jax.ShapeDtypeStruct((part, total), BF16),
            jax.ShapeDtypeStruct((part, total), BF16),
            jax.ShapeDtypeStruct((heads, total, HEAD_DIM), BF16),
            jax.ShapeDtypeStruct((heads, total, HEAD_DIM), BF16),
            jax.ShapeDtypeStruct((size, rows, width), BF16),
        ],
        scratch_shapes=[
            pltpu.VMEM((size, rows, width), BF16),
            pltpu.VMEM((width, 3 * part), BF16),
            pltpu.SemaphoreType.DMA((size, 2)),
            pltpu.SemaphoreType.DMA,
        ],
        compiler_params=pltpu.CompilerParams(vmem_limit_bytes=48 * 2**20),
        cost_estimate=pl.CostEstimate(flops=8 * 10**9, bytes_accessed=20 * 10**6, transcendentals=0),
        name="project",
    )(where, pair, other, gain, cosine, sine, mine, theirs)


def forward_back_kernel(
    place_ref, m0_ref, m1_ref, m2_ref, m3_ref, tokens_ref, up_ref, gain_ref, mine_ref, theirs_ref,
    result_ref, state_back_ref, low_ref, normed_ref, active_ref, inner_back_ref, b0_ref, b1_ref, b2_ref, b3_ref,
    buffer, sems,
):
    part, width = m0_ref.shape[0], tokens_ref.shape[1]
    size = buffer.shape[0]
    hidden = active_ref.shape[1]
    z = place_ref[0]

    @pl.when(pl.program_id(0) == 0)
    def _():
        load_rows(place_ref, mine_ref, theirs_ref, buffer, sems)

    expand = [buffer[:, (1 + t) * part : (2 + t) * part, :].reshape(width, width) for t in range(3)]
    contract = buffer[:, 4 * part : 4 * part + hidden // size, :].reshape(hidden, width)
    gain = gain_ref[...]

    state = tokens_ref[...].astype(F32)
    for k, ref in enumerate((m0_ref, m1_ref, m2_ref, m3_ref)):
        state = state + mul(ref[...], buffer[z ^ k, :part, :], TN)
    unit, inverse = unit_of(state)
    normed = (unit * gain).astype(BF16)
    normed_ref[...] = normed
    inner = jnp.concatenate([mul(normed, weight) for weight in expand], axis=1)
    first, second = inner[:, :hidden], inner[:, hidden:]
    chance = 0.5 + 0.5 * lax.erf(first * math.sqrt(0.5))
    gated = first * chance
    slope = chance + first * (jnp.exp(-0.5 * first * first) * (1.0 / math.sqrt(2.0 * math.pi)))
    active = (gated * second).astype(BF16)
    active_ref[...] = active
    result_ref[...] = (state + mul(active, contract)).astype(BF16)

    upstream = up_ref[...]
    active_back = mul(upstream, contract, NT).astype(BF16).astype(F32)
    inner_back = jnp.concatenate(
        [(active_back * second * slope).astype(BF16), (active_back * gated).astype(BF16)], axis=1
    )
    inner_back_ref[...] = inner_back
    normed_back = mul(inner_back[:, :width], expand[0], NT)
    normed_back = normed_back + mul(inner_back[:, width : 2 * width], expand[1], NT)
    normed_back = normed_back + mul(inner_back[:, 2 * width :], expand[2], NT)
    scaled = normed_back * gain
    mean = jnp.mean(scaled, axis=-1, keepdims=True)
    lean = jnp.mean(scaled * unit, axis=-1, keepdims=True)
    state_back = upstream.astype(F32) + inverse * (scaled - mean - unit * lean)
    state_back_ref[...] = state_back
    low = state_back.astype(BF16)
    low_ref[...] = low
    for k, ref in enumerate((b0_ref, b1_ref, b2_ref, b3_ref)):
        ref[...] = mul(buffer[z ^ k, :part, :], low, NT).astype(BF16)


def forward_back(where, merged, tokens, upstream, gain, mine, theirs, hidden, step=256):
    count, width = tokens.shape
    size, rows = mine.shape[0], 2 * mine.shape[1]
    part = width // size
    anywhere = pl.BlockSpec(memory_space=pl.ANY)
    columns = pl.BlockSpec((part, step), lambda i: (0, i))

    def some(lanes):
        return pl.BlockSpec((step, lanes), lambda i: (i, 0))

    lanes = [width, width, width, width, hidden, 2 * hidden]
    kinds = [BF16, F32, BF16, BF16, BF16, BF16]
    return pl.pallas_call(
        forward_back_kernel,
        grid=(count // step,),
        in_specs=[pl.BlockSpec(memory_space=pltpu.SMEM)]
        + [columns] * size
        + [some(width), some(width), pl.BlockSpec((1, width), lambda i: (0, 0)), anywhere, anywhere],
        out_specs=[some(n) for n in lanes] + [columns] * size,
        out_shape=[jax.ShapeDtypeStruct((count, n), kind) for n, kind in zip(lanes, kinds)]
        + [jax.ShapeDtypeStruct((part, count), BF16)] * size,
        scratch_shapes=[pltpu.VMEM((size, rows, width), BF16), pltpu.SemaphoreType.DMA((size, 2))],
        compiler_params=pltpu.CompilerParams(vmem_limit_bytes=56 * 2**20),
        cost_estimate=pl.CostEstimate(flops=14 * 10**9, bytes_accessed=20 * 10**6, transcendentals=0),
        name="forward_back",
    )(where, *merged, tokens, upstream, gain, mine, theirs)


def gradients_kernel(
    place_ref, m0_ref, m1_ref, m2_ref, m3_ref, up_ref, low_ref, normed_ref, active_ref, inner_back_ref, grads_ref
):
    z = place_ref[0]
    part, width = m0_ref.shape[0], up_ref.shape[1]
    size, rows, lanes = grads_ref.shape
    held = active_ref.shape[1] // size
    start = pl.multiple_of(place_ref[1] * lanes, 128)
    low = low_ref[:, pl.ds(start, lanes)]
    for k, ref in enumerate((m0_ref, m1_ref, m2_ref, m3_ref)):
        grads_ref[z ^ k, :part, :] = mul(ref[...], low).astype(BF16)
    normed = normed_ref[...]
    for t in range(3):
        grad = mul(normed, inner_back_ref[:, pl.ds(t * width + start, lanes)], TN)
        grads_ref[:, (1 + t) * part : (2 + t) * part, :] = grad.astype(BF16).reshape(size, part, lanes)
    grad = mul(active_ref[...], up_ref[:, pl.ds(start, lanes)], TN)
    grads_ref[:, 4 * part : 4 * part + held, :] = grad.astype(BF16).reshape(size, held, lanes)
    if rows > 4 * part + held:
        grads_ref[:, 4 * part + held :, :] = jnp.zeros((size, rows - 4 * part - held, lanes), BF16)


def gradients(where, merged, upstream, low, normed, active, inner_back, rows):
    size = len(merged)
    lanes = upstream.shape[1] // 2
    inside = pl.BlockSpec(memory_space=pltpu.VMEM)
    return pl.pallas_call(
        gradients_kernel,
        in_specs=[pl.BlockSpec(memory_space=pltpu.SMEM)] + [inside] * (size + 5),
        out_specs=inside,
        out_shape=jax.ShapeDtypeStruct((size, rows, lanes), BF16),
        compiler_params=pltpu.CompilerParams(vmem_limit_bytes=48 * 2**20),
        cost_estimate=pl.CostEstimate(flops=6 * 10**9, bytes_accessed=12 * 10**6, transcendentals=0),
        name="gradients",
    )(where, *merged, upstream, low, normed, active, inner_back)


def after(values, *others):
    return lax.optimization_barrier((values, others))[0]


def swap(values, axis, size, offset):
    return lax.ppermute(values, axis, [(i, i ^ offset) for i in range(size)])


def exchange(pieces, size):
    return [pieces[0]] + [swap(pieces[d], "fsdp", size, d) for d in range(1, size)]


def column(values, size, ranks, pairs):
    full = [
        (z * ranks + r, to * ranks + (r & ~1) + core)
        for z in range(size)
        for r in range(ranks)
        for to, core in pairs(z, r & 1)
    ]
    return lax.ppermute(values, ("fsdp", "rep"), full)


def collect(own, home, size, ranks):
    first = column(
        own, size, ranks, lambda z, c: [(z ^ 1, c) if c == z >> 1 else (z ^ 2, 1 - c)]
    )
    second = column(first, size, ranks, lambda z, c: [] if c == z >> 1 else [(z ^ 1, c)])
    low = jnp.where(home, own, first)
    high = jnp.where(home, first, second)
    pair = jnp.concatenate([low, high], axis=0)
    other = swap(pair, "rep", ranks, 1)
    return pair, other, second


def trade_out(pieces, size, ranks):
    def round_of(k):
        return lambda z, c: [((2 * c + (z & 1)) ^ k, z >> 1)]

    return [column(pieces[k], size, ranks, round_of(k)) for k in range(size)]


def trade_back(pieces, size, ranks):
    def round_of(k):
        return lambda z, c: [(2 * c + ((z ^ k) & 1), (z ^ k) >> 1)]

    return [column(pieces[k], size, ranks, round_of(k)) for k in range(size)]


def pick(blocks, index):
    return lax.dynamic_index_in_dim(blocks, index, 0, keepdims=False)


def reorder(blocks, z, size):
    return jnp.stack([pick(blocks, z ^ j) for j in range(size)])


def far(ranks):
    bits = []
    bit = 2
    while bit < ranks:
        bits.append(bit)
        bit *= 2
    return bits


def stage_bit(core, ranks, stage):
    bits = far(ranks)
    return bits[stage] if core == 0 else bits[len(bits) - 1 - stage]


def stage_swap(values, ranks, stage):
    return lax.ppermute(values, "rep", [(i, i ^ stage_bit(i & 1, ranks, stage)) for i in range(ranks)])


def stage_upper(r, ranks, stage):
    bit = jnp.where(r & 1 == 0, stage_bit(0, ranks, stage), stage_bit(1, ranks, stage))
    return r & bit != 0


def place(r, ranks):
    stages = len(far(ranks))
    total = jnp.where(r & 1 != 0, 1 << stages, 0)
    for stage in range(stages):
        total = total + jnp.where(stage_upper(r, ranks, stage), 1 << stage, 0)
    return total


def join(mine, other, upper):
    return jnp.concatenate([jnp.where(upper, other, mine), jnp.where(upper, mine, other)], axis=1)


def cut(values, upper):
    half = values.shape[1] // 2
    mine = jnp.where(upper, half, 0)
    sent = lax.dynamic_slice_in_dim(values, half - mine, half, 1)
    return sent, lax.dynamic_slice_in_dim(values, mine, half, 1)


def add(one, two):
    return (one.astype(F32) + two.astype(F32)).astype(BF16)


def grow(values, r, ranks, stages):
    for stage in stages:
        values = join(values, stage_swap(values, ranks, stage), stage_upper(r, ranks, stage))
    return values


def grow_flat(values, r, ranks, stages):
    for stage in stages:
        other = stage_swap(values, ranks, stage)
        upper = stage_upper(r, ranks, stage)
        values = jnp.concatenate(
            [jnp.where(upper, other, values), jnp.where(upper, values, other)], axis=0
        )
    return values


def shrink(values, r, ranks, stages):
    for stage in stages:
        sent, kept = cut(values, stage_upper(r, ranks, stage))
        values = add(kept, stage_swap(sent, ranks, stage))
    return values


def halves(values):
    middle = values.shape[-1] // 2
    return [values[..., :middle], values[..., middle:]]


def split_rows(shard, r, ranks):
    rows = shard.shape[0] // ranks
    return lax.dynamic_slice_in_dim(shard, place(r, ranks) * rows, rows, 0)


def finish_kernel(
    place_ref, mine_ref, other_ref, into_ref, expand_ref, gain_a_ref, gain_b_ref,
    into_sum_ref, gain_a_sum_ref, out_sum_ref, expand_sum_ref, gain_b_sum_ref, contract_sum_ref,
):
    first = place_ref[1] == 0
    part, width = out_sum_ref.shape
    held = contract_sum_ref.shape[0]
    pieces = mine_ref.shape[0]
    lines = 3 * part // pieces

    def gathered(start):
        rows = mine_ref.shape[1] if start else lines
        sides = []
        for one, two in ((mine_ref, other_ref), (other_ref, mine_ref)):
            blocks = [
                jnp.where(first, one[p, start:rows].astype(F32), two[p, start:rows].astype(F32))
                for p in range(pieces)
            ]
            sides.append(jnp.concatenate(blocks, axis=0))
        return sides

    blocks = [side[:, k * part : (k + 1) * part].T for side in gathered(0) for k in range(2)]
    total = jnp.zeros((part, 1), F32)
    for t in range(3):
        row = jnp.concatenate([block[:, t * part : (t + 1) * part] for block in blocks], axis=1)
        into_sum_ref[:, t * width : (t + 1) * width] = row
        weight = into_ref[:, t * width : (t + 1) * width].astype(F32)
        total = total + jnp.sum(row * weight, axis=1, keepdims=True)
    gain_a_sum_ref[...] = total / gain_a_ref[...].astype(F32)

    grads = jnp.concatenate(gathered(lines), axis=1)
    out_sum_ref[...] = grads[:part]
    total = jnp.zeros((part, 1), F32)
    for t in range(3):
        row = grads[(1 + t) * part : (2 + t) * part]
        expand_sum_ref[:, t * width : (t + 1) * width] = row
        weight = expand_ref[:, t * width : (t + 1) * width].astype(F32)
        total = total + jnp.sum(row * weight, axis=1, keepdims=True)
    gain_b_sum_ref[...] = total / gain_b_ref[...].astype(F32)
    contract_sum_ref[...] = grads[4 * part : 4 * part + held]


def finish(where, mine, other, projection_in, expansion, gain_a, gain_b, held):
    part, wide = projection_in.shape
    inside = pl.BlockSpec(memory_space=pltpu.VMEM)
    shapes = [(part, wide), (part, 1), (part, wide // 3), (part, wide), (part, 1), (held, wide // 3)]
    return pl.pallas_call(
        finish_kernel,
        in_specs=[pl.BlockSpec(memory_space=pltpu.SMEM)] + [inside] * 6,
        out_specs=[inside] * 6,
        out_shape=[jax.ShapeDtypeStruct(shape, F32) for shape in shapes],
        compiler_params=pltpu.CompilerParams(vmem_limit_bytes=48 * 2**20),
        name="finish",
    )(where, mine, other, projection_in, expansion, gain_a[:, None], gain_b[:, None])


def local(size, ranks, tokens, gain_a, projection_in, attention_out, gain_b, expansion, contraction, cotangent):
    z = lax.axis_index("fsdp")
    r = lax.axis_index("rep")
    core = r & 1
    group = 2 * core + (z & 1)
    home = core == z >> 1
    own = tokens[0]
    count, width = own.shape
    part = width // size
    hidden = contraction.shape[0]
    heads = HEADS // size

    stages = list(range(len(far(ranks))))
    where = jnp.stack([z, core]).astype(jnp.int32)
    where_other = jnp.stack([z, 1 - core]).astype(jnp.int32)
    columns = [projection_in[:, t * width : (t + 1) * width] for t in range(3)]
    piece = split_rows(jnp.concatenate(columns, axis=0), r, ranks)
    rows = piece.shape[0]
    gains = jnp.pad(jnp.concatenate([gain_a, gain_b])[None], ((0, 7), (0, width - 2 * part)))
    pieces = exchange([jnp.concatenate([piece, gains], axis=0)] * size, size)
    pair, other, second = collect(after(own, pieces[1]), home, size, ranks)
    pieces = jnp.stack(pieces)
    gains = reorder(pieces[:, rows, : 2 * part], z, size).astype(F32)
    gain_one = gains[:, :part].reshape(1, width)
    gain_two = gains[:, part:].reshape(1, width)
    into = grow(pieces[:, :rows], r, ranks, stages)
    into_other = swap(into, "rep", ranks, 1)

    freqs = THETA ** (-(jnp.arange(HALF, dtype=F32) * (2.0 / HEAD_DIM)))
    places = jnp.concatenate([(group ^ d) * count + jnp.arange(count, dtype=jnp.int32) for d in range(size)])
    angles = freqs[:, None] * places.astype(F32)[None, :]
    cosine, sine = jnp.cos(angles), jnp.sin(angles)
    normed, queries, keys_turned, values_turned, keys, values, into = project(
        where, pair, other, gain_one, cosine, sine, into, into_other, count
    )

    columns = [expansion[:, t * width : (t + 1) * width] for t in range(3)]
    stacked = jnp.concatenate([attention_out] + columns + [contraction], axis=0)
    pad = -stacked.shape[0] % max(32, 8 * ranks)
    stacked = jnp.concatenate([stacked, jnp.zeros((pad, width), BF16)], axis=0)
    rest = exchange([split_rows(after(stacked, second), r, ranks)] * size, size)
    merged = []
    logs = []
    rest = grow(jnp.stack(after(rest, queries)), r, ranks, stages[:1])
    ahead = []
    for head in range(heads):
        out, log = attend(head, queries, after(keys, *ahead), values_turned)
        merged.append(out)
        logs.append(log)
        if head == 0:
            ahead = [rest]
            rest = grow(after(rest, out), r, ranks, stages[1:-1])
            sides = halves(rest)
        if head < 2:
            sides[head] = grow(after(sides[head], out), r, ranks, stages[-1:])
            ahead = ahead if head == 0 else [sides[0]]
    rest = after(jnp.concatenate(sides, axis=2), merged[-1])
    rest_other = swap(rest, "rep", ranks, 1)
    own_merged = jnp.concatenate(merged, axis=0)

    merged = trade_out([own_merged[:, d * count : (d + 1) * count] for d in range(size)], size, ranks)
    upstream = cotangent[0]
    block_output, state_back, state_low, normed_two, active, inner_back, *merged_back = forward_back(
        where, merged, own, upstream, gain_two, rest, rest_other, size * hidden
    )
    arrived = trade_back(merged_back, size, ranks)
    own_upstream = jnp.concatenate(arrived, axis=1)

    sent, kept = [
        gradients(place, merged, upstream, state_low, normed_two, active, inner_back, stacked.shape[0])
        for place in (where_other, where)
    ]
    grads = add(kept, swap(sent, "rep", ranks, 1))

    turned_backs = []
    weight_backs = []
    received = []
    ahead = [grads]
    for head in range(heads):
        grad, weight_grad = attend_back(
            head, queries, keys_turned, keys, values, after(own_upstream, *ahead), own_merged, logs[head],
            cosine, sine, normed,
        )
        turned_backs.append(grad)
        weight_backs.append(weight_grad.reshape(3, HEAD_DIM, width))
        if head == 0:
            received = trade_out([grad[:, d * count : (d + 1) * count] for d in range(size)], size, ranks)
            grads = shrink(grads, r, ranks, stages[:0:-1])
            ahead = [grads]
        if head == 1:
            grads = shrink(grads, r, ranks, stages[:1])
            ahead = [grads] + received
    grads = exchange([pick(grads, z ^ d) for d in range(size)], size)
    later = jnp.concatenate(turned_backs[1:], axis=0)
    grads = sum(part.astype(F32) for part in after(grads, later)).astype(BF16)
    later = after(later, grads)
    later = trade_out([later[:, d * count : (d + 1) * count] for d in range(size)], size, ranks)
    received = [jnp.concatenate(both, axis=0) for both in zip(received, later)]

    into = [into[:, t * part : (t + 1) * part].reshape(width, width) for t in range(3)]
    projected_back = reorder(jnp.stack(received), z, size).reshape(size, heads, 3, HEAD_DIM, count)
    projected_back = projected_back.transpose(2, 0, 1, 3, 4).reshape(3, width, count)
    normed_back = sum(mul(projected_back[t], into[t], TT) for t in range(3))
    token_grad = (state_back + layer_norm_back(own.astype(F32), gain_one, normed_back))[None]

    into_grad = jnp.concatenate([grad[t] for t in range(3) for grad in weight_backs], axis=0)
    into_grad = shrink(into_grad[None], r, ranks, stages[::-1])[0]
    lines = into_grad.shape[0]
    blocks = into_grad.reshape(lines, size, part).transpose(1, 0, 2)
    blocks = lax.all_to_all(blocks, "fsdp", 0, 0).astype(F32)
    flat = jnp.concatenate([blocks[0] + blocks[2], blocks[1] + blocks[3]], axis=1).astype(BF16)
    both = grow_flat(jnp.concatenate([flat, grads], axis=0)[None], r, ranks, stages)
    into_sum, gain_one_sum, attention_out_sum, expansion_sum, gain_two_sum, contraction_sum = finish(
        where, both, swap(both, "rep", ranks, 1), projection_in, expansion, gain_a, gain_b, hidden
    )
    return (
        block_output[None],
        token_grad,
        gain_one_sum[:, 0],
        into_sum,
        attention_out_sum,
        gain_two_sum[:, 0],
        expansion_sum,
        contraction_sum,
    )


def solution(mesh):
    tokens, rows, line = P("rep", "fsdp", None), P("fsdp", None), P("fsdp")
    in_specs = (tokens, line, rows, rows, line, rows, rows, tokens)
    out_specs = (tokens, tokens, line, rows, rows, line, rows, rows)
    body = functools.partial(local, mesh.shape["fsdp"], mesh.shape["rep"])
    return jax.shard_map(body, mesh=mesh, in_specs=in_specs, out_specs=out_specs, check_vma=False)
```

```python
import functools
import math

import jax
import jax.numpy as jnp
from jax import lax
from jax.experimental import pallas as pl
from jax.experimental.pallas import tpu as pltpu
from jax.sharding import PartitionSpec as P

HEADS = 12
HEAD_DIM = 64
HALF = HEAD_DIM // 2
SCALE = 1.0 / math.sqrt(HEAD_DIM)
EPS = 1e-05
THETA = 160000.0
F32 = jnp.float32
BF16 = jnp.bfloat16
NN = (((1,), (0,)), ((), ()))
NT = (((1,), (1,)), ((), ()))
TN = (((0,), (0,)), ((), ()))
TT = (((0,), (1,)), ((), ()))


def mul(a, b, dims=NN):
    return lax.dot_general(a, b, dims, preferred_element_type=F32)


def attend_kernel(q_ref, k_ref, v_ref, out_ref, log_ref):
    scores = mul(k_ref[0], q_ref[...])
    highest = jnp.max(scores, axis=0, keepdims=True)
    raised = jnp.exp(scores - highest)
    total = jnp.sum(raised, axis=0, keepdims=True)
    mixed = mul(v_ref[...], raised.astype(BF16))
    out_ref[...] = (mixed / total).astype(BF16)
    log_ref[...] = highest + jnp.log(total)


def attend(head, queries, keys, values, step=256):
    count = queries.shape[1]
    return pl.pallas_call(
        attend_kernel,
        grid=(count // step,),
        in_specs=[
            pl.BlockSpec((HEAD_DIM, step), lambda i: (head, i)),
            pl.BlockSpec((1, count, HEAD_DIM), lambda i: (head, 0, 0)),
            pl.BlockSpec((HEAD_DIM, count), lambda i: (head, 0)),
        ],
        out_specs=[
            pl.BlockSpec((HEAD_DIM, step), lambda i: (0, i)),
            pl.BlockSpec((1, step), lambda i: (0, i)),
        ],
        out_shape=[
            jax.ShapeDtypeStruct((HEAD_DIM, count), BF16),
            jax.ShapeDtypeStruct((1, count), F32),
        ],
        compiler_params=pltpu.CompilerParams(vmem_limit_bytes=48 * 2**20),
        cost_estimate=pl.CostEstimate(
            flops=40 * count * count * HEAD_DIM,
            bytes_accessed=8 * HEAD_DIM * count,
            transcendentals=count * count,
        ),
        name="attend",
    )(queries, keys, values)


def turn_back(values, cosine, sine):
    first, second = values[:HALF], values[HALF:]
    return jnp.concatenate([first * cosine + second * sine, second * cosine - first * sine], axis=0)


def attend_back_kernel(
    q_ref, kt_ref, k_ref, v_ref, up_ref, out_ref, log_ref, cos_ref, sin_ref, normed_ref, grad_ref, weight_ref, dk_ref, dv_ref
):
    index = pl.program_id(0)
    step = q_ref.shape[1]

    @pl.when(index == 0)
    def _():
        dk_ref[...] = jnp.zeros_like(dk_ref)
        dv_ref[...] = jnp.zeros_like(dv_ref)

    upstream = up_ref[...]
    inner_sum = jnp.sum(upstream.astype(F32) * out_ref[...].astype(F32), axis=0, keepdims=True)
    chances = jnp.exp(mul(k_ref[0], q_ref[...]) - log_ref[...])
    prob_back = mul(v_ref[0], upstream)
    score_back = (chances * (prob_back - inner_sum)).astype(BF16)
    dv_ref[...] += mul(chances.astype(BF16), upstream, NT)
    dk_ref[...] += mul(score_back, q_ref[...], NT)
    columns = pl.ds(pl.multiple_of(index * step, step), step)
    query_back = mul(kt_ref[...], score_back) * SCALE
    grad_ref[pl.ds(0, HEAD_DIM), columns] = turn_back(
        query_back, cos_ref[:, columns], sin_ref[:, columns]
    ).astype(BF16)

    @pl.when(index == pl.num_programs(0) - 1)
    def _():
        key_back = turn_back(dk_ref[...].T, cos_ref[...], sin_ref[...])
        grad_ref[pl.ds(HEAD_DIM, HEAD_DIM), :] = key_back.astype(BF16)
        grad_ref[pl.ds(2 * HEAD_DIM, HEAD_DIM), :] = dv_ref[...].T.astype(BF16)
        weight_ref[...] = mul(grad_ref[...], normed_ref[...]).astype(BF16)


def attend_back(head, queries, keys_turned, keys, values, upstream, merged, logs, cosine, sine, normed, step=256):
    count, width = normed.shape
    some = pl.BlockSpec((HEAD_DIM, step), lambda i: (head, i))
    rows = pl.BlockSpec((1, count, HEAD_DIM), lambda i: (head, 0, 0))
    whole = pl.BlockSpec((HALF, count), lambda i: (0, 0))
    return pl.pallas_call(
        attend_back_kernel,
        grid=(count // step,),
        in_specs=[
            some,
            pl.BlockSpec((HEAD_DIM, count), lambda i: (head, 0)),
            rows,
            rows,
            some,
            some,
            pl.BlockSpec((1, step), lambda i: (0, i)),
            whole,
            whole,
            pl.BlockSpec((count, width), lambda i: (0, 0)),
        ],
        out_specs=[
            pl.BlockSpec((3 * HEAD_DIM, count), lambda i: (0, 0)),
            pl.BlockSpec((3 * HEAD_DIM, width), lambda i: (0, 0)),
        ],
        out_shape=[
            jax.ShapeDtypeStruct((3 * HEAD_DIM, count), BF16),
            jax.ShapeDtypeStruct((3 * HEAD_DIM, width), BF16),
        ],
        scratch_shapes=[pltpu.VMEM((count, HEAD_DIM), F32), pltpu.VMEM((count, HEAD_DIM), F32)],
        compiler_params=pltpu.CompilerParams(vmem_limit_bytes=48 * 2**20),
        cost_estimate=pl.CostEstimate(
            flops=56 * count * count * HEAD_DIM,
            bytes_accessed=16 * HEAD_DIM * count,
            transcendentals=count * count,
        ),
        name="attend_back",
    )(queries, keys_turned, keys, values, upstream, merged, logs, cosine, sine, normed)


def load_rows(place_ref, mine_ref, other_ref, buffer, sems):
    z, core = place_ref[0], place_ref[1]
    size, rows = mine_ref.shape[0], mine_ref.shape[1]
    copies = []
    for d in range(size):
        for k, (ref, side) in enumerate(((mine_ref, core), (other_ref, 1 - core))):
            start = pl.multiple_of(side * rows, 16)
            copies.append(
                pltpu.make_async_copy(ref.at[d], buffer.at[z ^ d, pl.ds(start, rows), :], sems.at[d, k])
            )
    for copy in copies:
        copy.start()
    for copy in copies:
        copy.wait()


def unit_of(values):
    centre = values - jnp.mean(values, axis=-1, keepdims=True)
    inverse = lax.rsqrt(jnp.mean(centre * centre, axis=-1, keepdims=True) + EPS)
    return centre * inverse, inverse


def turn(values, cosine, sine):
    first, second = values[:HALF], values[HALF:]
    return jnp.concatenate([first * cosine - second * sine, second * cosine + first * sine], axis=0)


def project_kernel(
    place_ref, pair_ref, other_ref, gain_ref, cos_ref, sin_ref, mine_ref, theirs_ref,
    normed_ref, q_ref, kt_ref, vt_ref, k_ref, v_ref, into_ref, buffer, weight, sems, out_sem,
):
    index = pl.program_id(0)
    part = q_ref.shape[0]
    size = buffer.shape[0]
    save = pltpu.make_async_copy(buffer, into_ref, out_sem)

    @pl.when(index == 0)
    def _():
        load_rows(place_ref, mine_ref, theirs_ref, buffer, sems)
        save.start()
        start = pl.multiple_of(place_ref[1] * 2 * part, 128)
        odd = place_ref[0] & 1 == 1
        for t in range(3):
            both = buffer[:, t * part : (t + 1) * part, pl.ds(start, 2 * part)].reshape(size * part, 2 * part)
            chosen = jnp.where(odd, both[:, part:].astype(F32), both[:, :part].astype(F32))
            weight[:, t * part : (t + 1) * part] = chosen.astype(BF16)

    block = jnp.where(index < 2, pair_ref[...].astype(F32), other_ref[...].astype(F32))
    normed = (unit_of(block)[0] * gain_ref[...]).astype(BF16)
    normed_ref[...] = normed
    projected = mul(normed, weight[...])
    turned = projected[:, : 2 * part].T
    cosine, sine = cos_ref[...], sin_ref[...]
    for head in range(part // HEAD_DIM):
        rows = slice(head * HEAD_DIM, (head + 1) * HEAD_DIM)
        queries = turn(turned[rows], cosine, sine).astype(BF16)
        q_ref[rows, :] = (queries.astype(F32) * SCALE).astype(BF16)
        keys = turn(turned[part + head * HEAD_DIM : part + (head + 1) * HEAD_DIM], cosine, sine)
        kt_ref[rows, :] = keys.astype(BF16)
        k_ref[head] = keys.astype(BF16).T
        start = 2 * part + head * HEAD_DIM
        v_ref[head] = projected[:, start : start + HEAD_DIM].astype(BF16)
    vt_ref[...] = projected[:, 2 * part :].astype(BF16).T

    @pl.when(index == pl.num_programs(0) - 1)
    def _():
        save.wait()


def project(where, pair, other, gain, cosine, sine, mine, theirs, count):
    width = pair.shape[1]
    size, rows = mine.shape[0], 2 * mine.shape[1]
    part = width // size
    heads = part // HEAD_DIM
    total = size * count
    anywhere = pl.BlockSpec(memory_space=pl.ANY)
    columns = pl.BlockSpec((part, count), lambda i: (0, i))
    return pl.pallas_call(
        project_kernel,
        grid=(size,),
        in_specs=[
            pl.BlockSpec(memory_space=pltpu.SMEM),
            pl.BlockSpec((count, width), lambda i: (jnp.minimum(i, 1), 0)),
            pl.BlockSpec((count, width), lambda i: (jnp.maximum(i - 2, 0), 0)),
            pl.BlockSpec((1, width), lambda i: (0, 0)),
            pl.BlockSpec((HALF, count), lambda i: (0, i)),
            pl.BlockSpec((HALF, count), lambda i: (0, i)),
            anywhere,
            anywhere,
        ],
        out_specs=[
            pl.BlockSpec((count, width), lambda i: (i, 0)),
            columns,
            columns,
            columns,
            pl.BlockSpec((heads, count, HEAD_DIM), lambda i: (0, i, 0)),
            pl.BlockSpec((heads, count, HEAD_DIM), lambda i: (0, i, 0)),
            anywhere,
        ],
        out_shape=[
            jax.ShapeDtypeStruct((total, width), BF16),
            jax.ShapeDtypeStruct((part, total), BF16),
            jax.ShapeDtypeStruct((part, total), BF16),
            jax.ShapeDtypeStruct((part, total), BF16),
            jax.ShapeDtypeStruct((heads, total, HEAD_DIM), BF16),
            jax.ShapeDtypeStruct((heads, total, HEAD_DIM), BF16),
            jax.ShapeDtypeStruct((size, rows, width), BF16),
        ],
        scratch_shapes=[
            pltpu.VMEM((size, rows, width), BF16),
            pltpu.VMEM((width, 3 * part), BF16),
            pltpu.SemaphoreType.DMA((size, 2)),
            pltpu.SemaphoreType.DMA,
        ],
        compiler_params=pltpu.CompilerParams(vmem_limit_bytes=48 * 2**20),
        cost_estimate=pl.CostEstimate(flops=8 * 10**9, bytes_accessed=20 * 10**6, transcendentals=0),
        name="project",
    )(where, pair, other, gain, cosine, sine, mine, theirs)


def forward_back_kernel(
    place_ref, m0_ref, m1_ref, m2_ref, m3_ref, tokens_ref, up_ref, gain_ref, mine_ref, theirs_ref,
    result_ref, state_back_ref, low_ref, normed_ref, active_ref, inner_back_ref, b0_ref, b1_ref, b2_ref, b3_ref,
    buffer, sems,
):
    part, width = m0_ref.shape[0], tokens_ref.shape[1]
    size = buffer.shape[0]
    hidden = active_ref.shape[1]
    z = place_ref[0]

    @pl.when(pl.program_id(0) == 0)
    def _():
        load_rows(place_ref, mine_ref, theirs_ref, buffer, sems)

    expand = [buffer[:, (1 + t) * part : (2 + t) * part, :].reshape(width, width) for t in range(3)]
    contract = buffer[:, 4 * part : 4 * part + hidden // size, :].reshape(hidden, width)
    gain = gain_ref[...]

    state = tokens_ref[...].astype(F32)
    for k, ref in enumerate((m0_ref, m1_ref, m2_ref, m3_ref)):
        state = state + mul(ref[...], buffer[z ^ k, :part, :], TN)
    unit, inverse = unit_of(state)
    normed = (unit * gain).astype(BF16)
    normed_ref[...] = normed
    inner = jnp.concatenate([mul(normed, weight) for weight in expand], axis=1)
    first, second = inner[:, :hidden], inner[:, hidden:]
    chance = 0.5 + 0.5 * lax.erf(first * math.sqrt(0.5))
    gated = first * chance
    slope = chance + first * (jnp.exp(-0.5 * first * first) * (1.0 / math.sqrt(2.0 * math.pi)))
    active = (gated * second).astype(BF16)
    active_ref[...] = active
    result_ref[...] = (state + mul(active, contract)).astype(BF16)

    upstream = up_ref[...]
    active_back = mul(upstream, contract, NT).astype(BF16).astype(F32)
    inner_back = jnp.concatenate(
        [(active_back * second * slope).astype(BF16), (active_back * gated).astype(BF16)], axis=1
    )
    inner_back_ref[...] = inner_back
    normed_back = mul(inner_back[:, :width], expand[0], NT)
    normed_back = normed_back + mul(inner_back[:, width : 2 * width], expand[1], NT)
    normed_back = normed_back + mul(inner_back[:, 2 * width :], expand[2], NT)
    scaled = normed_back * gain
    mean = jnp.mean(scaled, axis=-1, keepdims=True)
    lean = jnp.mean(scaled * unit, axis=-1, keepdims=True)
    state_back = upstream.astype(F32) + inverse * (scaled - mean - unit * lean)
    state_back_ref[...] = state_back
    low = state_back.astype(BF16)
    low_ref[...] = low
    for k, ref in enumerate((b0_ref, b1_ref, b2_ref, b3_ref)):
        ref[...] = mul(buffer[z ^ k, :part, :], low, NT).astype(BF16)


def forward_back(where, merged, tokens, upstream, gain, mine, theirs, hidden, step=256):
    count, width = tokens.shape
    size, rows = mine.shape[0], 2 * mine.shape[1]
    part = width // size
    anywhere = pl.BlockSpec(memory_space=pl.ANY)
    columns = pl.BlockSpec((part, step), lambda i: (0, i))

    def some(lanes):
        return pl.BlockSpec((step, lanes), lambda i: (i, 0))

    lanes = [width, width, width, width, hidden, 2 * hidden]
    kinds = [BF16, F32, BF16, BF16, BF16, BF16]
    return pl.pallas_call(
        forward_back_kernel,
        grid=(count // step,),
        in_specs=[pl.BlockSpec(memory_space=pltpu.SMEM)]
        + [columns] * size
        + [some(width), some(width), pl.BlockSpec((1, width), lambda i: (0, 0)), anywhere, anywhere],
        out_specs=[some(n) for n in lanes] + [columns] * size,
        out_shape=[jax.ShapeDtypeStruct((count, n), kind) for n, kind in zip(lanes, kinds)]
        + [jax.ShapeDtypeStruct((part, count), BF16)] * size,
        scratch_shapes=[pltpu.VMEM((size, rows, width), BF16), pltpu.SemaphoreType.DMA((size, 2))],
        compiler_params=pltpu.CompilerParams(vmem_limit_bytes=56 * 2**20),
        cost_estimate=pl.CostEstimate(flops=14 * 10**9, bytes_accessed=20 * 10**6, transcendentals=0),
        name="forward_back",
    )(where, *merged, tokens, upstream, gain, mine, theirs)


def gradients_kernel(
    place_ref, m0_ref, m1_ref, m2_ref, m3_ref, up_ref, low_ref, normed_ref, active_ref, inner_back_ref, grads_ref
):
    z = place_ref[0]
    part, width = m0_ref.shape[0], up_ref.shape[1]
    size, rows, lanes = grads_ref.shape
    held = active_ref.shape[1] // size
    start = pl.multiple_of(place_ref[1] * lanes, 128)
    low = low_ref[:, pl.ds(start, lanes)]
    for k, ref in enumerate((m0_ref, m1_ref, m2_ref, m3_ref)):
        grads_ref[z ^ k, :part, :] = mul(ref[...], low).astype(BF16)
    normed = normed_ref[...]
    for t in range(3):
        grad = mul(normed, inner_back_ref[:, pl.ds(t * width + start, lanes)], TN)
        grads_ref[:, (1 + t) * part : (2 + t) * part, :] = grad.astype(BF16).reshape(size, part, lanes)
    grad = mul(active_ref[...], up_ref[:, pl.ds(start, lanes)], TN)
    grads_ref[:, 4 * part : 4 * part + held, :] = grad.astype(BF16).reshape(size, held, lanes)
    if rows > 4 * part + held:
        grads_ref[:, 4 * part + held :, :] = jnp.zeros((size, rows - 4 * part - held, lanes), BF16)


def gradients(where, merged, upstream, low, normed, active, inner_back, rows):
    size = len(merged)
    lanes = upstream.shape[1] // 2
    inside = pl.BlockSpec(memory_space=pltpu.VMEM)
    return pl.pallas_call(
        gradients_kernel,
        in_specs=[pl.BlockSpec(memory_space=pltpu.SMEM)] + [inside] * (size + 5),
        out_specs=inside,
        out_shape=jax.ShapeDtypeStruct((size, rows, lanes), BF16),
        compiler_params=pltpu.CompilerParams(vmem_limit_bytes=60 * 2**20),
        cost_estimate=pl.CostEstimate(flops=6 * 10**9, bytes_accessed=12 * 10**6, transcendentals=0),
        name="gradients",
    )(where, *merged, upstream, low, normed, active, inner_back)


def token_kernel(
    place_ref, a0_ref, a1_ref, a2_ref, a3_ref, b0_ref, b1_ref, b2_ref, b3_ref,
    weight_ref, tokens_ref, back_ref, gain_ref, grad_ref, parts,
):
    z = place_ref[0]
    size, rows, width = weight_ref.shape
    part = rows // 3
    slots = ((a0_ref, b0_ref), (a1_ref, b1_ref), (a2_ref, b2_ref), (a3_ref, b3_ref))
    for k, (one, two) in enumerate(slots):
        first = (z ^ k) * part
        for head in range(part // HEAD_DIM):
            ref, start = (one, 0) if head == 0 else (two, (head - 1) * 3 * HEAD_DIM)
            for t in range(3):
                lines = pl.ds(pl.multiple_of(first + head * HEAD_DIM, HEAD_DIM), HEAD_DIM)
                parts[t, lines, :] = ref[start + t * HEAD_DIM : start + (t + 1) * HEAD_DIM, :]
    total = jnp.zeros((width, tokens_ref.shape[0]), F32)
    for t in range(3):
        total = total + mul(weight_ref[:, t * part : (t + 1) * part, :].reshape(width, width), parts[t])
    unit, inverse = unit_of(tokens_ref[...].astype(F32))
    scaled = total.T * gain_ref[...]
    mean = jnp.mean(scaled, axis=-1, keepdims=True)
    lean = jnp.mean(scaled * unit, axis=-1, keepdims=True)
    grad_ref[...] = back_ref[...] + inverse * (scaled - mean - unit * lean)


def token_back(where, early, late, weight, tokens, state_back, gain):
    count, width = tokens.shape
    inside = pl.BlockSpec(memory_space=pltpu.VMEM)
    return pl.pallas_call(
        token_kernel,
        in_specs=[pl.BlockSpec(memory_space=pltpu.SMEM)] + [inside] * (len(early) + len(late) + 4),
        out_specs=inside,
        out_shape=jax.ShapeDtypeStruct((count, width), F32),
        scratch_shapes=[pltpu.VMEM((3, width, count), BF16)],
        compiler_params=pltpu.CompilerParams(vmem_limit_bytes=48 * 2**20),
        cost_estimate=pl.CostEstimate(flops=5 * 10**9, bytes_accessed=12 * 10**6, transcendentals=0),
        name="token_back",
    )(where, *early, *late, weight, tokens, state_back, gain)


def after(values, *others):
    return lax.optimization_barrier((values, others))[0]


def swap(values, axis, size, offset):
    return lax.ppermute(values, axis, [(i, i ^ offset) for i in range(size)])


def exchange(pieces, size):
    return [pieces[0]] + [swap(pieces[d], "fsdp", size, d) for d in range(1, size)]


def column(values, size, ranks, pairs):
    full = [
        (z * ranks + r, to * ranks + (r & ~1) + core)
        for z in range(size)
        for r in range(ranks)
        for to, core in pairs(z, r & 1)
    ]
    return lax.ppermute(values, ("fsdp", "rep"), full)


def collect(own, home, size, ranks):
    first = column(
        own, size, ranks, lambda z, c: [(z ^ 1, c) if c == z >> 1 else (z ^ 2, 1 - c)]
    )
    second = column(first, size, ranks, lambda z, c: [] if c == z >> 1 else [(z ^ 1, c)])
    low = jnp.where(home, own, first)
    high = jnp.where(home, first, second)
    pair = jnp.concatenate([low, high], axis=0)
    other = swap(pair, "rep", ranks, 1)
    return pair, other, second


def trade_out(pieces, size, ranks, rounds=None):
    def round_of(k):
        return lambda z, c: [((2 * c + (z & 1)) ^ k, z >> 1)]

    return [column(pieces[k], size, ranks, round_of(k)) for k in rounds or range(size)]


def trade_back(pieces, size, ranks):
    def round_of(k):
        return lambda z, c: [(2 * c + ((z ^ k) & 1), (z ^ k) >> 1)]

    return [column(pieces[k], size, ranks, round_of(k)) for k in range(size)]


def pick(blocks, index):
    return lax.dynamic_index_in_dim(blocks, index, 0, keepdims=False)


def reorder(blocks, z, size):
    return jnp.stack([pick(blocks, z ^ j) for j in range(size)])


def far(ranks):
    bits = []
    bit = 2
    while bit < ranks:
        bits.append(bit)
        bit *= 2
    return bits


def stage_bit(core, ranks, stage):
    bits = far(ranks)
    return bits[stage] if core == 0 else bits[len(bits) - 1 - stage]


def stage_swap(values, ranks, stage):
    return lax.ppermute(values, "rep", [(i, i ^ stage_bit(i & 1, ranks, stage)) for i in range(ranks)])


def stage_upper(r, ranks, stage):
    bit = jnp.where(r & 1 == 0, stage_bit(0, ranks, stage), stage_bit(1, ranks, stage))
    return r & bit != 0


def place(r, ranks):
    stages = len(far(ranks))
    total = jnp.where(r & 1 != 0, 1 << stages, 0)
    for stage in range(stages):
        total = total + jnp.where(stage_upper(r, ranks, stage), 1 << stage, 0)
    return total


def join(mine, other, upper):
    return jnp.concatenate([jnp.where(upper, other, mine), jnp.where(upper, mine, other)], axis=1)


def cut(values, upper):
    half = values.shape[1] // 2
    mine = jnp.where(upper, half, 0)
    sent = lax.dynamic_slice_in_dim(values, half - mine, half, 1)
    return sent, lax.dynamic_slice_in_dim(values, mine, half, 1)


def add(one, two):
    return (one.astype(F32) + two.astype(F32)).astype(BF16)


def grow(values, r, ranks, stages):
    for stage in stages:
        values = join(values, stage_swap(values, ranks, stage), stage_upper(r, ranks, stage))
    return values


def grow_flat(values, r, ranks, stages):
    for stage in stages:
        other = stage_swap(values, ranks, stage)
        upper = stage_upper(r, ranks, stage)
        values = jnp.concatenate(
            [jnp.where(upper, other, values), jnp.where(upper, values, other)], axis=0
        )
    return values


def shrink(values, r, ranks, stages):
    for stage in stages:
        sent, kept = cut(values, stage_upper(r, ranks, stage))
        values = add(kept, stage_swap(sent, ranks, stage))
    return values


def halves(values):
    middle = values.shape[-1] // 2
    return [values[..., :middle], values[..., middle:]]


def split_rows(shard, r, ranks):
    rows = shard.shape[0] // ranks
    return lax.dynamic_slice_in_dim(shard, place(r, ranks) * rows, rows, 0)


def finish_kernel(
    place_ref, mine_ref, other_ref, into_ref, expand_ref, gain_a_ref, gain_b_ref,
    into_sum_ref, gain_a_sum_ref, out_sum_ref, expand_sum_ref, gain_b_sum_ref, contract_sum_ref,
):
    first = place_ref[1] == 0
    part, width = out_sum_ref.shape
    held = contract_sum_ref.shape[0]
    pieces = mine_ref.shape[0]
    lines = 3 * part // pieces

    def gathered(start):
        rows = mine_ref.shape[1] if start else lines
        sides = []
        for one, two in ((mine_ref, other_ref), (other_ref, mine_ref)):
            blocks = [
                jnp.where(first, one[p, start:rows].astype(F32), two[p, start:rows].astype(F32))
                for p in range(pieces)
            ]
            sides.append(jnp.concatenate(blocks, axis=0))
        return sides

    blocks = [side[:, k * part : (k + 1) * part].T for side in gathered(0) for k in range(2)]
    total = jnp.zeros((part, 1), F32)
    for t in range(3):
        row = jnp.concatenate([block[:, t * part : (t + 1) * part] for block in blocks], axis=1)
        into_sum_ref[:, t * width : (t + 1) * width] = row
        weight = into_ref[:, t * width : (t + 1) * width].astype(F32)
        total = total + jnp.sum(row * weight, axis=1, keepdims=True)
    gain_a_sum_ref[...] = total / gain_a_ref[...].astype(F32)

    grads = jnp.concatenate(gathered(lines), axis=1)
    out_sum_ref[...] = grads[:part]
    total = jnp.zeros((part, 1), F32)
    for t in range(3):
        row = grads[(1 + t) * part : (2 + t) * part]
        expand_sum_ref[:, t * width : (t + 1) * width] = row
        weight = expand_ref[:, t * width : (t + 1) * width].astype(F32)
        total = total + jnp.sum(row * weight, axis=1, keepdims=True)
    gain_b_sum_ref[...] = total / gain_b_ref[...].astype(F32)
    contract_sum_ref[...] = grads[4 * part : 4 * part + held]


def finish(where, mine, other, projection_in, expansion, gain_a, gain_b, held):
    part, wide = projection_in.shape
    inside = pl.BlockSpec(memory_space=pltpu.VMEM)
    shapes = [(part, wide), (part, 1), (part, wide // 3), (part, wide), (part, 1), (held, wide // 3)]
    return pl.pallas_call(
        finish_kernel,
        in_specs=[pl.BlockSpec(memory_space=pltpu.SMEM)] + [inside] * 6,
        out_specs=[inside] * 6,
        out_shape=[jax.ShapeDtypeStruct(shape, F32) for shape in shapes],
        compiler_params=pltpu.CompilerParams(vmem_limit_bytes=48 * 2**20),
        name="finish",
    )(where, mine, other, projection_in, expansion, gain_a[:, None], gain_b[:, None])


def local(size, ranks, tokens, gain_a, projection_in, attention_out, gain_b, expansion, contraction, cotangent):
    z = lax.axis_index("fsdp")
    r = lax.axis_index("rep")
    core = r & 1
    group = 2 * core + (z & 1)
    home = core == z >> 1
    own = tokens[0]
    count, width = own.shape
    part = width // size
    hidden = contraction.shape[0]
    heads = HEADS // size

    stages = list(range(len(far(ranks))))
    where = jnp.stack([z, core]).astype(jnp.int32)
    where_other = jnp.stack([z, 1 - core]).astype(jnp.int32)
    columns = [projection_in[:, t * width : (t + 1) * width] for t in range(3)]
    piece = split_rows(jnp.concatenate(columns, axis=0), r, ranks)
    rows = piece.shape[0]
    gains = jnp.pad(jnp.concatenate([gain_a, gain_b])[None], ((0, 7), (0, width - 2 * part)))
    pieces = exchange([jnp.concatenate([piece, gains], axis=0)] * size, size)
    pair, other, second = collect(after(own, pieces[1]), home, size, ranks)
    pieces = jnp.stack(pieces)
    gains = reorder(pieces[:, rows, : 2 * part], z, size).astype(F32)
    gain_one = gains[:, :part].reshape(1, width)
    gain_two = gains[:, part:].reshape(1, width)
    into = grow(pieces[:, :rows], r, ranks, stages)
    into_other = swap(into, "rep", ranks, 1)

    freqs = THETA ** (-(jnp.arange(HALF, dtype=F32) * (2.0 / HEAD_DIM)))
    places = jnp.concatenate([(group ^ d) * count + jnp.arange(count, dtype=jnp.int32) for d in range(size)])
    angles = freqs[:, None] * places.astype(F32)[None, :]
    cosine, sine = jnp.cos(angles), jnp.sin(angles)
    normed, queries, keys_turned, values_turned, keys, values, into = project(
        where, pair, other, gain_one, cosine, sine, into, into_other, count
    )

    columns = [expansion[:, t * width : (t + 1) * width] for t in range(3)]
    stacked = jnp.concatenate([attention_out] + columns + [contraction], axis=0)
    pad = -stacked.shape[0] % max(32, 8 * ranks)
    stacked = jnp.concatenate([stacked, jnp.zeros((pad, width), BF16)], axis=0)
    rest = exchange([split_rows(after(stacked, second), r, ranks)] * size, size)
    merged = []
    logs = []
    rest = grow(jnp.stack(after(rest, queries)), r, ranks, stages[:1])
    ahead = []
    for head in range(heads):
        out, log = attend(head, queries, after(keys, *ahead), values_turned)
        merged.append(out)
        logs.append(log)
        if head == 0:
            ahead = [rest]
            rest = grow(after(rest, out), r, ranks, stages[1:-1])
            sides = halves(rest)
        if head < 2:
            sides[head] = grow(after(sides[head], out), r, ranks, stages[-1:])
            ahead = ahead if head == 0 else [sides[0]]
    rest = after(jnp.concatenate(sides, axis=2), merged[-1])
    rest_other = swap(rest, "rep", ranks, 1)
    own_merged = jnp.concatenate(merged, axis=0)

    merged = trade_out([own_merged[:, d * count : (d + 1) * count] for d in range(size)], size, ranks)
    upstream = cotangent[0]
    block_output, state_back, state_low, normed_two, active, inner_back, *merged_back = forward_back(
        where, merged, own, upstream, gain_two, rest, rest_other, size * hidden
    )
    arrived = trade_back(merged_back, size, ranks)
    own_upstream = jnp.concatenate(arrived, axis=1)

    sent, kept = [
        gradients(
            place, merged, upstream, state_low, normed_two, after(active, block), inner_back, stacked.shape[0]
        )
        for place, block in zip((where_other, where), arrived)
    ]
    grads = add(kept, swap(sent, "rep", ranks, 1))

    turned_backs = []
    weight_backs = []
    received = []
    ahead = [grads]
    for head in range(heads):
        grad, weight_grad = attend_back(
            head, queries, keys_turned, keys, values, after(own_upstream, *ahead), own_merged, logs[head],
            cosine, sine, normed,
        )
        turned_backs.append(grad)
        weight_backs.append(weight_grad.reshape(3, HEAD_DIM, width))
        if head == 0:
            received = trade_out([grad[:, d * count : (d + 1) * count] for d in range(size)], size, ranks)
            grads = shrink(grads, r, ranks, stages[:0:-1])
            ahead = [grads]
        if head == 1:
            grads = shrink(grads, r, ranks, stages[:1])
            ahead = [grads] + received
    grads = exchange([pick(grads, z ^ d) for d in range(size)], size)
    later = jnp.concatenate(turned_backs[1:], axis=0)
    grads = sum(part.astype(F32) for part in grads).astype(BF16)
    weight_backs[2], grads = after((weight_backs[2], grads), later)
    later = [later[:, d * count : (d + 1) * count] for d in range(size)]
    arrived = trade_out(later, size, ranks)

    into_grad = jnp.concatenate([grad[t] for t in range(3) for grad in weight_backs], axis=0)
    into_grad = after(shrink(into_grad[None], r, ranks, stages[-1:]), arrived[0])
    into_grad = after(shrink(into_grad, r, ranks, stages[-2::-1]), arrived[1])[0]
    lines = into_grad.shape[0]
    blocks = into_grad.reshape(lines, size, part).transpose(1, 0, 2)
    blocks = exchange([pick(blocks, z ^ d) for d in range(size)], size)
    even, odd = (blocks[0].astype(F32) + blocks[2].astype(F32)), (blocks[1].astype(F32) + blocks[3].astype(F32))
    low = z & 1 == 0
    flat = jnp.concatenate([jnp.where(low, even, odd), jnp.where(low, odd, even)], axis=1).astype(BF16)
    both = grow_flat(jnp.concatenate([flat, grads], axis=0)[None], r, ranks, stages[:-1])
    both = after(grow_flat(after(both, arrived[2]), r, ranks, stages[-1:]), arrived[3])
    token_grad = token_back(where, received, arrived, into, own, state_back, gain_one)[None]
    into_sum, gain_one_sum, attention_out_sum, expansion_sum, gain_two_sum, contraction_sum = finish(
        where, both, swap(both, "rep", ranks, 1), projection_in, expansion, gain_a, gain_b, hidden
    )
    return (
        block_output[None],
        token_grad,
        gain_one_sum[:, 0],
        into_sum,
        attention_out_sum,
        gain_two_sum[:, 0],
        expansion_sum,
        contraction_sum,
    )


def solution(mesh):
    tokens, rows, line = P("rep", "fsdp", None), P("fsdp", None), P("fsdp")
    in_specs = (tokens, line, rows, rows, line, rows, rows, tokens)
    out_specs = (tokens, tokens, line, rows, rows, line, rows, rows)
    body = functools.partial(local, mesh.shape["fsdp"], mesh.shape["rep"])
    return jax.shard_map(body, mesh=mesh, in_specs=in_specs, out_specs=out_specs, check_vma=False)
```

```python
import functools
import math

import jax
import jax.numpy as jnp
from jax import lax
from jax.experimental import pallas as pl
from jax.experimental.pallas import tpu as pltpu
from jax.sharding import PartitionSpec as P

HEADS = 12
HEAD_DIM = 64
HALF = HEAD_DIM // 2
SCALE = 1.0 / math.sqrt(HEAD_DIM)
EPS = 1e-05
THETA = 160000.0
F32 = jnp.float32
BF16 = jnp.bfloat16
NN = (((1,), (0,)), ((), ()))
NT = (((1,), (1,)), ((), ()))
TN = (((0,), (0,)), ((), ()))
TT = (((0,), (1,)), ((), ()))


def mul(a, b, dims=NN):
    return lax.dot_general(a, b, dims, preferred_element_type=F32)


def attend_kernel(q_ref, k_ref, v_ref, out_ref, log_ref):
    scores = mul(k_ref[...].T, q_ref[...])
    highest = jnp.max(scores, axis=0, keepdims=True)
    raised = jnp.exp(scores - highest)
    total = jnp.sum(raised, axis=0, keepdims=True)
    mixed = mul(v_ref[...], raised.astype(BF16))
    out_ref[...] = (mixed / total).astype(BF16)
    log_ref[...] = highest + jnp.log(total)


def attend(head, queries, keys, values, step=1024):
    count = queries.shape[1]
    step = min(step, count)
    whole = pl.BlockSpec((HEAD_DIM, count), lambda i: (head, 0))
    return pl.pallas_call(
        attend_kernel,
        grid=(count // step,),
        in_specs=[pl.BlockSpec((HEAD_DIM, step), lambda i: (head, i)), whole, whole],
        out_specs=[
            pl.BlockSpec((HEAD_DIM, step), lambda i: (0, i)),
            pl.BlockSpec((1, step), lambda i: (0, i)),
        ],
        out_shape=[
            jax.ShapeDtypeStruct((HEAD_DIM, count), BF16),
            jax.ShapeDtypeStruct((1, count), F32),
        ],
        compiler_params=pltpu.CompilerParams(vmem_limit_bytes=48 * 2**20),
        cost_estimate=pl.CostEstimate(
            flops=28 * count * count * HEAD_DIM,
            bytes_accessed=8 * HEAD_DIM * count,
            transcendentals=count * count,
        ),
        name="attend",
    )(queries, keys, values)


def turn_back(values, cosine, sine):
    first, second = values[:HALF], values[HALF:]
    return jnp.concatenate([first * cosine + second * sine, second * cosine - first * sine], axis=0)


def attend_back_kernel(
    q_ref, kt_ref, vt_ref, up_ref, out_ref, log_ref, cos_ref, sin_ref, normed_ref,
    grad_ref, weight_ref, k_ref, v_ref, dk_ref, dv_ref,
):
    index = pl.program_id(0)
    step = q_ref.shape[1]

    @pl.when(index == 0)
    def _():
        k_ref[...] = kt_ref[...].T
        v_ref[...] = vt_ref[...].T
        dk_ref[...] = jnp.zeros_like(dk_ref)
        dv_ref[...] = jnp.zeros_like(dv_ref)

    upstream = up_ref[...]
    inner_sum = jnp.sum(upstream.astype(F32) * out_ref[...].astype(F32), axis=0, keepdims=True)
    chances = jnp.exp(mul(k_ref[...], q_ref[...]) - log_ref[...])
    prob_back = mul(v_ref[...], upstream)
    score_back = (chances * (prob_back - inner_sum)).astype(BF16)
    dv_ref[...] += mul(chances.astype(BF16), upstream, NT)
    dk_ref[...] += mul(score_back, q_ref[...], NT)
    columns = pl.ds(pl.multiple_of(index * step, step), step)
    query_back = mul(kt_ref[...], score_back) * SCALE
    grad_ref[pl.ds(0, HEAD_DIM), columns] = turn_back(
        query_back, cos_ref[:, columns], sin_ref[:, columns]
    ).astype(BF16)

    @pl.when(index == pl.num_programs(0) - 1)
    def _():
        key_back = turn_back(dk_ref[...].T, cos_ref[...], sin_ref[...])
        grad_ref[pl.ds(HEAD_DIM, HEAD_DIM), :] = key_back.astype(BF16)
        grad_ref[pl.ds(2 * HEAD_DIM, HEAD_DIM), :] = dv_ref[...].T.astype(BF16)
        weight_ref[...] = mul(grad_ref[...], normed_ref[...]).astype(BF16)


def attend_back(head, queries, keys, values, upstream, merged, log, cosine, sine, normed, step=512):
    count, width = normed.shape
    step = min(step, count)
    some = pl.BlockSpec((HEAD_DIM, step), lambda i: (head, i))
    whole = pl.BlockSpec((HEAD_DIM, count), lambda i: (head, 0))
    table = pl.BlockSpec((HALF, count), lambda i: (0, 0))
    return pl.pallas_call(
        attend_back_kernel,
        grid=(count // step,),
        in_specs=[
            some,
            whole,
            whole,
            some,
            some,
            pl.BlockSpec((1, step), lambda i: (0, i)),
            table,
            table,
            pl.BlockSpec((count, width), lambda i: (0, 0)),
        ],
        out_specs=[
            pl.BlockSpec((3 * HEAD_DIM, count), lambda i: (0, 0)),
            pl.BlockSpec((3 * HEAD_DIM, width), lambda i: (0, 0)),
        ],
        out_shape=[
            jax.ShapeDtypeStruct((3 * HEAD_DIM, count), BF16),
            jax.ShapeDtypeStruct((3 * HEAD_DIM, width), BF16),
        ],
        scratch_shapes=[
            pltpu.VMEM((count, HEAD_DIM), BF16),
            pltpu.VMEM((count, HEAD_DIM), BF16),
            pltpu.VMEM((count, HEAD_DIM), F32),
            pltpu.VMEM((count, HEAD_DIM), F32),
        ],
        compiler_params=pltpu.CompilerParams(vmem_limit_bytes=48 * 2**20),
        cost_estimate=pl.CostEstimate(
            flops=56 * count * count * HEAD_DIM,
            bytes_accessed=16 * HEAD_DIM * count,
            transcendentals=count * count,
        ),
        name="attend_back",
    )(queries, keys, values, upstream, merged, log, cosine, sine, normed)


def load_rows(place_ref, pairs, buffer, sems):
    z, core = place_ref[0], place_ref[1]
    size, rows, lanes = pairs[0][0].shape
    copies = []
    for d in range(size):
        for n, (mine, other) in enumerate(pairs):
            for k, (ref, side) in enumerate(((mine, core), (other, 1 - core))):
                start = pl.multiple_of(side * rows, 16)
                target = buffer.at[z ^ d, pl.ds(start, rows), pl.ds(n * lanes, lanes)]
                copies.append(pltpu.make_async_copy(ref.at[d], target, sems.at[d, n, k]))
    for copy in copies:
        copy.start()
    for copy in copies:
        copy.wait()


def unit_of(values):
    centre = values - jnp.mean(values, axis=-1, keepdims=True)
    inverse = lax.rsqrt(jnp.mean(centre * centre, axis=-1, keepdims=True) + EPS)
    return centre * inverse, inverse


def turn(values, cosine, sine):
    first, second = values[:HALF], values[HALF:]
    return jnp.concatenate([first * cosine - second * sine, second * cosine + first * sine], axis=0)


def project_kernel(
    place_ref, pair_ref, other_ref, gain_ref, cos_ref, sin_ref, mine_ref, theirs_ref,
    normed_ref, q_ref, kt_ref, vt_ref, buffer, weight, sems,
):
    index = pl.program_id(0)
    part = q_ref.shape[0]
    size = buffer.shape[0]

    @pl.when(index == 0)
    def _():
        load_rows(place_ref, [(mine_ref, theirs_ref)], buffer, sems)
        start = pl.multiple_of(place_ref[1] * 2 * part, 128)
        odd = place_ref[0] & 1 == 1
        for t in range(3):
            both = buffer[:, t * part : (t + 1) * part, pl.ds(start, 2 * part)].reshape(size * part, 2 * part)
            chosen = jnp.where(odd, both[:, part:].astype(F32), both[:, :part].astype(F32))
            weight[:, t * part : (t + 1) * part] = chosen.astype(BF16)

    block = jnp.where(index < 2, pair_ref[...].astype(F32), other_ref[...].astype(F32))
    normed = (unit_of(block)[0] * gain_ref[...]).astype(BF16)
    normed_ref[...] = normed
    projected = mul(normed, weight[...])
    turned = projected[:, : 2 * part].T
    cosine, sine = cos_ref[...], sin_ref[...]
    for head in range(part // HEAD_DIM):
        rows = slice(head * HEAD_DIM, (head + 1) * HEAD_DIM)
        queries = turn(turned[rows], cosine, sine).astype(BF16)
        q_ref[rows, :] = (queries.astype(F32) * SCALE).astype(BF16)
        keys = turn(turned[part + head * HEAD_DIM : part + (head + 1) * HEAD_DIM], cosine, sine)
        kt_ref[rows, :] = keys.astype(BF16)
    vt_ref[...] = projected[:, 2 * part :].astype(BF16).T


def project(where, pair, other, gain, cosine, sine, mine, theirs, count):
    width = pair.shape[1]
    size, rows = mine.shape[0], 2 * mine.shape[1]
    part = width // size
    total = size * count
    anywhere = pl.BlockSpec(memory_space=pl.ANY)
    columns = pl.BlockSpec((part, count), lambda i: (0, i))
    return pl.pallas_call(
        project_kernel,
        grid=(size,),
        in_specs=[
            pl.BlockSpec(memory_space=pltpu.SMEM),
            pl.BlockSpec((count, width), lambda i: (jnp.minimum(i, 1), 0)),
            pl.BlockSpec((count, width), lambda i: (jnp.maximum(i - 2, 0), 0)),
            pl.BlockSpec((1, width), lambda i: (0, 0)),
            pl.BlockSpec((HALF, count), lambda i: (0, i)),
            pl.BlockSpec((HALF, count), lambda i: (0, i)),
            anywhere,
            anywhere,
        ],
        out_specs=[
            pl.BlockSpec((count, width), lambda i: (i, 0)),
            columns,
            columns,
            columns,
        ],
        out_shape=[
            jax.ShapeDtypeStruct((total, width), BF16),
            jax.ShapeDtypeStruct((part, total), BF16),
            jax.ShapeDtypeStruct((part, total), BF16),
            jax.ShapeDtypeStruct((part, total), BF16),
        ],
        scratch_shapes=[
            pltpu.VMEM((size, rows, width), BF16),
            pltpu.VMEM((width, 3 * part), BF16),
            pltpu.SemaphoreType.DMA((size, 1, 2)),
        ],
        compiler_params=pltpu.CompilerParams(vmem_limit_bytes=48 * 2**20),
        cost_estimate=pl.CostEstimate(flops=8 * 10**9, bytes_accessed=20 * 10**6, transcendentals=0),
        name="project",
    )(where, pair, other, gain, cosine, sine, mine, theirs)


def forward_back_kernel(
    place_ref, m0_ref, m1_ref, m2_ref, m3_ref, tokens_ref, up_ref, gain_ref, l_ref, other_l_ref, r_ref, other_r_ref,
    result_ref, state_back_ref, low_ref, normed_ref, active_ref, inner_back_ref, b0_ref, b1_ref, b2_ref, b3_ref,
    buffer, sems,
):
    part, width = m0_ref.shape[0], tokens_ref.shape[1]
    size = buffer.shape[0]
    hidden = active_ref.shape[1]
    z = place_ref[0]

    @pl.when(pl.program_id(0) == 0)
    def _():
        load_rows(place_ref, [(l_ref, other_l_ref), (r_ref, other_r_ref)], buffer, sems)

    expand = [buffer[:, (1 + t) * part : (2 + t) * part, :].reshape(width, width) for t in range(3)]
    contract = buffer[:, 4 * part : 4 * part + hidden // size, :].reshape(hidden, width)
    gain = gain_ref[...]

    state = tokens_ref[...].astype(F32)
    for k, ref in enumerate((m0_ref, m1_ref, m2_ref, m3_ref)):
        state = state + mul(ref[...], buffer[z ^ k, :part, :], TN)
    unit, inverse = unit_of(state)
    normed = (unit * gain).astype(BF16)
    normed_ref[...] = normed
    inner = jnp.concatenate([mul(normed, weight) for weight in expand], axis=1)
    first, second = inner[:, :hidden], inner[:, hidden:]
    chance = 0.5 + 0.5 * lax.erf(first * math.sqrt(0.5))
    gated = first * chance
    slope = chance + first * (jnp.exp(-0.5 * first * first) * (1.0 / math.sqrt(2.0 * math.pi)))
    active = (gated * second).astype(BF16)
    active_ref[...] = active
    result_ref[...] = (state + mul(active, contract)).astype(BF16)

    upstream = up_ref[...]
    active_back = mul(upstream, contract, NT).astype(BF16).astype(F32)
    inner_back = jnp.concatenate(
        [(active_back * second * slope).astype(BF16), (active_back * gated).astype(BF16)], axis=1
    )
    inner_back_ref[...] = inner_back
    normed_back = mul(inner_back[:, :width], expand[0], NT)
    normed_back = normed_back + mul(inner_back[:, width : 2 * width], expand[1], NT)
    normed_back = normed_back + mul(inner_back[:, 2 * width :], expand[2], NT)
    scaled = normed_back * gain
    mean = jnp.mean(scaled, axis=-1, keepdims=True)
    lean = jnp.mean(scaled * unit, axis=-1, keepdims=True)
    state_back = upstream.astype(F32) + inverse * (scaled - mean - unit * lean)
    state_back_ref[...] = state_back
    low = state_back.astype(BF16)
    low_ref[...] = low
    for k, ref in enumerate((b0_ref, b1_ref, b2_ref, b3_ref)):
        ref[...] = mul(buffer[z ^ k, :part, :], low, NT).astype(BF16)


def forward_back(where, merged, tokens, upstream, gain, sides, hidden, step=256):
    count, width = tokens.shape
    size, rows = sides[0].shape[0], 2 * sides[0].shape[1]
    part = width // size
    anywhere = pl.BlockSpec(memory_space=pl.ANY)
    columns = pl.BlockSpec((part, step), lambda i: (0, i))

    def some(lanes):
        return pl.BlockSpec((step, lanes), lambda i: (i, 0))

    lanes = [width, width, width, width, hidden, 2 * hidden]
    kinds = [BF16, F32, BF16, BF16, BF16, BF16]
    return pl.pallas_call(
        forward_back_kernel,
        grid=(count // step,),
        in_specs=[pl.BlockSpec(memory_space=pltpu.SMEM)]
        + [columns] * size
        + [some(width), some(width), pl.BlockSpec((1, width), lambda i: (0, 0))]
        + [anywhere] * len(sides),
        out_specs=[some(n) for n in lanes] + [columns] * size,
        out_shape=[jax.ShapeDtypeStruct((count, n), kind) for n, kind in zip(lanes, kinds)]
        + [jax.ShapeDtypeStruct((part, count), BF16)] * size,
        scratch_shapes=[pltpu.VMEM((size, rows, width), BF16), pltpu.SemaphoreType.DMA((size, 2, 2))],
        compiler_params=pltpu.CompilerParams(vmem_limit_bytes=56 * 2**20),
        cost_estimate=pl.CostEstimate(flops=14 * 10**9, bytes_accessed=20 * 10**6, transcendentals=0),
        name="forward_back",
    )(where, *merged, tokens, upstream, gain, *sides)


def gradients_kernel(
    place_ref, m0_ref, m1_ref, m2_ref, m3_ref, up_ref, low_ref, normed_ref, active_ref, inner_back_ref,
    kept_ref, sent_ref,
):
    z, core = place_ref[0], place_ref[1]
    part, width = m0_ref.shape[0], up_ref.shape[1]
    size, rows, lanes = kept_ref.shape
    held = active_ref.shape[1] // size
    for grads_ref, side in ((sent_ref, 1 - core), (kept_ref, core)):
        start = pl.multiple_of(side * lanes, 128)
        low = low_ref[:, pl.ds(start, lanes)]
        for k, ref in enumerate((m0_ref, m1_ref, m2_ref, m3_ref)):
            grads_ref[z ^ k, :part, :] = mul(ref[...], low).astype(BF16)
        normed = normed_ref[...]
        for t in range(3):
            grad = mul(normed, inner_back_ref[:, pl.ds(t * width + start, lanes)], TN)
            grads_ref[:, (1 + t) * part : (2 + t) * part, :] = grad.astype(BF16).reshape(size, part, lanes)
        grad = mul(active_ref[...], up_ref[:, pl.ds(start, lanes)], TN)
        grads_ref[:, 4 * part : 4 * part + held, :] = grad.astype(BF16).reshape(size, held, lanes)
        if rows > 4 * part + held:
            grads_ref[:, 4 * part + held :, :] = jnp.zeros((size, rows - 4 * part - held, lanes), BF16)


def gradients(where, merged, upstream, low, normed, active, inner_back, rows):
    size = len(merged)
    inside = pl.BlockSpec(memory_space=pltpu.VMEM)
    return pl.pallas_call(
        gradients_kernel,
        in_specs=[pl.BlockSpec(memory_space=pltpu.SMEM)] + [inside] * (size + 5),
        out_specs=[inside] * 2,
        out_shape=[jax.ShapeDtypeStruct((size, rows, upstream.shape[1] // 2), BF16)] * 2,
        compiler_params=pltpu.CompilerParams(vmem_limit_bytes=60 * 2**20),
        cost_estimate=pl.CostEstimate(flops=12 * 10**9, bytes_accessed=12 * 10**6, transcendentals=0),
        name="gradients",
    )(where, *merged, upstream, low, normed, active, inner_back)


def token_kernel(
    place_ref, a0_ref, a1_ref, a2_ref, a3_ref, b0_ref, b1_ref, b2_ref, b3_ref,
    mine_ref, theirs_ref, tokens_ref, back_ref, gain_ref, grad_ref, parts, buffer, sems,
):
    z = place_ref[0]
    size, rows, width = buffer.shape
    load_rows(place_ref, [(mine_ref, theirs_ref)], buffer, sems)
    part = rows // 3
    slots = ((a0_ref, b0_ref), (a1_ref, b1_ref), (a2_ref, b2_ref), (a3_ref, b3_ref))
    for k, (one, two) in enumerate(slots):
        first = (z ^ k) * part
        for head in range(part // HEAD_DIM):
            ref, start = (one, 0) if head == 0 else (two, (head - 1) * 3 * HEAD_DIM)
            for t in range(3):
                lines = pl.ds(pl.multiple_of(first + head * HEAD_DIM, HEAD_DIM), HEAD_DIM)
                parts[t, lines, :] = ref[start + t * HEAD_DIM : start + (t + 1) * HEAD_DIM, :]
    total = jnp.zeros((width, tokens_ref.shape[0]), F32)
    for t in range(3):
        total = total + mul(buffer[:, t * part : (t + 1) * part, :].reshape(width, width), parts[t])
    unit, inverse = unit_of(tokens_ref[...].astype(F32))
    scaled = total.T * gain_ref[...]
    mean = jnp.mean(scaled, axis=-1, keepdims=True)
    lean = jnp.mean(scaled * unit, axis=-1, keepdims=True)
    grad_ref[...] = back_ref[...] + inverse * (scaled - mean - unit * lean)


def token_back(where, early, late, mine, theirs, tokens, state_back, gain):
    count, width = tokens.shape
    size, rows = mine.shape[0], 2 * mine.shape[1]
    inside = pl.BlockSpec(memory_space=pltpu.VMEM)
    anywhere = pl.BlockSpec(memory_space=pl.ANY)
    return pl.pallas_call(
        token_kernel,
        in_specs=[pl.BlockSpec(memory_space=pltpu.SMEM)]
        + [inside] * (len(early) + len(late))
        + [anywhere] * 2
        + [inside] * 3,
        out_specs=inside,
        out_shape=jax.ShapeDtypeStruct((count, width), F32),
        scratch_shapes=[
            pltpu.VMEM((3, width, count), BF16),
            pltpu.VMEM((size, rows, width), BF16),
            pltpu.SemaphoreType.DMA((size, 1, 2)),
        ],
        compiler_params=pltpu.CompilerParams(vmem_limit_bytes=48 * 2**20),
        cost_estimate=pl.CostEstimate(flops=5 * 10**9, bytes_accessed=12 * 10**6, transcendentals=0),
        name="token_back",
    )(where, *early, *late, mine, theirs, tokens, state_back, gain)


def after(values, *others):
    return lax.optimization_barrier((values, others))[0]


def swap(values, axis, size, offset):
    return lax.ppermute(values, axis, [(i, i ^ offset) for i in range(size)])


def exchange(pieces, size):
    return [pieces[0]] + [swap(pieces[d], "fsdp", size, d) for d in range(1, size)]


def column(values, size, ranks, pairs):
    full = [
        (z * ranks + r, to * ranks + (r & ~1) + core)
        for z in range(size)
        for r in range(ranks)
        for to, core in pairs(z, r & 1)
    ]
    return lax.ppermute(values, ("fsdp", "rep"), full)


def collect(own, home, size, ranks, early):
    first = column(
        own, size, ranks, lambda z, c: [(z ^ 1, c) if c == z >> 1 else (z ^ 2, 1 - c)]
    )
    second = column(first, size, ranks, lambda z, c: [] if c == z >> 1 else [(z ^ 1, c)])
    low = jnp.where(home, own, first)
    high = jnp.where(home, first, second)
    pair, early = after((jnp.concatenate([low, high], axis=0), early))
    other = swap(pair, "rep", ranks, 1)
    return pair, other, first, second, early


def trade_out(pieces, size, ranks, rounds=None):
    def round_of(k):
        return lambda z, c: [((2 * c + (z & 1)) ^ k, z >> 1)]

    return [column(pieces[k], size, ranks, round_of(k)) for k in rounds or range(size)]


def trade_back(pieces, size, ranks):
    def round_of(k):
        return lambda z, c: [(2 * c + ((z ^ k) & 1), (z ^ k) >> 1)]

    return [column(pieces[k], size, ranks, round_of(k)) for k in range(size)]


def pick(blocks, index):
    return lax.dynamic_index_in_dim(blocks, index, 0, keepdims=False)


def reorder(blocks, z, size):
    return jnp.stack([pick(blocks, z ^ j) for j in range(size)])


def far(ranks):
    bits = []
    bit = 2
    while bit < ranks:
        bits.append(bit)
        bit *= 2
    return bits


def stage_bit(core, ranks, stage):
    bits = far(ranks)
    return bits[stage] if core == 0 else bits[len(bits) - 1 - stage]


def stage_swap(values, ranks, stage):
    return lax.ppermute(values, "rep", [(i, i ^ stage_bit(i & 1, ranks, stage)) for i in range(ranks)])


def stage_upper(r, ranks, stage):
    bit = jnp.where(r & 1 == 0, stage_bit(0, ranks, stage), stage_bit(1, ranks, stage))
    return r & bit != 0


def place(r, ranks):
    stages = len(far(ranks))
    total = jnp.where(r & 1 != 0, 1 << stages, 0)
    for stage in range(stages):
        total = total + jnp.where(stage_upper(r, ranks, stage), 1 << stage, 0)
    return total


def join(mine, other, upper):
    return jnp.concatenate([jnp.where(upper, other, mine), jnp.where(upper, mine, other)], axis=1)


def cut(values, upper):
    half = values.shape[1] // 2
    mine = jnp.where(upper, half, 0)
    sent = lax.dynamic_slice_in_dim(values, half - mine, half, 1)
    return sent, lax.dynamic_slice_in_dim(values, mine, half, 1)


def add(one, two):
    return (one.astype(F32) + two.astype(F32)).astype(BF16)


def grow(values, r, ranks, stages):
    for stage in stages:
        values = join(values, stage_swap(values, ranks, stage), stage_upper(r, ranks, stage))
    return values


def grow_flat(values, r, ranks, stages):
    for stage in stages:
        other = stage_swap(values, ranks, stage)
        upper = stage_upper(r, ranks, stage)
        values = jnp.concatenate(
            [jnp.where(upper, other, values), jnp.where(upper, values, other)], axis=0
        )
    return values


def shrink(values, r, ranks, stages):
    for stage in stages:
        sent, kept = cut(values, stage_upper(r, ranks, stage))
        values = add(kept, stage_swap(sent, ranks, stage))
    return values


def halves(values):
    middle = values.shape[-1] // 2
    return [values[..., :middle], values[..., middle:]]


def split_rows(shard, r, ranks):
    rows = shard.shape[0] // ranks
    return lax.dynamic_slice_in_dim(shard, place(r, ranks) * rows, rows, 0)


def finish_kernel(
    place_ref, mine_ref, other_ref, into_ref, expand_ref, gain_a_ref, gain_b_ref,
    into_sum_ref, gain_a_sum_ref, out_sum_ref, expand_sum_ref, gain_b_sum_ref, contract_sum_ref,
):
    first = place_ref[1] == 0
    part, width = out_sum_ref.shape
    held = contract_sum_ref.shape[0]
    pieces = mine_ref.shape[0]
    lines = 3 * part // pieces

    def gathered(start):
        rows = mine_ref.shape[1] if start else lines
        sides = []
        for one, two in ((mine_ref, other_ref), (other_ref, mine_ref)):
            blocks = [
                jnp.where(first, one[p, start:rows].astype(F32), two[p, start:rows].astype(F32))
                for p in range(pieces)
            ]
            sides.append(jnp.concatenate(blocks, axis=0))
        return sides

    blocks = [side[:, k * part : (k + 1) * part].T for side in gathered(0) for k in range(2)]
    total = jnp.zeros((part, 1), F32)
    for t in range(3):
        row = jnp.concatenate([block[:, t * part : (t + 1) * part] for block in blocks], axis=1)
        into_sum_ref[:, t * width : (t + 1) * width] = row
        weight = into_ref[:, t * width : (t + 1) * width].astype(F32)
        total = total + jnp.sum(row * weight, axis=1, keepdims=True)
    gain_a_sum_ref[...] = total / gain_a_ref[...].astype(F32)

    grads = jnp.concatenate(gathered(lines), axis=1)
    out_sum_ref[...] = grads[:part]
    total = jnp.zeros((part, 1), F32)
    for t in range(3):
        row = grads[(1 + t) * part : (2 + t) * part]
        expand_sum_ref[:, t * width : (t + 1) * width] = row
        weight = expand_ref[:, t * width : (t + 1) * width].astype(F32)
        total = total + jnp.sum(row * weight, axis=1, keepdims=True)
    gain_b_sum_ref[...] = total / gain_b_ref[...].astype(F32)
    contract_sum_ref[...] = grads[4 * part : 4 * part + held]


def finish(where, mine, other, projection_in, expansion, gain_a, gain_b, held):
    part, wide = projection_in.shape
    inside = pl.BlockSpec(memory_space=pltpu.VMEM)
    shapes = [(part, wide), (part, 1), (part, wide // 3), (part, wide), (part, 1), (held, wide // 3)]
    return pl.pallas_call(
        finish_kernel,
        in_specs=[pl.BlockSpec(memory_space=pltpu.SMEM)] + [inside] * 6,
        out_specs=[inside] * 6,
        out_shape=[jax.ShapeDtypeStruct(shape, F32) for shape in shapes],
        compiler_params=pltpu.CompilerParams(vmem_limit_bytes=48 * 2**20),
        name="finish",
    )(where, mine, other, projection_in, expansion, gain_a[:, None], gain_b[:, None])


def local(size, ranks, tokens, gain_a, projection_in, attention_out, gain_b, expansion, contraction, cotangent):
    z = lax.axis_index("fsdp")
    r = lax.axis_index("rep")
    core = r & 1
    group = 2 * core + (z & 1)
    home = core == z >> 1
    own = tokens[0]
    count, width = own.shape
    part = width // size
    hidden = contraction.shape[0]
    heads = HEADS // size

    stages = list(range(len(far(ranks))))
    where = jnp.stack([z, core]).astype(jnp.int32)
    columns = [projection_in[:, t * width : (t + 1) * width] for t in range(3)]
    piece = split_rows(jnp.concatenate(columns, axis=0), r, ranks)
    rows = piece.shape[0]
    gains = jnp.pad(jnp.concatenate([gain_a, gain_b])[None], ((0, 7), (0, width - 2 * part)))
    pieces = jnp.stack(exchange([jnp.concatenate([piece, gains], axis=0)] * size, size))
    gains = reorder(pieces[:, rows, : 2 * part], z, size).astype(F32)
    gain_one = gains[:, :part].reshape(1, width)
    gain_two = gains[:, part:].reshape(1, width)
    freqs = THETA ** (-(jnp.arange(HALF, dtype=F32) * (2.0 / HEAD_DIM)))
    places = jnp.concatenate([(group ^ d) * count + jnp.arange(count, dtype=jnp.int32) for d in range(size)])
    angles = freqs[:, None] * places.astype(F32)[None, :]
    early = (gain_one, gain_two, jnp.cos(angles), jnp.sin(angles))
    pair, other, first, second, early = collect(own, home, size, ranks, early)
    gain_one, gain_two, cosine, sine = early
    into = grow(pieces[:, :rows], r, ranks, stages[:-1])
    into = grow(after(into, first), r, ranks, stages[-1:])
    into_other = swap(into, "rep", ranks, 1)
    normed, queries, keys, values = project(
        where, pair, other, gain_one, cosine, sine, into, into_other, count
    )

    columns = [expansion[:, t * width : (t + 1) * width] for t in range(3)]
    stacked = jnp.concatenate([attention_out] + columns + [contraction], axis=0)
    pad = -stacked.shape[0] % max(32, 8 * ranks)
    stacked = jnp.concatenate([stacked, jnp.zeros((pad, width), BF16)], axis=0)
    rest = exchange([split_rows(after(stacked, second), r, ranks)] * size, size)
    merged = []
    logs = []
    rest = grow(jnp.stack(after(rest, queries)), r, ranks, stages[:1])
    ahead = []
    for head in range(heads):
        out, log = attend(head, queries, after(keys, *ahead), values)
        merged.append(out)
        logs.append(log)
        if head == 0:
            ahead = [rest]
            sides = halves(grow(after(rest, out), r, ranks, stages[1:-1]))
            sides[0] = grow(after(sides[0], out), r, ranks, stages[-1:])
        if head == 1:
            sides[1] = after(sides[1], out)
            coming = stage_swap(sides[1], ranks, stages[-1])
            ahead = [sides[0]]
    sides[1] = join(sides[1], after(coming, merged[2]), stage_upper(r, ranks, stages[-1]))
    others = [swap(after(sides[0], merged[1]), "rep", ranks, 1), swap(sides[1], "rep", ranks, 1)]
    own_merged = after(jnp.concatenate(merged, axis=0), others[0])

    merged = trade_out([own_merged[:, d * count : (d + 1) * count] for d in range(size)], size, ranks)
    upstream = cotangent[0]
    block_output, state_back, state_low, normed_two, active, inner_back, *merged_back = forward_back(
        where, merged, own, upstream, gain_two, [sides[0], others[0], sides[1], others[1]], size * hidden
    )
    arrived = trade_back(merged_back, size, ranks)
    own_upstream = jnp.concatenate(arrived, axis=1)

    kept, sent = gradients(
        where, merged, upstream, state_low, normed_two, active, inner_back, stacked.shape[0]
    )
    sent = after(sent, *arrived)
    grads = add(kept, swap(sent, "rep", ranks, 1))

    turned_backs = []
    weight_backs = []
    received = []
    ahead = [grads]
    for head in range(heads):
        grad, weight_grad = attend_back(
            head, queries, keys, values, after(own_upstream, *ahead), own_merged, logs[head],
            cosine, sine, normed,
        )
        turned_backs.append(grad)
        weight_backs.append(weight_grad.reshape(3, HEAD_DIM, width))
        if head == 0:
            received = trade_out([grad[:, d * count : (d + 1) * count] for d in range(size)], size, ranks)
            grads = shrink(grads, r, ranks, stages[:0:-1])
            ahead = [grads]
        if head == 1:
            grads = shrink(grads, r, ranks, stages[:1])
            ahead = [grads] + received
    grads = exchange([pick(grads, z ^ d) for d in range(size)], size)
    later = jnp.concatenate(turned_backs[1:], axis=0)
    grads = sum(part.astype(F32) for part in grads).astype(BF16)
    weight_backs[2], grads = after((weight_backs[2], grads), later)
    later = [later[:, d * count : (d + 1) * count] for d in range(size)]
    arrived = trade_out(later, size, ranks)

    into_grad = jnp.concatenate([grad[t] for t in range(3) for grad in weight_backs], axis=0)
    into_grad = after(shrink(into_grad[None], r, ranks, stages[-1:]), arrived[0])
    into_grad = after(shrink(into_grad, r, ranks, stages[-2::-1]), arrived[1])[0]
    lines = into_grad.shape[0]
    blocks = into_grad.reshape(lines, size, part).transpose(1, 0, 2)
    blocks = exchange([pick(blocks, z ^ d) for d in range(size)], size)
    even, odd = (blocks[0].astype(F32) + blocks[2].astype(F32)), (blocks[1].astype(F32) + blocks[3].astype(F32))
    low = z & 1 == 0
    flat = jnp.concatenate([jnp.where(low, even, odd), jnp.where(low, odd, even)], axis=1).astype(BF16)
    both = grow_flat(jnp.concatenate([flat, grads], axis=0)[None], r, ranks, stages[:-1])
    both = after(grow_flat(after(both, arrived[2]), r, ranks, stages[-1:]), arrived[3])
    token_grad = token_back(where, received, arrived, into, into_other, own, state_back, gain_one)[None]
    into_sum, gain_one_sum, attention_out_sum, expansion_sum, gain_two_sum, contraction_sum = finish(
        where, both, swap(both, "rep", ranks, 1), projection_in, expansion, gain_a, gain_b, hidden
    )
    return (
        block_output[None],
        token_grad,
        gain_one_sum[:, 0],
        into_sum,
        attention_out_sum,
        gain_two_sum[:, 0],
        expansion_sum,
        contraction_sum,
    )


def solution(mesh):
    tokens, rows, line = P("rep", "fsdp", None), P("fsdp", None), P("fsdp")
    in_specs = (tokens, line, rows, rows, line, rows, rows, tokens)
    out_specs = (tokens, tokens, line, rows, rows, line, rows, rows)
    body = functools.partial(local, mesh.shape["fsdp"], mesh.shape["rep"])
    return jax.shard_map(body, mesh=mesh, in_specs=in_specs, out_specs=out_specs, check_vma=False)
```

```python
import functools
import math

import jax
import jax.numpy as jnp
from jax import lax
from jax.experimental import pallas as pl
from jax.experimental.pallas import tpu as pltpu
from jax.sharding import PartitionSpec as P

HEADS = 12
HEAD_DIM = 64
HALF = HEAD_DIM // 2
SCALE = 1.0 / math.sqrt(HEAD_DIM)
EPS = 1e-05
THETA = 160000.0
F32 = jnp.float32
BF16 = jnp.bfloat16
NN = (((1,), (0,)), ((), ()))
NT = (((1,), (1,)), ((), ()))
TN = (((0,), (0,)), ((), ()))
TT = (((0,), (1,)), ((), ()))


def mul(a, b, dims=NN):
    return lax.dot_general(a, b, dims, preferred_element_type=F32)


def attend_kernel(q_ref, k_ref, v_ref, out_ref, log_ref):
    scores = mul(k_ref[...].T, q_ref[...])
    highest = jnp.max(scores, axis=0, keepdims=True)
    raised = jnp.exp(scores - highest)
    total = jnp.sum(raised, axis=0, keepdims=True)
    mixed = mul(v_ref[...], raised.astype(BF16))
    out_ref[...] = (mixed / total).astype(BF16)
    log_ref[...] = highest + jnp.log(total)


def attend(head, queries, keys, values, step=1024):
    count = queries.shape[1]
    step = min(step, count)
    whole = pl.BlockSpec((HEAD_DIM, count), lambda i: (head, 0))
    return pl.pallas_call(
        attend_kernel,
        grid=(count // step,),
        in_specs=[pl.BlockSpec((HEAD_DIM, step), lambda i: (head, i)), whole, whole],
        out_specs=[
            pl.BlockSpec((HEAD_DIM, step), lambda i: (0, i)),
            pl.BlockSpec((1, step), lambda i: (0, i)),
        ],
        out_shape=[
            jax.ShapeDtypeStruct((HEAD_DIM, count), BF16),
            jax.ShapeDtypeStruct((1, count), F32),
        ],
        compiler_params=pltpu.CompilerParams(vmem_limit_bytes=48 * 2**20),
        cost_estimate=pl.CostEstimate(
            flops=28 * count * count * HEAD_DIM,
            bytes_accessed=8 * HEAD_DIM * count,
            transcendentals=count * count,
        ),
        name="attend",
    )(queries, keys, values)


def turn_back(values, cosine, sine):
    first, second = values[:HALF], values[HALF:]
    return jnp.concatenate([first * cosine + second * sine, second * cosine - first * sine], axis=0)


def attend_back_kernel(
    q_ref, kt_ref, vt_ref, u0_ref, u1_ref, u2_ref, u3_ref, out_ref, log_ref, cos_ref, sin_ref, normed_ref,
    grad_ref, weight_ref, up_ref, k_ref, v_ref, dk_ref, dv_ref,
):
    index = pl.program_id(0)
    step = q_ref.shape[1]

    @pl.when(index == 0)
    def _():
        for d, ref in enumerate((u0_ref, u1_ref, u2_ref, u3_ref)):
            up_ref[d] = ref[...]
        k_ref[...] = kt_ref[...].T
        v_ref[...] = vt_ref[...].T
        dk_ref[...] = jnp.zeros_like(dk_ref)
        dv_ref[...] = jnp.zeros_like(dv_ref)

    upstream = up_ref[index]
    inner_sum = jnp.sum(upstream.astype(F32) * out_ref[...].astype(F32), axis=0, keepdims=True)
    chances = jnp.exp(mul(k_ref[...], q_ref[...]) - log_ref[...])
    prob_back = mul(v_ref[...], upstream)
    score_back = (chances * (prob_back - inner_sum)).astype(BF16)
    dv_ref[...] += mul(chances.astype(BF16), upstream, NT)
    dk_ref[...] += mul(score_back, q_ref[...], NT)
    columns = pl.ds(pl.multiple_of(index * step, step), step)
    query_back = mul(kt_ref[...], score_back) * SCALE
    grad_ref[pl.ds(0, HEAD_DIM), columns] = turn_back(
        query_back, cos_ref[:, columns], sin_ref[:, columns]
    ).astype(BF16)

    @pl.when(index == pl.num_programs(0) - 1)
    def _():
        key_back = turn_back(dk_ref[...].T, cos_ref[...], sin_ref[...])
        grad_ref[pl.ds(HEAD_DIM, HEAD_DIM), :] = key_back.astype(BF16)
        grad_ref[pl.ds(2 * HEAD_DIM, HEAD_DIM), :] = dv_ref[...].T.astype(BF16)
        weight_ref[...] = mul(grad_ref[...], normed_ref[...]).astype(BF16)


def attend_back(head, queries, keys, values, upstream, merged, log, cosine, sine, normed):
    count, width = normed.shape
    step = upstream[0].shape[1]
    some = pl.BlockSpec((HEAD_DIM, step), lambda i: (head, i))
    whole = pl.BlockSpec((HEAD_DIM, count), lambda i: (head, 0))
    table = pl.BlockSpec((HALF, count), lambda i: (0, 0))
    return pl.pallas_call(
        attend_back_kernel,
        grid=(count // step,),
        in_specs=[
            some,
            whole,
            whole,
            *[pl.BlockSpec((HEAD_DIM, step), lambda i: (head, 0))] * len(upstream),
            some,
            pl.BlockSpec((1, step), lambda i: (0, i)),
            table,
            table,
            pl.BlockSpec((count, width), lambda i: (0, 0)),
        ],
        out_specs=[
            pl.BlockSpec((3 * HEAD_DIM, count), lambda i: (0, 0)),
            pl.BlockSpec((3 * HEAD_DIM, width), lambda i: (0, 0)),
        ],
        out_shape=[
            jax.ShapeDtypeStruct((3 * HEAD_DIM, count), BF16),
            jax.ShapeDtypeStruct((3 * HEAD_DIM, width), BF16),
        ],
        scratch_shapes=[
            pltpu.VMEM((len(upstream), HEAD_DIM, step), BF16),
            pltpu.VMEM((count, HEAD_DIM), BF16),
            pltpu.VMEM((count, HEAD_DIM), BF16),
            pltpu.VMEM((count, HEAD_DIM), F32),
            pltpu.VMEM((count, HEAD_DIM), F32),
        ],
        compiler_params=pltpu.CompilerParams(vmem_limit_bytes=48 * 2**20),
        cost_estimate=pl.CostEstimate(
            flops=56 * count * count * HEAD_DIM,
            bytes_accessed=16 * HEAD_DIM * count,
            transcendentals=count * count,
        ),
        name="attend_back",
    )(queries, keys, values, *upstream, merged, log, cosine, sine, normed)


def load_rows(place_ref, pairs, buffer, sems):
    z, core = place_ref[0], place_ref[1]
    size, rows, lanes = pairs[0][0].shape
    copies = []
    for d in range(size):
        for n, (mine, other) in enumerate(pairs):
            for k, (ref, side) in enumerate(((mine, core), (other, 1 - core))):
                start = pl.multiple_of(side * rows, 16)
                target = buffer.at[z ^ d, pl.ds(start, rows), pl.ds(n * lanes, lanes)]
                copies.append(pltpu.make_async_copy(ref.at[d], target, sems.at[d, n, k]))
    for copy in copies:
        copy.start()
    for copy in copies:
        copy.wait()


def unit_of(values):
    centre = values - jnp.mean(values, axis=-1, keepdims=True)
    inverse = lax.rsqrt(jnp.mean(centre * centre, axis=-1, keepdims=True) + EPS)
    return centre * inverse, inverse


def turn(values, cosine, sine):
    first, second = values[:HALF], values[HALF:]
    return jnp.concatenate([first * cosine - second * sine, second * cosine + first * sine], axis=0)


def project_kernel(
    place_ref, pair_ref, other_ref, gain_ref, cos_ref, sin_ref, mine_ref, theirs_ref,
    normed_ref, q_ref, kt_ref, vt_ref, buffer, weight, sems,
):
    index = pl.program_id(0)
    part = q_ref.shape[0]
    size = buffer.shape[0]

    @pl.when(index == 0)
    def _():
        load_rows(place_ref, [(mine_ref, theirs_ref)], buffer, sems)
        start = pl.multiple_of(place_ref[1] * 2 * part, 128)
        odd = place_ref[0] & 1 == 1
        for t in range(3):
            both = buffer[:, t * part : (t + 1) * part, pl.ds(start, 2 * part)].reshape(size * part, 2 * part)
            chosen = jnp.where(odd, both[:, part:].astype(F32), both[:, :part].astype(F32))
            weight[:, t * part : (t + 1) * part] = chosen.astype(BF16)

    block = jnp.where(index < 2, pair_ref[...].astype(F32), other_ref[...].astype(F32))
    normed = (unit_of(block)[0] * gain_ref[...]).astype(BF16)
    normed_ref[...] = normed
    projected = mul(normed, weight[...])
    turned = projected[:, : 2 * part].T
    cosine, sine = cos_ref[...], sin_ref[...]
    for head in range(part // HEAD_DIM):
        rows = slice(head * HEAD_DIM, (head + 1) * HEAD_DIM)
        queries = turn(turned[rows], cosine, sine).astype(BF16)
        q_ref[rows, :] = (queries.astype(F32) * SCALE).astype(BF16)
        keys = turn(turned[part + head * HEAD_DIM : part + (head + 1) * HEAD_DIM], cosine, sine)
        kt_ref[rows, :] = keys.astype(BF16)
    vt_ref[...] = projected[:, 2 * part :].astype(BF16).T


def project(where, pair, other, gain, cosine, sine, mine, theirs, count):
    width = pair.shape[1]
    size, rows = mine.shape[0], 2 * mine.shape[1]
    part = width // size
    total = size * count
    anywhere = pl.BlockSpec(memory_space=pl.ANY)
    columns = pl.BlockSpec((part, count), lambda i: (0, i))
    return pl.pallas_call(
        project_kernel,
        grid=(size,),
        in_specs=[
            pl.BlockSpec(memory_space=pltpu.SMEM),
            pl.BlockSpec((count, width), lambda i: (jnp.minimum(i, 1), 0)),
            pl.BlockSpec((count, width), lambda i: (jnp.maximum(i - 2, 0), 0)),
            pl.BlockSpec((1, width), lambda i: (0, 0)),
            pl.BlockSpec((HALF, count), lambda i: (0, i)),
            pl.BlockSpec((HALF, count), lambda i: (0, i)),
            anywhere,
            anywhere,
        ],
        out_specs=[
            pl.BlockSpec((count, width), lambda i: (i, 0)),
            columns,
            columns,
            columns,
        ],
        out_shape=[
            jax.ShapeDtypeStruct((total, width), BF16),
            jax.ShapeDtypeStruct((part, total), BF16),
            jax.ShapeDtypeStruct((part, total), BF16),
            jax.ShapeDtypeStruct((part, total), BF16),
        ],
        scratch_shapes=[
            pltpu.VMEM((size, rows, width), BF16),
            pltpu.VMEM((width, 3 * part), BF16),
            pltpu.SemaphoreType.DMA((size, 1, 2)),
        ],
        compiler_params=pltpu.CompilerParams(vmem_limit_bytes=48 * 2**20),
        cost_estimate=pl.CostEstimate(flops=8 * 10**9, bytes_accessed=20 * 10**6, transcendentals=0),
        name="project",
    )(where, pair, other, gain, cosine, sine, mine, theirs)


def forward_back_kernel(
    place_ref, m0_ref, m1_ref, m2_ref, m3_ref, tokens_ref, up_ref, gain_ref, mine_ref, theirs_ref,
    result_ref, state_back_ref, low_ref, normed_ref, active_ref, inner_back_ref, b0_ref, b1_ref, b2_ref, b3_ref,
    buffer, sems,
):
    part, width = m0_ref.shape[0], tokens_ref.shape[1]
    size = buffer.shape[0]
    hidden = active_ref.shape[1]
    z = place_ref[0]

    @pl.when(pl.program_id(0) == 0)
    def _():
        load_rows(place_ref, [(mine_ref, theirs_ref)], buffer, sems)

    expand = [buffer[:, (1 + t) * part : (2 + t) * part, :].reshape(width, width) for t in range(3)]
    contract = buffer[:, 4 * part : 4 * part + hidden // size, :].reshape(hidden, width)
    gain = gain_ref[...]

    state = tokens_ref[...].astype(F32)
    for k, ref in enumerate((m0_ref, m1_ref, m2_ref, m3_ref)):
        state = state + mul(ref[...], buffer[z ^ k, :part, :], TN)
    unit, inverse = unit_of(state)
    normed = (unit * gain).astype(BF16)
    normed_ref[...] = normed
    inner = jnp.concatenate([mul(normed, weight) for weight in expand], axis=1)
    first, second = inner[:, :hidden], inner[:, hidden:]
    chance = 0.5 + 0.5 * lax.erf(first * math.sqrt(0.5))
    gated = first * chance
    slope = chance + first * (jnp.exp(-0.5 * first * first) * (1.0 / math.sqrt(2.0 * math.pi)))
    active = (gated * second).astype(BF16)
    active_ref[...] = active
    result_ref[...] = (state + mul(active, contract)).astype(BF16)

    upstream = up_ref[...]
    active_back = mul(upstream, contract, NT).astype(BF16).astype(F32)
    inner_back = jnp.concatenate(
        [(active_back * second * slope).astype(BF16), (active_back * gated).astype(BF16)], axis=1
    )
    inner_back_ref[...] = inner_back
    normed_back = mul(inner_back[:, :width], expand[0], NT)
    normed_back = normed_back + mul(inner_back[:, width : 2 * width], expand[1], NT)
    normed_back = normed_back + mul(inner_back[:, 2 * width :], expand[2], NT)
    scaled = normed_back * gain
    mean = jnp.mean(scaled, axis=-1, keepdims=True)
    lean = jnp.mean(scaled * unit, axis=-1, keepdims=True)
    state_back = upstream.astype(F32) + inverse * (scaled - mean - unit * lean)
    state_back_ref[...] = state_back
    low = state_back.astype(BF16)
    low_ref[...] = low
    for k, ref in enumerate((b0_ref, b1_ref, b2_ref, b3_ref)):
        ref[...] = mul(buffer[z ^ k, :part, :], low, NT).astype(BF16)


def forward_back(where, merged, tokens, upstream, gain, sides, hidden, step=256):
    count, width = tokens.shape
    size, rows = sides[0].shape[0], 2 * sides[0].shape[1]
    part = width // size
    anywhere = pl.BlockSpec(memory_space=pl.ANY)
    columns = pl.BlockSpec((part, step), lambda i: (0, i))

    def some(lanes):
        return pl.BlockSpec((step, lanes), lambda i: (i, 0))

    lanes = [width, width, width, width, hidden, 2 * hidden]
    kinds = [BF16, F32, BF16, BF16, BF16, BF16]
    return pl.pallas_call(
        forward_back_kernel,
        grid=(count // step,),
        in_specs=[pl.BlockSpec(memory_space=pltpu.SMEM)]
        + [columns] * size
        + [some(width), some(width), pl.BlockSpec((1, width), lambda i: (0, 0))]
        + [anywhere] * len(sides),
        out_specs=[some(n) for n in lanes] + [columns] * size,
        out_shape=[jax.ShapeDtypeStruct((count, n), kind) for n, kind in zip(lanes, kinds)]
        + [jax.ShapeDtypeStruct((part, count), BF16)] * size,
        scratch_shapes=[pltpu.VMEM((size, rows, width), BF16), pltpu.SemaphoreType.DMA((size, 1, 2))],
        compiler_params=pltpu.CompilerParams(vmem_limit_bytes=56 * 2**20),
        cost_estimate=pl.CostEstimate(flops=14 * 10**9, bytes_accessed=20 * 10**6, transcendentals=0),
        name="forward_back",
    )(where, *merged, tokens, upstream, gain, *sides)


def gradients_kernel(
    place_ref, m0_ref, m1_ref, m2_ref, m3_ref, up_ref, low_ref, normed_ref, active_ref, inner_back_ref,
    kept_ref, sent_ref,
):
    z, core = place_ref[0], place_ref[1]
    part, width = m0_ref.shape[0], up_ref.shape[1]
    size, rows, lanes = kept_ref.shape
    held = active_ref.shape[1] // size
    for grads_ref, side in ((sent_ref, 1 - core), (kept_ref, core)):
        start = pl.multiple_of(side * lanes, 128)
        low = low_ref[:, pl.ds(start, lanes)]
        for k, ref in enumerate((m0_ref, m1_ref, m2_ref, m3_ref)):
            grads_ref[z ^ k, :part, :] = mul(ref[...], low).astype(BF16)
        normed = normed_ref[...]
        for t in range(3):
            grad = mul(normed, inner_back_ref[:, pl.ds(t * width + start, lanes)], TN)
            grads_ref[:, (1 + t) * part : (2 + t) * part, :] = grad.astype(BF16).reshape(size, part, lanes)
        grad = mul(active_ref[...], up_ref[:, pl.ds(start, lanes)], TN)
        grads_ref[:, 4 * part : 4 * part + held, :] = grad.astype(BF16).reshape(size, held, lanes)
        if rows > 4 * part + held:
            grads_ref[:, 4 * part + held :, :] = jnp.zeros((size, rows - 4 * part - held, lanes), BF16)


def gradients(where, merged, upstream, low, normed, active, inner_back, rows):
    size = len(merged)
    inside = pl.BlockSpec(memory_space=pltpu.VMEM)
    return pl.pallas_call(
        gradients_kernel,
        in_specs=[pl.BlockSpec(memory_space=pltpu.SMEM)] + [inside] * (size + 5),
        out_specs=[inside] * 2,
        out_shape=[jax.ShapeDtypeStruct((size, rows, upstream.shape[1] // 2), BF16)] * 2,
        compiler_params=pltpu.CompilerParams(vmem_limit_bytes=60 * 2**20),
        cost_estimate=pl.CostEstimate(flops=12 * 10**9, bytes_accessed=12 * 10**6, transcendentals=0),
        name="gradients",
    )(where, *merged, upstream, low, normed, active, inner_back)


def token_kernel(
    place_ref, a0_ref, a1_ref, a2_ref, a3_ref, b0_ref, b1_ref, b2_ref, b3_ref,
    mine_ref, theirs_ref, tokens_ref, back_ref, gain_ref, grad_ref, parts, buffer, sems,
):
    z = place_ref[0]
    size, rows, width = buffer.shape
    load_rows(place_ref, [(mine_ref, theirs_ref)], buffer, sems)
    part = rows // 3
    slots = ((a0_ref, b0_ref), (a1_ref, b1_ref), (a2_ref, b2_ref), (a3_ref, b3_ref))
    for k, (one, two) in enumerate(slots):
        first = (z ^ k) * part
        for head in range(part // HEAD_DIM):
            ref, start = (one, 0) if head == 0 else (two, (head - 1) * 3 * HEAD_DIM)
            for t in range(3):
                lines = pl.ds(pl.multiple_of(first + head * HEAD_DIM, HEAD_DIM), HEAD_DIM)
                parts[t, lines, :] = ref[start + t * HEAD_DIM : start + (t + 1) * HEAD_DIM, :]
    total = jnp.zeros((width, tokens_ref.shape[0]), F32)
    for t in range(3):
        total = total + mul(buffer[:, t * part : (t + 1) * part, :].reshape(width, width), parts[t])
    unit, inverse = unit_of(tokens_ref[...].astype(F32))
    scaled = total.T * gain_ref[...]
    mean = jnp.mean(scaled, axis=-1, keepdims=True)
    lean = jnp.mean(scaled * unit, axis=-1, keepdims=True)
    grad_ref[...] = back_ref[...] + inverse * (scaled - mean - unit * lean)


def token_back(where, early, late, mine, theirs, tokens, state_back, gain):
    count, width = tokens.shape
    size, rows = mine.shape[0], 2 * mine.shape[1]
    inside = pl.BlockSpec(memory_space=pltpu.VMEM)
    anywhere = pl.BlockSpec(memory_space=pl.ANY)
    return pl.pallas_call(
        token_kernel,
        in_specs=[pl.BlockSpec(memory_space=pltpu.SMEM)]
        + [inside] * (len(early) + len(late))
        + [anywhere] * 2
        + [inside] * 3,
        out_specs=inside,
        out_shape=jax.ShapeDtypeStruct((count, width), F32),
        scratch_shapes=[
            pltpu.VMEM((3, width, count), BF16),
            pltpu.VMEM((size, rows, width), BF16),
            pltpu.SemaphoreType.DMA((size, 1, 2)),
        ],
        compiler_params=pltpu.CompilerParams(vmem_limit_bytes=48 * 2**20),
        cost_estimate=pl.CostEstimate(flops=5 * 10**9, bytes_accessed=12 * 10**6, transcendentals=0),
        name="token_back",
    )(where, *early, *late, mine, theirs, tokens, state_back, gain)


def after(values, *others):
    return lax.optimization_barrier((values, others))[0]


def swap(values, axis, size, offset):
    return lax.ppermute(values, axis, [(i, i ^ offset) for i in range(size)])


def exchange(pieces, size):
    return [pieces[0]] + [swap(pieces[d], "fsdp", size, d) for d in range(1, size)]


def column(values, size, ranks, pairs):
    full = [
        (z * ranks + r, to * ranks + (r & ~1) + core)
        for z in range(size)
        for r in range(ranks)
        for to, core in pairs(z, r & 1)
    ]
    return lax.ppermute(values, ("fsdp", "rep"), full)


def collect(own, home, size, ranks, early):
    first = column(
        own, size, ranks, lambda z, c: [(z ^ 1, c) if c == z >> 1 else (z ^ 2, 1 - c)]
    )
    second = column(first, size, ranks, lambda z, c: [] if c == z >> 1 else [(z ^ 1, c)])
    low = jnp.where(home, own, first)
    high = jnp.where(home, first, second)
    pair, early = after((jnp.concatenate([low, high], axis=0), early))
    other = swap(pair, "rep", ranks, 1)
    return pair, other, first, second, early


def trade_out(pieces, size, ranks, rounds=None):
    def round_of(k):
        return lambda z, c: [((2 * c + (z & 1)) ^ k, z >> 1)]

    return [column(pieces[k], size, ranks, round_of(k)) for k in rounds or range(size)]


def trade_back(pieces, size, ranks):
    def round_of(k):
        return lambda z, c: [(2 * c + ((z ^ k) & 1), (z ^ k) >> 1)]

    return [column(pieces[k], size, ranks, round_of(k)) for k in range(size)]


def pick(blocks, index):
    return lax.dynamic_index_in_dim(blocks, index, 0, keepdims=False)


def reorder(blocks, z, size):
    return jnp.stack([pick(blocks, z ^ j) for j in range(size)])


def far(ranks):
    bits = []
    bit = 2
    while bit < ranks:
        bits.append(bit)
        bit *= 2
    return bits


def stage_bit(core, ranks, stage):
    bits = far(ranks)
    return bits[stage] if core == 0 else bits[len(bits) - 1 - stage]


def stage_swap(values, ranks, stage):
    return lax.ppermute(values, "rep", [(i, i ^ stage_bit(i & 1, ranks, stage)) for i in range(ranks)])


def stage_upper(r, ranks, stage):
    bit = jnp.where(r & 1 == 0, stage_bit(0, ranks, stage), stage_bit(1, ranks, stage))
    return r & bit != 0


def place(r, ranks):
    stages = len(far(ranks))
    total = jnp.where(r & 1 != 0, 1 << stages, 0)
    for stage in range(stages):
        total = total + jnp.where(stage_upper(r, ranks, stage), 1 << stage, 0)
    return total


def join(mine, other, upper):
    return jnp.concatenate([jnp.where(upper, other, mine), jnp.where(upper, mine, other)], axis=1)


def cut(values, upper):
    half = values.shape[1] // 2
    mine = jnp.where(upper, half, 0)
    sent = lax.dynamic_slice_in_dim(values, half - mine, half, 1)
    return sent, lax.dynamic_slice_in_dim(values, mine, half, 1)


def add(one, two):
    return (one.astype(F32) + two.astype(F32)).astype(BF16)


def grow(values, r, ranks, stages):
    for stage in stages:
        values = join(values, stage_swap(values, ranks, stage), stage_upper(r, ranks, stage))
    return values


def grow_flat(values, r, ranks, stages):
    for stage in stages:
        other = stage_swap(values, ranks, stage)
        upper = stage_upper(r, ranks, stage)
        values = jnp.concatenate(
            [jnp.where(upper, other, values), jnp.where(upper, values, other)], axis=0
        )
    return values


def shrink(values, r, ranks, stages):
    for stage in stages:
        sent, kept = cut(values, stage_upper(r, ranks, stage))
        values = add(kept, stage_swap(sent, ranks, stage))
    return values


def halves(values):
    middle = values.shape[-1] // 2
    return [values[..., :middle], values[..., middle:]]


def split_rows(shard, r, ranks):
    rows = shard.shape[0] // ranks
    return lax.dynamic_slice_in_dim(shard, place(r, ranks) * rows, rows, 0)


def finish_kernel(
    place_ref, mine_ref, other_ref, into_ref, expand_ref, gain_a_ref, gain_b_ref,
    into_sum_ref, gain_a_sum_ref, out_sum_ref, expand_sum_ref, gain_b_sum_ref, contract_sum_ref,
):
    first = place_ref[1] == 0
    part, width = out_sum_ref.shape
    held = contract_sum_ref.shape[0]
    pieces = mine_ref.shape[0]
    lines = 3 * part // pieces

    def gathered(start):
        rows = mine_ref.shape[1] if start else lines
        sides = []
        for one, two in ((mine_ref, other_ref), (other_ref, mine_ref)):
            blocks = [
                jnp.where(first, one[p, start:rows].astype(F32), two[p, start:rows].astype(F32))
                for p in range(pieces)
            ]
            sides.append(jnp.concatenate(blocks, axis=0))
        return sides

    blocks = [side[:, k * part : (k + 1) * part].T for side in gathered(0) for k in range(2)]
    total = jnp.zeros((part, 1), F32)
    for t in range(3):
        row = jnp.concatenate([block[:, t * part : (t + 1) * part] for block in blocks], axis=1)
        into_sum_ref[:, t * width : (t + 1) * width] = row
        weight = into_ref[:, t * width : (t + 1) * width].astype(F32)
        total = total + jnp.sum(row * weight, axis=1, keepdims=True)
    gain_a_sum_ref[...] = total.T / gain_a_ref[...].astype(F32)

    grads = jnp.concatenate(gathered(lines), axis=1)
    out_sum_ref[...] = grads[:part]
    total = jnp.zeros((part, 1), F32)
    for t in range(3):
        row = grads[(1 + t) * part : (2 + t) * part]
        expand_sum_ref[:, t * width : (t + 1) * width] = row
        weight = expand_ref[:, t * width : (t + 1) * width].astype(F32)
        total = total + jnp.sum(row * weight, axis=1, keepdims=True)
    gain_b_sum_ref[...] = total.T / gain_b_ref[...].astype(F32)
    contract_sum_ref[...] = grads[4 * part : 4 * part + held]


def finish(where, mine, other, projection_in, expansion, gain_a, gain_b, held):
    part, wide = projection_in.shape
    inside = pl.BlockSpec(memory_space=pltpu.VMEM)
    shapes = [(part, wide), (1, part), (part, wide // 3), (part, wide), (1, part), (held, wide // 3)]
    return pl.pallas_call(
        finish_kernel,
        in_specs=[pl.BlockSpec(memory_space=pltpu.SMEM)] + [inside] * 6,
        out_specs=[inside] * 6,
        out_shape=[jax.ShapeDtypeStruct(shape, F32) for shape in shapes],
        compiler_params=pltpu.CompilerParams(vmem_limit_bytes=48 * 2**20),
        name="finish",
    )(where, mine, other, projection_in, expansion, gain_a[None], gain_b[None])


def local(size, ranks, tokens, gain_a, projection_in, attention_out, gain_b, expansion, contraction, cotangent):
    z = lax.axis_index("fsdp")
    r = lax.axis_index("rep")
    core = r & 1
    group = 2 * core + (z & 1)
    home = core == z >> 1
    own = tokens[0]
    count, width = own.shape
    part = width // size
    hidden = contraction.shape[0]
    heads = HEADS // size

    stages = list(range(len(far(ranks))))
    where = jnp.stack([z, core]).astype(jnp.int32)
    columns = [projection_in[:, t * width : (t + 1) * width] for t in range(3)]
    piece = split_rows(jnp.concatenate(columns, axis=0), r, ranks)
    rows = piece.shape[0]
    gains = jnp.pad(jnp.concatenate([gain_a, gain_b])[None], ((0, 7), (0, width - 2 * part)))
    pieces = jnp.stack(exchange([jnp.concatenate([piece, gains], axis=0)] * size, size))
    gains = reorder(pieces[:, rows, : 2 * part], z, size).astype(F32)
    gain_one = gains[:, :part].reshape(1, width)
    gain_two = gains[:, part:].reshape(1, width)
    freqs = THETA ** (-(jnp.arange(HALF, dtype=F32) * (2.0 / HEAD_DIM)))
    places = jnp.concatenate([(group ^ d) * count + jnp.arange(count, dtype=jnp.int32) for d in range(size)])
    angles = freqs[:, None] * places.astype(F32)[None, :]
    early = (gain_one, gain_two, jnp.cos(angles), jnp.sin(angles))
    pair, other, first, second, early = collect(own, home, size, ranks, early)
    gain_one, gain_two, cosine, sine = early
    into = grow(pieces[:, :rows], r, ranks, stages[:-1])
    into = grow(after(into, first), r, ranks, stages[-1:])
    into_other = swap(into, "rep", ranks, 1)
    normed, queries, keys, values = project(
        where, pair, other, gain_one, cosine, sine, into, into_other, count
    )

    columns = [expansion[:, t * width : (t + 1) * width] for t in range(3)]
    stacked = jnp.concatenate([attention_out] + columns + [contraction], axis=0)
    pad = -stacked.shape[0] % max(32, 8 * ranks)
    stacked = jnp.concatenate([stacked, jnp.zeros((pad, width), BF16)], axis=0)
    rest = exchange([split_rows(after(stacked, second), r, ranks)] * size, size)
    merged = []
    logs = []
    for head in range(heads):
        out, log = attend(head, queries, after(keys, *merged[-1:]), values)
        merged.append(out)
        logs.append(log)
    rest = jnp.stack(after(rest, merged[0]))
    for stage in stages[:-1]:
        rest = join(rest, after(stage_swap(rest, ranks, stage), merged[-1]), stage_upper(r, ranks, stage))
    own_merged = jnp.concatenate(merged, axis=0)
    merged = trade_out([own_merged[:, d * count : (d + 1) * count] for d in range(size)], size, ranks)
    coming = after(stage_swap(rest, ranks, stages[-1]), *merged)
    rest = join(rest, coming, stage_upper(r, ranks, stages[-1]))
    rest_other = swap(rest, "rep", ranks, 1)
    upstream = cotangent[0]
    block_output, state_back, state_low, normed_two, active, inner_back, *merged_back = forward_back(
        where, merged, own, upstream, gain_two, [rest, rest_other], size * hidden
    )
    arrived = trade_back(merged_back, size, ranks)
    own_upstream = arrived

    kept, sent = gradients(
        where, merged, upstream, state_low, normed_two, active, inner_back, stacked.shape[0]
    )
    sent = after(sent, *arrived)
    grads = add(kept, swap(sent, "rep", ranks, 1))

    turned_backs = []
    weight_backs = []
    received = []
    ahead = [grads]
    for head in range(heads):
        grad, weight_grad = attend_back(
            head, queries, keys, values, after(own_upstream, *ahead), own_merged, logs[head],
            cosine, sine, normed,
        )
        turned_backs.append(grad)
        weight_backs.append(weight_grad.reshape(3, HEAD_DIM, width))
        if head == 0:
            received = trade_out([grad[:, d * count : (d + 1) * count] for d in range(size)], size, ranks)
            grads = shrink(grads, r, ranks, stages[:0:-1])
            ahead = [grads]
        if head == 1:
            grads = shrink(grads, r, ranks, stages[:1])
            ahead = [grads] + received
    grads = exchange([pick(grads, z ^ d) for d in range(size)], size)
    later = jnp.concatenate(turned_backs[1:], axis=0)
    grads = sum(part.astype(F32) for part in grads).astype(BF16)
    weight_backs[2], grads = after((weight_backs[2], grads), later)
    later = [later[:, d * count : (d + 1) * count] for d in range(size)]
    arrived = trade_out(later, size, ranks)

    into_grad = jnp.concatenate([grad[t] for t in range(3) for grad in weight_backs], axis=0)
    into_grad = after(shrink(into_grad[None], r, ranks, stages[-1:]), arrived[0])
    into_grad = after(shrink(into_grad, r, ranks, stages[-2::-1]), arrived[1])[0]
    lines = into_grad.shape[0]
    blocks = into_grad.reshape(lines, size, part).transpose(1, 0, 2)
    blocks = exchange([pick(blocks, z ^ d) for d in range(size)], size)
    even, odd = (blocks[0].astype(F32) + blocks[2].astype(F32)), (blocks[1].astype(F32) + blocks[3].astype(F32))
    low = z & 1 == 0
    flat = jnp.concatenate([jnp.where(low, even, odd), jnp.where(low, odd, even)], axis=1).astype(BF16)
    flat = after(flat, arrived[2])
    both = grow_flat(jnp.concatenate([flat, grads], axis=0)[None], r, ranks, stages[:-1])
    both = grow_flat(after(both, arrived[3]), r, ranks, stages[-1:])
    token_grad = token_back(where, received, arrived, into, into_other, own, state_back, gain_one)[None]
    into_sum, gain_one_sum, attention_out_sum, expansion_sum, gain_two_sum, contraction_sum = finish(
        where, both, swap(both, "rep", ranks, 1), projection_in, expansion, gain_a, gain_b, hidden
    )
    return (
        block_output[None],
        token_grad,
        gain_one_sum[0],
        into_sum,
        attention_out_sum,
        gain_two_sum[0],
        expansion_sum,
        contraction_sum,
    )


def solution(mesh):
    tokens, rows, line = P("rep", "fsdp", None), P("fsdp", None), P("fsdp")
    in_specs = (tokens, line, rows, rows, line, rows, rows, tokens)
    out_specs = (tokens, tokens, line, rows, rows, line, rows, rows)
    body = functools.partial(local, mesh.shape["fsdp"], mesh.shape["rep"])
    return jax.shard_map(body, mesh=mesh, in_specs=in_specs, out_specs=out_specs, check_vma=False)
```

```python
import functools
import math

import jax
import jax.numpy as jnp
from jax import lax
from jax.experimental import pallas as pl
from jax.experimental.pallas import tpu as pltpu
from jax.sharding import PartitionSpec as P

HEADS = 12
HEAD_DIM = 64
HALF = HEAD_DIM // 2
SCALE = 1.0 / math.sqrt(HEAD_DIM)
EPS = 1e-05
THETA = 160000.0
F32 = jnp.float32
BF16 = jnp.bfloat16
NN = (((1,), (0,)), ((), ()))
NT = (((1,), (1,)), ((), ()))
TN = (((0,), (0,)), ((), ()))
TT = (((0,), (1,)), ((), ()))


def mul(a, b, dims=NN):
    return lax.dot_general(a, b, dims, preferred_element_type=F32)


def attend_kernel(q_ref, k_ref, v_ref, out_ref, log_ref):
    scores = mul(k_ref[...].T, q_ref[...])
    highest = jnp.max(scores, axis=0, keepdims=True)
    raised = jnp.exp(scores - highest)
    total = jnp.sum(raised, axis=0, keepdims=True)
    mixed = mul(v_ref[...], raised.astype(BF16))
    out_ref[...] = (mixed / total).astype(BF16)
    log_ref[...] = highest + jnp.log(total)


def attend(head, queries, keys, values, step=1024):
    count = queries.shape[1]
    step = min(step, count)
    whole = pl.BlockSpec((HEAD_DIM, count), lambda i: (head, 0))
    return pl.pallas_call(
        attend_kernel,
        grid=(count // step,),
        in_specs=[pl.BlockSpec((HEAD_DIM, step), lambda i: (head, i)), whole, whole],
        out_specs=[
            pl.BlockSpec((HEAD_DIM, step), lambda i: (0, i)),
            pl.BlockSpec((1, step), lambda i: (0, i)),
        ],
        out_shape=[
            jax.ShapeDtypeStruct((HEAD_DIM, count), BF16),
            jax.ShapeDtypeStruct((1, count), F32),
        ],
        compiler_params=pltpu.CompilerParams(vmem_limit_bytes=48 * 2**20),
        cost_estimate=pl.CostEstimate(
            flops=28 * count * count * HEAD_DIM,
            bytes_accessed=8 * HEAD_DIM * count,
            transcendentals=count * count,
        ),
        name="attend",
    )(queries, keys, values)


def turn_back(values, cosine, sine):
    first, second = values[:HALF], values[HALF:]
    return jnp.concatenate([first * cosine + second * sine, second * cosine - first * sine], axis=0)


def attend_back_kernel(
    q_ref, kt_ref, vt_ref, u0_ref, u1_ref, u2_ref, u3_ref, out_ref, log_ref, cos_ref, sin_ref, normed_ref,
    grad_ref, weight_ref, up_ref, k_ref, v_ref, dk_ref, dv_ref,
):
    index = pl.program_id(0)
    step = q_ref.shape[1]

    @pl.when(index == 0)
    def _():
        for d, ref in enumerate((u0_ref, u1_ref, u2_ref, u3_ref)):
            up_ref[d] = ref[...]
        k_ref[...] = kt_ref[...].T
        v_ref[...] = vt_ref[...].T
        dk_ref[...] = jnp.zeros_like(dk_ref)
        dv_ref[...] = jnp.zeros_like(dv_ref)

    upstream = up_ref[index]
    inner_sum = jnp.sum(upstream.astype(F32) * out_ref[...].astype(F32), axis=0, keepdims=True)
    chances = jnp.exp(mul(k_ref[...], q_ref[...]) - log_ref[...])
    prob_back = mul(v_ref[...], upstream)
    score_back = (chances * (prob_back - inner_sum)).astype(BF16)
    dv_ref[...] += mul(chances.astype(BF16), upstream, NT)
    dk_ref[...] += mul(score_back, q_ref[...], NT)
    columns = pl.ds(pl.multiple_of(index * step, step), step)
    query_back = mul(kt_ref[...], score_back) * SCALE
    grad_ref[pl.ds(0, HEAD_DIM), columns] = turn_back(
        query_back, cos_ref[:, columns], sin_ref[:, columns]
    ).astype(BF16)

    @pl.when(index == pl.num_programs(0) - 1)
    def _():
        key_back = turn_back(dk_ref[...].T, cos_ref[...], sin_ref[...])
        grad_ref[pl.ds(HEAD_DIM, HEAD_DIM), :] = key_back.astype(BF16)
        grad_ref[pl.ds(2 * HEAD_DIM, HEAD_DIM), :] = dv_ref[...].T.astype(BF16)
        weight_ref[...] = mul(grad_ref[...], normed_ref[...]).astype(BF16)


def attend_back(head, queries, keys, values, upstream, merged, log, cosine, sine, normed):
    count, width = normed.shape
    step = upstream[0].shape[1]
    some = pl.BlockSpec((HEAD_DIM, step), lambda i: (head, i))
    whole = pl.BlockSpec((HEAD_DIM, count), lambda i: (head, 0))
    table = pl.BlockSpec((HALF, count), lambda i: (0, 0))
    return pl.pallas_call(
        attend_back_kernel,
        grid=(count // step,),
        in_specs=[
            some,
            whole,
            whole,
            *[pl.BlockSpec((HEAD_DIM, step), lambda i: (head, 0))] * len(upstream),
            some,
            pl.BlockSpec((1, step), lambda i: (0, i)),
            table,
            table,
            pl.BlockSpec((count, width), lambda i: (0, 0)),
        ],
        out_specs=[
            pl.BlockSpec((3 * HEAD_DIM, count), lambda i: (0, 0)),
            pl.BlockSpec((3 * HEAD_DIM, width), lambda i: (0, 0)),
        ],
        out_shape=[
            jax.ShapeDtypeStruct((3 * HEAD_DIM, count), BF16),
            jax.ShapeDtypeStruct((3 * HEAD_DIM, width), BF16),
        ],
        scratch_shapes=[
            pltpu.VMEM((len(upstream), HEAD_DIM, step), BF16),
            pltpu.VMEM((count, HEAD_DIM), BF16),
            pltpu.VMEM((count, HEAD_DIM), BF16),
            pltpu.VMEM((count, HEAD_DIM), F32),
            pltpu.VMEM((count, HEAD_DIM), F32),
        ],
        compiler_params=pltpu.CompilerParams(vmem_limit_bytes=48 * 2**20),
        cost_estimate=pl.CostEstimate(
            flops=56 * count * count * HEAD_DIM,
            bytes_accessed=16 * HEAD_DIM * count,
            transcendentals=count * count,
        ),
        name="attend_back",
    )(queries, keys, values, *upstream, merged, log, cosine, sine, normed)


def load_rows(place_ref, pairs, buffer, sems):
    z, core = place_ref[0], place_ref[1]
    size, rows, lanes = pairs[0][0].shape
    copies = []
    for d in range(size):
        for n, (mine, other) in enumerate(pairs):
            for k, (ref, side) in enumerate(((mine, core), (other, 1 - core))):
                start = pl.multiple_of(side * rows, 16)
                target = buffer.at[z ^ d, pl.ds(start, rows), pl.ds(n * lanes, lanes)]
                copies.append(pltpu.make_async_copy(ref.at[d], target, sems.at[d, n, k]))
    for copy in copies:
        copy.start()
    for copy in copies:
        copy.wait()


def unit_of(values):
    centre = values - jnp.mean(values, axis=-1, keepdims=True)
    inverse = lax.rsqrt(jnp.mean(centre * centre, axis=-1, keepdims=True) + EPS)
    return centre * inverse, inverse


def turn(values, cosine, sine):
    first, second = values[:HALF], values[HALF:]
    return jnp.concatenate([first * cosine - second * sine, second * cosine + first * sine], axis=0)


def project_kernel(
    place_ref, pair_ref, other_ref, gain_ref, cos_ref, sin_ref, mine_ref, theirs_ref,
    normed_ref, q_ref, kt_ref, vt_ref, buffer, weight, sems,
):
    index = pl.program_id(0)
    part = q_ref.shape[0]
    size = buffer.shape[0]

    @pl.when(index == 0)
    def _():
        load_rows(place_ref, [(mine_ref, theirs_ref)], buffer, sems)
        start = pl.multiple_of(place_ref[1] * 2 * part, 128)
        odd = place_ref[0] & 1 == 1
        for t in range(3):
            both = buffer[:, t * part : (t + 1) * part, pl.ds(start, 2 * part)].reshape(size * part, 2 * part)
            chosen = jnp.where(odd, both[:, part:].astype(F32), both[:, :part].astype(F32))
            weight[:, t * part : (t + 1) * part] = chosen.astype(BF16)

    block = jnp.where(index < 2, pair_ref[...].astype(F32), other_ref[...].astype(F32))
    normed = (unit_of(block)[0] * gain_ref[...]).astype(BF16)
    normed_ref[...] = normed
    projected = mul(normed, weight[...])
    turned = projected[:, : 2 * part].T
    cosine, sine = cos_ref[...], sin_ref[...]
    for head in range(part // HEAD_DIM):
        rows = slice(head * HEAD_DIM, (head + 1) * HEAD_DIM)
        queries = turn(turned[rows], cosine, sine).astype(BF16)
        q_ref[rows, :] = (queries.astype(F32) * SCALE).astype(BF16)
        keys = turn(turned[part + head * HEAD_DIM : part + (head + 1) * HEAD_DIM], cosine, sine)
        kt_ref[rows, :] = keys.astype(BF16)
    vt_ref[...] = projected[:, 2 * part :].astype(BF16).T


def project(where, pair, other, gain, cosine, sine, mine, theirs, count):
    width = pair.shape[1]
    size, rows = mine.shape[0], 2 * mine.shape[1]
    part = width // size
    total = size * count
    anywhere = pl.BlockSpec(memory_space=pl.ANY)
    columns = pl.BlockSpec((part, count), lambda i: (0, i))
    return pl.pallas_call(
        project_kernel,
        grid=(size,),
        in_specs=[
            pl.BlockSpec(memory_space=pltpu.SMEM),
            pl.BlockSpec((count, width), lambda i: (jnp.minimum(i, 1), 0)),
            pl.BlockSpec((count, width), lambda i: (jnp.maximum(i - 2, 0), 0)),
            pl.BlockSpec((1, width), lambda i: (0, 0)),
            pl.BlockSpec((HALF, count), lambda i: (0, i)),
            pl.BlockSpec((HALF, count), lambda i: (0, i)),
            anywhere,
            anywhere,
        ],
        out_specs=[
            pl.BlockSpec((count, width), lambda i: (i, 0)),
            columns,
            columns,
            columns,
        ],
        out_shape=[
            jax.ShapeDtypeStruct((total, width), BF16),
            jax.ShapeDtypeStruct((part, total), BF16),
            jax.ShapeDtypeStruct((part, total), BF16),
            jax.ShapeDtypeStruct((part, total), BF16),
        ],
        scratch_shapes=[
            pltpu.VMEM((size, rows, width), BF16),
            pltpu.VMEM((width, 3 * part), BF16),
            pltpu.SemaphoreType.DMA((size, 1, 2)),
        ],
        compiler_params=pltpu.CompilerParams(vmem_limit_bytes=48 * 2**20),
        cost_estimate=pl.CostEstimate(flops=8 * 10**9, bytes_accessed=20 * 10**6, transcendentals=0),
        name="project",
    )(where, pair, other, gain, cosine, sine, mine, theirs)


def forward_back_kernel(
    place_ref, m0_ref, m1_ref, m2_ref, m3_ref, tokens_ref, up_ref, gain_ref, mine_ref, theirs_ref,
    result_ref, state_back_ref, low_ref, normed_ref, active_ref, inner_back_ref, b0_ref, b1_ref, b2_ref, b3_ref,
    buffer, sems,
):
    part, width = m0_ref.shape[0], tokens_ref.shape[1]
    size = buffer.shape[0]
    hidden = active_ref.shape[1]
    z = place_ref[0]

    @pl.when(pl.program_id(0) == 0)
    def _():
        load_rows(place_ref, [(mine_ref, theirs_ref)], buffer, sems)

    expand = [buffer[:, (1 + t) * part : (2 + t) * part, :].reshape(width, width) for t in range(3)]
    contract = buffer[:, 4 * part : 4 * part + hidden // size, :].reshape(hidden, width)
    gain = gain_ref[...]

    state = tokens_ref[...].astype(F32)
    for k, ref in enumerate((m0_ref, m1_ref, m2_ref, m3_ref)):
        state = state + mul(ref[...], buffer[z ^ k, :part, :], TN)
    unit, inverse = unit_of(state)
    normed = (unit * gain).astype(BF16)
    normed_ref[...] = normed
    inner = jnp.concatenate([mul(normed, weight) for weight in expand], axis=1)
    first, second = inner[:, :hidden], inner[:, hidden:]
    chance = 0.5 + 0.5 * lax.erf(first * math.sqrt(0.5))
    gated = first * chance
    slope = chance + first * (jnp.exp(-0.5 * first * first) * (1.0 / math.sqrt(2.0 * math.pi)))
    active = (gated * second).astype(BF16)
    active_ref[...] = active
    result_ref[...] = (state + mul(active, contract)).astype(BF16)

    upstream = up_ref[...]
    active_back = mul(upstream, contract, NT).astype(BF16).astype(F32)
    inner_back = jnp.concatenate(
        [(active_back * second * slope).astype(BF16), (active_back * gated).astype(BF16)], axis=1
    )
    inner_back_ref[...] = inner_back
    normed_back = mul(inner_back[:, :width], expand[0], NT)
    normed_back = normed_back + mul(inner_back[:, width : 2 * width], expand[1], NT)
    normed_back = normed_back + mul(inner_back[:, 2 * width :], expand[2], NT)
    scaled = normed_back * gain
    mean = jnp.mean(scaled, axis=-1, keepdims=True)
    lean = jnp.mean(scaled * unit, axis=-1, keepdims=True)
    state_back = upstream.astype(F32) + inverse * (scaled - mean - unit * lean)
    state_back_ref[...] = state_back
    low = state_back.astype(BF16)
    low_ref[...] = low
    for k, ref in enumerate((b0_ref, b1_ref, b2_ref, b3_ref)):
        ref[...] = mul(buffer[z ^ k, :part, :], low, NT).astype(BF16)


def forward_back(where, merged, tokens, upstream, gain, sides, hidden, step=256):
    count, width = tokens.shape
    size, rows = sides[0].shape[0], 2 * sides[0].shape[1]
    part = width // size
    anywhere = pl.BlockSpec(memory_space=pl.ANY)
    columns = pl.BlockSpec((part, step), lambda i: (0, i))

    def some(lanes):
        return pl.BlockSpec((step, lanes), lambda i: (i, 0))

    lanes = [width, width, width, width, hidden, 2 * hidden]
    kinds = [BF16, F32, BF16, BF16, BF16, BF16]
    return pl.pallas_call(
        forward_back_kernel,
        grid=(count // step,),
        in_specs=[pl.BlockSpec(memory_space=pltpu.SMEM)]
        + [columns] * size
        + [some(width), some(width), pl.BlockSpec((1, width), lambda i: (0, 0))]
        + [anywhere] * len(sides),
        out_specs=[some(n) for n in lanes] + [columns] * size,
        out_shape=[jax.ShapeDtypeStruct((count, n), kind) for n, kind in zip(lanes, kinds)]
        + [jax.ShapeDtypeStruct((part, count), BF16)] * size,
        scratch_shapes=[pltpu.VMEM((size, rows, width), BF16), pltpu.SemaphoreType.DMA((size, 1, 2))],
        compiler_params=pltpu.CompilerParams(vmem_limit_bytes=56 * 2**20),
        cost_estimate=pl.CostEstimate(flops=14 * 10**9, bytes_accessed=20 * 10**6, transcendentals=0),
        name="forward_back",
    )(where, *merged, tokens, upstream, gain, *sides)


def gradients_kernel(
    place_ref, m0_ref, m1_ref, m2_ref, m3_ref, up_ref, low_ref, normed_ref, active_ref, inner_back_ref,
    kept_ref, sent_ref,
):
    z, core = place_ref[0], place_ref[1]
    part, width = m0_ref.shape[0], up_ref.shape[1]
    size, rows, lanes = kept_ref.shape
    held = active_ref.shape[1] // size
    for grads_ref, side in ((sent_ref, 1 - core), (kept_ref, core)):
        start = pl.multiple_of(side * lanes, 128)
        low = low_ref[:, pl.ds(start, lanes)]
        for k, ref in enumerate((m0_ref, m1_ref, m2_ref, m3_ref)):
            grads_ref[z ^ k, :part, :] = mul(ref[...], low).astype(BF16)
        normed = normed_ref[...]
        for t in range(3):
            grad = mul(normed, inner_back_ref[:, pl.ds(t * width + start, lanes)], TN)
            grads_ref[:, (1 + t) * part : (2 + t) * part, :] = grad.astype(BF16).reshape(size, part, lanes)
        grad = mul(active_ref[...], up_ref[:, pl.ds(start, lanes)], TN)
        grads_ref[:, 4 * part : 4 * part + held, :] = grad.astype(BF16).reshape(size, held, lanes)
        if rows > 4 * part + held:
            grads_ref[:, 4 * part + held :, :] = jnp.zeros((size, rows - 4 * part - held, lanes), BF16)


def gradients(where, merged, upstream, low, normed, active, inner_back, rows):
    size = len(merged)
    inside = pl.BlockSpec(memory_space=pltpu.VMEM)
    return pl.pallas_call(
        gradients_kernel,
        in_specs=[pl.BlockSpec(memory_space=pltpu.SMEM)] + [inside] * (size + 5),
        out_specs=[inside] * 2,
        out_shape=[jax.ShapeDtypeStruct((size, rows, upstream.shape[1] // 2), BF16)] * 2,
        compiler_params=pltpu.CompilerParams(vmem_limit_bytes=60 * 2**20),
        cost_estimate=pl.CostEstimate(flops=12 * 10**9, bytes_accessed=12 * 10**6, transcendentals=0),
        name="gradients",
    )(where, *merged, upstream, low, normed, active, inner_back)


def token_kernel(heads, place_ref, *refs):
    size = len(refs[: -9]) // heads
    pieces = refs[: heads * size]
    mine_ref, theirs_ref, tokens_ref, back_ref, gain_ref, grad_ref, parts, buffer, sems = refs[heads * size :]
    z = place_ref[0]
    width = buffer.shape[2]
    part = width // size
    load_rows(place_ref, [(mine_ref, theirs_ref)], buffer, sems)
    for head in range(heads):
        for k in range(size):
            ref = pieces[head * size + k]
            lines = pl.ds(pl.multiple_of((z ^ k) * part + head * HEAD_DIM, HEAD_DIM), HEAD_DIM)
            for t in range(3):
                parts[t, lines, :] = ref[t * HEAD_DIM : (t + 1) * HEAD_DIM, :]
    total = jnp.zeros((width, tokens_ref.shape[0]), F32)
    for t in range(3):
        total = total + mul(buffer[:, t * part : (t + 1) * part, :].reshape(width, width), parts[t])
    unit, inverse = unit_of(tokens_ref[...].astype(F32))
    scaled = total.T * gain_ref[...]
    mean = jnp.mean(scaled, axis=-1, keepdims=True)
    lean = jnp.mean(scaled * unit, axis=-1, keepdims=True)
    grad_ref[...] = back_ref[...] + inverse * (scaled - mean - unit * lean)


def token_back(where, received, mine, theirs, tokens, state_back, gain):
    count, width = tokens.shape
    size, rows = mine.shape[0], 2 * mine.shape[1]
    inside = pl.BlockSpec(memory_space=pltpu.VMEM)
    anywhere = pl.BlockSpec(memory_space=pl.ANY)
    pieces = [piece for rounds in received for piece in rounds]
    return pl.pallas_call(
        functools.partial(token_kernel, len(received)),
        in_specs=[pl.BlockSpec(memory_space=pltpu.SMEM)]
        + [inside] * len(pieces)
        + [anywhere] * 2
        + [inside] * 3,
        out_specs=inside,
        out_shape=jax.ShapeDtypeStruct((count, width), F32),
        scratch_shapes=[
            pltpu.VMEM((3, width, count), BF16),
            pltpu.VMEM((size, rows, width), BF16),
            pltpu.SemaphoreType.DMA((size, 1, 2)),
        ],
        compiler_params=pltpu.CompilerParams(vmem_limit_bytes=48 * 2**20),
        cost_estimate=pl.CostEstimate(flops=5 * 10**9, bytes_accessed=12 * 10**6, transcendentals=0),
        name="token_back",
    )(where, *pieces, mine, theirs, tokens, state_back, gain)


def after(values, *others):
    return lax.optimization_barrier((values, others))[0]


def swap(values, axis, size, offset):
    return lax.ppermute(values, axis, [(i, i ^ offset) for i in range(size)])


def exchange(pieces, size):
    return [pieces[0]] + [swap(pieces[d], "fsdp", size, d) for d in range(1, size)]


def column(values, size, ranks, pairs):
    full = [
        (z * ranks + r, to * ranks + (r & ~1) + core)
        for z in range(size)
        for r in range(ranks)
        for to, core in pairs(z, r & 1)
    ]
    return lax.ppermute(values, ("fsdp", "rep"), full)


def collect(own, home, size, ranks, early):
    first = column(
        own, size, ranks, lambda z, c: [(z ^ 1, c) if c == z >> 1 else (z ^ 2, 1 - c)]
    )
    second = column(first, size, ranks, lambda z, c: [] if c == z >> 1 else [(z ^ 1, c)])
    low = jnp.where(home, own, first)
    high = jnp.where(home, first, second)
    pair, early = after((jnp.concatenate([low, high], axis=0), early))
    other = swap(pair, "rep", ranks, 1)
    return pair, other, first, second, early


def trade_out(pieces, size, ranks, rounds=None):
    def round_of(k):
        return lambda z, c: [((2 * c + (z & 1)) ^ k, z >> 1)]

    return [column(pieces[k], size, ranks, round_of(k)) for k in rounds or range(size)]


def trade_back(pieces, size, ranks):
    def round_of(k):
        return lambda z, c: [(2 * c + ((z ^ k) & 1), (z ^ k) >> 1)]

    return [column(pieces[k], size, ranks, round_of(k)) for k in range(size)]


def pick(blocks, index):
    return lax.dynamic_index_in_dim(blocks, index, 0, keepdims=False)


def reorder(blocks, z, size):
    return jnp.stack([pick(blocks, z ^ j) for j in range(size)])


def far(ranks):
    bits = []
    bit = 2
    while bit < ranks:
        bits.append(bit)
        bit *= 2
    return bits


def stage_bit(core, ranks, stage):
    bits = far(ranks)
    return bits[stage] if core == 0 else bits[len(bits) - 1 - stage]


def stage_swap(values, ranks, stage):
    return lax.ppermute(values, "rep", [(i, i ^ stage_bit(i & 1, ranks, stage)) for i in range(ranks)])


def stage_upper(r, ranks, stage):
    bit = jnp.where(r & 1 == 0, stage_bit(0, ranks, stage), stage_bit(1, ranks, stage))
    return r & bit != 0


def place(r, ranks):
    stages = len(far(ranks))
    total = jnp.where(r & 1 != 0, 1 << stages, 0)
    for stage in range(stages):
        total = total + jnp.where(stage_upper(r, ranks, stage), 1 << stage, 0)
    return total


def join(mine, other, upper):
    return jnp.concatenate([jnp.where(upper, other, mine), jnp.where(upper, mine, other)], axis=1)


def cut(values, upper):
    half = values.shape[1] // 2
    mine = jnp.where(upper, half, 0)
    sent = lax.dynamic_slice_in_dim(values, half - mine, half, 1)
    return sent, lax.dynamic_slice_in_dim(values, mine, half, 1)


def add(one, two):
    return (one.astype(F32) + two.astype(F32)).astype(BF16)


def grow(values, r, ranks, stages):
    for stage in stages:
        values = join(values, stage_swap(values, ranks, stage), stage_upper(r, ranks, stage))
    return values


def grow_flat(values, r, ranks, stages):
    for stage in stages:
        other = stage_swap(values, ranks, stage)
        upper = stage_upper(r, ranks, stage)
        values = jnp.concatenate(
            [jnp.where(upper, other, values), jnp.where(upper, values, other)], axis=0
        )
    return values


def shrink(values, r, ranks, stages):
    for stage in stages:
        sent, kept = cut(values, stage_upper(r, ranks, stage))
        values = add(kept, stage_swap(sent, ranks, stage))
    return values


def halves(values):
    middle = values.shape[-1] // 2
    return [values[..., :middle], values[..., middle:]]


def split_rows(shard, r, ranks):
    rows = shard.shape[0] // ranks
    return lax.dynamic_slice_in_dim(shard, place(r, ranks) * rows, rows, 0)


def finish_kernel(
    place_ref, mine_ref, other_ref, into_ref, expand_ref, gain_a_ref, gain_b_ref,
    into_sum_ref, gain_a_sum_ref, out_sum_ref, expand_sum_ref, gain_b_sum_ref, contract_sum_ref,
):
    first = place_ref[1] == 0
    part, width = out_sum_ref.shape
    held = contract_sum_ref.shape[0]
    pieces = mine_ref.shape[0]
    lines = 3 * part // pieces

    def gathered(start):
        rows = mine_ref.shape[1] if start else lines
        sides = []
        for one, two in ((mine_ref, other_ref), (other_ref, mine_ref)):
            blocks = [
                jnp.where(first, one[p, start:rows].astype(F32), two[p, start:rows].astype(F32))
                for p in range(pieces)
            ]
            sides.append(jnp.concatenate(blocks, axis=0))
        return sides

    blocks = [side[:, k * part : (k + 1) * part].T for side in gathered(0) for k in range(2)]
    total = jnp.zeros((part, 1), F32)
    for t in range(3):
        row = jnp.concatenate([block[:, t * part : (t + 1) * part] for block in blocks], axis=1)
        into_sum_ref[:, t * width : (t + 1) * width] = row
        weight = into_ref[:, t * width : (t + 1) * width].astype(F32)
        total = total + jnp.sum(row * weight, axis=1, keepdims=True)
    gain_a_sum_ref[...] = total.T / gain_a_ref[...].astype(F32)

    grads = jnp.concatenate(gathered(lines), axis=1)
    out_sum_ref[...] = grads[:part]
    total = jnp.zeros((part, 1), F32)
    for t in range(3):
        row = grads[(1 + t) * part : (2 + t) * part]
        expand_sum_ref[:, t * width : (t + 1) * width] = row
        weight = expand_ref[:, t * width : (t + 1) * width].astype(F32)
        total = total + jnp.sum(row * weight, axis=1, keepdims=True)
    gain_b_sum_ref[...] = total.T / gain_b_ref[...].astype(F32)
    contract_sum_ref[...] = grads[4 * part : 4 * part + held]


def finish(where, mine, other, projection_in, expansion, gain_a, gain_b, held):
    part, wide = projection_in.shape
    inside = pl.BlockSpec(memory_space=pltpu.VMEM)
    shapes = [(part, wide), (1, part), (part, wide // 3), (part, wide), (1, part), (held, wide // 3)]
    return pl.pallas_call(
        finish_kernel,
        in_specs=[pl.BlockSpec(memory_space=pltpu.SMEM)] + [inside] * 6,
        out_specs=[inside] * 6,
        out_shape=[jax.ShapeDtypeStruct(shape, F32) for shape in shapes],
        compiler_params=pltpu.CompilerParams(vmem_limit_bytes=48 * 2**20),
        name="finish",
    )(where, mine, other, projection_in, expansion, gain_a[None], gain_b[None])


def local(size, ranks, tokens, gain_a, projection_in, attention_out, gain_b, expansion, contraction, cotangent):
    z = lax.axis_index("fsdp")
    r = lax.axis_index("rep")
    core = r & 1
    group = 2 * core + (z & 1)
    home = core == z >> 1
    own = tokens[0]
    count, width = own.shape
    part = width // size
    hidden = contraction.shape[0]
    heads = HEADS // size

    stages = list(range(len(far(ranks))))
    where = jnp.stack([z, core]).astype(jnp.int32)
    columns = [projection_in[:, t * width : (t + 1) * width] for t in range(3)]
    piece = split_rows(jnp.concatenate(columns, axis=0), r, ranks)
    rows = piece.shape[0]
    gains = jnp.pad(jnp.concatenate([gain_a, gain_b])[None], ((0, 7), (0, width - 2 * part)))
    pieces = jnp.stack(exchange([jnp.concatenate([piece, gains], axis=0)] * size, size))
    gains = reorder(pieces[:, rows, : 2 * part], z, size).astype(F32)
    gain_one = gains[:, :part].reshape(1, width)
    gain_two = gains[:, part:].reshape(1, width)
    freqs = THETA ** (-(jnp.arange(HALF, dtype=F32) * (2.0 / HEAD_DIM)))
    places = jnp.concatenate([(group ^ d) * count + jnp.arange(count, dtype=jnp.int32) for d in range(size)])
    angles = freqs[:, None] * places.astype(F32)[None, :]
    early = (gain_one, gain_two, jnp.cos(angles), jnp.sin(angles))
    pair, other, first, second, early = collect(own, home, size, ranks, early)
    gain_one, gain_two, cosine, sine = early
    into = grow(pieces[:, :rows], r, ranks, stages[:-1])
    into = grow(after(into, first), r, ranks, stages[-1:])
    into_other = swap(into, "rep", ranks, 1)
    normed, queries, keys, values = project(
        where, pair, other, gain_one, cosine, sine, into, into_other, count
    )

    columns = [expansion[:, t * width : (t + 1) * width] for t in range(3)]
    stacked = jnp.concatenate([attention_out] + columns + [contraction], axis=0)
    pad = -stacked.shape[0] % max(32, 8 * ranks)
    stacked = jnp.concatenate([stacked, jnp.zeros((pad, width), BF16)], axis=0)
    rest = exchange([split_rows(after(stacked, second), r, ranks)] * size, size)
    merged = []
    logs = []
    for head in range(heads):
        out, log = attend(head, queries, after(keys, *merged[-1:]), values)
        merged.append(out)
        logs.append(log)
    rest = jnp.stack(after(rest, merged[0]))
    for stage in stages[:-1]:
        rest = join(rest, after(stage_swap(rest, ranks, stage), merged[-1]), stage_upper(r, ranks, stage))
    own_merged = jnp.concatenate(merged, axis=0)
    merged = trade_out([own_merged[:, d * count : (d + 1) * count] for d in range(size)], size, ranks)
    coming = after(stage_swap(rest, ranks, stages[-1]), *merged)
    rest = join(rest, coming, stage_upper(r, ranks, stages[-1]))
    rest_other = swap(rest, "rep", ranks, 1)
    upstream = cotangent[0]
    block_output, state_back, state_low, normed_two, active, inner_back, *merged_back = forward_back(
        where, merged, own, upstream, gain_two, [rest, rest_other], size * hidden
    )
    arrived = trade_back(merged_back, size, ranks)
    own_upstream = arrived

    kept, sent = gradients(
        where, merged, upstream, state_low, normed_two, active, inner_back, stacked.shape[0]
    )
    sent = after(sent, *arrived)
    grads = add(kept, swap(sent, "rep", ranks, 1))

    turned_backs = []
    weight_backs = []
    received = []
    ahead = [grads]
    for head in range(heads):
        grad, weight_grad = attend_back(
            head, queries, keys, values, after(own_upstream, *ahead), own_merged, logs[head],
            cosine, sine, normed,
        )
        turned_backs.append(grad)
        weight_backs.append(weight_grad.reshape(3, HEAD_DIM, width))
        received.append(trade_out([grad[:, d * count : (d + 1) * count] for d in range(size)], size, ranks))
        if head == 0:
            grads = shrink(grads, r, ranks, stages[:0:-1])
            ahead = [grads]
        if head == 1:
            grads = shrink(grads, r, ranks, stages[:1])
            ahead = [grads] + received[0]

    pair = z & 2
    sent, kept = [lax.dynamic_slice_in_dim(grads, start, 2, 0) for start in (pair ^ 2, pair)]
    grads = add(kept, swap(sent, "fsdp", size, 2))
    weight_backs[2], grads = after((weight_backs[2], grads), turned_backs[2], *received[1][:2])
    into_grad = jnp.concatenate([grad[t] for t in range(3) for grad in weight_backs], axis=0)
    later, last = received[1:]
    into_grad = after(shrink(into_grad[None], r, ranks, stages[-1:]), later[2], last[0])
    into_grad = after(shrink(into_grad, r, ranks, stages[-2::-1]), later[3], last[1])[0]
    grads = add(pick(grads, z & 1), swap(pick(grads, z & 1 ^ 1), "fsdp", size, 1))
    lines = into_grad.shape[0]
    blocks = into_grad.reshape(lines, size, part).transpose(1, 0, 2)
    blocks = exchange([pick(blocks, z ^ d) for d in range(size)], size)
    even, odd = (blocks[0].astype(F32) + blocks[2].astype(F32)), (blocks[1].astype(F32) + blocks[3].astype(F32))
    low = z & 1 == 0
    flat = jnp.concatenate([jnp.where(low, even, odd), jnp.where(low, odd, even)], axis=1).astype(BF16)
    flat = after(flat, last[2])
    both = grow_flat(jnp.concatenate([flat, grads], axis=0)[None], r, ranks, stages[:-1])
    both = grow_flat(after(both, last[3]), r, ranks, stages[-1:])
    token_grad = token_back(where, received, into, into_other, own, state_back, gain_one)[None]
    both = after(both, token_grad)
    into_sum, gain_one_sum, attention_out_sum, expansion_sum, gain_two_sum, contraction_sum = finish(
        where, both, swap(both, "rep", ranks, 1), projection_in, expansion, gain_a, gain_b, hidden
    )
    return (
        block_output[None],
        token_grad,
        gain_one_sum[0],
        into_sum,
        attention_out_sum,
        gain_two_sum[0],
        expansion_sum,
        contraction_sum,
    )


def solution(mesh):
    tokens, rows, line = P("rep", "fsdp", None), P("fsdp", None), P("fsdp")
    in_specs = (tokens, line, rows, rows, line, rows, rows, tokens)
    out_specs = (tokens, tokens, line, rows, rows, line, rows, rows)
    body = functools.partial(local, mesh.shape["fsdp"], mesh.shape["rep"])
    return jax.shard_map(body, mesh=mesh, in_specs=in_specs, out_specs=out_specs, check_vma=False)
```

```python
import functools
import math

import jax
import jax.numpy as jnp
from jax import lax
from jax.experimental import pallas as pl
from jax.experimental.pallas import tpu as pltpu
from jax.sharding import PartitionSpec as P

HEADS = 12
HEAD_DIM = 64
HALF = HEAD_DIM // 2
SCALE = 1.0 / math.sqrt(HEAD_DIM)
EPS = 1e-05
THETA = 160000.0
F32 = jnp.float32
BF16 = jnp.bfloat16
NN = (((1,), (0,)), ((), ()))
NT = (((1,), (1,)), ((), ()))
TN = (((0,), (0,)), ((), ()))
TT = (((0,), (1,)), ((), ()))


def mul(a, b, dims=NN):
    return lax.dot_general(a, b, dims, preferred_element_type=F32)


def attend_kernel(q_ref, k_ref, v_ref, out_ref, log_ref):
    scores = mul(k_ref[...].T, q_ref[...])
    highest = jnp.max(scores, axis=0, keepdims=True)
    raised = jnp.exp(scores - highest)
    total = jnp.sum(raised, axis=0, keepdims=True)
    mixed = mul(v_ref[...], raised.astype(BF16))
    out_ref[...] = (mixed / total).astype(BF16)
    log_ref[...] = highest + jnp.log(total)


def attend(head, queries, keys, values, step=1024):
    count = queries.shape[1]
    step = min(step, count)
    whole = pl.BlockSpec((HEAD_DIM, count), lambda i: (head, 0))
    return pl.pallas_call(
        attend_kernel,
        grid=(count // step,),
        in_specs=[pl.BlockSpec((HEAD_DIM, step), lambda i: (head, i)), whole, whole],
        out_specs=[
            pl.BlockSpec((HEAD_DIM, step), lambda i: (0, i)),
            pl.BlockSpec((1, step), lambda i: (0, i)),
        ],
        out_shape=[
            jax.ShapeDtypeStruct((HEAD_DIM, count), BF16),
            jax.ShapeDtypeStruct((1, count), F32),
        ],
        compiler_params=pltpu.CompilerParams(vmem_limit_bytes=48 * 2**20),
        cost_estimate=pl.CostEstimate(
            flops=28 * count * count * HEAD_DIM,
            bytes_accessed=8 * HEAD_DIM * count,
            transcendentals=count * count,
        ),
        name="attend",
    )(queries, keys, values)


def turn_back(values, cosine, sine):
    first, second = values[:HALF], values[HALF:]
    return jnp.concatenate([first * cosine + second * sine, second * cosine - first * sine], axis=0)


def attend_back_kernel(
    q_ref, kt_ref, vt_ref, u0_ref, u1_ref, u2_ref, u3_ref, out_ref, log_ref, cos_ref, sin_ref, normed_ref,
    grad_ref, weight_ref, up_ref, k_ref, v_ref, dk_ref, dv_ref,
):
    index = pl.program_id(0)
    step = q_ref.shape[1]

    @pl.when(index == 0)
    def _():
        for d, ref in enumerate((u0_ref, u1_ref, u2_ref, u3_ref)):
            up_ref[d] = ref[...]
        k_ref[...] = kt_ref[...].T
        v_ref[...] = vt_ref[...].T
        dk_ref[...] = jnp.zeros_like(dk_ref)
        dv_ref[...] = jnp.zeros_like(dv_ref)

    upstream = up_ref[index]
    inner_sum = jnp.sum(upstream.astype(F32) * out_ref[...].astype(F32), axis=0, keepdims=True)
    chances = jnp.exp(mul(k_ref[...], q_ref[...]) - log_ref[...])
    prob_back = mul(v_ref[...], upstream)
    score_back = (chances * (prob_back - inner_sum)).astype(BF16)
    dv_ref[...] += mul(chances.astype(BF16), upstream, NT)
    dk_ref[...] += mul(score_back, q_ref[...], NT)
    columns = pl.ds(pl.multiple_of(index * step, step), step)
    query_back = mul(kt_ref[...], score_back) * SCALE
    grad_ref[pl.ds(0, HEAD_DIM), columns] = turn_back(
        query_back, cos_ref[:, columns], sin_ref[:, columns]
    ).astype(BF16)

    @pl.when(index == pl.num_programs(0) - 1)
    def _():
        key_back = turn_back(dk_ref[...].T, cos_ref[...], sin_ref[...])
        grad_ref[pl.ds(HEAD_DIM, HEAD_DIM), :] = key_back.astype(BF16)
        grad_ref[pl.ds(2 * HEAD_DIM, HEAD_DIM), :] = dv_ref[...].T.astype(BF16)
        weight_ref[...] = mul(grad_ref[...], normed_ref[...]).astype(BF16)


def attend_back(head, queries, keys, values, upstream, merged, log, cosine, sine, normed):
    count, width = normed.shape
    step = upstream[0].shape[1]
    some = pl.BlockSpec((HEAD_DIM, step), lambda i: (head, i))
    whole = pl.BlockSpec((HEAD_DIM, count), lambda i: (head, 0))
    table = pl.BlockSpec((HALF, count), lambda i: (0, 0))
    return pl.pallas_call(
        attend_back_kernel,
        grid=(count // step,),
        in_specs=[
            some,
            whole,
            whole,
            *[pl.BlockSpec((HEAD_DIM, step), lambda i: (head, 0))] * len(upstream),
            some,
            pl.BlockSpec((1, step), lambda i: (0, i)),
            table,
            table,
            pl.BlockSpec((count, width), lambda i: (0, 0)),
        ],
        out_specs=[
            pl.BlockSpec((3 * HEAD_DIM, count), lambda i: (0, 0)),
            pl.BlockSpec((3 * HEAD_DIM, width), lambda i: (0, 0)),
        ],
        out_shape=[
            jax.ShapeDtypeStruct((3 * HEAD_DIM, count), BF16),
            jax.ShapeDtypeStruct((3 * HEAD_DIM, width), BF16),
        ],
        scratch_shapes=[
            pltpu.VMEM((len(upstream), HEAD_DIM, step), BF16),
            pltpu.VMEM((count, HEAD_DIM), BF16),
            pltpu.VMEM((count, HEAD_DIM), BF16),
            pltpu.VMEM((count, HEAD_DIM), F32),
            pltpu.VMEM((count, HEAD_DIM), F32),
        ],
        compiler_params=pltpu.CompilerParams(vmem_limit_bytes=48 * 2**20),
        cost_estimate=pl.CostEstimate(
            flops=56 * count * count * HEAD_DIM,
            bytes_accessed=16 * HEAD_DIM * count,
            transcendentals=count * count,
        ),
        name="attend_back",
    )(queries, keys, values, *upstream, merged, log, cosine, sine, normed)


def load_rows(place_ref, pairs, buffer, sems):
    z, core = place_ref[0], place_ref[1]
    size, rows, lanes = pairs[0][0].shape
    copies = []
    for d in range(size):
        for n, (mine, other) in enumerate(pairs):
            for k, (ref, side) in enumerate(((mine, core), (other, 1 - core))):
                start = pl.multiple_of(side * rows, 16)
                target = buffer.at[z ^ d, pl.ds(start, rows), pl.ds(n * lanes, lanes)]
                copies.append(pltpu.make_async_copy(ref.at[d], target, sems.at[d, n, k]))
    for copy in copies:
        copy.start()
    for copy in copies:
        copy.wait()


def unit_of(values):
    centre = values - jnp.mean(values, axis=-1, keepdims=True)
    inverse = lax.rsqrt(jnp.mean(centre * centre, axis=-1, keepdims=True) + EPS)
    return centre * inverse, inverse


def turn(values, cosine, sine):
    first, second = values[:HALF], values[HALF:]
    return jnp.concatenate([first * cosine - second * sine, second * cosine + first * sine], axis=0)


def project_kernel(
    place_ref, pair_ref, other_ref, gain_ref, cos_ref, sin_ref, mine_ref, theirs_ref,
    normed_ref, q_ref, kt_ref, vt_ref, buffer, weight, sems,
):
    index = pl.program_id(0)
    part = q_ref.shape[0]
    size = buffer.shape[0]

    @pl.when(index == 0)
    def _():
        load_rows(place_ref, [(mine_ref, theirs_ref)], buffer, sems)
        start = pl.multiple_of(place_ref[1] * 2 * part, 128)
        odd = place_ref[0] & 1 == 1
        for t in range(3):
            both = buffer[:, t * part : (t + 1) * part, pl.ds(start, 2 * part)].reshape(size * part, 2 * part)
            chosen = jnp.where(odd, both[:, part:].astype(F32), both[:, :part].astype(F32))
            weight[:, t * part : (t + 1) * part] = chosen.astype(BF16)

    block = jnp.where(index < 2, pair_ref[...].astype(F32), other_ref[...].astype(F32))
    normed = (unit_of(block)[0] * gain_ref[...]).astype(BF16)
    normed_ref[...] = normed
    projected = mul(normed, weight[...])
    turned = projected[:, : 2 * part].T
    cosine, sine = cos_ref[...], sin_ref[...]
    for head in range(part // HEAD_DIM):
        rows = slice(head * HEAD_DIM, (head + 1) * HEAD_DIM)
        queries = turn(turned[rows], cosine, sine).astype(BF16)
        q_ref[rows, :] = (queries.astype(F32) * SCALE).astype(BF16)
        keys = turn(turned[part + head * HEAD_DIM : part + (head + 1) * HEAD_DIM], cosine, sine)
        kt_ref[rows, :] = keys.astype(BF16)
    vt_ref[...] = projected[:, 2 * part :].astype(BF16).T


def project(where, pair, other, gain, cosine, sine, mine, theirs, count):
    width = pair.shape[1]
    size, rows = mine.shape[0], 2 * mine.shape[1]
    part = width // size
    total = size * count
    anywhere = pl.BlockSpec(memory_space=pl.ANY)
    columns = pl.BlockSpec((part, count), lambda i: (0, i))
    return pl.pallas_call(
        project_kernel,
        grid=(size,),
        in_specs=[
            pl.BlockSpec(memory_space=pltpu.SMEM),
            pl.BlockSpec((count, width), lambda i: (jnp.minimum(i, 1), 0)),
            pl.BlockSpec((count, width), lambda i: (jnp.maximum(i - 2, 0), 0)),
            pl.BlockSpec((1, width), lambda i: (0, 0)),
            pl.BlockSpec((HALF, count), lambda i: (0, i)),
            pl.BlockSpec((HALF, count), lambda i: (0, i)),
            anywhere,
            anywhere,
        ],
        out_specs=[
            pl.BlockSpec((count, width), lambda i: (i, 0)),
            columns,
            columns,
            columns,
        ],
        out_shape=[
            jax.ShapeDtypeStruct((total, width), BF16),
            jax.ShapeDtypeStruct((part, total), BF16),
            jax.ShapeDtypeStruct((part, total), BF16),
            jax.ShapeDtypeStruct((part, total), BF16),
        ],
        scratch_shapes=[
            pltpu.VMEM((size, rows, width), BF16),
            pltpu.VMEM((width, 3 * part), BF16),
            pltpu.SemaphoreType.DMA((size, 1, 2)),
        ],
        compiler_params=pltpu.CompilerParams(vmem_limit_bytes=48 * 2**20),
        cost_estimate=pl.CostEstimate(flops=8 * 10**9, bytes_accessed=20 * 10**6, transcendentals=0),
        name="project",
    )(where, pair, other, gain, cosine, sine, mine, theirs)


def forward_back_kernel(
    place_ref, m0_ref, m1_ref, m2_ref, m3_ref, tokens_ref, up_ref, gain_ref, mine_ref, theirs_ref,
    result_ref, state_back_ref, low_ref, normed_ref, active_ref, inner_back_ref, b0_ref, b1_ref, b2_ref, b3_ref,
    buffer, sems,
):
    part, width = m0_ref.shape[0], tokens_ref.shape[1]
    size = buffer.shape[0]
    hidden = active_ref.shape[1]
    z = place_ref[0]

    @pl.when(pl.program_id(0) == 0)
    def _():
        load_rows(place_ref, [(mine_ref, theirs_ref)], buffer, sems)

    expand = [buffer[:, (1 + t) * part : (2 + t) * part, :].reshape(width, width) for t in range(3)]
    contract = buffer[:, 4 * part : 4 * part + hidden // size, :].reshape(hidden, width)
    gain = gain_ref[...]

    state = tokens_ref[...].astype(F32)
    for k, ref in enumerate((m0_ref, m1_ref, m2_ref, m3_ref)):
        state = state + mul(ref[...], buffer[z ^ k, :part, :], TN)
    unit, inverse = unit_of(state)
    normed = (unit * gain).astype(BF16)
    normed_ref[...] = normed
    inner = jnp.concatenate([mul(normed, weight) for weight in expand], axis=1)
    first, second = inner[:, :hidden], inner[:, hidden:]
    chance = 0.5 + 0.5 * lax.erf(first * math.sqrt(0.5))
    gated = first * chance
    slope = chance + first * (jnp.exp(-0.5 * first * first) * (1.0 / math.sqrt(2.0 * math.pi)))
    active = (gated * second).astype(BF16)
    active_ref[...] = active
    result_ref[...] = (state + mul(active, contract)).astype(BF16)

    upstream = up_ref[...]
    active_back = mul(upstream, contract, NT).astype(BF16).astype(F32)
    inner_back = jnp.concatenate(
        [(active_back * second * slope).astype(BF16), (active_back * gated).astype(BF16)], axis=1
    )
    inner_back_ref[...] = inner_back
    normed_back = mul(inner_back[:, :width], expand[0], NT)
    normed_back = normed_back + mul(inner_back[:, width : 2 * width], expand[1], NT)
    normed_back = normed_back + mul(inner_back[:, 2 * width :], expand[2], NT)
    scaled = normed_back * gain
    mean = jnp.mean(scaled, axis=-1, keepdims=True)
    lean = jnp.mean(scaled * unit, axis=-1, keepdims=True)
    state_back = upstream.astype(F32) + inverse * (scaled - mean - unit * lean)
    state_back_ref[...] = state_back
    low = state_back.astype(BF16)
    low_ref[...] = low
    for k, ref in enumerate((b0_ref, b1_ref, b2_ref, b3_ref)):
        ref[...] = mul(buffer[z ^ k, :part, :], low, NT).astype(BF16)


def forward_back(where, merged, tokens, upstream, gain, sides, hidden, step=256):
    count, width = tokens.shape
    size, rows = sides[0].shape[0], 2 * sides[0].shape[1]
    part = width // size
    anywhere = pl.BlockSpec(memory_space=pl.ANY)
    columns = pl.BlockSpec((part, step), lambda i: (0, i))

    def some(lanes):
        return pl.BlockSpec((step, lanes), lambda i: (i, 0))

    lanes = [width, width, width, width, hidden, 2 * hidden]
    kinds = [BF16, F32, BF16, BF16, BF16, BF16]
    return pl.pallas_call(
        forward_back_kernel,
        grid=(count // step,),
        in_specs=[pl.BlockSpec(memory_space=pltpu.SMEM)]
        + [columns] * size
        + [some(width), some(width), pl.BlockSpec((1, width), lambda i: (0, 0))]
        + [anywhere] * len(sides),
        out_specs=[some(n) for n in lanes] + [columns] * size,
        out_shape=[jax.ShapeDtypeStruct((count, n), kind) for n, kind in zip(lanes, kinds)]
        + [jax.ShapeDtypeStruct((part, count), BF16)] * size,
        scratch_shapes=[pltpu.VMEM((size, rows, width), BF16), pltpu.SemaphoreType.DMA((size, 1, 2))],
        compiler_params=pltpu.CompilerParams(vmem_limit_bytes=56 * 2**20),
        cost_estimate=pl.CostEstimate(flops=14 * 10**9, bytes_accessed=20 * 10**6, transcendentals=0),
        name="forward_back",
    )(where, *merged, tokens, upstream, gain, *sides)


def gradients_kernel(
    place_ref, m0_ref, m1_ref, m2_ref, m3_ref, up_ref, low_ref, normed_ref, active_ref, inner_back_ref,
    kept_ref, sent_ref,
):
    z, core = place_ref[0], place_ref[1]
    part, width = m0_ref.shape[0], up_ref.shape[1]
    size, rows, lanes = kept_ref.shape
    held = active_ref.shape[1] // size
    for grads_ref, side in ((sent_ref, 1 - core), (kept_ref, core)):
        start = pl.multiple_of(side * lanes, 128)
        low = low_ref[:, pl.ds(start, lanes)]
        for k, ref in enumerate((m0_ref, m1_ref, m2_ref, m3_ref)):
            grads_ref[z ^ k, :part, :] = mul(ref[...], low).astype(BF16)
        normed = normed_ref[...]
        for t in range(3):
            grad = mul(normed, inner_back_ref[:, pl.ds(t * width + start, lanes)], TN)
            grads_ref[:, (1 + t) * part : (2 + t) * part, :] = grad.astype(BF16).reshape(size, part, lanes)
        grad = mul(active_ref[...], up_ref[:, pl.ds(start, lanes)], TN)
        grads_ref[:, 4 * part : 4 * part + held, :] = grad.astype(BF16).reshape(size, held, lanes)
        if rows > 4 * part + held:
            grads_ref[:, 4 * part + held :, :] = jnp.zeros((size, rows - 4 * part - held, lanes), BF16)


def gradients(where, merged, upstream, low, normed, active, inner_back, rows):
    size = len(merged)
    inside = pl.BlockSpec(memory_space=pltpu.VMEM)
    return pl.pallas_call(
        gradients_kernel,
        in_specs=[pl.BlockSpec(memory_space=pltpu.SMEM)] + [inside] * (size + 5),
        out_specs=[inside] * 2,
        out_shape=[jax.ShapeDtypeStruct((size, rows, upstream.shape[1] // 2), BF16)] * 2,
        compiler_params=pltpu.CompilerParams(vmem_limit_bytes=60 * 2**20),
        cost_estimate=pl.CostEstimate(flops=12 * 10**9, bytes_accessed=12 * 10**6, transcendentals=0),
        name="gradients",
    )(where, *merged, upstream, low, normed, active, inner_back)


def token_kernel(heads, place_ref, *refs):
    size = len(refs[: -9]) // heads
    pieces = refs[: heads * size]
    mine_ref, theirs_ref, tokens_ref, back_ref, gain_ref, grad_ref, parts, buffer, sems = refs[heads * size :]
    z = place_ref[0]
    width = buffer.shape[2]
    part = width // size
    load_rows(place_ref, [(mine_ref, theirs_ref)], buffer, sems)
    for head in range(heads):
        for k in range(size):
            ref = pieces[head * size + k]
            lines = pl.ds(pl.multiple_of((z ^ k) * part + head * HEAD_DIM, HEAD_DIM), HEAD_DIM)
            for t in range(3):
                parts[t, lines, :] = ref[t * HEAD_DIM : (t + 1) * HEAD_DIM, :]
    total = jnp.zeros((width, tokens_ref.shape[0]), F32)
    for t in range(3):
        total = total + mul(buffer[:, t * part : (t + 1) * part, :].reshape(width, width), parts[t])
    unit, inverse = unit_of(tokens_ref[...].astype(F32))
    scaled = total.T * gain_ref[...]
    mean = jnp.mean(scaled, axis=-1, keepdims=True)
    lean = jnp.mean(scaled * unit, axis=-1, keepdims=True)
    grad_ref[...] = back_ref[...] + inverse * (scaled - mean - unit * lean)


def token_back(where, received, mine, theirs, tokens, state_back, gain):
    count, width = tokens.shape
    size, rows = mine.shape[0], 2 * mine.shape[1]
    inside = pl.BlockSpec(memory_space=pltpu.VMEM)
    anywhere = pl.BlockSpec(memory_space=pl.ANY)
    pieces = [piece for rounds in received for piece in rounds]
    return pl.pallas_call(
        functools.partial(token_kernel, len(received)),
        in_specs=[pl.BlockSpec(memory_space=pltpu.SMEM)]
        + [inside] * len(pieces)
        + [anywhere] * 2
        + [inside] * 3,
        out_specs=inside,
        out_shape=jax.ShapeDtypeStruct((count, width), F32),
        scratch_shapes=[
            pltpu.VMEM((3, width, count), BF16),
            pltpu.VMEM((size, rows, width), BF16),
            pltpu.SemaphoreType.DMA((size, 1, 2)),
        ],
        compiler_params=pltpu.CompilerParams(vmem_limit_bytes=48 * 2**20),
        cost_estimate=pl.CostEstimate(flops=5 * 10**9, bytes_accessed=12 * 10**6, transcendentals=0),
        name="token_back",
    )(where, *pieces, mine, theirs, tokens, state_back, gain)


def after(values, *others):
    return lax.optimization_barrier((values, others))[0]


def swap(values, axis, size, offset):
    return lax.ppermute(values, axis, [(i, i ^ offset) for i in range(size)])


def exchange(pieces, size):
    return [pieces[0]] + [swap(pieces[d], "fsdp", size, d) for d in range(1, size)]


def column(values, size, ranks, pairs):
    full = [
        (z * ranks + r, to * ranks + (r & ~1) + core)
        for z in range(size)
        for r in range(ranks)
        for to, core in pairs(z, r & 1)
    ]
    return lax.ppermute(values, ("fsdp", "rep"), full)


def collect(own, home, size, ranks, early):
    first = column(
        own, size, ranks, lambda z, c: [(z ^ 1, c) if c == z >> 1 else (z ^ 2, 1 - c)]
    )
    second = column(first, size, ranks, lambda z, c: [] if c == z >> 1 else [(z ^ 1, c)])
    low = jnp.where(home, own, first)
    high = jnp.where(home, first, second)
    pair, early = after((jnp.concatenate([low, high], axis=0), early))
    other = swap(pair, "rep", ranks, 1)
    return pair, other, first, second, early


def trade_out(pieces, size, ranks, rounds=None):
    def round_of(k):
        return lambda z, c: [((2 * c + (z & 1)) ^ k, z >> 1)]

    return [column(pieces[k], size, ranks, round_of(k)) for k in rounds or range(size)]


def trade_back(pieces, size, ranks):
    def round_of(k):
        return lambda z, c: [(2 * c + ((z ^ k) & 1), (z ^ k) >> 1)]

    return [column(pieces[k], size, ranks, round_of(k)) for k in range(size)]


def pick(blocks, index):
    return lax.dynamic_index_in_dim(blocks, index, 0, keepdims=False)


def reorder(blocks, z, size):
    return jnp.stack([pick(blocks, z ^ j) for j in range(size)])


def far(ranks):
    bits = []
    bit = 2
    while bit < ranks:
        bits.append(bit)
        bit *= 2
    return bits


def stage_bit(core, ranks, stage):
    bits = far(ranks)
    return bits[stage] if core == 0 else bits[len(bits) - 1 - stage]


def stage_swap(values, ranks, stage):
    return lax.ppermute(values, "rep", [(i, i ^ stage_bit(i & 1, ranks, stage)) for i in range(ranks)])


def stage_upper(r, ranks, stage):
    bit = jnp.where(r & 1 == 0, stage_bit(0, ranks, stage), stage_bit(1, ranks, stage))
    return r & bit != 0


def place(r, ranks):
    stages = len(far(ranks))
    total = jnp.where(r & 1 != 0, 1 << stages, 0)
    for stage in range(stages):
        total = total + jnp.where(stage_upper(r, ranks, stage), 1 << stage, 0)
    return total


def join(mine, other, upper):
    return jnp.concatenate([jnp.where(upper, other, mine), jnp.where(upper, mine, other)], axis=1)


def cut(values, upper):
    half = values.shape[1] // 2
    mine = jnp.where(upper, half, 0)
    sent = lax.dynamic_slice_in_dim(values, half - mine, half, 1)
    return sent, lax.dynamic_slice_in_dim(values, mine, half, 1)


def add(one, two):
    return (one.astype(F32) + two.astype(F32)).astype(BF16)


def grow(values, r, ranks, stages):
    for stage in stages:
        values = join(values, stage_swap(values, ranks, stage), stage_upper(r, ranks, stage))
    return values


def grow_flat(values, r, ranks, stages):
    for stage in stages:
        other = stage_swap(values, ranks, stage)
        upper = stage_upper(r, ranks, stage)
        values = jnp.concatenate(
            [jnp.where(upper, other, values), jnp.where(upper, values, other)], axis=0
        )
    return values


def shrink(values, r, ranks, stages):
    for stage in stages:
        sent, kept = cut(values, stage_upper(r, ranks, stage))
        values = add(kept, stage_swap(sent, ranks, stage))
    return values


def halves(values):
    middle = values.shape[-1] // 2
    return [values[..., :middle], values[..., middle:]]


def split_rows(shard, r, ranks):
    rows = shard.shape[0] // ranks
    return lax.dynamic_slice_in_dim(shard, place(r, ranks) * rows, rows, 0)


def finish_kernel(
    place_ref, mine_ref, other_ref, into_ref, expand_ref, gain_a_ref, gain_b_ref,
    into_sum_ref, gain_a_sum_ref, out_sum_ref, expand_sum_ref, gain_b_sum_ref, contract_sum_ref,
):
    first = place_ref[1] == 0
    part, width = out_sum_ref.shape
    held = contract_sum_ref.shape[0]
    pieces = mine_ref.shape[0]
    lines = 3 * part // pieces

    def gathered(start):
        rows = mine_ref.shape[1] if start else lines
        sides = []
        for one, two in ((mine_ref, other_ref), (other_ref, mine_ref)):
            blocks = [
                jnp.where(first, one[p, start:rows].astype(F32), two[p, start:rows].astype(F32))
                for p in range(pieces)
            ]
            sides.append(jnp.concatenate(blocks, axis=0))
        return sides

    blocks = [side[:, k * part : (k + 1) * part].T for side in gathered(0) for k in range(2)]
    total = jnp.zeros((part, 1), F32)
    for t in range(3):
        row = jnp.concatenate([block[:, t * part : (t + 1) * part] for block in blocks], axis=1)
        into_sum_ref[:, t * width : (t + 1) * width] = row
        weight = into_ref[:, t * width : (t + 1) * width].astype(F32)
        total = total + jnp.sum(row * weight, axis=1, keepdims=True)
    gain_a_sum_ref[...] = total.T / gain_a_ref[...].astype(F32)

    grads = jnp.concatenate(gathered(lines), axis=1)
    out_sum_ref[...] = grads[:part]
    total = jnp.zeros((part, 1), F32)
    for t in range(3):
        row = grads[(1 + t) * part : (2 + t) * part]
        expand_sum_ref[:, t * width : (t + 1) * width] = row
        weight = expand_ref[:, t * width : (t + 1) * width].astype(F32)
        total = total + jnp.sum(row * weight, axis=1, keepdims=True)
    gain_b_sum_ref[...] = total.T / gain_b_ref[...].astype(F32)
    contract_sum_ref[...] = grads[4 * part : 4 * part + held]


def finish(where, mine, other, projection_in, expansion, gain_a, gain_b, held):
    part, wide = projection_in.shape
    inside = pl.BlockSpec(memory_space=pltpu.VMEM)
    shapes = [(part, wide), (1, part), (part, wide // 3), (part, wide), (1, part), (held, wide // 3)]
    return pl.pallas_call(
        finish_kernel,
        in_specs=[pl.BlockSpec(memory_space=pltpu.SMEM)] + [inside] * 6,
        out_specs=[inside] * 6,
        out_shape=[jax.ShapeDtypeStruct(shape, F32) for shape in shapes],
        compiler_params=pltpu.CompilerParams(vmem_limit_bytes=48 * 2**20),
        name="finish",
    )(where, mine, other, projection_in, expansion, gain_a[None], gain_b[None])


def local(size, ranks, tokens, gain_a, projection_in, attention_out, gain_b, expansion, contraction, cotangent):
    z = lax.axis_index("fsdp")
    r = lax.axis_index("rep")
    core = r & 1
    group = 2 * core + (z & 1)
    home = core == z >> 1
    own = tokens[0]
    count, width = own.shape
    part = width // size
    hidden = contraction.shape[0]
    heads = HEADS // size

    stages = list(range(len(far(ranks))))
    where = jnp.stack([z, core]).astype(jnp.int32)
    columns = [projection_in[:, t * width : (t + 1) * width] for t in range(3)]
    piece = split_rows(jnp.concatenate(columns, axis=0), r, ranks)
    rows = piece.shape[0]
    gains = jnp.pad(jnp.concatenate([gain_a, gain_b])[None], ((0, 7), (0, width - 2 * part)))
    pieces = jnp.stack(exchange([jnp.concatenate([piece, gains], axis=0)] * size, size))
    gains = reorder(pieces[:, rows, : 2 * part], z, size).astype(F32)
    gain_one = gains[:, :part].reshape(1, width)
    gain_two = gains[:, part:].reshape(1, width)
    freqs = THETA ** (-(jnp.arange(HALF, dtype=F32) * (2.0 / HEAD_DIM)))
    places = jnp.concatenate([(group ^ d) * count + jnp.arange(count, dtype=jnp.int32) for d in range(size)])
    angles = freqs[:, None] * places.astype(F32)[None, :]
    early = (gain_one, gain_two, jnp.cos(angles), jnp.sin(angles))
    pair, other, first, second, early = collect(own, home, size, ranks, early)
    gain_one, gain_two, cosine, sine = early
    into = grow(pieces[:, :rows], r, ranks, stages[:-1])
    into = grow(after(into, first), r, ranks, stages[-1:])
    into_other = swap(into, "rep", ranks, 1)
    normed, queries, keys, values = project(
        where, pair, other, gain_one, cosine, sine, into, into_other, count
    )

    columns = [expansion[:, t * width : (t + 1) * width] for t in range(3)]
    stacked = jnp.concatenate([attention_out] + columns + [contraction], axis=0)
    pad = -stacked.shape[0] % max(32, 8 * ranks)
    stacked = jnp.concatenate([stacked, jnp.zeros((pad, width), BF16)], axis=0)
    rest = exchange([split_rows(after(stacked, second), r, ranks)] * size, size)
    merged = []
    logs = []
    for head in range(heads):
        out, log = attend(head, queries, after(keys, *merged[-1:]), values)
        merged.append(out)
        logs.append(log)
    rest = jnp.stack(after(rest, merged[0]))
    for stage in stages[:-1]:
        rest = join(rest, after(stage_swap(rest, ranks, stage), merged[-1]), stage_upper(r, ranks, stage))
    own_merged = jnp.concatenate(merged, axis=0)
    merged = trade_out([own_merged[:, d * count : (d + 1) * count] for d in range(size)], size, ranks)
    coming = after(stage_swap(rest, ranks, stages[-1]), *merged)
    rest = join(rest, coming, stage_upper(r, ranks, stages[-1]))
    rest_other = swap(rest, "rep", ranks, 1)
    upstream = cotangent[0]
    block_output, state_back, state_low, normed_two, active, inner_back, *merged_back = forward_back(
        where, merged, own, upstream, gain_two, [rest, rest_other], size * hidden
    )
    arrived = trade_back(merged_back, size, ranks)
    own_upstream = arrived

    kept, sent = gradients(
        where, merged, upstream, state_low, normed_two, active, inner_back, stacked.shape[0]
    )
    sent = after(sent, *arrived)
    other = swap(sent, "rep", ranks, 1)
    upper = stage_upper(r, ranks, stages[-1])
    (sent, kept), (other_sent, other) = cut(kept, upper), cut(other, upper)
    sent = add(sent, other_sent)

    turned_backs = []
    weight_backs = []
    received = []
    ahead = [sent]
    for head in range(heads):
        grad, weight_grad = attend_back(
            head, queries, keys, values, after(own_upstream, *ahead), own_merged, logs[head],
            cosine, sine, normed,
        )
        turned_backs.append(grad)
        weight_backs.append(weight_grad.reshape(3, HEAD_DIM, width))
        received.append(trade_out([grad[:, d * count : (d + 1) * count] for d in range(size)], size, ranks))
        if head == 0:
            coming = stage_swap(sent, ranks, stages[-1])
            grads = (kept.astype(F32) + other.astype(F32) + coming.astype(F32)).astype(BF16)
            grads = shrink(grads, r, ranks, stages[-2:0:-1])
            ahead = [grads]
        if head == 1:
            grads = shrink(grads, r, ranks, stages[:1])
            ahead = [grads] + received[0]

    sent, kept = [jnp.stack([pick(grads, bit), pick(grads, bit + 2)]) for bit in (z & 1 ^ 1, z & 1)]
    grads = add(kept, swap(sent, "fsdp", size, 1))
    weight_backs[2], grads = after((weight_backs[2], grads), turned_backs[2], *received[1][:2])
    into_grad = jnp.concatenate([grad[t] for t in range(3) for grad in weight_backs], axis=0)
    later, last = received[1:]
    into_grad = after(shrink(into_grad[None], r, ranks, stages[-1:]), later[2], last[0])
    into_grad = after(shrink(into_grad, r, ranks, stages[-2::-1]), later[3], last[1])[0]
    grads = add(pick(grads, z >> 1), swap(pick(grads, z >> 1 ^ 1), "fsdp", size, 2))
    lines = into_grad.shape[0]
    blocks = into_grad.reshape(lines, size, part).transpose(1, 0, 2)
    blocks = exchange([pick(blocks, z ^ d) for d in range(size)], size)
    even, odd = (blocks[0].astype(F32) + blocks[2].astype(F32)), (blocks[1].astype(F32) + blocks[3].astype(F32))
    low = z & 1 == 0
    flat = jnp.concatenate([jnp.where(low, even, odd), jnp.where(low, odd, even)], axis=1).astype(BF16)
    both = grow_flat(jnp.concatenate([flat, grads], axis=0)[None], r, ranks, stages[:-1])
    both = grow_flat(after(both, *last[2:]), r, ranks, stages[-1:])
    token_grad = token_back(where, received, into, into_other, own, state_back, gain_one)[None]
    both = after(both, token_grad)
    into_sum, gain_one_sum, attention_out_sum, expansion_sum, gain_two_sum, contraction_sum = finish(
        where, both, swap(both, "rep", ranks, 1), projection_in, expansion, gain_a, gain_b, hidden
    )
    return (
        block_output[None],
        token_grad,
        gain_one_sum[0],
        into_sum,
        attention_out_sum,
        gain_two_sum[0],
        expansion_sum,
        contraction_sum,
    )


def solution(mesh):
    tokens, rows, line = P("rep", "fsdp", None), P("fsdp", None), P("fsdp")
    in_specs = (tokens, line, rows, rows, line, rows, rows, tokens)
    out_specs = (tokens, tokens, line, rows, rows, line, rows, rows)
    body = functools.partial(local, mesh.shape["fsdp"], mesh.shape["rep"])
    return jax.shard_map(body, mesh=mesh, in_specs=in_specs, out_specs=out_specs, check_vma=False)
```

```python
import functools
import math

import jax
import jax.numpy as jnp
from jax import lax
from jax.experimental import pallas as pl
from jax.experimental.pallas import tpu as pltpu
from jax.sharding import PartitionSpec as P

HEADS = 12
HEAD_DIM = 64
HALF = HEAD_DIM // 2
SCALE = 1.0 / math.sqrt(HEAD_DIM)
EPS = 1e-05
THETA = 160000.0
F32 = jnp.float32
BF16 = jnp.bfloat16
NN = (((1,), (0,)), ((), ()))
NT = (((1,), (1,)), ((), ()))
TN = (((0,), (0,)), ((), ()))
TT = (((0,), (1,)), ((), ()))


def mul(a, b, dims=NN):
    return lax.dot_general(a, b, dims, preferred_element_type=F32)


def attend_kernel(q_ref, k_ref, v_ref, out_ref, log_ref):
    scores = mul(k_ref[...].T, q_ref[...])
    highest = jnp.max(scores, axis=0, keepdims=True)
    raised = jnp.exp(scores - highest)
    total = jnp.sum(raised, axis=0, keepdims=True)
    mixed = mul(v_ref[...], raised.astype(BF16))
    out_ref[...] = (mixed / total).astype(BF16)
    log_ref[...] = highest + jnp.log(total)


def attend(head, queries, keys, values, step=1024):
    count = queries.shape[1]
    step = min(step, count)
    whole = pl.BlockSpec((HEAD_DIM, count), lambda i: (head, 0))
    return pl.pallas_call(
        attend_kernel,
        grid=(count // step,),
        in_specs=[pl.BlockSpec((HEAD_DIM, step), lambda i: (head, i)), whole, whole],
        out_specs=[
            pl.BlockSpec((HEAD_DIM, step), lambda i: (0, i)),
            pl.BlockSpec((1, step), lambda i: (0, i)),
        ],
        out_shape=[
            jax.ShapeDtypeStruct((HEAD_DIM, count), BF16),
            jax.ShapeDtypeStruct((1, count), F32),
        ],
        compiler_params=pltpu.CompilerParams(vmem_limit_bytes=48 * 2**20),
        cost_estimate=pl.CostEstimate(
            flops=28 * count * count * HEAD_DIM,
            bytes_accessed=8 * HEAD_DIM * count,
            transcendentals=count * count,
        ),
        name="attend",
    )(queries, keys, values)


def turn_back(values, cosine, sine):
    first, second = values[:HALF], values[HALF:]
    return jnp.concatenate([first * cosine + second * sine, second * cosine - first * sine], axis=0)


def attend_back_kernel(
    q_ref, kt_ref, vt_ref, u0_ref, u1_ref, u2_ref, u3_ref, out_ref, log_ref, cos_ref, sin_ref, normed_ref,
    grad_ref, weight_ref, up_ref, k_ref, v_ref, dk_ref, dv_ref,
):
    index = pl.program_id(0)
    step = q_ref.shape[1]

    @pl.when(index == 0)
    def _():
        for d, ref in enumerate((u0_ref, u1_ref, u2_ref, u3_ref)):
            up_ref[d] = ref[...]
        k_ref[...] = kt_ref[...].T
        v_ref[...] = vt_ref[...].T
        dk_ref[...] = jnp.zeros_like(dk_ref)
        dv_ref[...] = jnp.zeros_like(dv_ref)

    upstream = up_ref[index]
    inner_sum = jnp.sum(upstream.astype(F32) * out_ref[...].astype(F32), axis=0, keepdims=True)
    chances = jnp.exp(mul(k_ref[...], q_ref[...]) - log_ref[...])
    prob_back = mul(v_ref[...], upstream)
    score_back = (chances * (prob_back - inner_sum)).astype(BF16)
    dv_ref[...] += mul(chances.astype(BF16), upstream, NT)
    dk_ref[...] += mul(score_back, q_ref[...], NT)
    columns = pl.ds(pl.multiple_of(index * step, step), step)
    query_back = mul(kt_ref[...], score_back) * SCALE
    grad_ref[pl.ds(0, HEAD_DIM), columns] = turn_back(
        query_back, cos_ref[:, columns], sin_ref[:, columns]
    ).astype(BF16)

    @pl.when(index == pl.num_programs(0) - 1)
    def _():
        key_back = turn_back(dk_ref[...].T, cos_ref[...], sin_ref[...])
        grad_ref[pl.ds(HEAD_DIM, HEAD_DIM), :] = key_back.astype(BF16)
        grad_ref[pl.ds(2 * HEAD_DIM, HEAD_DIM), :] = dv_ref[...].T.astype(BF16)
        weight_ref[...] = mul(grad_ref[...], normed_ref[...]).astype(BF16)


def attend_back(head, queries, keys, values, upstream, merged, log, cosine, sine, normed):
    count, width = normed.shape
    step = upstream[0].shape[1]
    some = pl.BlockSpec((HEAD_DIM, step), lambda i: (head, i))
    whole = pl.BlockSpec((HEAD_DIM, count), lambda i: (head, 0))
    table = pl.BlockSpec((HALF, count), lambda i: (0, 0))
    return pl.pallas_call(
        attend_back_kernel,
        grid=(count // step,),
        in_specs=[
            some,
            whole,
            whole,
            *[pl.BlockSpec((HEAD_DIM, step), lambda i: (head, 0))] * len(upstream),
            some,
            pl.BlockSpec((1, step), lambda i: (0, i)),
            table,
            table,
            pl.BlockSpec((count, width), lambda i: (0, 0)),
        ],
        out_specs=[
            pl.BlockSpec((3 * HEAD_DIM, count), lambda i: (0, 0)),
            pl.BlockSpec((3 * HEAD_DIM, width), lambda i: (0, 0)),
        ],
        out_shape=[
            jax.ShapeDtypeStruct((3 * HEAD_DIM, count), BF16),
            jax.ShapeDtypeStruct((3 * HEAD_DIM, width), BF16),
        ],
        scratch_shapes=[
            pltpu.VMEM((len(upstream), HEAD_DIM, step), BF16),
            pltpu.VMEM((count, HEAD_DIM), BF16),
            pltpu.VMEM((count, HEAD_DIM), BF16),
            pltpu.VMEM((count, HEAD_DIM), F32),
            pltpu.VMEM((count, HEAD_DIM), F32),
        ],
        compiler_params=pltpu.CompilerParams(vmem_limit_bytes=48 * 2**20),
        cost_estimate=pl.CostEstimate(
            flops=56 * count * count * HEAD_DIM,
            bytes_accessed=16 * HEAD_DIM * count,
            transcendentals=count * count,
        ),
        name="attend_back",
    )(queries, keys, values, *upstream, merged, log, cosine, sine, normed)


def load_rows(place_ref, pairs, buffer, sems):
    z, core = place_ref[0], place_ref[1]
    size, rows, lanes = pairs[0][0].shape
    copies = []
    for d in range(size):
        for n, (mine, other) in enumerate(pairs):
            for k, (ref, side) in enumerate(((mine, core), (other, 1 - core))):
                start = pl.multiple_of(side * rows, 16)
                target = buffer.at[z ^ d, pl.ds(start, rows), pl.ds(n * lanes, lanes)]
                copies.append(pltpu.make_async_copy(ref.at[d], target, sems.at[d, n, k]))
    for copy in copies:
        copy.start()
    for copy in copies:
        copy.wait()


def unit_of(values):
    centre = values - jnp.mean(values, axis=-1, keepdims=True)
    inverse = lax.rsqrt(jnp.mean(centre * centre, axis=-1, keepdims=True) + EPS)
    return centre * inverse, inverse


def turn(values, cosine, sine):
    first, second = values[:HALF], values[HALF:]
    return jnp.concatenate([first * cosine - second * sine, second * cosine + first * sine], axis=0)


def project_kernel(
    place_ref, pair_ref, other_ref, gain_ref, cos_ref, sin_ref, mine_ref, theirs_ref,
    normed_ref, q_ref, kt_ref, vt_ref, buffer, weight, sems,
):
    index = pl.program_id(0)
    part = q_ref.shape[0]
    size = buffer.shape[0]

    @pl.when(index == 0)
    def _():
        load_rows(place_ref, [(mine_ref, theirs_ref)], buffer, sems)
        start = pl.multiple_of(place_ref[1] * 2 * part, 128)
        odd = place_ref[0] & 1 == 1
        for t in range(3):
            both = buffer[:, t * part : (t + 1) * part, pl.ds(start, 2 * part)].reshape(size * part, 2 * part)
            chosen = jnp.where(odd, both[:, part:].astype(F32), both[:, :part].astype(F32))
            weight[:, t * part : (t + 1) * part] = chosen.astype(BF16)

    block = jnp.where(index < 2, pair_ref[...].astype(F32), other_ref[...].astype(F32))
    normed = (unit_of(block)[0] * gain_ref[...]).astype(BF16)
    normed_ref[...] = normed
    projected = mul(normed, weight[...])
    turned = projected[:, : 2 * part].T
    cosine, sine = cos_ref[...], sin_ref[...]
    for head in range(part // HEAD_DIM):
        rows = slice(head * HEAD_DIM, (head + 1) * HEAD_DIM)
        queries = turn(turned[rows], cosine, sine).astype(BF16)
        q_ref[rows, :] = (queries.astype(F32) * SCALE).astype(BF16)
        keys = turn(turned[part + head * HEAD_DIM : part + (head + 1) * HEAD_DIM], cosine, sine)
        kt_ref[rows, :] = keys.astype(BF16)
    vt_ref[...] = projected[:, 2 * part :].astype(BF16).T


def project(where, pair, other, gain, cosine, sine, mine, theirs, count):
    width = pair.shape[1]
    size, rows = mine.shape[0], 2 * mine.shape[1]
    part = width // size
    total = size * count
    anywhere = pl.BlockSpec(memory_space=pl.ANY)
    columns = pl.BlockSpec((part, count), lambda i: (0, i))
    return pl.pallas_call(
        project_kernel,
        grid=(size,),
        in_specs=[
            pl.BlockSpec(memory_space=pltpu.SMEM),
            pl.BlockSpec((count, width), lambda i: (jnp.minimum(i, 1), 0)),
            pl.BlockSpec((count, width), lambda i: (jnp.maximum(i - 2, 0), 0)),
            pl.BlockSpec((1, width), lambda i: (0, 0)),
            pl.BlockSpec((HALF, count), lambda i: (0, i)),
            pl.BlockSpec((HALF, count), lambda i: (0, i)),
            anywhere,
            anywhere,
        ],
        out_specs=[
            pl.BlockSpec((count, width), lambda i: (i, 0)),
            columns,
            columns,
            columns,
        ],
        out_shape=[
            jax.ShapeDtypeStruct((total, width), BF16),
            jax.ShapeDtypeStruct((part, total), BF16),
            jax.ShapeDtypeStruct((part, total), BF16),
            jax.ShapeDtypeStruct((part, total), BF16),
        ],
        scratch_shapes=[
            pltpu.VMEM((size, rows, width), BF16),
            pltpu.VMEM((width, 3 * part), BF16),
            pltpu.SemaphoreType.DMA((size, 1, 2)),
        ],
        compiler_params=pltpu.CompilerParams(vmem_limit_bytes=48 * 2**20),
        cost_estimate=pl.CostEstimate(flops=8 * 10**9, bytes_accessed=20 * 10**6, transcendentals=0),
        name="project",
    )(where, pair, other, gain, cosine, sine, mine, theirs)


def forward_back_kernel(
    place_ref, m0_ref, m1_ref, m2_ref, m3_ref, tokens_ref, up_ref, gain_ref, mine_ref, theirs_ref,
    result_ref, state_back_ref, low_ref, normed_ref, active_ref, inner_back_ref, b0_ref, b1_ref, b2_ref, b3_ref,
    buffer, sems,
):
    part, width = m0_ref.shape[0], tokens_ref.shape[1]
    size = buffer.shape[0]
    hidden = active_ref.shape[1]
    z = place_ref[0]

    @pl.when(pl.program_id(0) == 0)
    def _():
        load_rows(place_ref, [(mine_ref, theirs_ref)], buffer, sems)

    expand = [buffer[:, (1 + t) * part : (2 + t) * part, :].reshape(width, width) for t in range(3)]
    contract = buffer[:, 4 * part : 4 * part + hidden // size, :].reshape(hidden, width)
    gain = gain_ref[...]

    state = tokens_ref[...].astype(F32)
    for k, ref in enumerate((m0_ref, m1_ref, m2_ref, m3_ref)):
        state = state + mul(ref[...], buffer[z ^ k, :part, :], TN)
    unit, inverse = unit_of(state)
    normed = (unit * gain).astype(BF16)
    normed_ref[...] = normed
    inner = jnp.concatenate([mul(normed, weight) for weight in expand], axis=1)
    first, second = inner[:, :hidden], inner[:, hidden:]
    chance = 0.5 + 0.5 * lax.erf(first * math.sqrt(0.5))
    gated = first * chance
    slope = chance + first * (jnp.exp(-0.5 * first * first) * (1.0 / math.sqrt(2.0 * math.pi)))
    active = (gated * second).astype(BF16)
    active_ref[...] = active
    result_ref[...] = (state + mul(active, contract)).astype(BF16)

    upstream = up_ref[...]
    active_back = mul(upstream, contract, NT).astype(BF16).astype(F32)
    inner_back = jnp.concatenate(
        [(active_back * second * slope).astype(BF16), (active_back * gated).astype(BF16)], axis=1
    )
    inner_back_ref[...] = inner_back
    normed_back = mul(inner_back[:, :width], expand[0], NT)
    normed_back = normed_back + mul(inner_back[:, width : 2 * width], expand[1], NT)
    normed_back = normed_back + mul(inner_back[:, 2 * width :], expand[2], NT)
    scaled = normed_back * gain
    mean = jnp.mean(scaled, axis=-1, keepdims=True)
    lean = jnp.mean(scaled * unit, axis=-1, keepdims=True)
    state_back = upstream.astype(F32) + inverse * (scaled - mean - unit * lean)
    state_back_ref[...] = state_back
    low = state_back.astype(BF16)
    low_ref[...] = low
    for k, ref in enumerate((b0_ref, b1_ref, b2_ref, b3_ref)):
        ref[...] = mul(buffer[z ^ k, :part, :], low, NT).astype(BF16)


def forward_back(where, merged, tokens, upstream, gain, sides, hidden, step=256):
    count, width = tokens.shape
    size, rows = sides[0].shape[0], 2 * sides[0].shape[1]
    part = width // size
    anywhere = pl.BlockSpec(memory_space=pl.ANY)
    columns = pl.BlockSpec((part, step), lambda i: (0, i))

    def some(lanes):
        return pl.BlockSpec((step, lanes), lambda i: (i, 0))

    lanes = [width, width, width, width, hidden, 2 * hidden]
    kinds = [BF16, F32, BF16, BF16, BF16, BF16]
    return pl.pallas_call(
        forward_back_kernel,
        grid=(count // step,),
        in_specs=[pl.BlockSpec(memory_space=pltpu.SMEM)]
        + [columns] * size
        + [some(width), some(width), pl.BlockSpec((1, width), lambda i: (0, 0))]
        + [anywhere] * len(sides),
        out_specs=[some(n) for n in lanes] + [columns] * size,
        out_shape=[jax.ShapeDtypeStruct((count, n), kind) for n, kind in zip(lanes, kinds)]
        + [jax.ShapeDtypeStruct((part, count), BF16)] * size,
        scratch_shapes=[pltpu.VMEM((size, rows, width), BF16), pltpu.SemaphoreType.DMA((size, 1, 2))],
        compiler_params=pltpu.CompilerParams(vmem_limit_bytes=56 * 2**20),
        cost_estimate=pl.CostEstimate(flops=14 * 10**9, bytes_accessed=20 * 10**6, transcendentals=0),
        name="forward_back",
    )(where, *merged, tokens, upstream, gain, *sides)


def gradients_kernel(
    place_ref, m0_ref, m1_ref, m2_ref, m3_ref, up_ref, low_ref, normed_ref, active_ref, inner_back_ref,
    kept_ref, sent_ref,
):
    z, core = place_ref[0], place_ref[1]
    part, width = m0_ref.shape[0], up_ref.shape[1]
    size, rows, lanes = kept_ref.shape
    held = active_ref.shape[1] // size
    for grads_ref, side in ((sent_ref, 1 - core), (kept_ref, core)):
        start = pl.multiple_of(side * lanes, 128)
        low = low_ref[:, pl.ds(start, lanes)]
        for k, ref in enumerate((m0_ref, m1_ref, m2_ref, m3_ref)):
            grads_ref[z ^ k, :part, :] = mul(ref[...], low).astype(BF16)
        normed = normed_ref[...]
        for t in range(3):
            grad = mul(normed, inner_back_ref[:, pl.ds(t * width + start, lanes)], TN)
            grads_ref[:, (1 + t) * part : (2 + t) * part, :] = grad.astype(BF16).reshape(size, part, lanes)
        grad = mul(active_ref[...], up_ref[:, pl.ds(start, lanes)], TN)
        grads_ref[:, 4 * part : 4 * part + held, :] = grad.astype(BF16).reshape(size, held, lanes)
        if rows > 4 * part + held:
            grads_ref[:, 4 * part + held :, :] = jnp.zeros((size, rows - 4 * part - held, lanes), BF16)


def gradients(where, merged, upstream, low, normed, active, inner_back, rows):
    size = len(merged)
    inside = pl.BlockSpec(memory_space=pltpu.VMEM)
    return pl.pallas_call(
        gradients_kernel,
        in_specs=[pl.BlockSpec(memory_space=pltpu.SMEM)] + [inside] * (size + 5),
        out_specs=[inside] * 2,
        out_shape=[jax.ShapeDtypeStruct((size, rows, upstream.shape[1] // 2), BF16)] * 2,
        compiler_params=pltpu.CompilerParams(vmem_limit_bytes=60 * 2**20),
        cost_estimate=pl.CostEstimate(flops=12 * 10**9, bytes_accessed=12 * 10**6, transcendentals=0),
        name="gradients",
    )(where, *merged, upstream, low, normed, active, inner_back)


def token_kernel(heads, place_ref, *refs):
    size = len(refs[: -9]) // heads
    pieces = refs[: heads * size]
    mine_ref, theirs_ref, tokens_ref, back_ref, gain_ref, grad_ref, parts, buffer, sems = refs[heads * size :]
    z = place_ref[0]
    width = buffer.shape[2]
    part = width // size
    load_rows(place_ref, [(mine_ref, theirs_ref)], buffer, sems)
    for head in range(heads):
        for k in range(size):
            ref = pieces[head * size + k]
            lines = pl.ds(pl.multiple_of((z ^ k) * part + head * HEAD_DIM, HEAD_DIM), HEAD_DIM)
            for t in range(3):
                parts[t, lines, :] = ref[t * HEAD_DIM : (t + 1) * HEAD_DIM, :]
    total = jnp.zeros((width, tokens_ref.shape[0]), F32)
    for t in range(3):
        total = total + mul(buffer[:, t * part : (t + 1) * part, :].reshape(width, width), parts[t])
    unit, inverse = unit_of(tokens_ref[...].astype(F32))
    scaled = total.T * gain_ref[...]
    mean = jnp.mean(scaled, axis=-1, keepdims=True)
    lean = jnp.mean(scaled * unit, axis=-1, keepdims=True)
    grad_ref[...] = back_ref[...] + inverse * (scaled - mean - unit * lean)


def token_back(where, received, mine, theirs, tokens, state_back, gain):
    count, width = tokens.shape
    size, rows = mine.shape[0], 2 * mine.shape[1]
    inside = pl.BlockSpec(memory_space=pltpu.VMEM)
    anywhere = pl.BlockSpec(memory_space=pl.ANY)
    pieces = [piece for rounds in received for piece in rounds]
    return pl.pallas_call(
        functools.partial(token_kernel, len(received)),
        in_specs=[pl.BlockSpec(memory_space=pltpu.SMEM)]
        + [inside] * len(pieces)
        + [anywhere] * 2
        + [inside] * 3,
        out_specs=inside,
        out_shape=jax.ShapeDtypeStruct((count, width), F32),
        scratch_shapes=[
            pltpu.VMEM((3, width, count), BF16),
            pltpu.VMEM((size, rows, width), BF16),
            pltpu.SemaphoreType.DMA((size, 1, 2)),
        ],
        compiler_params=pltpu.CompilerParams(vmem_limit_bytes=48 * 2**20),
        cost_estimate=pl.CostEstimate(flops=5 * 10**9, bytes_accessed=12 * 10**6, transcendentals=0),
        name="token_back",
    )(where, *pieces, mine, theirs, tokens, state_back, gain)


def after(values, *others):
    return lax.optimization_barrier((values, others))[0]


def swap(values, axis, size, offset):
    return lax.ppermute(values, axis, [(i, i ^ offset) for i in range(size)])


def exchange(pieces, size):
    return [pieces[0]] + [swap(pieces[d], "fsdp", size, d) for d in range(1, size)]


def column(values, size, ranks, pairs):
    full = [
        (z * ranks + r, to * ranks + (r & ~1) + core)
        for z in range(size)
        for r in range(ranks)
        for to, core in pairs(z, r & 1)
    ]
    return lax.ppermute(values, ("fsdp", "rep"), full)


def collect(own, home, size, ranks, early):
    first = column(
        own, size, ranks, lambda z, c: [(z ^ 1, c) if c == z >> 1 else (z ^ 2, 1 - c)]
    )
    second = column(first, size, ranks, lambda z, c: [] if c == z >> 1 else [(z ^ 1, c)])
    low = jnp.where(home, own, first)
    high = jnp.where(home, first, second)
    pair, early = after((jnp.concatenate([low, high], axis=0), early))
    other = swap(pair, "rep", ranks, 1)
    return pair, other, first, second, early


def trade_out(pieces, size, ranks, rounds=None):
    def round_of(k):
        return lambda z, c: [((2 * c + (z & 1)) ^ k, z >> 1)]

    return [column(pieces[k], size, ranks, round_of(k)) for k in rounds or range(size)]


def trade_back(pieces, size, ranks):
    def round_of(k):
        return lambda z, c: [(2 * c + ((z ^ k) & 1), (z ^ k) >> 1)]

    return [column(pieces[k], size, ranks, round_of(k)) for k in range(size)]


def pick(blocks, index):
    return lax.dynamic_index_in_dim(blocks, index, 0, keepdims=False)


def reorder(blocks, z, size):
    return jnp.stack([pick(blocks, z ^ j) for j in range(size)])


def far(ranks):
    bits = []
    bit = 2
    while bit < ranks:
        bits.append(bit)
        bit *= 2
    return bits


def stage_bit(core, ranks, stage):
    bits = far(ranks)
    return bits[stage] if core == 0 else bits[len(bits) - 1 - stage]


def stage_swap(values, ranks, stage):
    return lax.ppermute(values, "rep", [(i, i ^ stage_bit(i & 1, ranks, stage)) for i in range(ranks)])


def stage_upper(r, ranks, stage):
    bit = jnp.where(r & 1 == 0, stage_bit(0, ranks, stage), stage_bit(1, ranks, stage))
    return r & bit != 0


def place(r, ranks):
    stages = len(far(ranks))
    total = jnp.where(r & 1 != 0, 1 << stages, 0)
    for stage in range(stages):
        total = total + jnp.where(stage_upper(r, ranks, stage), 1 << stage, 0)
    return total


def join(mine, other, upper):
    return jnp.concatenate([jnp.where(upper, other, mine), jnp.where(upper, mine, other)], axis=1)


def cut(values, upper):
    half = values.shape[1] // 2
    mine = jnp.where(upper, half, 0)
    sent = lax.dynamic_slice_in_dim(values, half - mine, half, 1)
    return sent, lax.dynamic_slice_in_dim(values, mine, half, 1)


def add(one, two):
    return (one.astype(F32) + two.astype(F32)).astype(BF16)


def grow(values, r, ranks, stages):
    for stage in stages:
        values = join(values, stage_swap(values, ranks, stage), stage_upper(r, ranks, stage))
    return values


def grow_flat(values, r, ranks, stages):
    for stage in stages:
        other = stage_swap(values, ranks, stage)
        upper = stage_upper(r, ranks, stage)
        values = jnp.concatenate(
            [jnp.where(upper, other, values), jnp.where(upper, values, other)], axis=0
        )
    return values


def shrink(values, r, ranks, stages):
    for stage in stages:
        sent, kept = cut(values, stage_upper(r, ranks, stage))
        values = add(kept, stage_swap(sent, ranks, stage))
    return values


def halves(values):
    middle = values.shape[-1] // 2
    return [values[..., :middle], values[..., middle:]]


def split_rows(shard, r, ranks):
    rows = shard.shape[0] // ranks
    return lax.dynamic_slice_in_dim(shard, place(r, ranks) * rows, rows, 0)


def finish_kernel(
    place_ref, mine_ref, other_ref, into_ref, expand_ref, gain_a_ref, gain_b_ref,
    into_sum_ref, gain_a_sum_ref, out_sum_ref, expand_sum_ref, gain_b_sum_ref, contract_sum_ref,
):
    first = place_ref[1] == 0
    part, width = out_sum_ref.shape
    held = contract_sum_ref.shape[0]
    pieces = mine_ref.shape[0]
    lines = 3 * part // pieces

    def gathered(start):
        rows = mine_ref.shape[1] if start else lines
        sides = []
        for one, two in ((mine_ref, other_ref), (other_ref, mine_ref)):
            blocks = [
                jnp.where(first, one[p, start:rows].astype(F32), two[p, start:rows].astype(F32))
                for p in range(pieces)
            ]
            sides.append(jnp.concatenate(blocks, axis=0))
        return sides

    blocks = [side[:, k * part : (k + 1) * part].T for side in gathered(0) for k in range(2)]
    total = jnp.zeros((part, 1), F32)
    for t in range(3):
        row = jnp.concatenate([block[:, t * part : (t + 1) * part] for block in blocks], axis=1)
        into_sum_ref[:, t * width : (t + 1) * width] = row
        weight = into_ref[:, t * width : (t + 1) * width].astype(F32)
        total = total + jnp.sum(row * weight, axis=1, keepdims=True)
    gain_a_sum_ref[...] = total.T / gain_a_ref[...].astype(F32)

    grads = jnp.concatenate(gathered(lines), axis=1)
    out_sum_ref[...] = grads[:part]
    total = jnp.zeros((part, 1), F32)
    for t in range(3):
        row = grads[(1 + t) * part : (2 + t) * part]
        expand_sum_ref[:, t * width : (t + 1) * width] = row
        weight = expand_ref[:, t * width : (t + 1) * width].astype(F32)
        total = total + jnp.sum(row * weight, axis=1, keepdims=True)
    gain_b_sum_ref[...] = total.T / gain_b_ref[...].astype(F32)
    contract_sum_ref[...] = grads[4 * part : 4 * part + held]


def finish(where, mine, other, projection_in, expansion, gain_a, gain_b, held):
    part, wide = projection_in.shape
    inside = pl.BlockSpec(memory_space=pltpu.VMEM)
    shapes = [(part, wide), (1, part), (part, wide // 3), (part, wide), (1, part), (held, wide // 3)]
    return pl.pallas_call(
        finish_kernel,
        in_specs=[pl.BlockSpec(memory_space=pltpu.SMEM)] + [inside] * 6,
        out_specs=[inside] * 6,
        out_shape=[jax.ShapeDtypeStruct(shape, F32) for shape in shapes],
        compiler_params=pltpu.CompilerParams(vmem_limit_bytes=48 * 2**20),
        name="finish",
    )(where, mine, other, projection_in, expansion, gain_a[None], gain_b[None])


def local(size, ranks, tokens, gain_a, projection_in, attention_out, gain_b, expansion, contraction, cotangent):
    z = lax.axis_index("fsdp")
    r = lax.axis_index("rep")
    core = r & 1
    group = 2 * core + (z & 1)
    home = core == z >> 1
    own = tokens[0]
    count, width = own.shape
    part = width // size
    hidden = contraction.shape[0]
    heads = HEADS // size

    stages = list(range(len(far(ranks))))
    where = jnp.stack([z, core]).astype(jnp.int32)
    columns = [projection_in[:, t * width : (t + 1) * width] for t in range(3)]
    piece = split_rows(jnp.concatenate(columns, axis=0), r, ranks)
    rows = piece.shape[0]
    gains = jnp.pad(jnp.concatenate([gain_a, gain_b])[None], ((0, 7), (0, width - 2 * part)))
    columns = [expansion[:, t * width : (t + 1) * width] for t in range(3)]
    stacked = jnp.concatenate([attention_out] + columns + [contraction], axis=0)
    pad = -stacked.shape[0] % max(32, 8 * ranks)
    stacked = jnp.concatenate([stacked, jnp.zeros((pad, width), BF16)], axis=0)
    piece = jnp.concatenate([piece, gains, split_rows(stacked, r, ranks)], axis=0)
    pieces = jnp.stack(exchange([piece] * size, size))
    gains = reorder(pieces[:, rows, : 2 * part], z, size).astype(F32)
    gain_one = gains[:, :part].reshape(1, width)
    gain_two = gains[:, part:].reshape(1, width)
    freqs = THETA ** (-(jnp.arange(HALF, dtype=F32) * (2.0 / HEAD_DIM)))
    places = jnp.concatenate([(group ^ d) * count + jnp.arange(count, dtype=jnp.int32) for d in range(size)])
    angles = freqs[:, None] * places.astype(F32)[None, :]
    early = (gain_one, gain_two, jnp.cos(angles), jnp.sin(angles))
    pair, other, first, second, early = collect(own, home, size, ranks, early)
    gain_one, gain_two, cosine, sine = early
    into = grow(pieces[:, :rows], r, ranks, stages[:-1])
    into = grow(after(into, first), r, ranks, stages[-1:])
    into_other = swap(into, "rep", ranks, 1)
    rest = after(pieces[:, rows + 8 :], into)
    normed, queries, keys, values = project(
        where, pair, other, gain_one, cosine, sine, into, into_other, count
    )

    merged = []
    logs = []
    for head in range(heads):
        out, log = attend(head, queries, after(keys, *merged[-1:]), values)
        merged.append(out)
        logs.append(log)
    for stage in stages[:-1]:
        rest = join(rest, after(stage_swap(rest, ranks, stage), queries), stage_upper(r, ranks, stage))
    coming = after(stage_swap(rest, ranks, stages[-1]), merged[-1])
    rest = join(rest, coming, stage_upper(r, ranks, stages[-1]))
    rest_other = swap(rest, "rep", ranks, 1)
    own_merged = jnp.concatenate(merged, axis=0)
    merged = trade_out([own_merged[:, d * count : (d + 1) * count] for d in range(size)], size, ranks)
    upstream = cotangent[0]
    block_output, state_back, state_low, normed_two, active, inner_back, *merged_back = forward_back(
        where, merged, own, upstream, gain_two, [rest, rest_other], size * hidden
    )
    arrived = trade_back(merged_back, size, ranks)
    own_upstream = arrived

    kept, sent = gradients(
        where, merged, upstream, state_low, normed_two, active, inner_back, stacked.shape[0]
    )
    sent = after(sent, *arrived)
    other = swap(sent, "rep", ranks, 1)
    upper = stage_upper(r, ranks, stages[-1])
    (sent, kept), (other_sent, other) = cut(kept, upper), cut(other, upper)
    sent = add(sent, other_sent)

    turned_backs = []
    weight_backs = []
    received = []
    ahead = [sent]
    for head in range(heads):
        grad, weight_grad = attend_back(
            head, queries, keys, values, after(own_upstream, *ahead), own_merged, logs[head],
            cosine, sine, normed,
        )
        turned_backs.append(grad)
        weight_backs.append(weight_grad.reshape(3, HEAD_DIM, width))
        received.append(trade_out([grad[:, d * count : (d + 1) * count] for d in range(size)], size, ranks))
        if head == 0:
            coming = stage_swap(sent, ranks, stages[-1])
            grads = (kept.astype(F32) + other.astype(F32) + coming.astype(F32)).astype(BF16)
            grads = shrink(grads, r, ranks, stages[-2:0:-1])
            ahead = [grads]
        if head == 1:
            grads = shrink(grads, r, ranks, stages[:1])
            ahead = [grads] + received[0]

    sent, kept = [jnp.stack([pick(grads, bit), pick(grads, bit + 2)]) for bit in (z & 1 ^ 1, z & 1)]
    grads = add(kept, swap(sent, "fsdp", size, 1))
    weight_backs[2], grads = after((weight_backs[2], grads), turned_backs[2], *received[1][:2])
    into_grad = jnp.concatenate([grad[t] for t in range(3) for grad in weight_backs], axis=0)
    later, last = received[1:]
    into_grad = after(shrink(into_grad[None], r, ranks, stages[-1:]), later[2], last[0])
    into_grad = after(shrink(into_grad, r, ranks, stages[-2::-1]), later[3], last[1])[0]
    grads = add(pick(grads, z >> 1), swap(pick(grads, z >> 1 ^ 1), "fsdp", size, 2))
    lines = into_grad.shape[0]
    blocks = into_grad.reshape(lines, size, part).transpose(1, 0, 2)
    blocks = exchange([pick(blocks, z ^ d) for d in range(size)], size)
    even, odd = (blocks[0].astype(F32) + blocks[2].astype(F32)), (blocks[1].astype(F32) + blocks[3].astype(F32))
    low = z & 1 == 0
    flat = jnp.concatenate([jnp.where(low, even, odd), jnp.where(low, odd, even)], axis=1).astype(BF16)
    both = grow_flat(jnp.concatenate([flat, grads], axis=0)[None], r, ranks, stages[:-1])
    both = grow_flat(after(both, *last[2:]), r, ranks, stages[-1:])
    token_grad = token_back(where, received, into, into_other, own, state_back, gain_one)[None]
    both = after(both, token_grad)
    into_sum, gain_one_sum, attention_out_sum, expansion_sum, gain_two_sum, contraction_sum = finish(
        where, both, swap(both, "rep", ranks, 1), projection_in, expansion, gain_a, gain_b, hidden
    )
    return (
        block_output[None],
        token_grad,
        gain_one_sum[0],
        into_sum,
        attention_out_sum,
        gain_two_sum[0],
        expansion_sum,
        contraction_sum,
    )


def solution(mesh):
    tokens, rows, line = P("rep", "fsdp", None), P("fsdp", None), P("fsdp")
    in_specs = (tokens, line, rows, rows, line, rows, rows, tokens)
    out_specs = (tokens, tokens, line, rows, rows, line, rows, rows)
    body = functools.partial(local, mesh.shape["fsdp"], mesh.shape["rep"])
    return jax.shard_map(body, mesh=mesh, in_specs=in_specs, out_specs=out_specs, check_vma=False)
```

```python
import functools
import math

import jax
import jax.numpy as jnp
from jax import lax
from jax.experimental import pallas as pl
from jax.experimental.pallas import tpu as pltpu
from jax.sharding import PartitionSpec as P

HEADS = 12
HEAD_DIM = 64
HALF = HEAD_DIM // 2
SCALE = 1.0 / math.sqrt(HEAD_DIM)
EPS = 1e-05
THETA = 160000.0
F32 = jnp.float32
BF16 = jnp.bfloat16
NN = (((1,), (0,)), ((), ()))
NT = (((1,), (1,)), ((), ()))
TN = (((0,), (0,)), ((), ()))
TT = (((0,), (1,)), ((), ()))


def mul(a, b, dims=NN):
    return lax.dot_general(a, b, dims, preferred_element_type=F32)


def attend_kernel(q_ref, k_ref, v_ref, out_ref, log_ref):
    scores = mul(k_ref[...].T, q_ref[...])
    highest = jnp.max(scores, axis=0, keepdims=True)
    raised = jnp.exp(scores - highest)
    total = jnp.sum(raised, axis=0, keepdims=True)
    mixed = mul(v_ref[...], raised.astype(BF16))
    out_ref[...] = (mixed / total).astype(BF16)
    log_ref[...] = highest + jnp.log(total)


def attend(head, queries, keys, values, step=1024):
    count = queries.shape[1]
    step = min(step, count)
    whole = pl.BlockSpec((HEAD_DIM, count), lambda i: (head, 0))
    return pl.pallas_call(
        attend_kernel,
        grid=(count // step,),
        in_specs=[pl.BlockSpec((HEAD_DIM, step), lambda i: (head, i)), whole, whole],
        out_specs=[
            pl.BlockSpec((HEAD_DIM, step), lambda i: (0, i)),
            pl.BlockSpec((1, step), lambda i: (0, i)),
        ],
        out_shape=[
            jax.ShapeDtypeStruct((HEAD_DIM, count), BF16),
            jax.ShapeDtypeStruct((1, count), F32),
        ],
        compiler_params=pltpu.CompilerParams(vmem_limit_bytes=48 * 2**20),
        cost_estimate=pl.CostEstimate(
            flops=28 * count * count * HEAD_DIM,
            bytes_accessed=8 * HEAD_DIM * count,
            transcendentals=count * count,
        ),
        name="attend",
    )(queries, keys, values)


def turn_back(values, cosine, sine):
    first, second = values[:HALF], values[HALF:]
    return jnp.concatenate([first * cosine + second * sine, second * cosine - first * sine], axis=0)


def attend_back_kernel(
    q_ref, kt_ref, vt_ref, u0_ref, u1_ref, u2_ref, u3_ref, out_ref, log_ref, cos_ref, sin_ref, normed_ref,
    grad_ref, weight_ref, up_ref, k_ref, v_ref, dk_ref, dv_ref,
):
    index = pl.program_id(0)
    step = q_ref.shape[1]

    @pl.when(index == 0)
    def _():
        for d, ref in enumerate((u0_ref, u1_ref, u2_ref, u3_ref)):
            up_ref[d] = ref[...]
        k_ref[...] = kt_ref[...].T
        v_ref[...] = vt_ref[...].T
        dk_ref[...] = jnp.zeros_like(dk_ref)
        dv_ref[...] = jnp.zeros_like(dv_ref)

    upstream = up_ref[index]
    inner_sum = jnp.sum(upstream.astype(F32) * out_ref[...].astype(F32), axis=0, keepdims=True)
    chances = jnp.exp(mul(k_ref[...], q_ref[...]) - log_ref[...])
    prob_back = mul(v_ref[...], upstream)
    score_back = (chances * (prob_back - inner_sum)).astype(BF16)
    dv_ref[...] += mul(chances.astype(BF16), upstream, NT)
    dk_ref[...] += mul(score_back, q_ref[...], NT)
    columns = pl.ds(pl.multiple_of(index * step, step), step)
    query_back = mul(kt_ref[...], score_back) * SCALE
    grad_ref[pl.ds(0, HEAD_DIM), columns] = turn_back(
        query_back, cos_ref[:, columns], sin_ref[:, columns]
    ).astype(BF16)

    @pl.when(index == pl.num_programs(0) - 1)
    def _():
        key_back = turn_back(dk_ref[...].T, cos_ref[...], sin_ref[...])
        grad_ref[pl.ds(HEAD_DIM, HEAD_DIM), :] = key_back.astype(BF16)
        grad_ref[pl.ds(2 * HEAD_DIM, HEAD_DIM), :] = dv_ref[...].T.astype(BF16)
        weight_ref[...] = mul(grad_ref[...], normed_ref[...]).astype(BF16)


def attend_back(head, queries, keys, values, upstream, merged, log, cosine, sine, normed):
    count, width = normed.shape
    step = upstream[0].shape[1]
    some = pl.BlockSpec((HEAD_DIM, step), lambda i: (head, i))
    whole = pl.BlockSpec((HEAD_DIM, count), lambda i: (head, 0))
    table = pl.BlockSpec((HALF, count), lambda i: (0, 0))
    return pl.pallas_call(
        attend_back_kernel,
        grid=(count // step,),
        in_specs=[
            some,
            whole,
            whole,
            *[pl.BlockSpec((HEAD_DIM, step), lambda i: (head, 0))] * len(upstream),
            some,
            pl.BlockSpec((1, step), lambda i: (0, i)),
            table,
            table,
            pl.BlockSpec((count, width), lambda i: (0, 0)),
        ],
        out_specs=[
            pl.BlockSpec((3 * HEAD_DIM, count), lambda i: (0, 0)),
            pl.BlockSpec((3 * HEAD_DIM, width), lambda i: (0, 0)),
        ],
        out_shape=[
            jax.ShapeDtypeStruct((3 * HEAD_DIM, count), BF16),
            jax.ShapeDtypeStruct((3 * HEAD_DIM, width), BF16),
        ],
        scratch_shapes=[
            pltpu.VMEM((len(upstream), HEAD_DIM, step), BF16),
            pltpu.VMEM((count, HEAD_DIM), BF16),
            pltpu.VMEM((count, HEAD_DIM), BF16),
            pltpu.VMEM((count, HEAD_DIM), F32),
            pltpu.VMEM((count, HEAD_DIM), F32),
        ],
        compiler_params=pltpu.CompilerParams(vmem_limit_bytes=48 * 2**20),
        cost_estimate=pl.CostEstimate(
            flops=56 * count * count * HEAD_DIM,
            bytes_accessed=16 * HEAD_DIM * count,
            transcendentals=count * count,
        ),
        name="attend_back",
    )(queries, keys, values, *upstream, merged, log, cosine, sine, normed)


def row_copies(place_ref, mine, other, buffer, sems):
    z, core = place_ref[0], place_ref[1]
    size, rows, _ = mine.shape
    copies = []
    for d in range(size):
        for k, (ref, side) in enumerate(((mine, core), (other, 1 - core))):
            target = buffer.at[z ^ d, pl.ds(pl.multiple_of(side * rows, 16), rows), :]
            copies.append(pltpu.make_async_copy(ref.at[d], target, sems.at[d, k]))
    return copies


def unit_of(values):
    centre = values - jnp.mean(values, axis=-1, keepdims=True)
    inverse = lax.rsqrt(jnp.mean(centre * centre, axis=-1, keepdims=True) + EPS)
    return centre * inverse, inverse


def turn(values, cosine, sine):
    first, second = values[:HALF], values[HALF:]
    return jnp.concatenate([first * cosine - second * sine, second * cosine + first * sine], axis=0)


def project_kernel(
    place_ref, pair_ref, other_ref, gain_ref, cos_ref, sin_ref, mine_ref, theirs_ref,
    normed_ref, q_ref, kt_ref, vt_ref, buffer, weight, sems,
):
    index = pl.program_id(0)
    part = q_ref.shape[0]
    size = buffer.shape[0]

    @pl.when(index == 0)
    def _():
        for copy in row_copies(place_ref, mine_ref, theirs_ref, buffer, sems):
            copy.start()

    block = jnp.where(index < 2, pair_ref[...].astype(F32), other_ref[...].astype(F32))
    normed = (unit_of(block)[0] * gain_ref[...]).astype(BF16)
    normed_ref[...] = normed

    @pl.when(index == 0)
    def _():
        for copy in row_copies(place_ref, mine_ref, theirs_ref, buffer, sems):
            copy.wait()
        start = pl.multiple_of(place_ref[1] * 2 * part, 128)
        odd = place_ref[0] & 1 == 1
        for t in range(3):
            both = buffer[:, t * part : (t + 1) * part, pl.ds(start, 2 * part)].reshape(size * part, 2 * part)
            chosen = jnp.where(odd, both[:, part:].astype(F32), both[:, :part].astype(F32))
            weight[:, t * part : (t + 1) * part] = chosen.astype(BF16)

    projected = mul(normed, weight[...])
    turned = projected[:, : 2 * part].T
    cosine, sine = cos_ref[...], sin_ref[...]
    for head in range(part // HEAD_DIM):
        rows = slice(head * HEAD_DIM, (head + 1) * HEAD_DIM)
        queries = turn(turned[rows], cosine, sine).astype(BF16)
        q_ref[rows, :] = (queries.astype(F32) * SCALE).astype(BF16)
        keys = turn(turned[part + head * HEAD_DIM : part + (head + 1) * HEAD_DIM], cosine, sine)
        kt_ref[rows, :] = keys.astype(BF16)
    vt_ref[...] = projected[:, 2 * part :].astype(BF16).T


def project(where, pair, other, gain, cosine, sine, mine, theirs, count):
    width = pair.shape[1]
    size, rows = mine.shape[0], 2 * mine.shape[1]
    part = width // size
    total = size * count
    anywhere = pl.BlockSpec(memory_space=pl.ANY)
    columns = pl.BlockSpec((part, count), lambda i: (0, i))
    return pl.pallas_call(
        project_kernel,
        grid=(size,),
        in_specs=[
            pl.BlockSpec(memory_space=pltpu.SMEM),
            pl.BlockSpec((count, width), lambda i: (jnp.minimum(i, 1), 0)),
            pl.BlockSpec((count, width), lambda i: (jnp.maximum(i - 2, 0), 0)),
            pl.BlockSpec((1, width), lambda i: (0, 0)),
            pl.BlockSpec((HALF, count), lambda i: (0, i)),
            pl.BlockSpec((HALF, count), lambda i: (0, i)),
            anywhere,
            anywhere,
        ],
        out_specs=[
            pl.BlockSpec((count, width), lambda i: (i, 0)),
            columns,
            columns,
            columns,
        ],
        out_shape=[
            jax.ShapeDtypeStruct((total, width), BF16),
            jax.ShapeDtypeStruct((part, total), BF16),
            jax.ShapeDtypeStruct((part, total), BF16),
            jax.ShapeDtypeStruct((part, total), BF16),
        ],
        scratch_shapes=[
            pltpu.VMEM((size, rows, width), BF16),
            pltpu.VMEM((width, 3 * part), BF16),
            pltpu.SemaphoreType.DMA((size, 2)),
        ],
        compiler_params=pltpu.CompilerParams(vmem_limit_bytes=62 * 2**20),
        cost_estimate=pl.CostEstimate(flops=8 * 10**9, bytes_accessed=20 * 10**6, transcendentals=0),
        name="project",
    )(where, pair, other, gain, cosine, sine, mine, theirs)


def forward_back_kernel(
    place_ref, m0_ref, m1_ref, m2_ref, m3_ref, tokens_ref, up_ref, gain_ref, mine_ref, theirs_ref,
    result_ref, state_back_ref, low_ref, normed_ref, active_ref, inner_back_ref, b0_ref, b1_ref, b2_ref, b3_ref,
    buffer, sems,
):
    part, width = m0_ref.shape[0], tokens_ref.shape[1]
    size = buffer.shape[0]
    hidden = active_ref.shape[1]
    z = place_ref[0]

    @pl.when(pl.program_id(0) == 0)
    def _():
        copies = row_copies(place_ref, mine_ref, theirs_ref, buffer, sems)
        for copy in copies:
            copy.start()
        for copy in copies:
            copy.wait()

    expand = [buffer[:, (1 + t) * part : (2 + t) * part, :].reshape(width, width) for t in range(3)]
    contract = buffer[:, 4 * part : 4 * part + hidden // size, :].reshape(hidden, width)
    gain = gain_ref[...]

    state = tokens_ref[...].astype(F32)
    for k, ref in enumerate((m0_ref, m1_ref, m2_ref, m3_ref)):
        state = state + mul(ref[...], buffer[z ^ k, :part, :], TN)
    unit, inverse = unit_of(state)
    normed = (unit * gain).astype(BF16)
    normed_ref[...] = normed
    inner = jnp.concatenate([mul(normed, weight) for weight in expand], axis=1)
    first, second = inner[:, :hidden], inner[:, hidden:]
    chance = 0.5 + 0.5 * lax.erf(first * math.sqrt(0.5))
    gated = first * chance
    slope = chance + first * (jnp.exp(-0.5 * first * first) * (1.0 / math.sqrt(2.0 * math.pi)))
    active = (gated * second).astype(BF16)
    active_ref[...] = active
    result_ref[...] = (state + mul(active, contract)).astype(BF16)

    upstream = up_ref[...]
    active_back = mul(upstream, contract, NT).astype(BF16).astype(F32)
    inner_back = jnp.concatenate(
        [(active_back * second * slope).astype(BF16), (active_back * gated).astype(BF16)], axis=1
    )
    inner_back_ref[...] = inner_back
    normed_back = mul(inner_back[:, :width], expand[0], NT)
    normed_back = normed_back + mul(inner_back[:, width : 2 * width], expand[1], NT)
    normed_back = normed_back + mul(inner_back[:, 2 * width :], expand[2], NT)
    scaled = normed_back * gain
    mean = jnp.mean(scaled, axis=-1, keepdims=True)
    lean = jnp.mean(scaled * unit, axis=-1, keepdims=True)
    state_back = upstream.astype(F32) + inverse * (scaled - mean - unit * lean)
    state_back_ref[...] = state_back
    low = state_back.astype(BF16)
    low_ref[...] = low
    for k, ref in enumerate((b0_ref, b1_ref, b2_ref, b3_ref)):
        ref[...] = mul(buffer[z ^ k, :part, :], low, NT).astype(BF16)


def forward_back(where, merged, tokens, upstream, gain, sides, hidden, step=256):
    count, width = tokens.shape
    size, rows = sides[0].shape[0], 2 * sides[0].shape[1]
    part = width // size
    anywhere = pl.BlockSpec(memory_space=pl.ANY)
    columns = pl.BlockSpec((part, step), lambda i: (0, i))

    def some(lanes):
        return pl.BlockSpec((step, lanes), lambda i: (i, 0))

    lanes = [width, width, width, width, hidden, 2 * hidden]
    kinds = [BF16, F32, BF16, BF16, BF16, BF16]
    return pl.pallas_call(
        forward_back_kernel,
        grid=(count // step,),
        in_specs=[pl.BlockSpec(memory_space=pltpu.SMEM)]
        + [columns] * size
        + [some(width), some(width), pl.BlockSpec((1, width), lambda i: (0, 0))]
        + [anywhere] * len(sides),
        out_specs=[some(n) for n in lanes] + [columns] * size,
        out_shape=[jax.ShapeDtypeStruct((count, n), kind) for n, kind in zip(lanes, kinds)]
        + [jax.ShapeDtypeStruct((part, count), BF16)] * size,
        scratch_shapes=[pltpu.VMEM((size, rows, width), BF16), pltpu.SemaphoreType.DMA((size, 2))],
        compiler_params=pltpu.CompilerParams(vmem_limit_bytes=62 * 2**20),
        cost_estimate=pl.CostEstimate(flops=14 * 10**9, bytes_accessed=20 * 10**6, transcendentals=0),
        name="forward_back",
    )(where, *merged, tokens, upstream, gain, *sides)


def gradients_kernel(
    place_ref, m0_ref, m1_ref, m2_ref, m3_ref, up_ref, low_ref, normed_ref, active_ref, inner_back_ref,
    kept_ref, sent_ref,
):
    z, core = place_ref[0], place_ref[1]
    part, width = m0_ref.shape[0], up_ref.shape[1]
    size, rows, lanes = kept_ref.shape
    held = active_ref.shape[1] // size
    for grads_ref, side in ((sent_ref, 1 - core), (kept_ref, core)):
        start = pl.multiple_of(side * lanes, 128)
        low = low_ref[:, pl.ds(start, lanes)]
        for k, ref in enumerate((m0_ref, m1_ref, m2_ref, m3_ref)):
            grads_ref[z ^ k, :part, :] = mul(ref[...], low).astype(BF16)
        normed = normed_ref[...]
        for t in range(3):
            grad = mul(normed, inner_back_ref[:, pl.ds(t * width + start, lanes)], TN)
            grads_ref[:, (1 + t) * part : (2 + t) * part, :] = grad.astype(BF16).reshape(size, part, lanes)
        grad = mul(active_ref[...], up_ref[:, pl.ds(start, lanes)], TN)
        grads_ref[:, 4 * part : 4 * part + held, :] = grad.astype(BF16).reshape(size, held, lanes)
        if rows > 4 * part + held:
            grads_ref[:, 4 * part + held :, :] = jnp.zeros((size, rows - 4 * part - held, lanes), BF16)


def gradients(where, merged, upstream, low, normed, active, inner_back, rows):
    size = len(merged)
    inside = pl.BlockSpec(memory_space=pltpu.VMEM)
    return pl.pallas_call(
        gradients_kernel,
        in_specs=[pl.BlockSpec(memory_space=pltpu.SMEM)] + [inside] * (size + 5),
        out_specs=[inside] * 2,
        out_shape=[jax.ShapeDtypeStruct((size, rows, upstream.shape[1] // 2), BF16)] * 2,
        compiler_params=pltpu.CompilerParams(vmem_limit_bytes=60 * 2**20),
        cost_estimate=pl.CostEstimate(flops=12 * 10**9, bytes_accessed=12 * 10**6, transcendentals=0),
        name="gradients",
    )(where, *merged, upstream, low, normed, active, inner_back)


def token_kernel(heads, place_ref, *refs):
    size = len(refs[: -9]) // heads
    pieces = refs[: heads * size]
    mine_ref, theirs_ref, tokens_ref, back_ref, gain_ref, grad_ref, parts, buffer, sems = refs[heads * size :]
    z = place_ref[0]
    width = buffer.shape[2]
    part = width // size
    copies = row_copies(place_ref, mine_ref, theirs_ref, buffer, sems)
    for copy in copies:
        copy.start()
    for head in range(heads):
        for k in range(size):
            ref = pieces[head * size + k]
            lines = pl.ds(pl.multiple_of((z ^ k) * part + head * HEAD_DIM, HEAD_DIM), HEAD_DIM)
            for t in range(3):
                parts[t, lines, :] = ref[t * HEAD_DIM : (t + 1) * HEAD_DIM, :]
    for copy in copies:
        copy.wait()
    total = jnp.zeros((width, tokens_ref.shape[0]), F32)
    for t in range(3):
        total = total + mul(buffer[:, t * part : (t + 1) * part, :].reshape(width, width), parts[t])
    unit, inverse = unit_of(tokens_ref[...].astype(F32))
    scaled = total.T * gain_ref[...]
    mean = jnp.mean(scaled, axis=-1, keepdims=True)
    lean = jnp.mean(scaled * unit, axis=-1, keepdims=True)
    grad_ref[...] = back_ref[...] + inverse * (scaled - mean - unit * lean)


def token_back(where, received, mine, theirs, tokens, state_back, gain):
    count, width = tokens.shape
    size, rows = mine.shape[0], 2 * mine.shape[1]
    inside = pl.BlockSpec(memory_space=pltpu.VMEM)
    anywhere = pl.BlockSpec(memory_space=pl.ANY)
    pieces = [piece for rounds in received for piece in rounds]
    return pl.pallas_call(
        functools.partial(token_kernel, len(received)),
        in_specs=[pl.BlockSpec(memory_space=pltpu.SMEM)]
        + [inside] * len(pieces)
        + [anywhere] * 2
        + [inside] * 3,
        out_specs=inside,
        out_shape=jax.ShapeDtypeStruct((count, width), F32),
        scratch_shapes=[
            pltpu.VMEM((3, width, count), BF16),
            pltpu.VMEM((size, rows, width), BF16),
            pltpu.SemaphoreType.DMA((size, 2)),
        ],
        compiler_params=pltpu.CompilerParams(vmem_limit_bytes=48 * 2**20),
        cost_estimate=pl.CostEstimate(flops=5 * 10**9, bytes_accessed=12 * 10**6, transcendentals=0),
        name="token_back",
    )(where, *pieces, mine, theirs, tokens, state_back, gain)


def after(values, *others):
    return lax.optimization_barrier((values, others))[0]


def swap(values, axis, size, offset):
    return lax.ppermute(values, axis, [(i, i ^ offset) for i in range(size)])


def exchange(pieces, size):
    return [pieces[0]] + [swap(pieces[d], "fsdp", size, d) for d in range(1, size)]


def column(values, size, ranks, pairs):
    full = [
        (z * ranks + r, to * ranks + (r & ~1) + core)
        for z in range(size)
        for r in range(ranks)
        for to, core in pairs(z, r & 1)
    ]
    return lax.ppermute(values, ("fsdp", "rep"), full)


def collect(own, home, size, ranks, early):
    first = column(
        own, size, ranks, lambda z, c: [(z ^ 1, c) if c == z >> 1 else (z ^ 2, 1 - c)]
    )
    second = column(first, size, ranks, lambda z, c: [] if c == z >> 1 else [(z ^ 1, c)])
    low = jnp.where(home, own, first)
    high = jnp.where(home, first, second)
    pair, early = after((jnp.concatenate([low, high], axis=0), early))
    other = swap(pair, "rep", ranks, 1)
    return pair, other, first, second, early


def trade_out(pieces, size, ranks, rounds=None):
    def round_of(k):
        return lambda z, c: [((2 * c + (z & 1)) ^ k, z >> 1)]

    return [column(pieces[k], size, ranks, round_of(k)) for k in rounds or range(size)]


def trade_back(pieces, size, ranks):
    def round_of(k):
        return lambda z, c: [(2 * c + ((z ^ k) & 1), (z ^ k) >> 1)]

    return [column(pieces[k], size, ranks, round_of(k)) for k in range(size)]


def pick(blocks, index):
    return lax.dynamic_index_in_dim(blocks, index, 0, keepdims=False)


def reorder(blocks, z, size):
    return jnp.stack([pick(blocks, z ^ j) for j in range(size)])


def far(ranks):
    bits = []
    bit = 2
    while bit < ranks:
        bits.append(bit)
        bit *= 2
    return bits


def stage_bit(core, ranks, stage):
    bits = far(ranks)
    return bits[stage] if core == 0 else bits[len(bits) - 1 - stage]


def stage_swap(values, ranks, stage):
    return lax.ppermute(values, "rep", [(i, i ^ stage_bit(i & 1, ranks, stage)) for i in range(ranks)])


def stage_upper(r, ranks, stage):
    bit = jnp.where(r & 1 == 0, stage_bit(0, ranks, stage), stage_bit(1, ranks, stage))
    return r & bit != 0


def place(r, ranks):
    stages = len(far(ranks))
    total = jnp.where(r & 1 != 0, 1 << stages, 0)
    for stage in range(stages):
        total = total + jnp.where(stage_upper(r, ranks, stage), 1 << stage, 0)
    return total


def join(mine, other, upper):
    return jnp.concatenate([jnp.where(upper, other, mine), jnp.where(upper, mine, other)], axis=1)


def cut(values, upper):
    half = values.shape[1] // 2
    mine = jnp.where(upper, half, 0)
    sent = lax.dynamic_slice_in_dim(values, half - mine, half, 1)
    return sent, lax.dynamic_slice_in_dim(values, mine, half, 1)


def add(one, two):
    return (one.astype(F32) + two.astype(F32)).astype(BF16)


def grow(values, r, ranks, stages):
    for stage in stages:
        values = join(values, stage_swap(values, ranks, stage), stage_upper(r, ranks, stage))
    return values


def grow_flat(values, r, ranks, stages):
    for stage in stages:
        other = stage_swap(values, ranks, stage)
        upper = stage_upper(r, ranks, stage)
        values = jnp.concatenate(
            [jnp.where(upper, other, values), jnp.where(upper, values, other)], axis=0
        )
    return values


def shrink(values, r, ranks, stages):
    for stage in stages:
        sent, kept = cut(values, stage_upper(r, ranks, stage))
        values = add(kept, stage_swap(sent, ranks, stage))
    return values


def halves(values):
    middle = values.shape[-1] // 2
    return [values[..., :middle], values[..., middle:]]


def split_rows(shard, r, ranks):
    rows = shard.shape[0] // ranks
    return lax.dynamic_slice_in_dim(shard, place(r, ranks) * rows, rows, 0)


def finish_kernel(
    place_ref, mine_ref, other_ref, into_ref, expand_ref, gain_a_ref, gain_b_ref,
    into_sum_ref, gain_a_sum_ref, out_sum_ref, expand_sum_ref, gain_b_sum_ref, contract_sum_ref,
):
    first = place_ref[1] == 0
    part, width = out_sum_ref.shape
    held = contract_sum_ref.shape[0]
    pieces = mine_ref.shape[0]
    lines = 3 * part // pieces

    def gathered(start):
        rows = mine_ref.shape[1] if start else lines
        sides = []
        for one, two in ((mine_ref, other_ref), (other_ref, mine_ref)):
            blocks = [
                jnp.where(first, one[p, start:rows].astype(F32), two[p, start:rows].astype(F32))
                for p in range(pieces)
            ]
            sides.append(jnp.concatenate(blocks, axis=0))
        return sides

    blocks = [side[:, k * part : (k + 1) * part].T for side in gathered(0) for k in range(2)]
    total = jnp.zeros((part, 1), F32)
    for t in range(3):
        row = jnp.concatenate([block[:, t * part : (t + 1) * part] for block in blocks], axis=1)
        into_sum_ref[:, t * width : (t + 1) * width] = row
        weight = into_ref[:, t * width : (t + 1) * width].astype(F32)
        total = total + jnp.sum(row * weight, axis=1, keepdims=True)
    gain_a_sum_ref[...] = total.T / gain_a_ref[...].astype(F32)

    grads = jnp.concatenate(gathered(lines), axis=1)
    out_sum_ref[...] = grads[:part]
    total = jnp.zeros((part, 1), F32)
    for t in range(3):
        row = grads[(1 + t) * part : (2 + t) * part]
        expand_sum_ref[:, t * width : (t + 1) * width] = row
        weight = expand_ref[:, t * width : (t + 1) * width].astype(F32)
        total = total + jnp.sum(row * weight, axis=1, keepdims=True)
    gain_b_sum_ref[...] = total.T / gain_b_ref[...].astype(F32)
    contract_sum_ref[...] = grads[4 * part : 4 * part + held]


def finish(where, mine, other, projection_in, expansion, gain_a, gain_b, held):
    part, wide = projection_in.shape
    inside = pl.BlockSpec(memory_space=pltpu.VMEM)
    shapes = [(part, wide), (1, part), (part, wide // 3), (part, wide), (1, part), (held, wide // 3)]
    return pl.pallas_call(
        finish_kernel,
        in_specs=[pl.BlockSpec(memory_space=pltpu.SMEM)] + [inside] * 6,
        out_specs=[inside] * 6,
        out_shape=[jax.ShapeDtypeStruct(shape, F32) for shape in shapes],
        compiler_params=pltpu.CompilerParams(vmem_limit_bytes=48 * 2**20),
        name="finish",
    )(where, mine, other, projection_in, expansion, gain_a[None], gain_b[None])


def local(size, ranks, tokens, gain_a, projection_in, attention_out, gain_b, expansion, contraction, cotangent):
    z = lax.axis_index("fsdp")
    r = lax.axis_index("rep")
    core = r & 1
    group = 2 * core + (z & 1)
    home = core == z >> 1
    own = tokens[0]
    count, width = own.shape
    part = width // size
    hidden = contraction.shape[0]
    heads = HEADS // size

    stages = list(range(len(far(ranks))))
    where = jnp.stack([z, core]).astype(jnp.int32)
    columns = [projection_in[:, t * width : (t + 1) * width] for t in range(3)]
    piece = split_rows(jnp.concatenate(columns, axis=0), r, ranks)
    rows = piece.shape[0]
    gains = jnp.pad(jnp.concatenate([gain_a, gain_b])[None], ((0, 7), (0, width - 2 * part)))
    pieces = jnp.stack(exchange([jnp.concatenate([piece, gains], axis=0)] * size, size))
    gains = reorder(pieces[:, rows, : 2 * part], z, size).astype(F32)
    gain_one = gains[:, :part].reshape(1, width)
    gain_two = gains[:, part:].reshape(1, width)
    freqs = THETA ** (-(jnp.arange(HALF, dtype=F32) * (2.0 / HEAD_DIM)))
    places = jnp.concatenate([(group ^ d) * count + jnp.arange(count, dtype=jnp.int32) for d in range(size)])
    angles = freqs[:, None] * places.astype(F32)[None, :]
    early = (gain_one, gain_two, jnp.cos(angles), jnp.sin(angles))
    pair, other, first, second, early = collect(own, home, size, ranks, early)
    gain_one, gain_two, cosine, sine = early
    into = grow(pieces[:, :rows], r, ranks, stages[:-1])
    into = grow(after(into, first), r, ranks, stages[-1:])
    into_other = swap(into, "rep", ranks, 1)
    normed, queries, keys, values = project(
        where, pair, other, gain_one, cosine, sine, into, into_other, count
    )

    columns = [expansion[:, t * width : (t + 1) * width] for t in range(3)]
    stacked = jnp.concatenate([attention_out] + columns + [contraction], axis=0)
    pad = -stacked.shape[0] % max(32, 8 * ranks)
    stacked = jnp.concatenate([stacked, jnp.zeros((pad, width), BF16)], axis=0)
    rest = exchange([split_rows(after(stacked, second), r, ranks)] * size, size)
    merged = []
    logs = []
    for head in range(heads):
        out, log = attend(head, queries, after(keys, *merged[-1:]), values)
        merged.append(out)
        logs.append(log)
    rest = jnp.stack(after(rest, merged[0]))
    for stage in stages[:-1]:
        rest = join(rest, after(stage_swap(rest, ranks, stage), merged[-1]), stage_upper(r, ranks, stage))
    own_merged = jnp.concatenate(merged, axis=0)
    merged = trade_out([own_merged[:, d * count : (d + 1) * count] for d in range(size)], size, ranks)
    coming = after(stage_swap(rest, ranks, stages[-1]), *merged)
    rest = join(rest, coming, stage_upper(r, ranks, stages[-1]))
    rest_other = swap(rest, "rep", ranks, 1)
    upstream = cotangent[0]
    block_output, state_back, state_low, normed_two, active, inner_back, *merged_back = forward_back(
        where, merged, own, upstream, gain_two, [rest, rest_other], size * hidden
    )
    arrived = trade_back(merged_back, size, ranks)
    own_upstream = arrived

    kept, sent = gradients(
        where, merged, upstream, state_low, normed_two, active, inner_back, stacked.shape[0]
    )
    sent = after(sent, *arrived[:3])
    other = swap(sent, "rep", ranks, 1)
    upper = stage_upper(r, ranks, stages[-1])
    (sent, kept), (other_sent, other) = cut(kept, upper), cut(other, upper)
    sent = add(sent, other_sent)

    turned_backs = []
    weight_backs = []
    received = []
    ahead = [sent]
    for head in range(heads):
        grad, weight_grad = attend_back(
            head, queries, keys, values, after(own_upstream, *ahead), own_merged, logs[head],
            cosine, sine, normed,
        )
        turned_backs.append(grad)
        weight_backs.append(weight_grad.reshape(3, HEAD_DIM, width))
        received.append(trade_out([grad[:, d * count : (d + 1) * count] for d in range(size)], size, ranks))
        if head == 0:
            coming = stage_swap(sent, ranks, stages[-1])
            grads = (kept.astype(F32) + other.astype(F32) + coming.astype(F32)).astype(BF16)
            grads = shrink(grads, r, ranks, stages[-2:0:-1])
            ahead = [grads]
        if head == 1:
            grads = shrink(grads, r, ranks, stages[:1])
            ahead = [grads] + received[0]

    sent, kept = [jnp.stack([pick(grads, bit), pick(grads, bit + 2)]) for bit in (z & 1 ^ 1, z & 1)]
    grads = add(kept, swap(sent, "fsdp", size, 1))
    weight_backs[2], grads = after((weight_backs[2], grads), turned_backs[2], *received[1][:2])
    into_grad = jnp.concatenate([grad[t] for t in range(3) for grad in weight_backs], axis=0)
    later, last = received[1:]
    into_grad = after(shrink(into_grad[None], r, ranks, stages[-1:]), later[2], last[0])
    into_grad = after(shrink(into_grad, r, ranks, stages[-2::-1]), later[3], last[1])[0]
    grads = add(pick(grads, z >> 1), swap(pick(grads, z >> 1 ^ 1), "fsdp", size, 2))
    lines = into_grad.shape[0]
    blocks = into_grad.reshape(lines, size, part).transpose(1, 0, 2)
    blocks = exchange([pick(blocks, z ^ d) for d in range(size)], size)
    even, odd = (blocks[0].astype(F32) + blocks[2].astype(F32)), (blocks[1].astype(F32) + blocks[3].astype(F32))
    low = z & 1 == 0
    flat = jnp.concatenate([jnp.where(low, even, odd), jnp.where(low, odd, even)], axis=1).astype(BF16)
    both = grow_flat(jnp.concatenate([flat, grads], axis=0)[None], r, ranks, stages[:-1])
    both = grow_flat(after(both, *last[2:]), r, ranks, stages[-1:])
    token_grad = token_back(where, received, into, into_other, own, state_back, gain_one)[None]
    both = after(both, token_grad)
    into_sum, gain_one_sum, attention_out_sum, expansion_sum, gain_two_sum, contraction_sum = finish(
        where, both, swap(both, "rep", ranks, 1), projection_in, expansion, gain_a, gain_b, hidden
    )
    return (
        block_output[None],
        token_grad,
        gain_one_sum[0],
        into_sum,
        attention_out_sum,
        gain_two_sum[0],
        expansion_sum,
        contraction_sum,
    )


def solution(mesh):
    tokens, rows, line = P("rep", "fsdp", None), P("fsdp", None), P("fsdp")
    in_specs = (tokens, line, rows, rows, line, rows, rows, tokens)
    out_specs = (tokens, tokens, line, rows, rows, line, rows, rows)
    body = functools.partial(local, mesh.shape["fsdp"], mesh.shape["rep"])
    return jax.shard_map(body, mesh=mesh, in_specs=in_specs, out_specs=out_specs, check_vma=False)
```

```python
import functools
import math

import jax
import jax.numpy as jnp
from jax import lax
from jax.experimental import pallas as pl
from jax.experimental.pallas import tpu as pltpu
from jax.sharding import PartitionSpec as P

HEADS = 12
HEAD_DIM = 64
HALF = HEAD_DIM // 2
SCALE = 1.0 / math.sqrt(HEAD_DIM)
EPS = 1e-05
THETA = 160000.0
F32 = jnp.float32
BF16 = jnp.bfloat16
NN = (((1,), (0,)), ((), ()))
NT = (((1,), (1,)), ((), ()))
TN = (((0,), (0,)), ((), ()))
TT = (((0,), (1,)), ((), ()))


def mul(a, b, dims=NN):
    return lax.dot_general(a, b, dims, preferred_element_type=F32)


def attend_kernel(q_ref, k_ref, v_ref, out_ref, log_ref):
    scores = mul(k_ref[...].T, q_ref[...])
    highest = jnp.max(scores, axis=0, keepdims=True)
    raised = jnp.exp(scores - highest)
    total = jnp.sum(raised, axis=0, keepdims=True)
    mixed = mul(v_ref[...], raised.astype(BF16))
    out_ref[...] = (mixed / total).astype(BF16)
    log_ref[...] = highest + jnp.log(total)


def attend(head, queries, keys, values, step=1024):
    count = queries.shape[1]
    step = min(step, count)
    whole = pl.BlockSpec((HEAD_DIM, count), lambda i: (head, 0))
    return pl.pallas_call(
        attend_kernel,
        grid=(count // step,),
        in_specs=[pl.BlockSpec((HEAD_DIM, step), lambda i: (head, i)), whole, whole],
        out_specs=[
            pl.BlockSpec((HEAD_DIM, step), lambda i: (0, i)),
            pl.BlockSpec((1, step), lambda i: (0, i)),
        ],
        out_shape=[
            jax.ShapeDtypeStruct((HEAD_DIM, count), BF16),
            jax.ShapeDtypeStruct((1, count), F32),
        ],
        compiler_params=pltpu.CompilerParams(vmem_limit_bytes=26 * 2**20),
        cost_estimate=pl.CostEstimate(
            flops=28 * count * count * HEAD_DIM,
            bytes_accessed=8 * HEAD_DIM * count,
            transcendentals=count * count,
        ),
        name="attend",
    )(queries, keys, values)


def turn_back(values, cosine, sine):
    first, second = values[:HALF], values[HALF:]
    return jnp.concatenate([first * cosine + second * sine, second * cosine - first * sine], axis=0)


def attend_back_kernel(
    q_ref, kt_ref, vt_ref, u0_ref, u1_ref, u2_ref, u3_ref, out_ref, log_ref, cos_ref, sin_ref, normed_ref,
    grad_ref, weight_ref, up_ref, k_ref, v_ref, dk_ref, dv_ref,
):
    index = pl.program_id(0)
    step = q_ref.shape[1]

    @pl.when(index == 0)
    def _():
        for d, ref in enumerate((u0_ref, u1_ref, u2_ref, u3_ref)):
            up_ref[d] = ref[...]
        k_ref[...] = kt_ref[...].T
        v_ref[...] = vt_ref[...].T
        dk_ref[...] = jnp.zeros_like(dk_ref)
        dv_ref[...] = jnp.zeros_like(dv_ref)

    upstream = up_ref[index]
    inner_sum = jnp.sum(upstream.astype(F32) * out_ref[...].astype(F32), axis=0, keepdims=True)
    chances = jnp.exp(mul(k_ref[...], q_ref[...]) - log_ref[...])
    prob_back = mul(v_ref[...], upstream)
    score_back = (chances * (prob_back - inner_sum)).astype(BF16)
    dv_ref[...] += mul(chances.astype(BF16), upstream, NT)
    dk_ref[...] += mul(score_back, q_ref[...], NT)
    columns = pl.ds(pl.multiple_of(index * step, step), step)
    query_back = mul(kt_ref[...], score_back) * SCALE
    grad_ref[pl.ds(0, HEAD_DIM), columns] = turn_back(
        query_back, cos_ref[:, columns], sin_ref[:, columns]
    ).astype(BF16)

    @pl.when(index == pl.num_programs(0) - 1)
    def _():
        key_back = turn_back(dk_ref[...].T, cos_ref[...], sin_ref[...])
        grad_ref[pl.ds(HEAD_DIM, HEAD_DIM), :] = key_back.astype(BF16)
        grad_ref[pl.ds(2 * HEAD_DIM, HEAD_DIM), :] = dv_ref[...].T.astype(BF16)
        weight_ref[...] = mul(grad_ref[...], normed_ref[...]).astype(BF16)


def attend_back(head, queries, keys, values, upstream, merged, log, cosine, sine, normed):
    count, width = normed.shape
    step = upstream[0].shape[1]
    some = pl.BlockSpec((HEAD_DIM, step), lambda i: (head, i))
    whole = pl.BlockSpec((HEAD_DIM, count), lambda i: (head, 0))
    table = pl.BlockSpec((HALF, count), lambda i: (0, 0))
    return pl.pallas_call(
        attend_back_kernel,
        grid=(count // step,),
        in_specs=[
            some,
            whole,
            whole,
            *[pl.BlockSpec((HEAD_DIM, step), lambda i: (head, 0))] * len(upstream),
            some,
            pl.BlockSpec((1, step), lambda i: (0, i)),
            table,
            table,
            pl.BlockSpec((count, width), lambda i: (0, 0)),
        ],
        out_specs=[
            pl.BlockSpec((3 * HEAD_DIM, count), lambda i: (0, 0)),
            pl.BlockSpec((3 * HEAD_DIM, width), lambda i: (0, 0)),
        ],
        out_shape=[
            jax.ShapeDtypeStruct((3 * HEAD_DIM, count), BF16),
            jax.ShapeDtypeStruct((3 * HEAD_DIM, width), BF16),
        ],
        scratch_shapes=[
            pltpu.VMEM((len(upstream), HEAD_DIM, step), BF16),
            pltpu.VMEM((count, HEAD_DIM), BF16),
            pltpu.VMEM((count, HEAD_DIM), BF16),
            pltpu.VMEM((count, HEAD_DIM), F32),
            pltpu.VMEM((count, HEAD_DIM), F32),
        ],
        compiler_params=pltpu.CompilerParams(vmem_limit_bytes=24 * 2**20),
        cost_estimate=pl.CostEstimate(
            flops=56 * count * count * HEAD_DIM,
            bytes_accessed=16 * HEAD_DIM * count,
            transcendentals=count * count,
        ),
        name="attend_back",
    )(queries, keys, values, *upstream, merged, log, cosine, sine, normed)


def row_copies(place_ref, mine, other, buffer, sems):
    z, core = place_ref[0], place_ref[1]
    size, rows, _ = mine.shape
    copies = []
    for d in range(size):
        for k, (ref, side) in enumerate(((mine, core), (other, 1 - core))):
            target = buffer.at[z ^ d, pl.ds(pl.multiple_of(side * rows, 16), rows), :]
            copies.append(pltpu.make_async_copy(ref.at[d], target, sems.at[d, k]))
    return copies


def unit_of(values):
    centre = values - jnp.mean(values, axis=-1, keepdims=True)
    inverse = lax.rsqrt(jnp.mean(centre * centre, axis=-1, keepdims=True) + EPS)
    return centre * inverse, inverse


def turn(values, cosine, sine):
    first, second = values[:HALF], values[HALF:]
    return jnp.concatenate([first * cosine - second * sine, second * cosine + first * sine], axis=0)


def project_kernel(
    place_ref, pair_ref, other_ref, gain_ref, cos_ref, sin_ref, mine_ref, theirs_ref,
    normed_ref, q_ref, kt_ref, vt_ref, buffer, weight, sems,
):
    index = pl.program_id(0)
    part = q_ref.shape[0]
    size = buffer.shape[0]

    @pl.when(index == 0)
    def _():
        for copy in row_copies(place_ref, mine_ref, theirs_ref, buffer, sems):
            copy.start()

    block = jnp.where(index < 2, pair_ref[...].astype(F32), other_ref[...].astype(F32))
    normed = (unit_of(block)[0] * gain_ref[...]).astype(BF16)
    normed_ref[...] = normed

    @pl.when(index == 0)
    def _():
        for copy in row_copies(place_ref, mine_ref, theirs_ref, buffer, sems):
            copy.wait()
        start = pl.multiple_of(place_ref[1] * 2 * part, 128)
        odd = place_ref[0] & 1 == 1
        for t in range(3):
            both = buffer[:, t * part : (t + 1) * part, pl.ds(start, 2 * part)].reshape(size * part, 2 * part)
            chosen = jnp.where(odd, both[:, part:].astype(F32), both[:, :part].astype(F32))
            weight[:, t * part : (t + 1) * part] = chosen.astype(BF16)

    projected = mul(normed, weight[...])
    turned = projected[:, : 2 * part].T
    cosine, sine = cos_ref[...], sin_ref[...]
    for head in range(part // HEAD_DIM):
        rows = slice(head * HEAD_DIM, (head + 1) * HEAD_DIM)
        queries = turn(turned[rows], cosine, sine).astype(BF16)
        q_ref[rows, :] = (queries.astype(F32) * SCALE).astype(BF16)
        keys = turn(turned[part + head * HEAD_DIM : part + (head + 1) * HEAD_DIM], cosine, sine)
        kt_ref[rows, :] = keys.astype(BF16)
    vt_ref[...] = projected[:, 2 * part :].astype(BF16).T


def project(where, pair, other, gain, cosine, sine, mine, theirs, count):
    width = pair.shape[1]
    size, rows = mine.shape[0], 2 * mine.shape[1]
    part = width // size
    total = size * count
    anywhere = pl.BlockSpec(memory_space=pl.ANY)
    columns = pl.BlockSpec((part, count), lambda i: (0, i))
    return pl.pallas_call(
        project_kernel,
        grid=(size,),
        in_specs=[
            pl.BlockSpec(memory_space=pltpu.SMEM),
            pl.BlockSpec((count, width), lambda i: (jnp.minimum(i, 1), 0)),
            pl.BlockSpec((count, width), lambda i: (jnp.maximum(i - 2, 0), 0)),
            pl.BlockSpec((1, width), lambda i: (0, 0)),
            pl.BlockSpec((HALF, count), lambda i: (0, i)),
            pl.BlockSpec((HALF, count), lambda i: (0, i)),
            anywhere,
            anywhere,
        ],
        out_specs=[
            pl.BlockSpec((count, width), lambda i: (i, 0)),
            columns,
            columns,
            columns,
        ],
        out_shape=[
            jax.ShapeDtypeStruct((total, width), BF16),
            jax.ShapeDtypeStruct((part, total), BF16),
            jax.ShapeDtypeStruct((part, total), BF16),
            jax.ShapeDtypeStruct((part, total), BF16),
        ],
        scratch_shapes=[
            pltpu.VMEM((size, rows, width), BF16),
            pltpu.VMEM((width, 3 * part), BF16),
            pltpu.SemaphoreType.DMA((size, 2)),
        ],
        compiler_params=pltpu.CompilerParams(vmem_limit_bytes=18 * 2**20),
        cost_estimate=pl.CostEstimate(flops=8 * 10**9, bytes_accessed=20 * 10**6, transcendentals=0),
        name="project",
    )(where, pair, other, gain, cosine, sine, mine, theirs)


def forward_back_kernel(
    place_ref, m0_ref, m1_ref, m2_ref, m3_ref, tokens_ref, up_ref, gain_ref, mine_ref, theirs_ref,
    result_ref, state_back_ref, low_ref, normed_ref, active_ref, inner_back_ref, b0_ref, b1_ref, b2_ref, b3_ref,
    buffer, sems,
):
    part, width = m0_ref.shape[0], tokens_ref.shape[1]
    size = buffer.shape[0]
    hidden = active_ref.shape[1]
    z = place_ref[0]

    @pl.when(pl.program_id(0) == 0)
    def _():
        copies = row_copies(place_ref, mine_ref, theirs_ref, buffer, sems)
        for copy in copies:
            copy.start()
        for copy in copies:
            copy.wait()

    expand = [buffer[:, (1 + t) * part : (2 + t) * part, :].reshape(width, width) for t in range(3)]
    contract = buffer[:, 4 * part : 4 * part + hidden // size, :].reshape(hidden, width)
    gain = gain_ref[...]

    state = tokens_ref[...].astype(F32)
    for k, ref in enumerate((m0_ref, m1_ref, m2_ref, m3_ref)):
        state = state + mul(ref[...], buffer[z ^ k, :part, :], TN)
    unit, inverse = unit_of(state)
    normed = (unit * gain).astype(BF16)
    normed_ref[...] = normed
    inner = jnp.concatenate([mul(normed, weight) for weight in expand], axis=1)
    first, second = inner[:, :hidden], inner[:, hidden:]
    chance = 0.5 + 0.5 * lax.erf(first * math.sqrt(0.5))
    gated = first * chance
    slope = chance + first * (jnp.exp(-0.5 * first * first) * (1.0 / math.sqrt(2.0 * math.pi)))
    active = (gated * second).astype(BF16)
    active_ref[...] = active
    result_ref[...] = (state + mul(active, contract)).astype(BF16)

    upstream = up_ref[...]
    active_back = mul(upstream, contract, NT).astype(BF16).astype(F32)
    inner_back = jnp.concatenate(
        [(active_back * second * slope).astype(BF16), (active_back * gated).astype(BF16)], axis=1
    )
    inner_back_ref[...] = inner_back
    normed_back = mul(inner_back[:, :width], expand[0], NT)
    normed_back = normed_back + mul(inner_back[:, width : 2 * width], expand[1], NT)
    normed_back = normed_back + mul(inner_back[:, 2 * width :], expand[2], NT)
    scaled = normed_back * gain
    mean = jnp.mean(scaled, axis=-1, keepdims=True)
    lean = jnp.mean(scaled * unit, axis=-1, keepdims=True)
    state_back = upstream.astype(F32) + inverse * (scaled - mean - unit * lean)
    state_back_ref[...] = state_back
    low = state_back.astype(BF16)
    low_ref[...] = low
    for k, ref in enumerate((b0_ref, b1_ref, b2_ref, b3_ref)):
        ref[...] = mul(buffer[z ^ k, :part, :], low, NT).astype(BF16)


def forward_back(where, merged, tokens, upstream, gain, sides, hidden, step=256):
    count, width = tokens.shape
    size, rows = sides[0].shape[0], 2 * sides[0].shape[1]
    part = width // size
    anywhere = pl.BlockSpec(memory_space=pl.ANY)
    columns = pl.BlockSpec((part, step), lambda i: (0, i))

    def some(lanes):
        return pl.BlockSpec((step, lanes), lambda i: (i, 0))

    lanes = [width, width, width, width, hidden, 2 * hidden]
    kinds = [BF16, F32, BF16, BF16, BF16, BF16]
    return pl.pallas_call(
        forward_back_kernel,
        grid=(count // step,),
        in_specs=[pl.BlockSpec(memory_space=pltpu.SMEM)]
        + [columns] * size
        + [some(width), some(width), pl.BlockSpec((1, width), lambda i: (0, 0))]
        + [anywhere] * len(sides),
        out_specs=[some(n) for n in lanes] + [columns] * size,
        out_shape=[jax.ShapeDtypeStruct((count, n), kind) for n, kind in zip(lanes, kinds)]
        + [jax.ShapeDtypeStruct((part, count), BF16)] * size,
        scratch_shapes=[pltpu.VMEM((size, rows, width), BF16), pltpu.SemaphoreType.DMA((size, 2))],
        compiler_params=pltpu.CompilerParams(vmem_limit_bytes=26 * 2**20),
        cost_estimate=pl.CostEstimate(flops=14 * 10**9, bytes_accessed=20 * 10**6, transcendentals=0),
        name="forward_back",
    )(where, *merged, tokens, upstream, gain, *sides)


def gradients_kernel(
    place_ref, m0_ref, m1_ref, m2_ref, m3_ref, up_ref, low_ref, normed_ref, active_ref, inner_back_ref,
    kept_ref, sent_ref,
):
    z, core = place_ref[0], place_ref[1]
    part, width = m0_ref.shape[0], up_ref.shape[1]
    size, rows, lanes = kept_ref.shape
    held = active_ref.shape[1] // size
    for grads_ref, side in ((sent_ref, 1 - core), (kept_ref, core)):
        start = pl.multiple_of(side * lanes, 128)
        low = low_ref[:, pl.ds(start, lanes)]
        for k, ref in enumerate((m0_ref, m1_ref, m2_ref, m3_ref)):
            grads_ref[z ^ k, :part, :] = mul(ref[...], low).astype(BF16)
        normed = normed_ref[...]
        for t in range(3):
            grad = mul(normed, inner_back_ref[:, pl.ds(t * width + start, lanes)], TN)
            grads_ref[:, (1 + t) * part : (2 + t) * part, :] = grad.astype(BF16).reshape(size, part, lanes)
        grad = mul(active_ref[...], up_ref[:, pl.ds(start, lanes)], TN)
        grads_ref[:, 4 * part : 4 * part + held, :] = grad.astype(BF16).reshape(size, held, lanes)
        if rows > 4 * part + held:
            grads_ref[:, 4 * part + held :, :] = jnp.zeros((size, rows - 4 * part - held, lanes), BF16)


def gradients(where, merged, upstream, low, normed, active, inner_back, rows):
    size = len(merged)
    inside = pl.BlockSpec(memory_space=pltpu.VMEM)
    return pl.pallas_call(
        gradients_kernel,
        in_specs=[pl.BlockSpec(memory_space=pltpu.SMEM)] + [inside] * (size + 5),
        out_specs=[inside] * 2,
        out_shape=[jax.ShapeDtypeStruct((size, rows, upstream.shape[1] // 2), BF16)] * 2,
        compiler_params=pltpu.CompilerParams(vmem_limit_bytes=22 * 2**20),
        cost_estimate=pl.CostEstimate(flops=12 * 10**9, bytes_accessed=12 * 10**6, transcendentals=0),
        name="gradients",
    )(where, *merged, upstream, low, normed, active, inner_back)


def token_kernel(heads, place_ref, *refs):
    size = len(refs[: -9]) // heads
    pieces = refs[: heads * size]
    mine_ref, theirs_ref, tokens_ref, back_ref, gain_ref, grad_ref, parts, buffer, sems = refs[heads * size :]
    z = place_ref[0]
    width = buffer.shape[2]
    part = width // size
    copies = row_copies(place_ref, mine_ref, theirs_ref, buffer, sems)
    for copy in copies:
        copy.start()
    for head in range(heads):
        for k in range(size):
            ref = pieces[head * size + k]
            lines = pl.ds(pl.multiple_of((z ^ k) * part + head * HEAD_DIM, HEAD_DIM), HEAD_DIM)
            for t in range(3):
                parts[t, lines, :] = ref[t * HEAD_DIM : (t + 1) * HEAD_DIM, :]
    for copy in copies:
        copy.wait()
    total = jnp.zeros((width, tokens_ref.shape[0]), F32)
    for t in range(3):
        total = total + mul(buffer[:, t * part : (t + 1) * part, :].reshape(width, width), parts[t])
    unit, inverse = unit_of(tokens_ref[...].astype(F32))
    scaled = total.T * gain_ref[...]
    mean = jnp.mean(scaled, axis=-1, keepdims=True)
    lean = jnp.mean(scaled * unit, axis=-1, keepdims=True)
    grad_ref[...] = back_ref[...] + inverse * (scaled - mean - unit * lean)


def token_back(where, received, mine, theirs, tokens, state_back, gain):
    count, width = tokens.shape
    size, rows = mine.shape[0], 2 * mine.shape[1]
    inside = pl.BlockSpec(memory_space=pltpu.VMEM)
    anywhere = pl.BlockSpec(memory_space=pl.ANY)
    pieces = [piece for rounds in received for piece in rounds]
    return pl.pallas_call(
        functools.partial(token_kernel, len(received)),
        in_specs=[pl.BlockSpec(memory_space=pltpu.SMEM)]
        + [inside] * len(pieces)
        + [anywhere] * 2
        + [inside] * 3,
        out_specs=inside,
        out_shape=jax.ShapeDtypeStruct((count, width), F32),
        scratch_shapes=[
            pltpu.VMEM((3, width, count), BF16),
            pltpu.VMEM((size, rows, width), BF16),
            pltpu.SemaphoreType.DMA((size, 2)),
        ],
        compiler_params=pltpu.CompilerParams(vmem_limit_bytes=18 * 2**20),
        cost_estimate=pl.CostEstimate(flops=5 * 10**9, bytes_accessed=12 * 10**6, transcendentals=0),
        name="token_back",
    )(where, *pieces, mine, theirs, tokens, state_back, gain)


def after(values, *others):
    return lax.optimization_barrier((values, others))[0]


def swap(values, axis, size, offset):
    return lax.ppermute(values, axis, [(i, i ^ offset) for i in range(size)])


def exchange(pieces, size):
    return [pieces[0]] + [swap(pieces[d], "fsdp", size, d) for d in range(1, size)]


def column(values, size, ranks, pairs):
    full = [
        (z * ranks + r, to * ranks + (r & ~1) + core)
        for z in range(size)
        for r in range(ranks)
        for to, core in pairs(z, r & 1)
    ]
    return lax.ppermute(values, ("fsdp", "rep"), full)


def collect(own, home, size, ranks, early):
    first = column(
        own, size, ranks, lambda z, c: [(z ^ 1, c) if c == z >> 1 else (z ^ 2, 1 - c)]
    )
    second = column(first, size, ranks, lambda z, c: [] if c == z >> 1 else [(z ^ 1, c)])
    low = jnp.where(home, own, first)
    high = jnp.where(home, first, second)
    pair, early = after((jnp.concatenate([low, high], axis=0), early))
    other = swap(pair, "rep", ranks, 1)
    return pair, other, first, second, early


def trade_out(pieces, size, ranks, rounds=None):
    def round_of(k):
        return lambda z, c: [((2 * c + (z & 1)) ^ k, z >> 1)]

    return [column(pieces[k], size, ranks, round_of(k)) for k in rounds or range(size)]


def trade_back(pieces, size, ranks):
    def round_of(k):
        return lambda z, c: [(2 * c + ((z ^ k) & 1), (z ^ k) >> 1)]

    return [column(pieces[k], size, ranks, round_of(k)) for k in range(size)]


def pick(blocks, index):
    return lax.dynamic_index_in_dim(blocks, index, 0, keepdims=False)


def reorder(blocks, z, size):
    return jnp.stack([pick(blocks, z ^ j) for j in range(size)])


def far(ranks):
    bits = []
    bit = 2
    while bit < ranks:
        bits.append(bit)
        bit *= 2
    return bits


def stage_bit(core, ranks, stage):
    bits = far(ranks)
    return bits[stage] if core == 0 else bits[len(bits) - 1 - stage]


def stage_swap(values, ranks, stage):
    return lax.ppermute(values, "rep", [(i, i ^ stage_bit(i & 1, ranks, stage)) for i in range(ranks)])


def stage_upper(r, ranks, stage):
    bit = jnp.where(r & 1 == 0, stage_bit(0, ranks, stage), stage_bit(1, ranks, stage))
    return r & bit != 0


def place(r, ranks):
    stages = len(far(ranks))
    total = jnp.where(r & 1 != 0, 1 << stages, 0)
    for stage in range(stages):
        total = total + jnp.where(stage_upper(r, ranks, stage), 1 << stage, 0)
    return total


def join(mine, other, upper):
    return jnp.concatenate([jnp.where(upper, other, mine), jnp.where(upper, mine, other)], axis=1)


def cut(values, upper):
    half = values.shape[1] // 2
    mine = jnp.where(upper, half, 0)
    sent = lax.dynamic_slice_in_dim(values, half - mine, half, 1)
    return sent, lax.dynamic_slice_in_dim(values, mine, half, 1)


def add(one, two):
    return (one.astype(F32) + two.astype(F32)).astype(BF16)


def grow(values, r, ranks, stages):
    for stage in stages:
        values = join(values, stage_swap(values, ranks, stage), stage_upper(r, ranks, stage))
    return values


def grow_flat(values, r, ranks, stages):
    for stage in stages:
        other = stage_swap(values, ranks, stage)
        upper = stage_upper(r, ranks, stage)
        values = jnp.concatenate(
            [jnp.where(upper, other, values), jnp.where(upper, values, other)], axis=0
        )
    return values


def shrink(values, r, ranks, stages):
    for stage in stages:
        sent, kept = cut(values, stage_upper(r, ranks, stage))
        values = add(kept, stage_swap(sent, ranks, stage))
    return values


def halves(values):
    middle = values.shape[-1] // 2
    return [values[..., :middle], values[..., middle:]]


def split_rows(shard, r, ranks):
    rows = shard.shape[0] // ranks
    return lax.dynamic_slice_in_dim(shard, place(r, ranks) * rows, rows, 0)


def finish_kernel(
    place_ref, mine_ref, other_ref, into_ref, expand_ref, gain_a_ref, gain_b_ref,
    into_sum_ref, gain_a_sum_ref, out_sum_ref, expand_sum_ref, gain_b_sum_ref, contract_sum_ref,
):
    first = place_ref[1] == 0
    part, width = out_sum_ref.shape
    held = contract_sum_ref.shape[0]
    pieces = mine_ref.shape[0]
    lines = 3 * part // pieces

    def gathered(start):
        rows = mine_ref.shape[1] if start else lines
        sides = []
        for one, two in ((mine_ref, other_ref), (other_ref, mine_ref)):
            blocks = [
                jnp.where(first, one[p, start:rows].astype(F32), two[p, start:rows].astype(F32))
                for p in range(pieces)
            ]
            sides.append(jnp.concatenate(blocks, axis=0))
        return sides

    blocks = [side[:, k * part : (k + 1) * part].T for side in gathered(0) for k in range(2)]
    total = jnp.zeros((part, 1), F32)
    for t in range(3):
        row = jnp.concatenate([block[:, t * part : (t + 1) * part] for block in blocks], axis=1)
        into_sum_ref[:, t * width : (t + 1) * width] = row
        weight = into_ref[:, t * width : (t + 1) * width].astype(F32)
        total = total + jnp.sum(row * weight, axis=1, keepdims=True)
    gain_a_sum_ref[...] = total.T / gain_a_ref[...].astype(F32)

    grads = jnp.concatenate(gathered(lines), axis=1)
    out_sum_ref[...] = grads[:part]
    total = jnp.zeros((part, 1), F32)
    for t in range(3):
        row = grads[(1 + t) * part : (2 + t) * part]
        expand_sum_ref[:, t * width : (t + 1) * width] = row
        weight = expand_ref[:, t * width : (t + 1) * width].astype(F32)
        total = total + jnp.sum(row * weight, axis=1, keepdims=True)
    gain_b_sum_ref[...] = total.T / gain_b_ref[...].astype(F32)
    contract_sum_ref[...] = grads[4 * part : 4 * part + held]


def finish(where, mine, other, projection_in, expansion, gain_a, gain_b, held):
    part, wide = projection_in.shape
    inside = pl.BlockSpec(memory_space=pltpu.VMEM)
    shapes = [(part, wide), (1, part), (part, wide // 3), (part, wide), (1, part), (held, wide // 3)]
    return pl.pallas_call(
        finish_kernel,
        in_specs=[pl.BlockSpec(memory_space=pltpu.SMEM)] + [inside] * 6,
        out_specs=[inside] * 6,
        out_shape=[jax.ShapeDtypeStruct(shape, F32) for shape in shapes],
        compiler_params=pltpu.CompilerParams(vmem_limit_bytes=20 * 2**20),
        name="finish",
    )(where, mine, other, projection_in, expansion, gain_a[None], gain_b[None])


def local(size, ranks, tokens, gain_a, projection_in, attention_out, gain_b, expansion, contraction, cotangent):
    z = lax.axis_index("fsdp")
    r = lax.axis_index("rep")
    core = r & 1
    group = 2 * core + (z & 1)
    home = core == z >> 1
    own = tokens[0]
    count, width = own.shape
    part = width // size
    hidden = contraction.shape[0]
    heads = HEADS // size

    stages = list(range(len(far(ranks))))
    where = jnp.stack([z, core]).astype(jnp.int32)
    columns = [projection_in[:, t * width : (t + 1) * width] for t in range(3)]
    piece = split_rows(jnp.concatenate(columns, axis=0), r, ranks)
    rows = piece.shape[0]
    gains = jnp.pad(jnp.concatenate([gain_a, gain_b])[None], ((0, 7), (0, width - 2 * part)))
    pieces = jnp.stack(exchange([jnp.concatenate([piece, gains], axis=0)] * size, size))
    gains = reorder(pieces[:, rows, : 2 * part], z, size).astype(F32)
    gain_one = gains[:, :part].reshape(1, width)
    gain_two = gains[:, part:].reshape(1, width)
    freqs = THETA ** (-(jnp.arange(HALF, dtype=F32) * (2.0 / HEAD_DIM)))
    places = jnp.concatenate([(group ^ d) * count + jnp.arange(count, dtype=jnp.int32) for d in range(size)])
    angles = freqs[:, None] * places.astype(F32)[None, :]
    early = (gain_one, gain_two, jnp.cos(angles), jnp.sin(angles))
    pair, other, first, second, early = collect(own, home, size, ranks, early)
    gain_one, gain_two, cosine, sine = early
    into = grow(pieces[:, :rows], r, ranks, stages[:-1])
    into = grow(after(into, first), r, ranks, stages[-1:])
    into_other = swap(into, "rep", ranks, 1)
    normed, queries, keys, values = project(
        where, pair, other, gain_one, cosine, sine, into, into_other, count
    )

    columns = [expansion[:, t * width : (t + 1) * width] for t in range(3)]
    stacked = jnp.concatenate([attention_out] + columns + [contraction], axis=0)
    pad = -stacked.shape[0] % max(32, 8 * ranks)
    stacked = jnp.concatenate([stacked, jnp.zeros((pad, width), BF16)], axis=0)
    rest = exchange([split_rows(after(stacked, second), r, ranks)] * size, size)
    merged = []
    logs = []
    for head in range(heads):
        out, log = attend(head, queries, after(keys, *merged[-1:]), values)
        merged.append(out)
        logs.append(log)
    rest = jnp.stack(after(rest, merged[0]))
    for stage in stages[:-1]:
        rest = join(rest, after(stage_swap(rest, ranks, stage), merged[-1]), stage_upper(r, ranks, stage))
    own_merged = jnp.concatenate(merged, axis=0)
    merged = trade_out([own_merged[:, d * count : (d + 1) * count] for d in range(size)], size, ranks)
    coming = after(stage_swap(rest, ranks, stages[-1]), *merged)
    rest = join(rest, coming, stage_upper(r, ranks, stages[-1]))
    rest_other = swap(rest, "rep", ranks, 1)
    upstream = cotangent[0]
    block_output, state_back, state_low, normed_two, active, inner_back, *merged_back = forward_back(
        where, merged, own, upstream, gain_two, [rest, rest_other], size * hidden
    )
    arrived = trade_back(merged_back, size, ranks)
    own_upstream = arrived

    kept, sent = gradients(
        where, merged, upstream, state_low, normed_two, active, inner_back, stacked.shape[0]
    )
    sent = after(sent, *arrived[:3])
    other = swap(sent, "rep", ranks, 1)
    upper = stage_upper(r, ranks, stages[-1])
    (sent, kept), (other_sent, other) = cut(kept, upper), cut(other, upper)
    sent = add(sent, other_sent)

    turned_backs = []
    weight_backs = []
    received = []
    ahead = [sent]
    for head in range(heads):
        grad, weight_grad = attend_back(
            head, queries, keys, values, after(own_upstream, *ahead), own_merged, logs[head],
            cosine, sine, normed,
        )
        turned_backs.append(grad)
        weight_backs.append(weight_grad.reshape(3, HEAD_DIM, width))
        received.append(trade_out([grad[:, d * count : (d + 1) * count] for d in range(size)], size, ranks))
        if head == 0:
            coming = stage_swap(sent, ranks, stages[-1])
            grads = (kept.astype(F32) + other.astype(F32) + coming.astype(F32)).astype(BF16)
            grads = shrink(grads, r, ranks, stages[-2:0:-1])
            ahead = [grads]
        if head == 1:
            grads = shrink(grads, r, ranks, stages[:1])
            ahead = [grads] + received[0]

    sent, kept = [jnp.stack([pick(grads, bit), pick(grads, bit + 2)]) for bit in (z & 1 ^ 1, z & 1)]
    grads = add(kept, swap(sent, "fsdp", size, 1))
    weight_backs[2], grads = after((weight_backs[2], grads), turned_backs[2], *received[1][:2])
    into_grad = jnp.concatenate([grad[t] for t in range(3) for grad in weight_backs], axis=0)
    later, last = received[1:]
    into_grad = after(shrink(into_grad[None], r, ranks, stages[-1:]), later[2], last[0])
    into_grad = after(shrink(into_grad, r, ranks, stages[-2::-1]), later[3], last[1])[0]
    grads = add(pick(grads, z >> 1), swap(pick(grads, z >> 1 ^ 1), "fsdp", size, 2))
    lines = into_grad.shape[0]
    blocks = into_grad.reshape(lines, size, part).transpose(1, 0, 2)
    blocks = exchange([pick(blocks, z ^ d) for d in range(size)], size)
    even, odd = (blocks[0].astype(F32) + blocks[2].astype(F32)), (blocks[1].astype(F32) + blocks[3].astype(F32))
    low = z & 1 == 0
    flat = jnp.concatenate([jnp.where(low, even, odd), jnp.where(low, odd, even)], axis=1).astype(BF16)
    both = grow_flat(jnp.concatenate([flat, grads], axis=0)[None], r, ranks, stages[:-1])
    both = grow_flat(after(both, *last[2:]), r, ranks, stages[-1:])
    token_grad = token_back(where, received, into, into_other, own, state_back, gain_one)[None]
    both = after(both, token_grad)
    into_sum, gain_one_sum, attention_out_sum, expansion_sum, gain_two_sum, contraction_sum = finish(
        where, both, swap(both, "rep", ranks, 1), projection_in, expansion, gain_a, gain_b, hidden
    )
    return (
        block_output[None],
        token_grad,
        gain_one_sum[0],
        into_sum,
        attention_out_sum,
        gain_two_sum[0],
        expansion_sum,
        contraction_sum,
    )


def solution(mesh):
    tokens, rows, line = P("rep", "fsdp", None), P("fsdp", None), P("fsdp")
    in_specs = (tokens, line, rows, rows, line, rows, rows, tokens)
    out_specs = (tokens, tokens, line, rows, rows, line, rows, rows)
    body = functools.partial(local, mesh.shape["fsdp"], mesh.shape["rep"])
    return jax.shard_map(body, mesh=mesh, in_specs=in_specs, out_specs=out_specs, check_vma=False)
```

```python
import functools
import math

import jax
import jax.numpy as jnp
from jax import lax
from jax.experimental import pallas as pl
from jax.experimental.pallas import tpu as pltpu
from jax.sharding import PartitionSpec as P

HEADS = 12
HEAD_DIM = 64
HALF = HEAD_DIM // 2
SCALE = 1.0 / math.sqrt(HEAD_DIM)
EPS = 1e-05
THETA = 160000.0
F32 = jnp.float32
BF16 = jnp.bfloat16
NN = (((1,), (0,)), ((), ()))
NT = (((1,), (1,)), ((), ()))
TN = (((0,), (0,)), ((), ()))
TT = (((0,), (1,)), ((), ()))


def mul(a, b, dims=NN):
    return lax.dot_general(a, b, dims, preferred_element_type=F32)


def attend_kernel(q_ref, k_ref, v_ref, out_ref, log_ref):
    scores = mul(k_ref[...].T, q_ref[...])
    highest = jnp.max(scores, axis=0, keepdims=True)
    raised = jnp.exp(scores - highest)
    total = jnp.sum(raised, axis=0, keepdims=True)
    mixed = mul(v_ref[...], raised.astype(BF16))
    out_ref[...] = (mixed / total).astype(BF16)
    log_ref[...] = highest + jnp.log(total)


def attend(head, queries, keys, values, step=1024):
    count = queries.shape[1]
    step = min(step, count)
    whole = pl.BlockSpec((HEAD_DIM, count), lambda i: (head, 0))
    return pl.pallas_call(
        attend_kernel,
        grid=(count // step,),
        in_specs=[pl.BlockSpec((HEAD_DIM, step), lambda i: (head, i)), whole, whole],
        out_specs=[
            pl.BlockSpec((HEAD_DIM, step), lambda i: (0, i)),
            pl.BlockSpec((1, step), lambda i: (0, i)),
        ],
        out_shape=[
            jax.ShapeDtypeStruct((HEAD_DIM, count), BF16),
            jax.ShapeDtypeStruct((1, count), F32),
        ],
        compiler_params=pltpu.CompilerParams(vmem_limit_bytes=26 * 2**20),
        cost_estimate=pl.CostEstimate(
            flops=28 * count * count * HEAD_DIM,
            bytes_accessed=8 * HEAD_DIM * count,
            transcendentals=count * count,
        ),
        name="attend",
    )(queries, keys, values)


def turn_back(values, cosine, sine):
    first, second = values[:HALF], values[HALF:]
    return jnp.concatenate([first * cosine + second * sine, second * cosine - first * sine], axis=0)


def attend_back_kernel(
    q_ref, kt_ref, vt_ref, u0_ref, u1_ref, u2_ref, u3_ref, out_ref, log_ref, cos_ref, sin_ref, normed_ref,
    grad_ref, weight_ref, up_ref, k_ref, v_ref, dk_ref, dv_ref,
):
    index = pl.program_id(0)
    step = q_ref.shape[1]

    @pl.when(index == 0)
    def _():
        for d, ref in enumerate((u0_ref, u1_ref, u2_ref, u3_ref)):
            up_ref[d] = ref[...]
        k_ref[...] = kt_ref[...].T
        v_ref[...] = vt_ref[...].T
        dk_ref[...] = jnp.zeros_like(dk_ref)
        dv_ref[...] = jnp.zeros_like(dv_ref)

    upstream = up_ref[index]
    inner_sum = jnp.sum(upstream.astype(F32) * out_ref[...].astype(F32), axis=0, keepdims=True)
    chances = jnp.exp(mul(k_ref[...], q_ref[...]) - log_ref[...])
    prob_back = mul(v_ref[...], upstream)
    score_back = (chances * (prob_back - inner_sum)).astype(BF16)
    dv_ref[...] += mul(chances.astype(BF16), upstream, NT)
    dk_ref[...] += mul(score_back, q_ref[...], NT)
    columns = pl.ds(pl.multiple_of(index * step, step), step)
    query_back = mul(kt_ref[...], score_back) * SCALE
    grad_ref[pl.ds(0, HEAD_DIM), columns] = turn_back(
        query_back, cos_ref[:, columns], sin_ref[:, columns]
    ).astype(BF16)

    @pl.when(index == pl.num_programs(0) - 1)
    def _():
        key_back = turn_back(dk_ref[...].T, cos_ref[...], sin_ref[...])
        grad_ref[pl.ds(HEAD_DIM, HEAD_DIM), :] = key_back.astype(BF16)
        grad_ref[pl.ds(2 * HEAD_DIM, HEAD_DIM), :] = dv_ref[...].T.astype(BF16)
        weight_ref[...] = mul(grad_ref[...], normed_ref[...]).astype(BF16)


def attend_back(head, queries, keys, values, upstream, merged, log, cosine, sine, normed):
    count, width = normed.shape
    step = upstream[0].shape[1]
    some = pl.BlockSpec((HEAD_DIM, step), lambda i: (head, i))
    whole = pl.BlockSpec((HEAD_DIM, count), lambda i: (head, 0))
    table = pl.BlockSpec((HALF, count), lambda i: (0, 0))
    return pl.pallas_call(
        attend_back_kernel,
        grid=(count // step,),
        in_specs=[
            some,
            whole,
            whole,
            *[pl.BlockSpec((HEAD_DIM, step), lambda i: (head, 0))] * len(upstream),
            some,
            pl.BlockSpec((1, step), lambda i: (0, i)),
            table,
            table,
            pl.BlockSpec((count, width), lambda i: (0, 0)),
        ],
        out_specs=[
            pl.BlockSpec((3 * HEAD_DIM, count), lambda i: (0, 0)),
            pl.BlockSpec((3 * HEAD_DIM, width), lambda i: (0, 0)),
        ],
        out_shape=[
            jax.ShapeDtypeStruct((3 * HEAD_DIM, count), BF16),
            jax.ShapeDtypeStruct((3 * HEAD_DIM, width), BF16),
        ],
        scratch_shapes=[
            pltpu.VMEM((len(upstream), HEAD_DIM, step), BF16),
            pltpu.VMEM((count, HEAD_DIM), BF16),
            pltpu.VMEM((count, HEAD_DIM), BF16),
            pltpu.VMEM((count, HEAD_DIM), F32),
            pltpu.VMEM((count, HEAD_DIM), F32),
        ],
        compiler_params=pltpu.CompilerParams(vmem_limit_bytes=24 * 2**20),
        cost_estimate=pl.CostEstimate(
            flops=56 * count * count * HEAD_DIM,
            bytes_accessed=16 * HEAD_DIM * count,
            transcendentals=count * count,
        ),
        name="attend_back",
    )(queries, keys, values, *upstream, merged, log, cosine, sine, normed)


def row_copies(place_ref, mine, other, buffer, sems):
    z, core = place_ref[0], place_ref[1]
    size, rows, _ = mine.shape
    copies = []
    for d in range(size):
        for k, (ref, side) in enumerate(((mine, core), (other, 1 - core))):
            target = buffer.at[z ^ d, pl.ds(pl.multiple_of(side * rows, 16), rows), :]
            copies.append(pltpu.make_async_copy(ref.at[d], target, sems.at[d, k]))
    return copies


def unit_of(values):
    centre = values - jnp.mean(values, axis=-1, keepdims=True)
    inverse = lax.rsqrt(jnp.mean(centre * centre, axis=-1, keepdims=True) + EPS)
    return centre * inverse, inverse


def turn(values, cosine, sine):
    first, second = values[:HALF], values[HALF:]
    return jnp.concatenate([first * cosine - second * sine, second * cosine + first * sine], axis=0)


def project_kernel(
    place_ref, pair_ref, other_ref, gain_ref, cos_ref, sin_ref, mine_ref, theirs_ref,
    normed_ref, q_ref, kt_ref, vt_ref, buffer, weight, sems,
):
    index = pl.program_id(0)
    part = q_ref.shape[0]
    size = buffer.shape[0]

    @pl.when(index == 0)
    def _():
        for copy in row_copies(place_ref, mine_ref, theirs_ref, buffer, sems):
            copy.start()

    block = jnp.where(index < 2, pair_ref[...].astype(F32), other_ref[...].astype(F32))
    normed = (unit_of(block)[0] * gain_ref[...]).astype(BF16)
    normed_ref[...] = normed

    @pl.when(index == 0)
    def _():
        for copy in row_copies(place_ref, mine_ref, theirs_ref, buffer, sems):
            copy.wait()
        start = pl.multiple_of(place_ref[1] * 2 * part, 128)
        odd = place_ref[0] & 1 == 1
        for t in range(3):
            both = buffer[:, t * part : (t + 1) * part, pl.ds(start, 2 * part)].reshape(size * part, 2 * part)
            chosen = jnp.where(odd, both[:, part:].astype(F32), both[:, :part].astype(F32))
            weight[:, t * part : (t + 1) * part] = chosen.astype(BF16)

    projected = mul(normed, weight[...])
    turned = projected[:, : 2 * part].T
    cosine, sine = cos_ref[...], sin_ref[...]
    for head in range(part // HEAD_DIM):
        rows = slice(head * HEAD_DIM, (head + 1) * HEAD_DIM)
        queries = turn(turned[rows], cosine, sine).astype(BF16)
        q_ref[rows, :] = (queries.astype(F32) * SCALE).astype(BF16)
        keys = turn(turned[part + head * HEAD_DIM : part + (head + 1) * HEAD_DIM], cosine, sine)
        kt_ref[rows, :] = keys.astype(BF16)
    vt_ref[...] = projected[:, 2 * part :].astype(BF16).T


def project(where, pair, other, gain, cosine, sine, mine, theirs, count):
    width = pair.shape[1]
    size, rows = mine.shape[0], 2 * mine.shape[1]
    part = width // size
    total = size * count
    anywhere = pl.BlockSpec(memory_space=pl.ANY)
    columns = pl.BlockSpec((part, count), lambda i: (0, i))
    return pl.pallas_call(
        project_kernel,
        grid=(size,),
        in_specs=[
            pl.BlockSpec(memory_space=pltpu.SMEM),
            pl.BlockSpec((count, width), lambda i: (jnp.minimum(i, 1), 0)),
            pl.BlockSpec((count, width), lambda i: (jnp.maximum(i - 2, 0), 0)),
            pl.BlockSpec((1, width), lambda i: (0, 0)),
            pl.BlockSpec((HALF, count), lambda i: (0, i)),
            pl.BlockSpec((HALF, count), lambda i: (0, i)),
            anywhere,
            anywhere,
        ],
        out_specs=[
            pl.BlockSpec((count, width), lambda i: (i, 0)),
            columns,
            columns,
            columns,
        ],
        out_shape=[
            jax.ShapeDtypeStruct((total, width), BF16),
            jax.ShapeDtypeStruct((part, total), BF16),
            jax.ShapeDtypeStruct((part, total), BF16),
            jax.ShapeDtypeStruct((part, total), BF16),
        ],
        scratch_shapes=[
            pltpu.VMEM((size, rows, width), BF16),
            pltpu.VMEM((width, 3 * part), BF16),
            pltpu.SemaphoreType.DMA((size, 2)),
        ],
        compiler_params=pltpu.CompilerParams(vmem_limit_bytes=18 * 2**20),
        cost_estimate=pl.CostEstimate(flops=8 * 10**9, bytes_accessed=20 * 10**6, transcendentals=0),
        name="project",
    )(where, pair, other, gain, cosine, sine, mine, theirs)


def forward_back_kernel(
    place_ref, m0_ref, m1_ref, m2_ref, m3_ref, tokens_ref, up_ref, gain_ref, mine_ref, theirs_ref,
    result_ref, state_back_ref, low_ref, normed_ref, active_ref, inner_back_ref, b0_ref, b1_ref, b2_ref, b3_ref,
    buffer, sems,
):
    part, width = m0_ref.shape[0], tokens_ref.shape[1]
    size = buffer.shape[0]
    hidden = active_ref.shape[1]
    z = place_ref[0]

    @pl.when(pl.program_id(0) == 0)
    def _():
        copies = row_copies(place_ref, mine_ref, theirs_ref, buffer, sems)
        for copy in copies:
            copy.start()
        for copy in copies:
            copy.wait()

    expand = [buffer[:, (1 + t) * part : (2 + t) * part, :].reshape(width, width) for t in range(3)]
    contract = buffer[:, 4 * part : 4 * part + hidden // size, :].reshape(hidden, width)
    gain = gain_ref[...]

    state = tokens_ref[...].astype(F32)
    for k, ref in enumerate((m0_ref, m1_ref, m2_ref, m3_ref)):
        state = state + mul(ref[...], buffer[z ^ k, :part, :], TN)
    unit, inverse = unit_of(state)
    normed = (unit * gain).astype(BF16)
    normed_ref[...] = normed
    inner = jnp.concatenate([mul(normed, weight) for weight in expand], axis=1)
    first, second = inner[:, :hidden], inner[:, hidden:]
    chance = 0.5 + 0.5 * lax.erf(first * math.sqrt(0.5))
    gated = first * chance
    slope = chance + first * (jnp.exp(-0.5 * first * first) * (1.0 / math.sqrt(2.0 * math.pi)))
    active = (gated * second).astype(BF16)
    active_ref[...] = active
    result_ref[...] = (state + mul(active, contract)).astype(BF16)

    upstream = up_ref[...]
    active_back = mul(upstream, contract, NT).astype(BF16).astype(F32)
    inner_back = jnp.concatenate(
        [(active_back * second * slope).astype(BF16), (active_back * gated).astype(BF16)], axis=1
    )
    inner_back_ref[...] = inner_back
    normed_back = mul(inner_back[:, :width], expand[0], NT)
    normed_back = normed_back + mul(inner_back[:, width : 2 * width], expand[1], NT)
    normed_back = normed_back + mul(inner_back[:, 2 * width :], expand[2], NT)
    scaled = normed_back * gain
    mean = jnp.mean(scaled, axis=-1, keepdims=True)
    lean = jnp.mean(scaled * unit, axis=-1, keepdims=True)
    state_back = upstream.astype(F32) + inverse * (scaled - mean - unit * lean)
    state_back_ref[...] = state_back
    low = state_back.astype(BF16)
    low_ref[...] = low
    for k, ref in enumerate((b0_ref, b1_ref, b2_ref, b3_ref)):
        ref[...] = mul(buffer[z ^ k, :part, :], low, NT).astype(BF16)


def forward_back(where, merged, tokens, upstream, gain, sides, hidden, step=256):
    count, width = tokens.shape
    size, rows = sides[0].shape[0], 2 * sides[0].shape[1]
    part = width // size
    anywhere = pl.BlockSpec(memory_space=pl.ANY)
    columns = pl.BlockSpec((part, step), lambda i: (0, i))

    def some(lanes):
        return pl.BlockSpec((step, lanes), lambda i: (i, 0))

    lanes = [width, width, width, width, hidden, 2 * hidden]
    kinds = [BF16, F32, BF16, BF16, BF16, BF16]
    return pl.pallas_call(
        forward_back_kernel,
        grid=(count // step,),
        in_specs=[pl.BlockSpec(memory_space=pltpu.SMEM)]
        + [columns] * size
        + [some(width), some(width), pl.BlockSpec((1, width), lambda i: (0, 0))]
        + [anywhere] * len(sides),
        out_specs=[some(n) for n in lanes] + [columns] * size,
        out_shape=[jax.ShapeDtypeStruct((count, n), kind) for n, kind in zip(lanes, kinds)]
        + [jax.ShapeDtypeStruct((part, count), BF16)] * size,
        scratch_shapes=[pltpu.VMEM((size, rows, width), BF16), pltpu.SemaphoreType.DMA((size, 2))],
        compiler_params=pltpu.CompilerParams(vmem_limit_bytes=26 * 2**20),
        cost_estimate=pl.CostEstimate(flops=14 * 10**9, bytes_accessed=20 * 10**6, transcendentals=0),
        name="forward_back",
    )(where, *merged, tokens, upstream, gain, *sides)


def gradients_kernel(
    place_ref, m0_ref, m1_ref, m2_ref, m3_ref, up_ref, low_ref, normed_ref, active_ref, inner_back_ref,
    kept_ref, sent_ref,
):
    z, core = place_ref[0], place_ref[1]
    part, width = m0_ref.shape[0], up_ref.shape[1]
    size, rows, lanes = kept_ref.shape
    held = active_ref.shape[1] // size
    for grads_ref, side in ((sent_ref, 1 - core), (kept_ref, core)):
        start = pl.multiple_of(side * lanes, 128)
        low = low_ref[:, pl.ds(start, lanes)]
        for k, ref in enumerate((m0_ref, m1_ref, m2_ref, m3_ref)):
            grads_ref[z ^ k, :part, :] = mul(ref[...], low).astype(BF16)
        normed = normed_ref[...]
        for t in range(3):
            grad = mul(normed, inner_back_ref[:, pl.ds(t * width + start, lanes)], TN)
            grads_ref[:, (1 + t) * part : (2 + t) * part, :] = grad.astype(BF16).reshape(size, part, lanes)
        grad = mul(active_ref[...], up_ref[:, pl.ds(start, lanes)], TN)
        grads_ref[:, 4 * part : 4 * part + held, :] = grad.astype(BF16).reshape(size, held, lanes)
        if rows > 4 * part + held:
            grads_ref[:, 4 * part + held :, :] = jnp.zeros((size, rows - 4 * part - held, lanes), BF16)


def gradients(where, merged, upstream, low, normed, active, inner_back, rows):
    size = len(merged)
    inside = pl.BlockSpec(memory_space=pltpu.VMEM)
    return pl.pallas_call(
        gradients_kernel,
        in_specs=[pl.BlockSpec(memory_space=pltpu.SMEM)] + [inside] * (size + 5),
        out_specs=[inside] * 2,
        out_shape=[jax.ShapeDtypeStruct((size, rows, upstream.shape[1] // 2), BF16)] * 2,
        compiler_params=pltpu.CompilerParams(vmem_limit_bytes=22 * 2**20),
        cost_estimate=pl.CostEstimate(flops=12 * 10**9, bytes_accessed=12 * 10**6, transcendentals=0),
        name="gradients",
    )(where, *merged, upstream, low, normed, active, inner_back)


def token_kernel(heads, place_ref, *refs):
    size = len(refs[: -9]) // heads
    pieces = refs[: heads * size]
    mine_ref, theirs_ref, tokens_ref, back_ref, gain_ref, grad_ref, parts, buffer, sems = refs[heads * size :]
    z = place_ref[0]
    width = buffer.shape[2]
    part = width // size
    copies = row_copies(place_ref, mine_ref, theirs_ref, buffer, sems)
    for copy in copies:
        copy.start()
    for head in range(heads):
        for k in range(size):
            ref = pieces[head * size + k]
            lines = pl.ds(pl.multiple_of((z ^ k) * part + head * HEAD_DIM, HEAD_DIM), HEAD_DIM)
            for t in range(3):
                parts[t, lines, :] = ref[t * HEAD_DIM : (t + 1) * HEAD_DIM, :]
    for copy in copies:
        copy.wait()
    total = jnp.zeros((width, tokens_ref.shape[0]), F32)
    for t in range(3):
        total = total + mul(buffer[:, t * part : (t + 1) * part, :].reshape(width, width), parts[t])
    unit, inverse = unit_of(tokens_ref[...].astype(F32))
    scaled = total.T * gain_ref[...]
    mean = jnp.mean(scaled, axis=-1, keepdims=True)
    lean = jnp.mean(scaled * unit, axis=-1, keepdims=True)
    grad_ref[...] = back_ref[...] + inverse * (scaled - mean - unit * lean)


def token_back(where, received, mine, theirs, tokens, state_back, gain):
    count, width = tokens.shape
    size, rows = mine.shape[0], 2 * mine.shape[1]
    inside = pl.BlockSpec(memory_space=pltpu.VMEM)
    anywhere = pl.BlockSpec(memory_space=pl.ANY)
    pieces = [piece for rounds in received for piece in rounds]
    return pl.pallas_call(
        functools.partial(token_kernel, len(received)),
        in_specs=[pl.BlockSpec(memory_space=pltpu.SMEM)]
        + [inside] * len(pieces)
        + [anywhere] * 2
        + [inside] * 3,
        out_specs=inside,
        out_shape=jax.ShapeDtypeStruct((count, width), F32),
        scratch_shapes=[
            pltpu.VMEM((3, width, count), BF16),
            pltpu.VMEM((size, rows, width), BF16),
            pltpu.SemaphoreType.DMA((size, 2)),
        ],
        compiler_params=pltpu.CompilerParams(vmem_limit_bytes=18 * 2**20),
        cost_estimate=pl.CostEstimate(flops=5 * 10**9, bytes_accessed=12 * 10**6, transcendentals=0),
        name="token_back",
    )(where, *pieces, mine, theirs, tokens, state_back, gain)


def after(values, *others):
    return lax.optimization_barrier((values, others))[0]


def swap(values, axis, size, offset):
    return lax.ppermute(values, axis, [(i, i ^ offset) for i in range(size)])


def exchange(pieces, size):
    return [pieces[0]] + [swap(pieces[d], "fsdp", size, d) for d in range(1, size)]


def column(values, size, ranks, pairs):
    full = [
        (z * ranks + r, to * ranks + (r & ~1) + core)
        for z in range(size)
        for r in range(ranks)
        for to, core in pairs(z, r & 1)
    ]
    return lax.ppermute(values, ("fsdp", "rep"), full)


def collect(own, home, size, ranks, early):
    first = column(
        own, size, ranks, lambda z, c: [(z ^ 1, c) if c == z >> 1 else (z ^ 2, 1 - c)]
    )
    second = column(first, size, ranks, lambda z, c: [] if c == z >> 1 else [(z ^ 1, c)])
    low = jnp.where(home, own, first)
    high = jnp.where(home, first, second)
    pair, early = after((jnp.concatenate([low, high], axis=0), early))
    other = swap(pair, "rep", ranks, 1)
    return pair, other, first, second, early


def trade_out(pieces, size, ranks, rounds=None):
    def round_of(k):
        return lambda z, c: [((2 * c + (z & 1)) ^ k, z >> 1)]

    return [column(pieces[k], size, ranks, round_of(k)) for k in rounds or range(size)]


def trade_back(pieces, size, ranks):
    def round_of(k):
        return lambda z, c: [(2 * c + ((z ^ k) & 1), (z ^ k) >> 1)]

    return [column(pieces[k], size, ranks, round_of(k)) for k in range(size)]


def pick(blocks, index):
    return lax.dynamic_index_in_dim(blocks, index, 0, keepdims=False)


def reorder(blocks, z, size):
    return jnp.stack([pick(blocks, z ^ j) for j in range(size)])


def far(ranks):
    bits = []
    bit = 2
    while bit < ranks:
        bits.append(bit)
        bit *= 2
    return bits


def stage_bit(core, ranks, stage):
    bits = far(ranks)
    return bits[stage] if core == 0 else bits[len(bits) - 1 - stage]


def stage_swap(values, ranks, stage):
    return lax.ppermute(values, "rep", [(i, i ^ stage_bit(i & 1, ranks, stage)) for i in range(ranks)])


def stage_upper(r, ranks, stage):
    bit = jnp.where(r & 1 == 0, stage_bit(0, ranks, stage), stage_bit(1, ranks, stage))
    return r & bit != 0


def place(r, ranks):
    stages = len(far(ranks))
    total = jnp.where(r & 1 != 0, 1 << stages, 0)
    for stage in range(stages):
        total = total + jnp.where(stage_upper(r, ranks, stage), 1 << stage, 0)
    return total


def join(mine, other, upper):
    return jnp.concatenate([jnp.where(upper, other, mine), jnp.where(upper, mine, other)], axis=1)


def cut(values, upper):
    half = values.shape[1] // 2
    mine = jnp.where(upper, half, 0)
    sent = lax.dynamic_slice_in_dim(values, half - mine, half, 1)
    return sent, lax.dynamic_slice_in_dim(values, mine, half, 1)


def add(one, two):
    return (one.astype(F32) + two.astype(F32)).astype(BF16)


def grow(values, r, ranks, stages):
    for stage in stages:
        values = join(values, stage_swap(values, ranks, stage), stage_upper(r, ranks, stage))
    return values


def grow_flat(values, r, ranks, stages):
    for stage in stages:
        other = stage_swap(values, ranks, stage)
        upper = stage_upper(r, ranks, stage)
        values = jnp.concatenate(
            [jnp.where(upper, other, values), jnp.where(upper, values, other)], axis=0
        )
    return values


def shrink(values, r, ranks, stages):
    for stage in stages:
        sent, kept = cut(values, stage_upper(r, ranks, stage))
        values = add(kept, stage_swap(sent, ranks, stage))
    return values


def halves(values):
    middle = values.shape[-1] // 2
    return [values[..., :middle], values[..., middle:]]


def split_rows(shard, r, ranks):
    rows = shard.shape[0] // ranks
    return lax.dynamic_slice_in_dim(shard, place(r, ranks) * rows, rows, 0)


def finish_kernel(
    place_ref, mine_ref, other_ref, into_ref, expand_ref, gain_a_ref, gain_b_ref,
    into_sum_ref, gain_a_sum_ref, out_sum_ref, expand_sum_ref, gain_b_sum_ref, contract_sum_ref,
):
    first = place_ref[1] == 0
    part, width = out_sum_ref.shape
    held = contract_sum_ref.shape[0]
    pieces = mine_ref.shape[0]
    lines = 3 * part // pieces

    def gathered(start):
        rows = mine_ref.shape[1] if start else lines
        sides = []
        for one, two in ((mine_ref, other_ref), (other_ref, mine_ref)):
            blocks = [
                jnp.where(first, one[p, start:rows].astype(F32), two[p, start:rows].astype(F32))
                for p in range(pieces)
            ]
            sides.append(jnp.concatenate(blocks, axis=0))
        return sides

    blocks = [side[:, k * part : (k + 1) * part].T for side in gathered(0) for k in range(2)]
    total = jnp.zeros((part, 1), F32)
    for t in range(3):
        row = jnp.concatenate([block[:, t * part : (t + 1) * part] for block in blocks], axis=1)
        into_sum_ref[:, t * width : (t + 1) * width] = row
        weight = into_ref[:, t * width : (t + 1) * width].astype(F32)
        total = total + jnp.sum(row * weight, axis=1, keepdims=True)
    gain_a_sum_ref[...] = total.T / gain_a_ref[...].astype(F32)

    grads = jnp.concatenate(gathered(lines), axis=1)
    out_sum_ref[...] = grads[:part]
    total = jnp.zeros((part, 1), F32)
    for t in range(3):
        row = grads[(1 + t) * part : (2 + t) * part]
        expand_sum_ref[:, t * width : (t + 1) * width] = row
        weight = expand_ref[:, t * width : (t + 1) * width].astype(F32)
        total = total + jnp.sum(row * weight, axis=1, keepdims=True)
    gain_b_sum_ref[...] = total.T / gain_b_ref[...].astype(F32)
    contract_sum_ref[...] = grads[4 * part : 4 * part + held]


def finish(where, mine, other, projection_in, expansion, gain_a, gain_b, held):
    part, wide = projection_in.shape
    inside = pl.BlockSpec(memory_space=pltpu.VMEM)
    shapes = [(part, wide), (1, part), (part, wide // 3), (part, wide), (1, part), (held, wide // 3)]
    return pl.pallas_call(
        finish_kernel,
        in_specs=[pl.BlockSpec(memory_space=pltpu.SMEM)] + [inside] * 6,
        out_specs=[inside] * 6,
        out_shape=[jax.ShapeDtypeStruct(shape, F32) for shape in shapes],
        compiler_params=pltpu.CompilerParams(vmem_limit_bytes=20 * 2**20),
        name="finish",
    )(where, mine, other, projection_in, expansion, gain_a[None], gain_b[None])


def local(size, ranks, tokens, gain_a, projection_in, attention_out, gain_b, expansion, contraction, cotangent):
    z = lax.axis_index("fsdp")
    r = lax.axis_index("rep")
    core = r & 1
    group = 2 * core + (z & 1)
    home = core == z >> 1
    own = tokens[0]
    count, width = own.shape
    part = width // size
    hidden = contraction.shape[0]
    heads = HEADS // size

    stages = list(range(len(far(ranks))))
    where = jnp.stack([z, core]).astype(jnp.int32)
    columns = [projection_in[:, t * width : (t + 1) * width] for t in range(3)]
    piece = split_rows(jnp.concatenate(columns, axis=0), r, ranks)
    rows = piece.shape[0]
    gains = jnp.pad(jnp.concatenate([gain_a, gain_b])[None], ((0, 7), (0, width - 2 * part)))
    pieces = jnp.stack(exchange([jnp.concatenate([piece, gains], axis=0)] * size, size))
    gains = reorder(pieces[:, rows, : 2 * part], z, size).astype(F32)
    gain_one = gains[:, :part].reshape(1, width)
    gain_two = gains[:, part:].reshape(1, width)
    freqs = THETA ** (-(jnp.arange(HALF, dtype=F32) * (2.0 / HEAD_DIM)))
    places = jnp.concatenate([(group ^ d) * count + jnp.arange(count, dtype=jnp.int32) for d in range(size)])
    angles = freqs[:, None] * places.astype(F32)[None, :]
    early = (gain_one, gain_two, jnp.cos(angles), jnp.sin(angles))
    pair, other, first, second, early = collect(own, home, size, ranks, early)
    gain_one, gain_two, cosine, sine = early
    into = grow(pieces[:, :rows], r, ranks, stages[:-1])
    into = grow(after(into, first), r, ranks, stages[-1:])
    into_other = swap(into, "rep", ranks, 1)
    normed, queries, keys, values = project(
        where, pair, other, gain_one, cosine, sine, into, into_other, count
    )

    columns = [expansion[:, t * width : (t + 1) * width] for t in range(3)]
    stacked = jnp.concatenate([attention_out] + columns + [contraction], axis=0)
    pad = -stacked.shape[0] % max(32, 8 * ranks)
    stacked = jnp.concatenate([stacked, jnp.zeros((pad, width), BF16)], axis=0)
    rest = exchange([split_rows(after(stacked, second), r, ranks)] * size, size)
    merged = []
    logs = []
    for head in range(heads):
        out, log = attend(head, queries, after(keys, *merged[-1:]), values)
        merged.append(out)
        logs.append(log)
    rest = jnp.stack(after(rest, merged[0]))
    for stage in stages[:-1]:
        rest = join(rest, after(stage_swap(rest, ranks, stage), merged[-1]), stage_upper(r, ranks, stage))
    own_merged = jnp.concatenate(merged, axis=0)
    merged = trade_out([own_merged[:, d * count : (d + 1) * count] for d in range(size)], size, ranks)
    coming = after(stage_swap(rest, ranks, stages[-1]), *merged)
    rest = join(rest, coming, stage_upper(r, ranks, stages[-1]))
    rest_other = swap(rest, "rep", ranks, 1)
    upstream = cotangent[0]
    block_output, state_back, state_low, normed_two, active, inner_back, *merged_back = forward_back(
        where, merged, own, upstream, gain_two, [rest, rest_other], size * hidden
    )
    arrived = trade_back(merged_back, size, ranks)
    own_upstream = arrived

    kept, sent = gradients(
        where, merged, upstream, state_low, normed_two, active, inner_back, stacked.shape[0]
    )
    sent = after(sent, *arrived[:3])
    other = swap(sent, "rep", ranks, 1)
    upper = stage_upper(r, ranks, stages[-1])
    (sent, kept), (other_sent, other) = cut(kept, upper), cut(other, upper)
    sent = add(sent, other_sent)

    turned_backs = []
    weight_backs = []
    received = []
    ahead = [sent]
    for head in range(heads):
        grad, weight_grad = attend_back(
            head, queries, keys, values, after(own_upstream, *ahead), own_merged, logs[head],
            cosine, sine, normed,
        )
        turned_backs.append(grad)
        weight_backs.append(weight_grad.reshape(3, HEAD_DIM, width))
        received.append(trade_out([grad[:, d * count : (d + 1) * count] for d in range(size)], size, ranks))
        if head == 0:
            coming = stage_swap(sent, ranks, stages[-1])
            grads = (kept.astype(F32) + other.astype(F32) + coming.astype(F32)).astype(BF16)
            grads = shrink(grads, r, ranks, stages[-2:0:-1])
            ahead = [grads]
        if head == 1:
            grads = shrink(grads, r, ranks, stages[:1])
            ahead = [grads] + received[0]

    sent, kept = [jnp.stack([pick(grads, bit), pick(grads, bit + 2)]) for bit in (z & 1 ^ 1, z & 1)]
    grads = add(kept, swap(sent, "fsdp", size, 1))
    weight_backs[2], grads = after((weight_backs[2], grads), turned_backs[2], *received[1][:2])
    into_grad = jnp.concatenate([grad[t] for t in range(3) for grad in weight_backs], axis=0)
    later, last = received[1:]
    into_grad = after(shrink(into_grad[None], r, ranks, stages[-1:]), later[2], last[0])
    into_grad = after(shrink(into_grad, r, ranks, stages[-2::-1]), later[3], last[1])[0]
    grads = add(pick(grads, z >> 1), swap(pick(grads, z >> 1 ^ 1), "fsdp", size, 2))
    blocks = exchange(
        [lax.dynamic_slice_in_dim(into_grad, (z ^ d) * part, part, 1) for d in range(size)], size
    )
    even, odd = (blocks[0].astype(F32) + blocks[2].astype(F32)), (blocks[1].astype(F32) + blocks[3].astype(F32))
    low = z & 1 == 0
    flat = jnp.concatenate([jnp.where(low, even, odd), jnp.where(low, odd, even)], axis=1).astype(BF16)
    both = grow_flat(jnp.concatenate([flat, grads], axis=0)[None], r, ranks, stages[:-1])
    both = grow_flat(after(both, *last[2:]), r, ranks, stages[-1:])
    token_grad = token_back(where, received, into, into_other, own, state_back, gain_one)[None]
    both = after(both, token_grad)
    into_sum, gain_one_sum, attention_out_sum, expansion_sum, gain_two_sum, contraction_sum = finish(
        where, both, swap(both, "rep", ranks, 1), projection_in, expansion, gain_a, gain_b, hidden
    )
    return (
        block_output[None],
        token_grad,
        gain_one_sum[0],
        into_sum,
        attention_out_sum,
        gain_two_sum[0],
        expansion_sum,
        contraction_sum,
    )


def solution(mesh):
    tokens, rows, line = P("rep", "fsdp", None), P("fsdp", None), P("fsdp")
    in_specs = (tokens, line, rows, rows, line, rows, rows, tokens)
    out_specs = (tokens, tokens, line, rows, rows, line, rows, rows)
    body = functools.partial(local, mesh.shape["fsdp"], mesh.shape["rep"])
    return jax.shard_map(body, mesh=mesh, in_specs=in_specs, out_specs=out_specs, check_vma=False)
```

```python
import functools
import math

import jax
import jax.numpy as jnp
from jax import lax
from jax.experimental import pallas as pl
from jax.experimental.pallas import tpu as pltpu
from jax.sharding import PartitionSpec as P

HEADS = 12
HEAD_DIM = 64
HALF = HEAD_DIM // 2
SCALE = 1.0 / math.sqrt(HEAD_DIM)
EPS = 1e-05
THETA = 160000.0
F32 = jnp.float32
BF16 = jnp.bfloat16
NN = (((1,), (0,)), ((), ()))
NT = (((1,), (1,)), ((), ()))
TN = (((0,), (0,)), ((), ()))
TT = (((0,), (1,)), ((), ()))


def mul(a, b, dims=NN):
    return lax.dot_general(a, b, dims, preferred_element_type=F32)


def attend_kernel(q_ref, k_ref, v_ref, out_ref, log_ref):
    scores = mul(k_ref[...].T, q_ref[...])
    highest = jnp.max(scores, axis=0, keepdims=True)
    raised = jnp.exp(scores - highest)
    total = jnp.sum(raised, axis=0, keepdims=True)
    mixed = mul(v_ref[...], raised.astype(BF16))
    out_ref[...] = (mixed / total).astype(BF16)
    log_ref[...] = highest + jnp.log(total)


def attend(head, queries, keys, values, step=1024):
    count = queries.shape[1]
    step = min(step, count)
    whole = pl.BlockSpec((HEAD_DIM, count), lambda i: (head, 0))
    return pl.pallas_call(
        attend_kernel,
        grid=(count // step,),
        in_specs=[pl.BlockSpec((HEAD_DIM, step), lambda i: (head, i)), whole, whole],
        out_specs=[
            pl.BlockSpec((HEAD_DIM, step), lambda i: (0, i)),
            pl.BlockSpec((1, step), lambda i: (0, i)),
        ],
        out_shape=[
            jax.ShapeDtypeStruct((HEAD_DIM, count), BF16),
            jax.ShapeDtypeStruct((1, count), F32),
        ],
        compiler_params=pltpu.CompilerParams(vmem_limit_bytes=26 * 2**20),
        cost_estimate=pl.CostEstimate(
            flops=28 * count * count * HEAD_DIM,
            bytes_accessed=8 * HEAD_DIM * count,
            transcendentals=count * count,
        ),
        name="attend",
    )(queries, keys, values)


def turn_back(values, cosine, sine):
    first, second = values[:HALF], values[HALF:]
    return jnp.concatenate([first * cosine + second * sine, second * cosine - first * sine], axis=0)


def attend_back_kernel(
    q_ref, kt_ref, vt_ref, u0_ref, u1_ref, u2_ref, u3_ref, out_ref, log_ref, cos_ref, sin_ref, normed_ref,
    grad_ref, weight_ref, up_ref, k_ref, v_ref, dk_ref, dv_ref,
):
    index = pl.program_id(0)
    step = q_ref.shape[1]

    @pl.when(index == 0)
    def _():
        for d, ref in enumerate((u0_ref, u1_ref, u2_ref, u3_ref)):
            up_ref[d] = ref[...]
        k_ref[...] = kt_ref[...].T
        v_ref[...] = vt_ref[...].T
        dk_ref[...] = jnp.zeros_like(dk_ref)
        dv_ref[...] = jnp.zeros_like(dv_ref)

    upstream = up_ref[index]
    inner_sum = jnp.sum(upstream.astype(F32) * out_ref[...].astype(F32), axis=0, keepdims=True)
    chances = jnp.exp(mul(k_ref[...], q_ref[...]) - log_ref[...])
    prob_back = mul(v_ref[...], upstream)
    score_back = (chances * (prob_back - inner_sum)).astype(BF16)
    dv_ref[...] += mul(chances.astype(BF16), upstream, NT)
    dk_ref[...] += mul(score_back, q_ref[...], NT)
    columns = pl.ds(pl.multiple_of(index * step, step), step)
    query_back = mul(kt_ref[...], score_back) * SCALE
    grad_ref[pl.ds(0, HEAD_DIM), columns] = turn_back(
        query_back, cos_ref[:, columns], sin_ref[:, columns]
    ).astype(BF16)

    @pl.when(index == pl.num_programs(0) - 1)
    def _():
        key_back = turn_back(dk_ref[...].T, cos_ref[...], sin_ref[...])
        grad_ref[pl.ds(HEAD_DIM, HEAD_DIM), :] = key_back.astype(BF16)
        grad_ref[pl.ds(2 * HEAD_DIM, HEAD_DIM), :] = dv_ref[...].T.astype(BF16)
        weight_ref[...] = mul(grad_ref[...], normed_ref[...]).astype(BF16)


def attend_back(head, queries, keys, values, upstream, merged, log, cosine, sine, normed):
    count, width = normed.shape
    step = upstream[0].shape[1]
    some = pl.BlockSpec((HEAD_DIM, step), lambda i: (head, i))
    whole = pl.BlockSpec((HEAD_DIM, count), lambda i: (head, 0))
    table = pl.BlockSpec((HALF, count), lambda i: (0, 0))
    return pl.pallas_call(
        attend_back_kernel,
        grid=(count // step,),
        in_specs=[
            some,
            whole,
            whole,
            *[pl.BlockSpec((HEAD_DIM, step), lambda i: (head, 0))] * len(upstream),
            some,
            pl.BlockSpec((1, step), lambda i: (0, i)),
            table,
            table,
            pl.BlockSpec((count, width), lambda i: (0, 0)),
        ],
        out_specs=[
            pl.BlockSpec((3 * HEAD_DIM, count), lambda i: (0, 0)),
            pl.BlockSpec((3 * HEAD_DIM, width), lambda i: (0, 0)),
        ],
        out_shape=[
            jax.ShapeDtypeStruct((3 * HEAD_DIM, count), BF16),
            jax.ShapeDtypeStruct((3 * HEAD_DIM, width), BF16),
        ],
        scratch_shapes=[
            pltpu.VMEM((len(upstream), HEAD_DIM, step), BF16),
            pltpu.VMEM((count, HEAD_DIM), BF16),
            pltpu.VMEM((count, HEAD_DIM), BF16),
            pltpu.VMEM((count, HEAD_DIM), F32),
            pltpu.VMEM((count, HEAD_DIM), F32),
        ],
        compiler_params=pltpu.CompilerParams(vmem_limit_bytes=24 * 2**20),
        cost_estimate=pl.CostEstimate(
            flops=56 * count * count * HEAD_DIM,
            bytes_accessed=16 * HEAD_DIM * count,
            transcendentals=count * count,
        ),
        name="attend_back",
    )(queries, keys, values, *upstream, merged, log, cosine, sine, normed)


def row_copies(place_ref, mine, other, buffer, sems):
    z, core = place_ref[0], place_ref[1]
    size, rows, _ = mine.shape
    copies = []
    for d in range(size):
        for k, (ref, side) in enumerate(((mine, core), (other, 1 - core))):
            target = buffer.at[z ^ d, pl.ds(pl.multiple_of(side * rows, 16), rows), :]
            copies.append(pltpu.make_async_copy(ref.at[d], target, sems.at[d, k]))
    return copies


def unit_of(values):
    centre = values - jnp.mean(values, axis=-1, keepdims=True)
    inverse = lax.rsqrt(jnp.mean(centre * centre, axis=-1, keepdims=True) + EPS)
    return centre * inverse, inverse


def turn(values, cosine, sine):
    first, second = values[:HALF], values[HALF:]
    return jnp.concatenate([first * cosine - second * sine, second * cosine + first * sine], axis=0)


def project_kernel(
    place_ref, pair_ref, other_ref, gain_ref, cos_ref, sin_ref, mine_ref, theirs_ref,
    normed_ref, q_ref, kt_ref, vt_ref, buffer, weight, sems,
):
    index = pl.program_id(0)
    part = q_ref.shape[0]
    size = buffer.shape[0]

    @pl.when(index == 0)
    def _():
        for copy in row_copies(place_ref, mine_ref, theirs_ref, buffer, sems):
            copy.start()

    block = jnp.where(index < 2, pair_ref[...].astype(F32), other_ref[...].astype(F32))
    normed = (unit_of(block)[0] * gain_ref[...]).astype(BF16)
    normed_ref[...] = normed

    @pl.when(index == 0)
    def _():
        for copy in row_copies(place_ref, mine_ref, theirs_ref, buffer, sems):
            copy.wait()
        start = pl.multiple_of(place_ref[1] * 2 * part, 128)
        odd = place_ref[0] & 1 == 1
        for t in range(3):
            both = buffer[:, t * part : (t + 1) * part, pl.ds(start, 2 * part)].reshape(size * part, 2 * part)
            chosen = jnp.where(odd, both[:, part:].astype(F32), both[:, :part].astype(F32))
            weight[:, t * part : (t + 1) * part] = chosen.astype(BF16)

    projected = mul(normed, weight[...])
    turned = projected[:, : 2 * part].T
    cosine, sine = cos_ref[...], sin_ref[...]
    for head in range(part // HEAD_DIM):
        rows = slice(head * HEAD_DIM, (head + 1) * HEAD_DIM)
        queries = turn(turned[rows], cosine, sine).astype(BF16)
        q_ref[rows, :] = (queries.astype(F32) * SCALE).astype(BF16)
        keys = turn(turned[part + head * HEAD_DIM : part + (head + 1) * HEAD_DIM], cosine, sine)
        kt_ref[rows, :] = keys.astype(BF16)
    vt_ref[...] = projected[:, 2 * part :].astype(BF16).T


def project(where, pair, other, gain, cosine, sine, mine, theirs, count):
    width = pair.shape[1]
    size, rows = mine.shape[0], 2 * mine.shape[1]
    part = width // size
    total = size * count
    anywhere = pl.BlockSpec(memory_space=pl.ANY)
    columns = pl.BlockSpec((part, count), lambda i: (0, i))
    return pl.pallas_call(
        project_kernel,
        grid=(size,),
        in_specs=[
            pl.BlockSpec(memory_space=pltpu.SMEM),
            pl.BlockSpec((count, width), lambda i: (jnp.minimum(i, 1), 0)),
            pl.BlockSpec((count, width), lambda i: (jnp.maximum(i - 2, 0), 0)),
            pl.BlockSpec((1, width), lambda i: (0, 0)),
            pl.BlockSpec((HALF, count), lambda i: (0, i)),
            pl.BlockSpec((HALF, count), lambda i: (0, i)),
            anywhere,
            anywhere,
        ],
        out_specs=[
            pl.BlockSpec((count, width), lambda i: (i, 0)),
            columns,
            columns,
            columns,
        ],
        out_shape=[
            jax.ShapeDtypeStruct((total, width), BF16),
            jax.ShapeDtypeStruct((part, total), BF16),
            jax.ShapeDtypeStruct((part, total), BF16),
            jax.ShapeDtypeStruct((part, total), BF16),
        ],
        scratch_shapes=[
            pltpu.VMEM((size, rows, width), BF16),
            pltpu.VMEM((width, 3 * part), BF16),
            pltpu.SemaphoreType.DMA((size, 2)),
        ],
        compiler_params=pltpu.CompilerParams(vmem_limit_bytes=48 * 2**20),
        cost_estimate=pl.CostEstimate(flops=8 * 10**9, bytes_accessed=20 * 10**6, transcendentals=0),
        name="project",
    )(where, pair, other, gain, cosine, sine, mine, theirs)


def forward_back_kernel(
    place_ref, m0_ref, m1_ref, m2_ref, m3_ref, tokens_ref, up_ref, gain_ref, mine_ref, theirs_ref,
    result_ref, state_back_ref, low_ref, normed_ref, active_ref, inner_back_ref, b0_ref, b1_ref, b2_ref, b3_ref,
    buffer, sems,
):
    part, width = m0_ref.shape[0], tokens_ref.shape[1]
    size = buffer.shape[0]
    hidden = active_ref.shape[1]
    z = place_ref[0]

    @pl.when(pl.program_id(0) == 0)
    def _():
        copies = row_copies(place_ref, mine_ref, theirs_ref, buffer, sems)
        for copy in copies:
            copy.start()
        for copy in copies:
            copy.wait()

    expand = [buffer[:, (1 + t) * part : (2 + t) * part, :].reshape(width, width) for t in range(3)]
    contract = buffer[:, 4 * part : 4 * part + hidden // size, :].reshape(hidden, width)
    gain = gain_ref[...]

    state = tokens_ref[...].astype(F32)
    for k, ref in enumerate((m0_ref, m1_ref, m2_ref, m3_ref)):
        state = state + mul(ref[...], buffer[z ^ k, :part, :], TN)
    unit, inverse = unit_of(state)
    normed = (unit * gain).astype(BF16)
    normed_ref[...] = normed
    inner = jnp.concatenate([mul(normed, weight) for weight in expand], axis=1)
    first, second = inner[:, :hidden], inner[:, hidden:]
    chance = 0.5 + 0.5 * lax.erf(first * math.sqrt(0.5))
    gated = first * chance
    slope = chance + first * (jnp.exp(-0.5 * first * first) * (1.0 / math.sqrt(2.0 * math.pi)))
    active = (gated * second).astype(BF16)
    active_ref[...] = active
    result_ref[...] = (state + mul(active, contract)).astype(BF16)

    upstream = up_ref[...]
    active_back = mul(upstream, contract, NT).astype(BF16).astype(F32)
    inner_back = jnp.concatenate(
        [(active_back * second * slope).astype(BF16), (active_back * gated).astype(BF16)], axis=1
    )
    inner_back_ref[...] = inner_back
    normed_back = mul(inner_back[:, :width], expand[0], NT)
    normed_back = normed_back + mul(inner_back[:, width : 2 * width], expand[1], NT)
    normed_back = normed_back + mul(inner_back[:, 2 * width :], expand[2], NT)
    scaled = normed_back * gain
    mean = jnp.mean(scaled, axis=-1, keepdims=True)
    lean = jnp.mean(scaled * unit, axis=-1, keepdims=True)
    state_back = upstream.astype(F32) + inverse * (scaled - mean - unit * lean)
    state_back_ref[...] = state_back
    low = state_back.astype(BF16)
    low_ref[...] = low
    for k, ref in enumerate((b0_ref, b1_ref, b2_ref, b3_ref)):
        ref[...] = mul(buffer[z ^ k, :part, :], low, NT).astype(BF16)


def forward_back(where, merged, tokens, upstream, gain, sides, hidden, step=256):
    count, width = tokens.shape
    size, rows = sides[0].shape[0], 2 * sides[0].shape[1]
    part = width // size
    anywhere = pl.BlockSpec(memory_space=pl.ANY)
    columns = pl.BlockSpec((part, step), lambda i: (0, i))

    def some(lanes):
        return pl.BlockSpec((step, lanes), lambda i: (i, 0))

    lanes = [width, width, width, width, hidden, 2 * hidden]
    kinds = [BF16, F32, BF16, BF16, BF16, BF16]
    return pl.pallas_call(
        forward_back_kernel,
        grid=(count // step,),
        in_specs=[pl.BlockSpec(memory_space=pltpu.SMEM)]
        + [columns] * size
        + [some(width), some(width), pl.BlockSpec((1, width), lambda i: (0, 0))]
        + [anywhere] * len(sides),
        out_specs=[some(n) for n in lanes] + [columns] * size,
        out_shape=[jax.ShapeDtypeStruct((count, n), kind) for n, kind in zip(lanes, kinds)]
        + [jax.ShapeDtypeStruct((part, count), BF16)] * size,
        scratch_shapes=[pltpu.VMEM((size, rows, width), BF16), pltpu.SemaphoreType.DMA((size, 2))],
        compiler_params=pltpu.CompilerParams(vmem_limit_bytes=26 * 2**20),
        cost_estimate=pl.CostEstimate(flops=14 * 10**9, bytes_accessed=20 * 10**6, transcendentals=0),
        name="forward_back",
    )(where, *merged, tokens, upstream, gain, *sides)


def gradients_kernel(
    place_ref, m0_ref, m1_ref, m2_ref, m3_ref, up_ref, low_ref, normed_ref, active_ref, inner_back_ref,
    kept_ref, sent_ref,
):
    z, core = place_ref[0], place_ref[1]
    part, width = m0_ref.shape[0], up_ref.shape[1]
    size, rows, lanes = kept_ref.shape
    held = active_ref.shape[1] // size
    for grads_ref, side in ((sent_ref, 1 - core), (kept_ref, core)):
        start = pl.multiple_of(side * lanes, 128)
        low = low_ref[:, pl.ds(start, lanes)]
        for k, ref in enumerate((m0_ref, m1_ref, m2_ref, m3_ref)):
            grads_ref[z ^ k, :part, :] = mul(ref[...], low).astype(BF16)
        normed = normed_ref[...]
        for t in range(3):
            grad = mul(normed, inner_back_ref[:, pl.ds(t * width + start, lanes)], TN)
            grads_ref[:, (1 + t) * part : (2 + t) * part, :] = grad.astype(BF16).reshape(size, part, lanes)
        grad = mul(active_ref[...], up_ref[:, pl.ds(start, lanes)], TN)
        grads_ref[:, 4 * part : 4 * part + held, :] = grad.astype(BF16).reshape(size, held, lanes)
        if rows > 4 * part + held:
            grads_ref[:, 4 * part + held :, :] = jnp.zeros((size, rows - 4 * part - held, lanes), BF16)


def gradients(where, merged, upstream, low, normed, active, inner_back, rows):
    size = len(merged)
    inside = pl.BlockSpec(memory_space=pltpu.VMEM)
    return pl.pallas_call(
        gradients_kernel,
        in_specs=[pl.BlockSpec(memory_space=pltpu.SMEM)] + [inside] * (size + 5),
        out_specs=[inside] * 2,
        out_shape=[jax.ShapeDtypeStruct((size, rows, upstream.shape[1] // 2), BF16)] * 2,
        compiler_params=pltpu.CompilerParams(vmem_limit_bytes=22 * 2**20),
        cost_estimate=pl.CostEstimate(flops=12 * 10**9, bytes_accessed=12 * 10**6, transcendentals=0),
        name="gradients",
    )(where, *merged, upstream, low, normed, active, inner_back)


def token_kernel(heads, place_ref, *refs):
    size = len(refs[: -9]) // heads
    pieces = refs[: heads * size]
    mine_ref, theirs_ref, tokens_ref, back_ref, gain_ref, grad_ref, parts, buffer, sems = refs[heads * size :]
    z = place_ref[0]
    width = buffer.shape[2]
    part = width // size
    copies = row_copies(place_ref, mine_ref, theirs_ref, buffer, sems)
    for copy in copies:
        copy.start()
    for head in range(heads):
        for k in range(size):
            ref = pieces[head * size + k]
            lines = pl.ds(pl.multiple_of((z ^ k) * part + head * HEAD_DIM, HEAD_DIM), HEAD_DIM)
            for t in range(3):
                parts[t, lines, :] = ref[t * HEAD_DIM : (t + 1) * HEAD_DIM, :]
    for copy in copies:
        copy.wait()
    total = jnp.zeros((width, tokens_ref.shape[0]), F32)
    for t in range(3):
        total = total + mul(buffer[:, t * part : (t + 1) * part, :].reshape(width, width), parts[t])
    unit, inverse = unit_of(tokens_ref[...].astype(F32))
    scaled = total.T * gain_ref[...]
    mean = jnp.mean(scaled, axis=-1, keepdims=True)
    lean = jnp.mean(scaled * unit, axis=-1, keepdims=True)
    grad_ref[...] = back_ref[...] + inverse * (scaled - mean - unit * lean)


def token_back(where, received, mine, theirs, tokens, state_back, gain):
    count, width = tokens.shape
    size, rows = mine.shape[0], 2 * mine.shape[1]
    inside = pl.BlockSpec(memory_space=pltpu.VMEM)
    anywhere = pl.BlockSpec(memory_space=pl.ANY)
    pieces = [piece for rounds in received for piece in rounds]
    return pl.pallas_call(
        functools.partial(token_kernel, len(received)),
        in_specs=[pl.BlockSpec(memory_space=pltpu.SMEM)]
        + [inside] * len(pieces)
        + [anywhere] * 2
        + [inside] * 3,
        out_specs=inside,
        out_shape=jax.ShapeDtypeStruct((count, width), F32),
        scratch_shapes=[
            pltpu.VMEM((3, width, count), BF16),
            pltpu.VMEM((size, rows, width), BF16),
            pltpu.SemaphoreType.DMA((size, 2)),
        ],
        compiler_params=pltpu.CompilerParams(vmem_limit_bytes=18 * 2**20),
        cost_estimate=pl.CostEstimate(flops=5 * 10**9, bytes_accessed=12 * 10**6, transcendentals=0),
        name="token_back",
    )(where, *pieces, mine, theirs, tokens, state_back, gain)


def after(values, *others):
    return lax.optimization_barrier((values, others))[0]


def swap(values, axis, size, offset):
    return lax.ppermute(values, axis, [(i, i ^ offset) for i in range(size)])


def exchange(pieces, size):
    return [pieces[0]] + [swap(pieces[d], "fsdp", size, d) for d in range(1, size)]


def column(values, size, ranks, pairs):
    full = [
        (z * ranks + r, to * ranks + (r & ~1) + core)
        for z in range(size)
        for r in range(ranks)
        for to, core in pairs(z, r & 1)
    ]
    return lax.ppermute(values, ("fsdp", "rep"), full)


def collect(own, home, size, ranks, early):
    first = column(
        own, size, ranks, lambda z, c: [(z ^ 1, c) if c == z >> 1 else (z ^ 2, 1 - c)]
    )
    second = column(first, size, ranks, lambda z, c: [] if c == z >> 1 else [(z ^ 1, c)])
    low = jnp.where(home, own, first)
    high = jnp.where(home, first, second)
    pair, early = after((jnp.concatenate([low, high], axis=0), early))
    other = swap(pair, "rep", ranks, 1)
    return pair, other, first, second, early


def trade_out(pieces, size, ranks, rounds=None):
    def round_of(k):
        return lambda z, c: [((2 * c + (z & 1)) ^ k, z >> 1)]

    return [column(pieces[k], size, ranks, round_of(k)) for k in rounds or range(size)]


def trade_back(pieces, size, ranks):
    def round_of(k):
        return lambda z, c: [(2 * c + ((z ^ k) & 1), (z ^ k) >> 1)]

    return [column(pieces[k], size, ranks, round_of(k)) for k in range(size)]


def pick(blocks, index):
    return lax.dynamic_index_in_dim(blocks, index, 0, keepdims=False)


def reorder(blocks, z, size):
    return jnp.stack([pick(blocks, z ^ j) for j in range(size)])


def far(ranks):
    bits = []
    bit = 2
    while bit < ranks:
        bits.append(bit)
        bit *= 2
    return bits


def stage_bit(core, ranks, stage):
    bits = far(ranks)
    return bits[stage] if core == 0 else bits[len(bits) - 1 - stage]


def stage_swap(values, ranks, stage):
    return lax.ppermute(values, "rep", [(i, i ^ stage_bit(i & 1, ranks, stage)) for i in range(ranks)])


def stage_upper(r, ranks, stage):
    bit = jnp.where(r & 1 == 0, stage_bit(0, ranks, stage), stage_bit(1, ranks, stage))
    return r & bit != 0


def place(r, ranks):
    stages = len(far(ranks))
    total = jnp.where(r & 1 != 0, 1 << stages, 0)
    for stage in range(stages):
        total = total + jnp.where(stage_upper(r, ranks, stage), 1 << stage, 0)
    return total


def join(mine, other, upper):
    return jnp.concatenate([jnp.where(upper, other, mine), jnp.where(upper, mine, other)], axis=1)


def cut(values, upper):
    half = values.shape[1] // 2
    mine = jnp.where(upper, half, 0)
    sent = lax.dynamic_slice_in_dim(values, half - mine, half, 1)
    return sent, lax.dynamic_slice_in_dim(values, mine, half, 1)


def add(one, two):
    return (one.astype(F32) + two.astype(F32)).astype(BF16)


def grow(values, r, ranks, stages):
    for stage in stages:
        values = join(values, stage_swap(values, ranks, stage), stage_upper(r, ranks, stage))
    return values


def grow_flat(values, r, ranks, stages):
    for stage in stages:
        other = stage_swap(values, ranks, stage)
        upper = stage_upper(r, ranks, stage)
        values = jnp.concatenate(
            [jnp.where(upper, other, values), jnp.where(upper, values, other)], axis=0
        )
    return values


def shrink(values, r, ranks, stages):
    for stage in stages:
        sent, kept = cut(values, stage_upper(r, ranks, stage))
        values = add(kept, stage_swap(sent, ranks, stage))
    return values


def halves(values):
    middle = values.shape[-1] // 2
    return [values[..., :middle], values[..., middle:]]


def split_rows(shard, r, ranks):
    rows = shard.shape[0] // ranks
    return lax.dynamic_slice_in_dim(shard, place(r, ranks) * rows, rows, 0)


def finish_kernel(
    place_ref, mine_ref, other_ref, into_ref, expand_ref, gain_a_ref, gain_b_ref,
    into_sum_ref, gain_a_sum_ref, out_sum_ref, expand_sum_ref, gain_b_sum_ref, contract_sum_ref,
):
    first = place_ref[1] == 0
    part, width = out_sum_ref.shape
    held = contract_sum_ref.shape[0]
    pieces = mine_ref.shape[0]
    lines = 3 * part // pieces

    def gathered(start):
        rows = mine_ref.shape[1] if start else lines
        sides = []
        for one, two in ((mine_ref, other_ref), (other_ref, mine_ref)):
            blocks = [
                jnp.where(first, one[p, start:rows].astype(F32), two[p, start:rows].astype(F32))
                for p in range(pieces)
            ]
            sides.append(jnp.concatenate(blocks, axis=0))
        return sides

    blocks = [side[:, k * part : (k + 1) * part].T for side in gathered(0) for k in range(2)]
    total = jnp.zeros((part, 1), F32)
    for t in range(3):
        row = jnp.concatenate([block[:, t * part : (t + 1) * part] for block in blocks], axis=1)
        into_sum_ref[:, t * width : (t + 1) * width] = row
        weight = into_ref[:, t * width : (t + 1) * width].astype(F32)
        total = total + jnp.sum(row * weight, axis=1, keepdims=True)
    gain_a_sum_ref[...] = total.T / gain_a_ref[...].astype(F32)

    grads = jnp.concatenate(gathered(lines), axis=1)
    out_sum_ref[...] = grads[:part]
    total = jnp.zeros((part, 1), F32)
    for t in range(3):
        row = grads[(1 + t) * part : (2 + t) * part]
        expand_sum_ref[:, t * width : (t + 1) * width] = row
        weight = expand_ref[:, t * width : (t + 1) * width].astype(F32)
        total = total + jnp.sum(row * weight, axis=1, keepdims=True)
    gain_b_sum_ref[...] = total.T / gain_b_ref[...].astype(F32)
    contract_sum_ref[...] = grads[4 * part : 4 * part + held]


def finish(where, mine, other, projection_in, expansion, gain_a, gain_b, held):
    part, wide = projection_in.shape
    inside = pl.BlockSpec(memory_space=pltpu.VMEM)
    shapes = [(part, wide), (1, part), (part, wide // 3), (part, wide), (1, part), (held, wide // 3)]
    return pl.pallas_call(
        finish_kernel,
        in_specs=[pl.BlockSpec(memory_space=pltpu.SMEM)] + [inside] * 6,
        out_specs=[inside] * 6,
        out_shape=[jax.ShapeDtypeStruct(shape, F32) for shape in shapes],
        compiler_params=pltpu.CompilerParams(vmem_limit_bytes=20 * 2**20),
        name="finish",
    )(where, mine, other, projection_in, expansion, gain_a[None], gain_b[None])


def local(size, ranks, tokens, gain_a, projection_in, attention_out, gain_b, expansion, contraction, cotangent):
    z = lax.axis_index("fsdp")
    r = lax.axis_index("rep")
    core = r & 1
    group = 2 * core + (z & 1)
    home = core == z >> 1
    own = tokens[0]
    count, width = own.shape
    part = width // size
    hidden = contraction.shape[0]
    heads = HEADS // size

    stages = list(range(len(far(ranks))))
    where = jnp.stack([z, core]).astype(jnp.int32)
    columns = [projection_in[:, t * width : (t + 1) * width] for t in range(3)]
    piece = split_rows(jnp.concatenate(columns, axis=0), r, ranks)
    rows = piece.shape[0]
    gains = jnp.pad(jnp.concatenate([gain_a, gain_b])[None], ((0, 7), (0, width - 2 * part)))
    pieces = jnp.stack(exchange([jnp.concatenate([piece, gains], axis=0)] * size, size))
    gains = reorder(pieces[:, rows, : 2 * part], z, size).astype(F32)
    gain_one = gains[:, :part].reshape(1, width)
    gain_two = gains[:, part:].reshape(1, width)
    freqs = THETA ** (-(jnp.arange(HALF, dtype=F32) * (2.0 / HEAD_DIM)))
    places = jnp.concatenate([(group ^ d) * count + jnp.arange(count, dtype=jnp.int32) for d in range(size)])
    angles = freqs[:, None] * places.astype(F32)[None, :]
    early = (gain_one, gain_two, jnp.cos(angles), jnp.sin(angles))
    pair, other, first, second, early = collect(own, home, size, ranks, early)
    gain_one, gain_two, cosine, sine = early
    into = grow(pieces[:, :rows], r, ranks, stages[:-1])
    into = grow(after(into, first), r, ranks, stages[-1:])
    into_other = swap(into, "rep", ranks, 1)
    normed, queries, keys, values = project(
        where, pair, other, gain_one, cosine, sine, into, into_other, count
    )

    columns = [expansion[:, t * width : (t + 1) * width] for t in range(3)]
    stacked = jnp.concatenate([attention_out] + columns + [contraction], axis=0)
    pad = -stacked.shape[0] % max(32, 8 * ranks)
    stacked = jnp.concatenate([stacked, jnp.zeros((pad, width), BF16)], axis=0)
    rest = exchange([split_rows(after(stacked, second), r, ranks)] * size, size)
    merged = []
    logs = []
    for head in range(heads):
        out, log = attend(head, queries, after(keys, *merged[-1:]), values)
        merged.append(out)
        logs.append(log)
    rest = jnp.stack(after(rest, merged[0]))
    for stage in stages[:-1]:
        rest = join(rest, after(stage_swap(rest, ranks, stage), merged[-1]), stage_upper(r, ranks, stage))
    own_merged = jnp.concatenate(merged, axis=0)
    merged = trade_out([own_merged[:, d * count : (d + 1) * count] for d in range(size)], size, ranks)
    coming = after(stage_swap(rest, ranks, stages[-1]), *merged)
    rest = join(rest, coming, stage_upper(r, ranks, stages[-1]))
    rest_other = swap(rest, "rep", ranks, 1)
    upstream = cotangent[0]
    block_output, state_back, state_low, normed_two, active, inner_back, *merged_back = forward_back(
        where, merged, own, upstream, gain_two, [rest, rest_other], size * hidden
    )
    arrived = trade_back(merged_back, size, ranks)
    own_upstream = arrived

    kept, sent = gradients(
        where, merged, upstream, state_low, normed_two, active, inner_back, stacked.shape[0]
    )
    sent = after(sent, *arrived[:3])
    other = swap(sent, "rep", ranks, 1)
    upper = stage_upper(r, ranks, stages[-1])
    (sent, kept), (other_sent, other) = cut(kept, upper), cut(other, upper)
    sent = add(sent, other_sent)

    turned_backs = []
    weight_backs = []
    received = []
    ahead = [sent]
    for head in range(heads):
        grad, weight_grad = attend_back(
            head, queries, keys, values, after(own_upstream, *ahead), own_merged, logs[head],
            cosine, sine, normed,
        )
        turned_backs.append(grad)
        weight_backs.append(weight_grad.reshape(3, HEAD_DIM, width))
        received.append(trade_out([grad[:, d * count : (d + 1) * count] for d in range(size)], size, ranks))
        if head == 0:
            coming = stage_swap(sent, ranks, stages[-1])
            grads = (kept.astype(F32) + other.astype(F32) + coming.astype(F32)).astype(BF16)
            grads = shrink(grads, r, ranks, stages[-2:0:-1])
            ahead = [grads]
        if head == 1:
            grads = shrink(grads, r, ranks, stages[:1])
            ahead = [grads] + received[0]

    sent, kept = [jnp.stack([pick(grads, bit), pick(grads, bit + 2)]) for bit in (z & 1 ^ 1, z & 1)]
    grads = add(kept, swap(sent, "fsdp", size, 1))
    weight_backs[2], grads = after((weight_backs[2], grads), turned_backs[2], *received[1][:2])
    into_grad = jnp.concatenate([grad[t] for t in range(3) for grad in weight_backs], axis=0)
    later, last = received[1:]
    into_grad = after(shrink(into_grad[None], r, ranks, stages[-1:]), later[2], last[0])
    into_grad = after(shrink(into_grad, r, ranks, stages[-2::-1]), later[3], last[1])[0]
    grads = add(pick(grads, z >> 1), swap(pick(grads, z >> 1 ^ 1), "fsdp", size, 2))
    blocks = exchange(
        [lax.dynamic_slice_in_dim(into_grad, (z ^ d) * part, part, 1) for d in range(size)], size
    )
    even, odd = (blocks[0].astype(F32) + blocks[2].astype(F32)), (blocks[1].astype(F32) + blocks[3].astype(F32))
    low = z & 1 == 0
    flat = jnp.concatenate([jnp.where(low, even, odd), jnp.where(low, odd, even)], axis=1).astype(BF16)
    both = grow_flat(jnp.concatenate([flat, grads], axis=0)[None], r, ranks, stages[:-1])
    both = grow_flat(after(both, *last[2:]), r, ranks, stages[-1:])
    token_grad = token_back(where, received, into, into_other, own, state_back, gain_one)[None]
    both = after(both, token_grad)
    into_sum, gain_one_sum, attention_out_sum, expansion_sum, gain_two_sum, contraction_sum = finish(
        where, both, swap(both, "rep", ranks, 1), projection_in, expansion, gain_a, gain_b, hidden
    )
    return (
        block_output[None],
        token_grad,
        gain_one_sum[0],
        into_sum,
        attention_out_sum,
        gain_two_sum[0],
        expansion_sum,
        contraction_sum,
    )


def solution(mesh):
    tokens, rows, line = P("rep", "fsdp", None), P("fsdp", None), P("fsdp")
    in_specs = (tokens, line, rows, rows, line, rows, rows, tokens)
    out_specs = (tokens, tokens, line, rows, rows, line, rows, rows)
    body = functools.partial(local, mesh.shape["fsdp"], mesh.shape["rep"])
    return jax.shard_map(body, mesh=mesh, in_specs=in_specs, out_specs=out_specs, check_vma=False)
```
